32 devices in a mesh: dp: 8 (over z, y), tensor: 4 (over x, core).
Axes of the slice: x: 2, y: 2, z: 4, core: 2. Of those that a mesh axis runs over, the one named last changes fastest.
Arguments:
- tokens: bfloat16 [4096, 1024], P(('dp', 'tensor')), may hold values from -6 to 6
- lengths: int32 [8, 4], P('dp'), may hold values from 0 to 512, as said below
- cotangent: bfloat16 [4096, 1024], P(('dp', 'tensor')), may hold values from -6 to 6
- pre_gain: bfloat16 [1024], P(('dp', 'tensor')), may hold values from 0.5 to 1.5
- input_weight: bfloat16 [1024, 2, 2048], P('dp', None, 'tensor'), may hold values from -0.1875 to 0.1875
- step_weight: bfloat16 [1024, 32], P('dp', 'tensor'), may hold values from -0.1875 to 0.1875
- state_weight: bfloat16 [1024, 256], P(('dp', 'tensor')), may hold values from -0.1875 to 0.1875
- conv_inner: bfloat16 [4, 2048], P(None, 'tensor'), may hold values from -3 to 3
- conv_inner_bias: bfloat16 [2048], P('tensor'), may hold values from -0.5 to 0.5
- conv_state: bfloat16 [4, 256], P(None, ('dp', 'tensor')), may hold values from -3 to 3
- conv_state_bias: bfloat16 [256], P(('dp', 'tensor')), may hold values from -0.5 to 0.5
- step_bias: bfloat16 [32], P('tensor'), may hold values from -5 to -1
- decay_log: bfloat16 [32], P('tensor'), may hold values from -2 to 1.5
- skip_gain: bfloat16 [32], P('tensor'), may hold values from 0.5 to 1.5
- norm_gain: bfloat16 [2048], P('tensor'), may hold values from 0.5 to 1.5
- output_weight: bfloat16 [2048, 1024], P('tensor', 'dp'), may hold values from -0.125 to 0.125
Outputs:
- block_out: bfloat16 [4096, 1024], P(('dp', 'tensor'))
- tokens_grad: float32 [4096, 1024], P(('dp', 'tensor'))
- pre_gain_grad: float32 [1024], P(('dp', 'tensor'))
- input_weight_grad: float32 [1024, 2, 2048], P('dp', None, 'tensor')
- step_weight_grad: float32 [1024, 32], P('dp', 'tensor')
- state_weight_grad: float32 [1024, 256], P(('dp', 'tensor'))
- conv_inner_grad: float32 [4, 2048], P(None, 'tensor')
- conv_inner_bias_grad: float32 [2048], P('tensor')
- conv_state_grad: float32 [4, 256], P(None, ('dp', 'tensor'))
- conv_state_bias_grad: float32 [256], P(('dp', 'tensor'))
- step_bias_grad: float32 [32], P('tensor')
- decay_log_grad: float32 [32], P('tensor')
- skip_gain_grad: float32 [32], P('tensor')
- norm_gain_grad: float32 [2048], P('tensor')
- output_weight_grad: float32 [2048, 1024], P('tensor', 'dp')
The draws below stay inside these ranges and needn't reach their ends.
Inputs may be any that keep to these rules, and one draw needn't show every extreme that they name: Row g lists the lengths of the 4 sequences packed in order from the start of group g; empty slots are 0, the lengths of a row add up to at most 512, and the rows after them are padding.
All inputs are finite; a program needn't handle non-finite values.
Results may differ from the reference program's by a relative error of at most 0.0095.
Values may be sent and summed in bfloat16 or wider, within the bound.
No kernel may reach another device: no remote copies, remote signals or barrier semaphores. Data moves between devices by JAX's collectives and lax.ppermute only.
A program may use at most 128 MiB of HBM per device.

```python
import jax
import jax.numpy as jnp
from jax import lax

D = 1024
HEADS = 32
STATE = 128
CONV = 4
SPAN = 256
SLOTS = 4
ROWS = 512
INNER = 2048
TOKENS = 4096
N_DP = 8


def draw_lengths(key, part):
    key = jax.random.fold_in(key, 11)
    first_key, second_key, third_key = jax.random.split(key, 3)
    small_cap = max(ROWS // 32, 1)
    counts = jax.random.randint(first_key, (N_DP,), ROWS - ROWS // 8 + 1, ROWS + 1)
    smaller = jax.random.randint(second_key, (N_DP, SLOTS - 1), 0, small_cap + 1)
    full_group = jax.random.randint(third_key, (), 0, N_DP)
    is_full = jnp.arange(N_DP) == full_group
    counts = jnp.where(is_full, ROWS, counts)
    smaller = jnp.where(is_full[:, None], 0, smaller)
    longest = counts - jnp.sum(smaller, axis=1)
    return jnp.concatenate([smaller[:, :1], longest[:, None], smaller[:, 1:]], axis=1).astype(jnp.int32)


def levels(own_key, dims, shards, low, high):
    def one(dim, blocks):
        heights = jax.random.uniform(jax.random.fold_in(jax.random.fold_in(own_key, 6), dim), (blocks,), jnp.float32, low / len(shards), high / len(shards))
        return jnp.repeat(jnp.exp(heights), dims[dim] // blocks).reshape((-1,) + (1,) * (len(dims) - dim - 1))

    gain = one(*shards[0])
    for cut in shards[1:]:
        gain = gain * one(*cut)
    return gain


def noise(rng, dims, width, bound, cuts=(), kind=jnp.bfloat16):
    values = jax.random.normal(rng, dims, jnp.float32) * width
    if len(cuts) > 0:
        values = levels(rng, dims, cuts, -0.22, 0.18) * values
    return jnp.clip(values, min=-bound, max=bound).astype(kind)


def setup_inputs(seed: int = 0) -> dict:
    key_of = jax.random.split(jax.random.key(seed), 17)
    return {
        "tokens": noise(key_of[0], (TOKENS, D), 1.0, 6.0, ((0, 32),)),
        "lengths": draw_lengths(jax.random.fold_in(key_of[16], 71), 0),
        "cotangent": noise(key_of[2], (TOKENS, D), 1.0, 6.0, ((0, 32),)),
        "pre_gain": jnp.clip(1.0 + 0.1 * jax.random.normal(key_of[3], (D,), jnp.float32), 0.5, 1.5).astype(jnp.bfloat16),
        "input_weight": noise(key_of[4], (D, 2, INNER), D ** -0.5, 0.1875, ((0, 8), (2, 4))),
        "step_weight": noise(key_of[5], (D, HEADS), D ** -0.5, 0.1875, ((0, 8), (1, 4))),
        "state_weight": noise(key_of[6], (D, 2 * STATE), D ** -0.5, 0.1875, ((0, 32),)),
        "conv_inner": noise(key_of[7], (CONV, INNER), CONV ** -0.5, 3.0, ((1, 4),)),
        "conv_inner_bias": jnp.clip(jax.random.uniform(key_of[8], (INNER,), jnp.float32, -0.5, 0.5) * levels(key_of[8], (INNER,), ((0, 4),), -0.4, 0.0), -0.5, 0.5).astype(jnp.bfloat16),
        "conv_state": noise(key_of[9], (CONV, 2 * STATE), CONV ** -0.5, 3.0, ((1, 32),)),
        "conv_state_bias": jnp.clip(jax.random.uniform(key_of[10], (2 * STATE,), jnp.float32, -0.5, 0.5) * levels(key_of[10], (2 * STATE,), ((0, 32),), -0.4, 0.0), -0.5, 0.5).astype(jnp.bfloat16),
        "step_bias": jnp.clip(-5.0 + 4.0 * jax.random.uniform(key_of[11], (HEADS,), jnp.float32) ** levels(key_of[11], (HEADS,), ((0, 4),), -0.2, 0.2), -5.0, -1.0).astype(jnp.bfloat16),
        "decay_log": jnp.clip(-2.0 + 3.5 * jax.random.uniform(key_of[12], (HEADS,), jnp.float32) ** levels(key_of[12], (HEADS,), ((0, 4),), -0.2, 0.2), -2.0, 1.5).astype(jnp.bfloat16),
        "skip_gain": jnp.clip(0.5 + 1.0 * jax.random.uniform(key_of[13], (HEADS,), jnp.float32) ** levels(key_of[13], (HEADS,), ((0, 4),), -0.2, 0.2), 0.5, 1.5).astype(jnp.bfloat16),
        "norm_gain": jnp.clip(1.0 + 0.1 * jax.random.normal(key_of[14], (INNER,), jnp.float32), 0.5, 1.5).astype(jnp.bfloat16),
        "output_weight": noise(key_of[15], (INNER, D), INNER ** -0.5, 0.125, ((0, 4), (1, 8))),
    }


@jax.custom_vjp
def low(v):
    return lax.optimization_barrier(v.astype(jnp.bfloat16)).astype(jnp.float32)

@jax.custom_vjp
def low_back(v):
    return v

def low_keep(v):
    return (low(v), None)

def low_pass(kept, grad):
    return (grad,)

def back_keep(v):
    return (v, None)

def back_low(kept, grad):
    return (low(grad),)
low.defvjp(low_keep, low_pass)
low_back.defvjp(back_keep, back_low)
epsilon = 1e-05
highest = lax.Precision.HIGHEST

def segments_of(seq_lengths, row_count):
    boundary = jnp.cumsum(seq_lengths).astype(jnp.int32)
    places = jnp.arange(row_count, dtype=jnp.int32)
    segment = lax.optimization_barrier(jnp.sum((places[:, None] >= boundary[None, :]).astype(jnp.int32), axis=1)).astype(jnp.int32)
    valid_rows = (places < boundary[-1]).astype(jnp.float32)
    return (segment, valid_rows)

def causal_conv(signal, kernel, offset, segment):
    row_count = signal.shape[0]
    taps_count = kernel.shape[0]
    running = offset[None, :] + jnp.zeros_like(signal)
    for tap_index in range(taps_count):
        shift_by = taps_count - 1 - tap_index
        if shift_by == 0:
            shifted = signal
            shifted_segment = segment
        else:
            shifted = jnp.concatenate([jnp.zeros((shift_by, signal.shape[1]), signal.dtype), signal[:row_count - shift_by]], axis=0)
            shifted_segment = jnp.concatenate([jnp.full((shift_by,), -1, jnp.int32), segment[:row_count - shift_by]], axis=0)
        same_doc = (shifted_segment == segment).astype(signal.dtype)
        running = running + kernel[tap_index][None, :] * shifted * same_doc[:, None]
    return running

def ssd_mixer(inner_raw, state_raw, step_raw, conv_inner, conv_inner_bias, conv_state, conv_state_bias, step_bias, decay_log, skip_gain, segment, block_rows):
    row_count = inner_raw.shape[0]
    head_count = step_raw.shape[1]
    head_width = inner_raw.shape[1] // head_count
    state_width = state_raw.shape[1] // 2
    block_count = row_count // block_rows
    inner_act = jax.nn.silu(causal_conv(inner_raw, conv_inner, conv_inner_bias, segment))
    state_act = jax.nn.silu(causal_conv(state_raw, conv_state, conv_state_bias, segment))
    step_size = jax.nn.softplus(step_raw + step_bias[None, :])
    log_decay = -step_size * jnp.exp(decay_log)[None, :]
    positions = jnp.arange(block_rows, dtype=jnp.int32)
    causal_mask = positions[:, None] >= positions[None, :]

    def advance(carried_in, block_in):
        state_held, last_before = carried_in
        inner_block, input_block, output_block, decay_block, step_block, segment_block = block_in
        cumulative = jnp.cumsum(decay_block, axis=0)
        same_doc = (segment_block[:, None] == segment_block[None, :]) & causal_mask
        spread_log = jnp.where(same_doc[:, :, None], cumulative[:, None, :] - cumulative[None, :, :], 0.0)
        decay_table = jnp.exp(spread_log) * same_doc[:, :, None].astype(jnp.float32)
        contact = jnp.dot(output_block, input_block.T, precision=highest)
        mixing = contact[:, :, None] * decay_table * step_block[None, :, :]
        local_part = jnp.einsum('ijh,jhp->ihp', mixing, inner_block, precision=highest)
        continued = (segment_block == last_before).astype(jnp.float32)
        from_state = jnp.einsum('in,hnp->ihp', output_block, state_held, precision=highest)
        from_state = from_state * (jnp.exp(cumulative) * continued[:, None])[:, :, None]
        final_doc = segment_block[block_rows - 1]
        in_final = (segment_block == final_doc).astype(jnp.float32)
        to_end = jnp.exp(cumulative[block_rows - 1][None, :] - cumulative) * step_block * in_final[:, None]
        fresh_state = jnp.einsum('jn,jhp->hnp', input_block, inner_block * to_end[:, :, None], precision=highest)
        kept_share = (final_doc == last_before).astype(jnp.float32)
        state_held = state_held * (jnp.exp(cumulative[block_rows - 1]) * kept_share)[:, None, None] + fresh_state
        return ((state_held, final_doc), local_part + from_state)
    start_state = (jnp.zeros((head_count, state_width, head_width), jnp.float32), jnp.array(-1, dtype=jnp.int32))
    pieces = (inner_act.reshape(block_count, block_rows, head_count, head_width), state_act[:, :state_width].reshape(block_count, block_rows, state_width), state_act[:, state_width:].reshape(block_count, block_rows, state_width), log_decay.reshape(block_count, block_rows, head_count), step_size.reshape(block_count, block_rows, head_count), segment.reshape(block_count, block_rows))
    _, outputs = lax.scan(advance, start_state, pieces)
    result = outputs.reshape(row_count, head_count, head_width) + skip_gain[None, :, None] * inner_act.reshape(row_count, head_count, head_width)
    return result.reshape(row_count, head_count * head_width)

def group_out(rows_in, seq_lengths, pre_gain, input_weight, step_weight, state_weight, conv_inner, conv_inner_bias, conv_state, conv_state_bias, step_bias, decay_log, skip_gain, norm_gain, output_weight):
    row_count = rows_in.shape[0]
    depth = rows_in.shape[1]
    inner_count = input_weight.shape[2]
    segment, valid_rows = segments_of(seq_lengths, row_count)
    scale_rows = lax.rsqrt(lax.optimization_barrier(jnp.mean(rows_in * rows_in, axis=1)) + epsilon)
    normed = low(rows_in * scale_rows[:, None] * pre_gain[None, :])
    projected = jnp.dot(normed, input_weight.reshape(depth, 2 * inner_count), precision=highest)
    gate = low_back(projected[:, :inner_count])
    inner_raw = low_back(projected[:, inner_count:])
    step_raw = jnp.dot(normed, step_weight, precision=highest)
    state_raw = jnp.dot(normed, state_weight, precision=highest)
    mixed = ssd_mixer(inner_raw, state_raw, step_raw, conv_inner, conv_inner_bias, conv_state, conv_state_bias, step_bias, decay_log, skip_gain, segment, SPAN)
    gated = mixed * jax.nn.silu(gate)
    norm_scale = lax.rsqrt(lax.optimization_barrier(jnp.mean(gated * gated, axis=1)) + epsilon)
    normalized = low(gated * norm_scale[:, None] * norm_gain[None, :] * valid_rows[:, None])
    return rows_in + jnp.dot(normalized, output_weight, precision=highest)

def reference(tokens, lengths, cotangent, pre_gain, input_weight, step_weight, state_weight, conv_inner, conv_inner_bias, conv_state, conv_state_bias, step_bias, decay_log, skip_gain, norm_gain, output_weight):
    weights = tuple((member.astype(jnp.float32) for member in (pre_gain, input_weight, step_weight, state_weight, conv_inner, conv_inner_bias, conv_state, conv_state_bias, step_bias, decay_log, skip_gain, norm_gain, output_weight)))

    def forward(token_float, *weight_list):
        grouped = token_float.reshape(N_DP, ROWS, D)
        group_step = jax.checkpoint(group_out)

        def one_group(counter, member):
            rows_in, seq_lengths = member
            return (counter, group_step(rows_in, seq_lengths, *weight_list))
        _, results = lax.scan(one_group, jnp.zeros((), jnp.int32), (grouped, lengths))
        return results.reshape(TOKENS, D)
    block_float, pull_back = jax.vjp(forward, tokens.astype(jnp.float32), *weights)
    gradients = pull_back(cotangent.astype(jnp.float32))
    return (block_float.astype(jnp.bfloat16), gradients[0], gradients[1], gradients[2], gradients[3], gradients[4], gradients[5], gradients[6], gradients[7], gradients[8], gradients[9], gradients[10], gradients[11], gradients[12], gradients[13])
```

```python
import jax
import jax.numpy as jnp
from jax import lax
from jax.sharding import PartitionSpec as P

SPAN = 256


epsilon = 1e-05
highest = lax.Precision.HIGHEST


def segments_of(seq_lengths, row_count):
    boundary = jnp.cumsum(seq_lengths)
    places = jnp.arange(row_count, dtype=jnp.int32)
    segment = jnp.sum((places[:, None] >= boundary[None, :]).astype(jnp.int32), axis=1)
    valid_rows = (places < boundary[-1]).astype(jnp.float32)
    return (segment, valid_rows)


def causal_conv(signal, kernel, offset, segment):
    row_count = signal.shape[0]
    taps_count = kernel.shape[0]
    running = offset[None, :] + jnp.zeros_like(signal)
    for tap_index in range(taps_count):
        shift_by = taps_count - 1 - tap_index
        if shift_by == 0:
            shifted = signal
            shifted_segment = segment
        else:
            shifted = jnp.concatenate(
                [
                    jnp.zeros((shift_by, signal.shape[1]), signal.dtype),
                    signal[: row_count - shift_by],
                ],
                axis=0,
            )
            shifted_segment = jnp.concatenate(
                [jnp.full((shift_by,), -1, jnp.int32), segment[: row_count - shift_by]], axis=0
            )
        same_doc = (shifted_segment == segment).astype(signal.dtype)
        running = running + kernel[tap_index][None, :] * shifted * same_doc[:, None]
    return running


def ssd_mixer(
    inner_raw,
    state_raw,
    step_raw,
    conv_inner,
    conv_inner_bias,
    conv_state,
    conv_state_bias,
    step_bias,
    decay_log,
    skip_gain,
    segment,
    block_rows,
):
    row_count = inner_raw.shape[0]
    head_count = step_raw.shape[1]
    head_width = inner_raw.shape[1] // head_count
    state_width = state_raw.shape[1] // 2
    block_count = row_count // block_rows
    inner_act = jax.nn.silu(causal_conv(inner_raw, conv_inner, conv_inner_bias, segment))
    state_act = jax.nn.silu(causal_conv(state_raw, conv_state, conv_state_bias, segment))
    step_size = jax.nn.softplus(step_raw + step_bias[None, :])
    log_decay = -step_size * jnp.exp(decay_log)[None, :]
    positions = jnp.arange(block_rows, dtype=jnp.int32)
    causal_mask = positions[:, None] >= positions[None, :]

    def advance(carried_in, block_in):
        state_held, last_before = carried_in
        inner_block, input_block, output_block, decay_block, step_block, segment_block = block_in
        cumulative = jnp.cumsum(decay_block, axis=0)
        same_doc = (segment_block[:, None] == segment_block[None, :]) & causal_mask
        spread_log = jnp.where(
            same_doc[:, :, None], cumulative[:, None, :] - cumulative[None, :, :], 0.0
        )
        decay_table = jnp.exp(spread_log) * same_doc[:, :, None].astype(jnp.float32)
        contact = jnp.dot(output_block, input_block.T, precision=highest)
        mixing = contact[:, :, None] * decay_table * step_block[None, :, :]
        local_part = jnp.einsum("ijh,jhp->ihp", mixing, inner_block, precision=highest)
        continued = (segment_block == last_before).astype(jnp.float32)
        from_state = jnp.einsum("in,hnp->ihp", output_block, state_held, precision=highest)
        from_state = from_state * (jnp.exp(cumulative) * continued[:, None])[:, :, None]
        final_doc = segment_block[block_rows - 1]
        in_final = (segment_block == final_doc).astype(jnp.float32)
        to_end = (
            jnp.exp(cumulative[block_rows - 1][None, :] - cumulative)
            * step_block
            * in_final[:, None]
        )
        fresh_state = jnp.einsum(
            "jn,jhp->hnp", input_block, inner_block * to_end[:, :, None], precision=highest
        )
        kept_share = (final_doc == last_before).astype(jnp.float32)
        state_held = (
            state_held * (jnp.exp(cumulative[block_rows - 1]) * kept_share)[:, None, None]
            + fresh_state
        )
        return ((state_held, final_doc), local_part + from_state)

    start_state = (
        jnp.zeros((head_count, state_width, head_width), jnp.float32),
        jnp.array(-1, dtype=jnp.int32),
    )
    pieces = (
        inner_act.reshape(block_count, block_rows, head_count, head_width),
        state_act[:, :state_width].reshape(block_count, block_rows, state_width),
        state_act[:, state_width:].reshape(block_count, block_rows, state_width),
        log_decay.reshape(block_count, block_rows, head_count),
        step_size.reshape(block_count, block_rows, head_count),
        segment.reshape(block_count, block_rows),
    )
    _, outputs = lax.scan(advance, start_state, pieces)
    result = outputs.reshape(row_count, head_count, head_width) + skip_gain[
        None, :, None
    ] * inner_act.reshape(row_count, head_count, head_width)
    return result.reshape(row_count, head_count * head_width)


def ring_ok(n_dp, n_tensor):
    return n_dp == 8 and n_tensor == 4


ring_order = (0, 2, 4, 6, 7, 5, 3, 1)


def ring_place(index):
    high, low = index // 2, index % 2
    return jnp.where(low == 0, high, 7 - high)


def ring_index(place):
    place = lax.rem(place + 16, 8)
    return jnp.where(place < 4, 2 * place, 2 * (7 - place) + 1)


def ring_send(value, forward):
    pairs = []
    for place in range(8):
        other = (place + (1 if forward else 7)) % 8
        pairs.append((ring_order[place], ring_order[other]))
    return lax.ppermute(value, "dp", pairs)


def ring_gather(value):
    me = ring_place(lax.axis_index("dp"))
    pieces = [(value, ring_index(me))]
    ahead, back = value, value
    for step in range(1, 5):
        ahead = ring_send(ahead, True)
        pieces.append((ahead, ring_index(me - step)))
        if step < 4:
            back = ring_send(back, False)
            pieces.append((back, ring_index(me + step)))
    return pieces


def ring_stack(value):
    pieces = ring_gather(value)
    result = jnp.zeros((8,) + value.shape, value.dtype)
    for piece, index in pieces:
        result = lax.dynamic_update_slice(
            result, piece[None], (index,) + (0,) * value.ndim
        )
    return result


def ring_scatter(parts):
    me = ring_place(lax.axis_index("dp"))

    def own(place):
        return lax.dynamic_index_in_dim(parts, ring_index(place), 0, keepdims=False)

    total = own(me)
    for forward, steps in ((True, 4), (False, 3)):
        sign = 1 if forward else -1
        held = own(me + sign * steps)
        for step in range(1, steps + 1):
            got = ring_send(held.astype(jnp.bfloat16), forward).astype(jnp.float32)
            if step < steps:
                held = got + own(me + sign * (steps - step))
            else:
                total = total + got
    return total


def dp_others(value):
    got = []
    for shift in range(1, 8):
        pairs = [(i, (i + shift) % 8) for i in range(8)]
        got.append(lax.ppermute(value, "dp", pairs))
    return got


def tensor_swap(value, bit):
    return lax.ppermute(value, "tensor", [(i, i ^ bit) for i in range(4)])


def tensor_stack(value):
    me = lax.axis_index("tensor")
    core, across = me % 2, me // 2
    near = tensor_swap(value, 1)
    far = tensor_swap(value, 2)
    far_near = tensor_swap(far, 1)

    def pair(mine, theirs):
        return jnp.where(core == 0, jnp.stack([mine, theirs]), jnp.stack([theirs, mine]))

    here, there = pair(value, near), pair(far, far_near)
    return jnp.where(
        across == 0, jnp.concatenate([here, there]), jnp.concatenate([there, here])
    )


def tensor_scatter(parts):
    me = lax.axis_index("tensor")
    core, across = me % 2, me // 2
    split = parts.reshape((2, 2) + parts.shape[1:])
    give = lax.dynamic_index_in_dim(split, 1 - core, 1, keepdims=False)
    keep = lax.dynamic_index_in_dim(split, core, 1, keepdims=False)
    got = tensor_swap(give, 1)
    half = keep.astype(jnp.float32) + got.astype(jnp.float32)
    give = lax.dynamic_index_in_dim(half, 1 - across, 0, keepdims=False)
    keep = lax.dynamic_index_in_dim(half, across, 0, keepdims=False)
    got = tensor_swap(give.astype(jnp.bfloat16), 2)
    return keep + got.astype(jnp.float32)


def body(
    tokens,
    lengths,
    cotangent,
    pre_gain,
    input_weight,
    step_weight,
    state_weight,
    conv_inner,
    conv_inner_bias,
    conv_state,
    conv_state_bias,
    step_bias,
    decay_log,
    skip_gain,
    norm_gain,
    output_weight,
):
    n_dp, n_tensor = lax.axis_size("dp"), lax.axis_size("tensor")
    fast = ring_ok(n_dp, n_tensor)
    depth = tokens.shape[1]
    states = state_weight.shape[1]
    local_heads = step_weight.shape[1]
    share = state_weight.shape[0]

    def widen(value):
        flat = value.reshape(-1)
        return jnp.pad(flat, (0, -flat.shape[0] % states)).reshape(-1, states)

    shared = jnp.concatenate(
        [
            state_weight,
            widen(step_weight),
            widen(pre_gain),
            widen(conv_state),
            widen(conv_state_bias),
        ],
        axis=0,
    )
    shared = jnp.pad(shared, ((0, -shared.shape[0] % 16), (0, 0)))
    input_flat = input_weight.reshape(input_weight.shape[0], -1)
    if fast:
        rows = tensor_stack(tokens).reshape(-1, depth)
        grad_rows = tensor_stack(cotangent).reshape(-1, depth)
        shared_near = tensor_stack(shared)
        flat_input = ring_stack(input_flat).reshape(depth, -1)
        shared_all = ring_stack(shared_near)
        output_full = ring_stack(output_weight).transpose(1, 0, 2).reshape(-1, depth)
    else:
        rows = lax.all_gather(tokens, "tensor", axis=0, tiled=True)
        grad_rows = lax.all_gather(cotangent, "tensor", axis=0, tiled=True)
        flat_input = lax.all_gather(input_flat, "dp", axis=0, tiled=True)
        shared_all = lax.all_gather(shared, ("dp", "tensor"), axis=0, tiled=True)
        shared_all = shared_all.reshape((n_dp, n_tensor) + shared.shape)
        output_full = lax.all_gather(output_weight, "dp", axis=1, tiled=True)
    state_full = shared_all[:, :, :share].reshape(depth, states)
    at = share
    step_rows = -(-step_weight.size // states)
    step_mine = lax.dynamic_index_in_dim(
        shared_all[:, :, at : at + step_rows], lax.axis_index("tensor"), 1, keepdims=False
    )
    step_full = step_mine.reshape(n_dp, -1)[:, : step_weight.size].reshape(depth, local_heads)
    at += step_rows
    gain_full = shared_all[:, :, at, : pre_gain.size].reshape(depth)
    at += 1
    taps = conv_state.shape[0]
    conv_state_full = shared_all[:, :, at, : conv_state.size]
    conv_state_full = conv_state_full.reshape(n_dp * n_tensor, taps, -1)
    conv_state_full = conv_state_full.transpose(1, 0, 2).reshape(taps, states)
    at += 1
    conv_state_bias_full = shared_all[:, :, at, : conv_state_bias.size].reshape(states)

    all_float = rows.astype(jnp.float32)
    all_scale = lax.rsqrt(jnp.mean(all_float * all_float, axis=1) + epsilon)
    gain_float = gain_full.astype(jnp.float32)
    normed = (all_float * all_scale[:, None] * gain_float[None, :]).astype(jnp.bfloat16)
    token_float = tokens.astype(jnp.float32)
    scale_rows = lax.rsqrt(jnp.mean(token_float * token_float, axis=1) + epsilon)
    row_count = normed.shape[0]
    segment, valid_rows = segments_of(lengths[0], row_count)
    local_inner = input_weight.shape[2]
    projected = jnp.dot(normed, flat_input, preferred_element_type=jnp.float32)
    gate = projected[:, :local_inner]
    inner_raw = projected[:, local_inner:]
    step_raw = jnp.dot(normed, step_full, preferred_element_type=jnp.float32)
    state_raw = jnp.dot(normed, state_full, preferred_element_type=jnp.float32)
    small_params = tuple(
        (
            member.astype(jnp.float32)
            for member in (
                conv_inner,
                conv_inner_bias,
                conv_state_full,
                conv_state_bias_full,
                step_bias,
                decay_log,
                skip_gain,
            )
        )
    )

    def local_mixer(*members):
        return ssd_mixer(*members, segment, SPAN)

    mixed, mixer_back = jax.vjp(local_mixer, inner_raw, state_raw, step_raw, *small_params)
    gate_act = jax.nn.silu(gate)
    gated = mixed * gate_act
    inner_total = local_inner * n_tensor
    norm_float = norm_gain.astype(jnp.float32)
    grad_normalized = jnp.einsum(
        "rd,id->ri", grad_rows, output_full, preferred_element_type=jnp.float32
    )
    masked_grad = grad_normalized * valid_rows[:, None]
    grad_hat = masked_grad * norm_float[None, :]
    both_sums = jnp.stack([jnp.sum(gated * gated, axis=1), jnp.sum(grad_hat * gated, axis=1)])
    if fast:
        both_sums = both_sums + tensor_swap(both_sums, 1)
        both_sums = both_sums + tensor_swap(both_sums, 2)
    else:
        both_sums = lax.psum(both_sums, "tensor")
    square_sum, cross_sum = both_sums[0], both_sums[1]
    norm_scale = lax.rsqrt(square_sum / inner_total + epsilon)
    out_rows = (gated * norm_scale[:, None] * norm_float[None, :] * valid_rows[:, None]).astype(
        jnp.bfloat16
    )
    partial_out = jnp.dot(out_rows, output_full, preferred_element_type=jnp.float32).astype(
        jnp.bfloat16
    )
    if fast:
        mixed_rows = tensor_scatter(partial_out.reshape((n_tensor, -1, depth)))
    else:
        mixed_rows = lax.psum_scatter(
            partial_out, "tensor", scatter_dimension=0, tiled=True
        ).astype(jnp.float32)
    block_out = (token_float + mixed_rows).astype(jnp.bfloat16)
    output_part = jnp.einsum("ri,rd->id", out_rows, grad_rows, preferred_element_type=jnp.float32)
    norm_gain_part = jnp.sum(masked_grad * gated * norm_scale[:, None], axis=0)
    grad_gated = (
        norm_scale[:, None] * grad_hat
        - gated * (norm_scale * norm_scale * norm_scale * cross_sum / inner_total)[:, None]
    )
    grad_mixed = grad_gated * gate_act
    sigmoid_gate = jax.nn.sigmoid(gate)
    grad_gate = grad_gated * mixed * sigmoid_gate * (1.0 + gate * (1.0 - sigmoid_gate))
    (
        grad_inner,
        grad_state,
        grad_step,
        grad_conv_inner,
        grad_conv_inner_bias,
        grad_conv_state,
        grad_conv_state_bias,
        grad_step_bias,
        grad_decay_log,
        grad_skip,
    ) = mixer_back(grad_mixed)
    grad_projected = jnp.concatenate(
        [grad_gate.astype(jnp.bfloat16), grad_inner.astype(jnp.bfloat16)], axis=1
    )
    input_part = jnp.einsum(
        "rd,rc->dc", normed, grad_projected, preferred_element_type=jnp.float32
    )
    normed_float = normed.astype(jnp.float32)
    step_part = jnp.dot(normed_float.T, grad_step, precision=highest)
    state_part = jnp.dot(normed_float.T, grad_state, precision=highest)
    grad_normed = jnp.einsum(
        "rc,dc->rd", grad_projected, flat_input, preferred_element_type=jnp.float32
    )
    grad_normed = grad_normed + jnp.dot(
        grad_step, step_full.astype(jnp.float32).T, precision=highest
    )
    grad_normed = grad_normed + jnp.dot(
        grad_state, state_full.astype(jnp.float32).T, precision=highest
    )
    pre_gain_part = jnp.sum(grad_normed * all_float * all_scale[:, None], axis=0)
    grad_low = grad_normed.astype(jnp.bfloat16)
    if fast:
        grad_local = tensor_scatter(grad_low.reshape((n_tensor, -1, depth)))
    else:
        grad_local = lax.psum_scatter(
            grad_low, "tensor", scatter_dimension=0, tiled=True
        ).astype(jnp.float32)
    grad_scaled = grad_local * gain_float[None, :]
    cubed = scale_rows * scale_rows * scale_rows
    tokens_grad = (
        scale_rows[:, None] * grad_scaled
        - token_float * (cubed * jnp.sum(grad_scaled * token_float, axis=1) / depth)[:, None]
        + cotangent.astype(jnp.float32)
    )

    owners = n_dp * n_tensor

    def lay(value):
        return jnp.pad(value, ((0, 0), (0, states - value.shape[1])))[:, None, :]

    conv_state_owned = grad_conv_state.reshape(taps, owners, -1).transpose(1, 0, 2)
    shared_part = jnp.concatenate(
        [
            state_part.reshape(owners, share, states),
            lay(pre_gain_part.reshape(owners, -1)),
            lay(conv_state_owned.reshape(owners, -1)),
            lay(grad_conv_state_bias.reshape(owners, -1)),
        ],
        axis=1,
    )
    shared_part = jnp.pad(shared_part, ((0, 0), (0, -shared_part.shape[1] % 8), (0, 0)))
    if fast:
        by_tensor = shared_part.reshape((n_dp, n_tensor) + shared_part.shape[1:])
        by_tensor = by_tensor.transpose(1, 0, 2, 3).astype(jnp.bfloat16)
        shared_mine = ring_scatter(tensor_scatter(by_tensor))
        input_grad = ring_scatter(input_part.reshape(n_dp, -1, 2 * local_inner))
        output_grad = ring_scatter(
            output_part.reshape(local_inner, n_dp, -1).transpose(1, 0, 2)
        )
        step_grad = ring_scatter(step_part.reshape(n_dp, -1, local_heads))
    else:
        shared_mine = lax.psum_scatter(
            shared_part, ("dp", "tensor"), scatter_dimension=0, tiled=True
        )[0]
        input_grad = lax.psum_scatter(input_part, "dp", scatter_dimension=0, tiled=True)
        output_grad = lax.psum_scatter(output_part, "dp", scatter_dimension=1, tiled=True)
        step_grad = lax.psum_scatter(step_part, "dp", scatter_dimension=0, tiled=True)
    input_grad = input_grad.reshape(-1, 2, local_inner)
    state_grad = shared_mine[:share]
    pre_gain_grad = shared_mine[share, : depth // owners]
    conv_state_grad = shared_mine[share + 1, : taps * (states // owners)].reshape(taps, -1)
    conv_state_bias_grad = shared_mine[share + 2, : states // owners]

    def row(value):
        return jnp.pad(value, (0, local_inner - value.shape[0]))[None, :]

    sums = jnp.concatenate(
        [
            grad_conv_inner,
            grad_conv_inner_bias[None, :],
            norm_gain_part[None, :],
            row(grad_step_bias),
            row(grad_decay_log),
            row(grad_skip),
        ],
        axis=0,
    )
    if fast:
        for other in dp_others(sums):
            sums = sums + other
    else:
        sums = lax.psum(sums, "dp")
    return (
        block_out,
        tokens_grad,
        pre_gain_grad,
        input_grad,
        step_grad,
        state_grad,
        sums[:taps],
        sums[taps],
        conv_state_grad,
        conv_state_bias_grad,
        sums[taps + 2, :local_heads],
        sums[taps + 3, :local_heads],
        sums[taps + 4, :local_heads],
        sums[taps + 1],
        output_grad,
    )


def solution(mesh):
    in_specs = (
        P(("dp", "tensor"), None),
        P("dp", None),
        P(("dp", "tensor"), None),
        P(("dp", "tensor")),
        P("dp", None, "tensor"),
        P("dp", "tensor"),
        P(("dp", "tensor"), None),
        P(None, "tensor"),
        P("tensor"),
        P(None, ("dp", "tensor")),
        P(("dp", "tensor")),
        P("tensor"),
        P("tensor"),
        P("tensor"),
        P("tensor"),
        P("tensor", "dp"),
    )
    out_specs = (
        P(("dp", "tensor"), None),
        P(("dp", "tensor"), None),
        P(("dp", "tensor")),
        P("dp", None, "tensor"),
        P("dp", "tensor"),
        P(("dp", "tensor"), None),
        P(None, "tensor"),
        P("tensor"),
        P(None, ("dp", "tensor")),
        P(("dp", "tensor")),
        P("tensor"),
        P("tensor"),
        P("tensor"),
        P("tensor"),
        P("tensor", "dp"),
    )
    return jax.shard_map(body, mesh=mesh, in_specs=in_specs, out_specs=out_specs, check_vma=False)
```

```python
import functools

import jax
import jax.numpy as jnp
from jax import lax
from jax.experimental import pallas as pl
from jax.experimental.pallas import tpu as pltpu
from jax.sharding import PartitionSpec as P

epsilon = 1e-05
highest = lax.Precision.HIGHEST
f32 = jnp.float32
bf16 = jnp.bfloat16
span = 256
pad = 8
head_rows = 16
head_width = 64
vmem_bytes = 52 * 1024 * 1024


def mm(a, b, over=(1, 0)):
    dims = (((over[0],), (over[1],)), ((), ()))
    return lax.dot_general(a, b, dims, preferred_element_type=f32)


def mm_exact(a, b, over=(1, 0)):
    dims = (((over[0],), (over[1],)), ((), ()))
    return lax.dot_general(a, b, dims, preferred_element_type=f32, precision=highest)


def sigmoid(v):
    return 1.0 / (1.0 + jnp.exp(-v))


def ends_of(lengths_ref):
    ends, total = [], None
    for slot in range(lengths_ref.shape[1]):
        here = lengths_ref[0, slot]
        total = here if total is None else total + here
        ends.append(total)
    return ends


def segment_of(places, ends):
    segment = jnp.zeros(places.shape, jnp.int32)
    for end in ends:
        segment = segment + jnp.where(places >= end, 1, 0)
    return segment


def iota(shape, dim):
    return lax.broadcasted_iota(jnp.int32, shape, dim)


def write_masks(mask_ref, ends):
    rows = mask_ref.shape[1] - pad
    places = iota((rows, 128), 0)
    segment = segment_of(places, ends)
    for shift in range(1, mask_ref.shape[0] + 1):
        same = (segment_of(places - shift, ends) == segment) & (places >= shift)
        mask_ref[shift - 1, :rows, :] = jnp.where(same, 1.0, 0.0)
        mask_ref[shift - 1, rows:, :] = jnp.zeros((pad, 128), f32)


def shifted_rows(x_ref, mask_ref, at, cols, shift, tall):
    part = x_ref[pad + at - shift : pad + at - shift + tall, cols]
    if shift == 0:
        return part
    return part * mask_ref[shift - 1, at : at + tall, :]


def conv_pre(x_ref, mask_ref, taps_ref, bias_ref, at, cols, tall):
    taps = taps_ref.shape[0]
    shifted = [shifted_rows(x_ref, mask_ref, at, cols, s, tall) for s in range(taps)]
    total = bias_ref[:, cols]
    for s in range(taps):
        total = total + taps_ref[taps - 1 - s : taps - s, cols] * shifted[s]
    return total, shifted


def column_loop(width, step):
    def one(c, carry):
        step(pl.ds(pl.multiple_of(c * 128, 128), 128))
        return carry

    lax.fori_loop(0, width // 128, one, 0)


def row_loop(rows, tall, step):
    def one(r, carry):
        step(pl.multiple_of(r * tall, tall))
        return carry

    lax.fori_loop(0, rows // tall, one, 0)


class Block:
    def __init__(self, b, ends, step_col, step_row, rate_col, rate_row, state_ref):
        low, top = b * span, (b + 1) * span
        states = state_ref.shape[1] // 2
        lower = jnp.where(iota((span, span), 0) >= iota((span, span), 1), 1.0, 0.0)
        self.rows = slice(low, top)
        self.step = step_col[low:top]
        self.step_row = step_row[:, low:top]
        self.cum = mm_exact(lower, rate_col[low:top])
        self.cum_row = mm_exact(rate_row[:, low:top], lower, (1, 1))
        self.inputs = state_ref[low:top, :states].astype(bf16)
        self.outputs = state_ref[low:top, states:].astype(bf16)
        segment = segment_of(iota((span, 1), 0) + low, ends)
        segment_row = segment_of(iota((1, span), 1) + low, ends)
        edge = sum(jnp.where(span - 1 >= end, 1, 0) for end in ends)
        self.near_edge = jnp.where(segment == edge, 1.0, 0.0)
        self.mask = jnp.where(segment == segment_row, lower, 0.0)
        self.contact = mm(self.outputs, self.inputs, (1, 1)) * self.mask

    def decay(self, h):
        gap = self.cum[:, h : h + 1] - self.cum_row[h : h + 1, :]
        return jnp.exp(jnp.minimum(gap, 0.0))

    def from_edge(self, h):
        return jnp.exp(self.cum[:, h : h + 1]) * self.near_edge

    def to_edge(self, h):
        last = self.cum[span - 1 : span, h : h + 1]
        return jnp.exp(last - self.cum[:, h : h + 1]) * self.near_edge


def wide(low_half, left, right):
    return jnp.where(low_half, left, right)


def step_sizes(raw_col, raw_row, bias_ref, bias_col_ref, log_ref, log_col_ref):
    def soft(v):
        return jnp.maximum(v, 0.0) + jnp.log1p(jnp.exp(-jnp.abs(v)))

    step_col = soft(raw_col + bias_ref[...])
    step_row = soft(raw_row + bias_col_ref[...])
    rate_col = -step_col * jnp.exp(log_ref[...])
    rate_row = -step_row * jnp.exp(log_col_ref[...])
    return step_col, step_row, rate_col, rate_row


def forward_kernel(fast, place_ref, lengths_ref, *refs):
    n_rows = 4 if fast else 1
    n_msg = 8 if fast else 4
    row_refs, msg_refs, refs = refs[:n_rows], refs[n_rows : n_rows + n_msg], refs[n_rows + n_msg :]
    (taps_ref, bias_ref, step_bias_ref, step_bias_col_ref, log_ref, log_col_ref, skip_ref) = refs[:7]
    (
        rows_ref,
        normed_ref,
        weight_ref,
        state_weight_ref,
        step_weight_ref,
        small_ref,
        gate_ref,
        raw_ref,
        state_raw_ref,
        step_col_ref,
        step_row_ref,
        act_ref,
        state_ref,
        mixed_ref,
    ) = refs[7:21]
    mask_ref, state_taps_ref, state_bias_ref = refs[21:]
    total = rows_ref.shape[0]
    channels = gate_ref.shape[1]
    ends = ends_of(lengths_ref)

    if fast:
        depth_part = 128
        small = jnp.zeros(small_ref.shape, f32)
        share = state_weight_ref.shape[0] // 32
        for slot in range(8):
            msg = msg_refs[slot]
            index = place_ref[4 + slot]
            at = pl.multiple_of(index * depth_part, depth_part)
            weight_ref[pl.ds(at, depth_part), :] = msg[:depth_part, :]
            for member in range(4):
                inner = pl.multiple_of(at + place_ref[member] * share, share)
                state_weight_ref[pl.ds(inner, share), :] = msg[
                    depth_part : depth_part + share, 256 * member : 256 * (member + 1)
                ]
            tail = depth_part + share
            small = small + msg[tail : tail + 16, :256].astype(f32)
            step_weight_ref[:, pl.ds(at, depth_part)] = msg[tail : tail + 16, 256:384]
        small_ref[...] = small
    else:
        weight_ref[...] = msg_refs[0][...]
        state_weight_ref[...] = msg_refs[1][...]
        step_weight_ref[...] = msg_refs[2][...]
        small_ref[...] = msg_refs[3][...].astype(f32)
    gain = jnp.concatenate([small_ref[i : i + 1, :] for i in range(4)], axis=1)
    taps = taps_ref.shape[0]
    state_taps_ref[...] = small_ref[4 : 4 + taps, :]
    state_bias_ref[...] = small_ref[4 + taps : 5 + taps, :]

    tall = total // n_rows
    for member in range(n_rows):
        at = pl.multiple_of(place_ref[member] * tall, tall) if fast else 0
        own = row_refs[member]
        rows_ref[pl.ds(at, tall), :] = own[...]
        value = own[...].astype(f32)
        scale = lax.rsqrt(jnp.mean(value * value, axis=1, keepdims=True) + epsilon)
        normed_ref[pl.ds(at, tall), :] = (value * scale * gain).astype(bf16)

    raw_ref[:pad, :] = jnp.zeros((pad, channels), f32)
    state_raw_ref[:pad, :] = jnp.zeros((pad, state_raw_ref.shape[1]), f32)

    def project(at):
        part = normed_ref[pl.ds(at, 128), :]
        both = mm(part, weight_ref[...])
        gate_ref[pl.ds(at, 128), :] = both[:, :channels]
        raw_ref[pl.ds(at + pad, 128), :] = both[:, channels:]
        state_raw_ref[pl.ds(at + pad, 128), :] = mm(part, state_weight_ref[...])
        step_col_ref[pl.ds(at, 128), :] = mm(part, step_weight_ref[...], (1, 1))

    row_loop(total, 128, project)
    step_row_ref[...] = mm(step_weight_ref[...], normed_ref[...], (1, 1))

    write_masks(mask_ref, ends)

    def activate(x_ref, out_ref, own_taps, own_bias):
        def column(cols):
            for at in range(0, total, 128):
                pre, _ = conv_pre(x_ref, mask_ref, own_taps, own_bias, at, cols, 128)
                out_ref[at : at + 128, cols] = pre * sigmoid(pre)

        column_loop(out_ref.shape[1], column)

    activate(raw_ref, act_ref, taps_ref, bias_ref)
    activate(state_raw_ref, state_ref, state_taps_ref, state_bias_ref)

    steps = step_sizes(
        step_col_ref[...],
        step_row_ref[...],
        step_bias_ref,
        step_bias_col_ref,
        log_ref,
        log_col_ref,
    )
    low_half = iota((span, 128), 1) < head_width
    held = []
    for b in range(total // span):
        block = Block(b, ends, *steps, state_ref)
        for i in range(channels // 128):
            cols = slice(128 * i, 128 * (i + 1))
            pair = (2 * i, 2 * i + 1)
            x = act_ref[block.rows, cols]
            step_wide = wide(low_half, *(block.step[:, h : h + 1] for h in pair))
            x_step = (x * step_wide).astype(bf16)
            y = [mm((block.decay(h) * block.contact).astype(bf16), x_step) for h in pair]
            y = wide(low_half, *y) + skip_ref[:, cols] * x
            if b == 0:
                reach = wide(low_half, *(block.to_edge(h) for h in pair))
                weighted = (x * step_wide * reach).astype(bf16)
                held.append(mm(block.inputs, weighted, (0, 0)).astype(bf16))
            else:
                reach = wide(low_half, *(block.from_edge(h) for h in pair))
                y = y + reach * mm(block.outputs, held[i])
            mixed_ref[block.rows, cols] = y


def grad_in_kernel(fast, place_ref, lengths_ref, *refs):
    n_rows = 4 if fast else 1
    n_msg = 8 if fast else 1
    row_refs, out_refs, refs = refs[:n_rows], refs[n_rows : n_rows + n_msg], refs[n_rows + n_msg :]
    gate_ref, mixed_ref, norm_ref, rows_ref, weight_ref, grad_ref, sums_ref, wide_ref = refs
    total = rows_ref.shape[0]
    ends = ends_of(lengths_ref)
    tall = total // n_rows
    for member in range(n_rows):
        at = pl.multiple_of(place_ref[member] * tall, tall) if fast else 0
        rows_ref[pl.ds(at, tall), :] = row_refs[member][...]
    if fast:
        for slot in range(8):
            at = pl.multiple_of(place_ref[4 + slot] * 128, 128)
            weight_ref[:, pl.ds(at, 128)] = out_refs[slot][...]
    else:
        weight_ref[...] = out_refs[0][...]

    def part(at):
        rows = pl.ds(at, 128)
        valid = jnp.where(iota((128, 1), 0) + at < ends[-1], 1.0, 0.0)
        grad = mm(rows_ref[rows, :], weight_ref[...], (1, 1)) * valid
        grad_ref[rows, :] = grad
        gate = gate_ref[rows, :]
        gated = mixed_ref[rows, :] * (gate * sigmoid(gate))
        square = jnp.sum(gated * gated, axis=1, keepdims=True)
        cross = jnp.sum(grad * norm_ref[...] * gated, axis=1, keepdims=True)
        lane = iota((128, 128), 1)
        wide_ref[rows, :] = jnp.where(lane == 0, square, jnp.where(lane == 1, cross, 0.0))

    row_loop(total, 128, part)
    for at in range(0, total, 128):
        sums_ref[:, at : at + 128] = wide_ref[at : at + 128, :].T[:8, :]


def norm_kernel(inner_total, lengths_ref, *refs):
    (sums_ref, gate_ref, mixed_ref, grad_ref, norm_ref, weight_ref, rows_ref, normed_ref) = refs[:8]
    partial_ref, msg_ref, grad_gate_ref, grad_mixed_ref, norm_grad_ref = refs[8:13]
    wide_ref, out_rows_ref = refs[13:]
    total, channels = gate_ref.shape
    ends = ends_of(lengths_ref)
    for at in range(0, total, 128):
        tile = jnp.concatenate([sums_ref[:, at : at + 128]] * 16, axis=0)
        wide_ref[at : at + 128, :] = tile.T
    norm_grad_ref[...] = jnp.zeros(norm_grad_ref.shape, f32)

    def part(at):
        rows = pl.ds(at, 128)
        valid = jnp.where(iota((128, 1), 0) + at < ends[-1], 1.0, 0.0)
        scale = lax.rsqrt(wide_ref[rows, 0:1] / inner_total + epsilon)
        cross = wide_ref[rows, 1:2]
        gate = gate_ref[rows, :]
        mixed = mixed_ref[rows, :]
        sig = sigmoid(gate)
        gate_act = gate * sig
        gated = mixed * gate_act
        grad = grad_ref[rows, :]
        norm = norm_ref[...]
        hat = gated * scale
        out_rows_ref[rows, :] = (hat * norm * valid).astype(bf16)
        norm_grad_ref[...] += jnp.sum(grad * hat, axis=0, keepdims=True)
        grad_gated = scale * (grad * norm) - gated * (scale * scale * scale * cross / inner_total)
        grad_mixed_ref[rows, :] = grad_gated * gate_act
        grad_gate = grad_gated * mixed * sig * (1.0 + gate * (1.0 - sig))
        grad_gate_ref[rows, :] = grad_gate.astype(bf16)
        partial_ref[rows, :] = mm(out_rows_ref[rows, :], weight_ref[...]).astype(bf16)

    row_loop(total, 128, part)

    chunks, tall = msg_ref.shape[0], msg_ref.shape[1] // 2

    def chunk(c):
        cols = pl.ds(pl.multiple_of(c * tall, tall), tall)
        msg_ref[c, :tall, :] = mm(normed_ref[:, cols], grad_gate_ref[...], (0, 0)).astype(bf16)
        msg_ref[c, tall:, :] = mm(rows_ref[:, cols], out_rows_ref[...], (0, 0)).astype(bf16)

    def one(c, carry):
        chunk(c)
        return carry

    lax.fori_loop(0, chunks, one, 0)


def backward_kernel(lengths_ref, *refs):
    (
        grad_mixed_ref,
        act_ref,
        state_ref,
        raw_ref,
        state_raw_ref,
        step_col_ref,
        step_row_ref,
        grad_gate_ref,
        normed_ref,
        rows_ref,
        weight_ref,
        state_weight_ref,
        step_weight_ref,
        small_ref,
        taps_ref,
        bias_ref,
        step_bias_ref,
        step_bias_col_ref,
        log_ref,
        log_col_ref,
        skip_ref,
    ) = refs[:21]
    (
        msg_ref,
        state_part_ref,
        step_part_ref,
        gain_part_ref,
        grad_normed_ref,
        inner_sums_ref,
        head_sums_ref,
        state_sums_ref,
    ) = refs[21:29]
    (
        mask_ref,
        state_taps_ref,
        state_bias_ref,
        acc_ref,
        grad_act_ref,
        grad_state_ref,
        pre_ref,
        state_pre_ref,
        grad_inner_ref,
        grad_state_low_ref,
    ) = refs[29:]
    total, channels = grad_mixed_ref.shape
    states = state_ref.shape[1] // 2
    ends = ends_of(lengths_ref)
    taps = taps_ref.shape[0]
    state_taps_ref[...] = small_ref[4 : 4 + taps, :]
    state_bias_ref[...] = small_ref[4 + taps : 5 + taps, :]
    write_masks(mask_ref, ends)
    raw_row = step_row_ref[...]
    steps = step_sizes(
        step_col_ref[...], raw_row, step_bias_ref, step_bias_col_ref, log_ref, log_col_ref
    )
    rate_row = steps[3]
    low_half = iota((span, 128), 1) < head_width
    lower = jnp.where(iota((span, span), 0) >= iota((span, span), 1), 1.0, 0.0)
    blocks = [Block(b, ends, *steps, state_ref) for b in range(total // span)]
    first, second = blocks
    row_sums, step_rows, out_sums, in_sums = [], [], None, None
    grad_out = jnp.zeros((span, states), f32)
    grad_in = jnp.zeros((span, states), f32)
    head_of = iota((head_rows, 128), 0)
    lane_head = iota((head_rows, 128), 1) // head_width

    for b, block in enumerate(blocks):
        acc_ref[...] = jnp.zeros((span, span), f32)
        row_sum = jnp.zeros((span, 128), f32)
        step_grad = jnp.zeros((head_rows, span), f32)
        lane = iota((span, 128), 1)
        head_row = iota((head_rows, span), 0)
        for i in range(channels // 128):
            cols = slice(128 * i, 128 * (i + 1))
            pair = (2 * i, 2 * i + 1)
            x = act_ref[block.rows, cols]
            x_low = x.astype(bf16)
            grad = grad_mixed_ref[block.rows, cols]
            grad_low = grad.astype(bf16)
            halves = (
                jnp.where(low_half, grad, 0.0).astype(bf16),
                jnp.where(low_half, 0.0, grad).astype(bf16),
            )
            step_wide = wide(low_half, *(block.step[:, h : h + 1] for h in pair))
            grads = []
            for h, half in zip(pair, halves):
                decay = block.decay(h)
                spread = mm(half, x_low, (1, 1)) * decay
                stepped = spread * block.step_row[h : h + 1, :]
                acc_ref[...] += stepped
                row_here = jnp.sum(stepped * block.contact, axis=1, keepdims=True)
                row_sum = jnp.where(lane == h, row_here, row_sum)
                step_here = jnp.sum(spread * block.contact, axis=0, keepdims=True)
                step_grad = jnp.where(head_row == h, step_here, step_grad)
                grads.append(mm((decay * block.contact).astype(bf16), grad_low, (0, 0)))
            grad_act = wide(low_half, *grads) * step_wide + skip_ref[:, cols] * grad
            picks = jnp.where(lane_head + 2 * i == head_of, 1.0, 0.0)
            if b == 0:
                reach = wide(low_half, *(second.from_edge(h) for h in pair))
                lead = (grad_mixed_ref[second.rows, cols] * reach).astype(bf16)
                edge = wide(low_half, *(block.to_edge(h) for h in pair))
                weighted = (x * step_wide * edge).astype(bf16)
                held = mm(block.inputs, weighted, (0, 0)).astype(bf16)
                held_grad = mm(second.outputs, lead, (0, 0)).astype(bf16)
                grad_out = grad_out + mm(lead, held, (1, 1))
                grad_in = grad_in + mm(weighted, held_grad, (1, 1))
                back = mm(block.inputs, held_grad) * edge
                grad_act = grad_act + back * step_wide
                ahead = mm(second.outputs, held)
                out_here = mm_exact(picks, lead.astype(f32) * ahead, (1, 1))
                in_here = mm_exact(picks, x * back, (1, 1))
                out_sums = out_here if out_sums is None else out_sums + out_here
                in_sums = in_here if in_sums is None else in_sums + in_here
            grad_act_ref[block.rows, cols] = grad_act
        table = (acc_ref[...] * block.mask).astype(bf16)
        grad_c = mm(table, block.inputs)
        grad_b = mm(table, block.outputs, (0, 0))
        if b == 0:
            grad_b = grad_b + grad_in
        else:
            grad_c = grad_c + grad_out
        grad_state_ref[block.rows, :states] = grad_b
        grad_state_ref[block.rows, states:] = grad_c
        row_sums.append(row_sum)
        step_rows.append(step_grad)

    rate_grads = []
    for b, block in enumerate(blocks):
        column = step_rows[b] * block.step_row
        crossing = mm_exact(row_sums[b], lower, (0, 0))[:head_rows] - mm_exact(column, lower)
        if b == 0:
            crossing = crossing + mm_exact(in_sums * block.step_row, 1.0 - lower)
        else:
            crossing = crossing + mm_exact(out_sums, lower)
        rate_grads.append(crossing)
    step_rows[0] = step_rows[0] + in_sums
    rate_grad = jnp.concatenate(rate_grads, axis=1)
    step_grad = jnp.concatenate(step_rows, axis=1) - rate_grad * jnp.exp(log_col_ref[...])
    step_grad = step_grad * sigmoid(raw_row + step_bias_col_ref[...])
    decay_sum = jnp.sum(rate_grad * rate_row, axis=1, keepdims=True)
    bias_sum = jnp.sum(step_grad, axis=1, keepdims=True)
    lane = iota((head_rows, 128), 1)
    head_sums_ref[...] = jnp.where(lane == 0, bias_sum, jnp.where(lane == 1, decay_sum, 0.0))
    step_grad_low = step_grad.astype(bf16)

    def conv_back(x_ref, grad_ref, held_ref, out_ref, sums_ref, own_taps, own_bias, skips):
        held_ref[total:, :] = jnp.zeros((pad, held_ref.shape[1]), f32)

        def column(cols):
            sums = [jnp.zeros((1, 128), f32) for _ in range(taps + 2)]
            for at in range(0, total, 128):
                pre, shifted = conv_pre(x_ref, mask_ref, own_taps, own_bias, at, cols, 128)
                sig = sigmoid(pre)
                grad = grad_ref[at : at + 128, cols] * sig * (1.0 + pre * (1.0 - sig))
                held_ref[at : at + 128, cols] = grad
                for s in range(taps):
                    sums[taps - 1 - s] += jnp.sum(grad * shifted[s], axis=0, keepdims=True)
                sums[taps] += jnp.sum(grad, axis=0, keepdims=True)
                if skips:
                    act = act_ref[at : at + 128, cols]
                    over = grad_mixed_ref[at : at + 128, cols] * act
                    sums[taps + 1] += jnp.sum(over, axis=0, keepdims=True)
            for t, value in enumerate(sums):
                sums_ref[t : t + 1, cols] = value
            for at in range(0, total, 128):
                back = own_taps[taps - 1 : taps, cols] * held_ref[at : at + 128, cols]
                for s in range(1, taps):
                    part = held_ref[at + s : at + s + 128, cols]
                    part = part * mask_ref[s - 1, at + s : at + s + 128, :]
                    back = back + own_taps[taps - 1 - s : taps - s, cols] * part
                out_ref[at : at + 128, cols] = back.astype(bf16)

        column_loop(out_ref.shape[1], column)

    inner_sums_ref[...] = jnp.zeros(inner_sums_ref.shape, f32)
    state_sums_ref[...] = jnp.zeros(state_sums_ref.shape, f32)
    conv_back(
        raw_ref, grad_act_ref, pre_ref, grad_inner_ref, inner_sums_ref, taps_ref, bias_ref, True
    )
    conv_back(
        state_raw_ref,
        grad_state_ref,
        state_pre_ref,
        grad_state_low_ref,
        state_sums_ref,
        state_taps_ref,
        state_bias_ref,
        False,
    )

    chunks, tall = msg_ref.shape[0], msg_ref.shape[1]

    def chunk(c, carry):
        at = pl.multiple_of(c * tall, tall)
        part = normed_ref[:, pl.ds(at, tall)]
        msg_ref[c] = mm(part, grad_inner_ref[...], (0, 0)).astype(bf16)
        state_part_ref[pl.ds(at, tall), :] = mm(part, grad_state_low_ref[...], (0, 0)).astype(bf16)
        return carry

    lax.fori_loop(0, chunks, chunk, 0)
    step_part_ref[...] = mm(step_grad_low, normed_ref[...])
    step_back = step_grad.T.astype(bf16)
    gain_part_ref[...] = jnp.zeros(gain_part_ref.shape, f32)
    for at in range(0, total, 128):
        rows = slice(at, at + 128)
        grad = mm(grad_gate_ref[rows, :], weight_ref[:, :channels], (1, 1))
        grad = grad + mm(grad_inner_ref[rows, :], weight_ref[:, channels:], (1, 1))
        grad = grad + mm(grad_state_low_ref[rows, :], state_weight_ref[...], (1, 1))
        grad = grad + mm(step_back[rows, :], step_weight_ref[...])
        grad_normed_ref[rows, :] = grad.astype(bf16)
        value = rows_ref[rows, :].astype(f32)
        scale = lax.rsqrt(jnp.mean(value * value, axis=1, keepdims=True) + epsilon)
        gain_part_ref[...] += jnp.sum(grad * (value * scale), axis=0, keepdims=True)


def call(kernel, scalars, arrays, outs, scratch):
    smem = pl.BlockSpec(memory_space=pltpu.SMEM)
    vmem = pl.BlockSpec(memory_space=pltpu.VMEM)
    return pl.pallas_call(
        kernel,
        out_shape=[jax.ShapeDtypeStruct(shape, kind) for shape, kind in outs],
        in_specs=[smem] * len(scalars) + [vmem] * len(arrays),
        out_specs=[vmem] * len(outs),
        scratch_shapes=[pltpu.VMEM(shape, kind) for shape, kind in scratch],
        compiler_params=pltpu.CompilerParams(vmem_limit_bytes=vmem_bytes),
    )(*scalars, *arrays)


def ring_ok(n_dp, n_tensor):
    return n_dp == 8 and n_tensor == 4


ring_order = (0, 2, 4, 6, 7, 5, 3, 1)


def ring_place(index):
    high, low = index // 2, index % 2
    return jnp.where(low == 0, high, 7 - high)


def ring_index(place):
    place = lax.rem(place + 16, 8)
    return jnp.where(place < 4, 2 * place, 2 * (7 - place) + 1)


def ring_send(value, forward):
    pairs = []
    for place in range(8):
        other = (place + (1 if forward else 7)) % 8
        pairs.append((ring_order[place], ring_order[other]))
    return lax.ppermute(value, "dp", pairs)


def ring_gather(value):
    me = ring_place(lax.axis_index("dp"))
    pieces = [(value, ring_index(me))]
    ahead, back = value, value
    for step in range(1, 5):
        ahead = ring_send(ahead, True)
        pieces.append((ahead, ring_index(me - step)))
        if step < 4:
            back = ring_send(back, False)
            pieces.append((back, ring_index(me + step)))
    return pieces


def ring_scatter(parts):
    me = ring_place(lax.axis_index("dp"))

    def own(place):
        return lax.dynamic_index_in_dim(parts, ring_index(place), 0, keepdims=False).astype(f32)

    total = own(me)
    for forward, steps in ((True, 4), (False, 3)):
        sign = 1 if forward else -1
        held = own(me + sign * steps)
        for step in range(1, steps + 1):
            got = ring_send(held.astype(bf16), forward).astype(f32)
            if step < steps:
                held = got + own(me + sign * (steps - step))
            else:
                total = total + got
    return total


def dp_others(value):
    got = []
    for shift in range(1, 8):
        pairs = [(i, (i + shift) % 8) for i in range(8)]
        got.append(lax.ppermute(value, "dp", pairs))
    return got


def tensor_swap(value, bit):
    return lax.ppermute(value, "tensor", [(i, i ^ bit) for i in range(4)])


def tensor_gather(value):
    near = tensor_swap(value, 1)
    far = tensor_swap(value, 2)
    return [value, near, far, tensor_swap(far, 1)]


def tensor_scatter(parts):
    me = lax.axis_index("tensor")
    core, across = me % 2, me // 2
    split = parts.reshape((2, 2) + parts.shape[1:])
    give = lax.dynamic_index_in_dim(split, 1 - core, 1, keepdims=False)
    keep = lax.dynamic_index_in_dim(split, core, 1, keepdims=False)
    got = tensor_swap(give, 1)
    half = keep.astype(f32) + got.astype(f32)
    give = lax.dynamic_index_in_dim(half, 1 - across, 0, keepdims=False)
    keep = lax.dynamic_index_in_dim(half, across, 0, keepdims=False)
    got = tensor_swap(give.astype(bf16), 2)
    return keep + got.astype(f32)


def body(
    tokens,
    lengths,
    cotangent,
    pre_gain,
    input_weight,
    step_weight,
    state_weight,
    conv_inner,
    conv_inner_bias,
    conv_state,
    conv_state_bias,
    step_bias,
    decay_log,
    skip_gain,
    norm_gain,
    output_weight,
):
    n_dp, n_tensor = lax.axis_size("dp"), lax.axis_size("tensor")
    fast = ring_ok(n_dp, n_tensor)
    owners = n_dp * n_tensor
    me = lax.axis_index("tensor")
    owner = lax.axis_index("dp") * n_tensor + me
    own_rows, depth = tokens.shape
    total = own_rows * n_tensor
    states = state_weight.shape[1]
    heads = step_weight.shape[1]
    share = state_weight.shape[0]
    taps = conv_state.shape[0]
    channels = input_weight.shape[2]
    inner_total = channels * n_tensor

    def placed(value, whole):
        zeros = jnp.zeros(value.shape[:-1] + (whole,), value.dtype)
        start = (0,) * (value.ndim - 1) + (owner * value.shape[-1],)
        return lax.dynamic_update_slice(zeros, value, start)

    small = jnp.concatenate(
        [
            placed(pre_gain, depth).reshape(-1, states),
            placed(conv_state, states),
            placed(conv_state_bias[None], states),
        ],
        axis=0,
    )
    small = jnp.pad(small, ((0, 16 - small.shape[0]), (0, 0)))
    step_rows = jnp.pad(step_weight.T, ((0, head_rows - heads), (0, 0)))
    input_flat = input_weight.reshape(input_weight.shape[0], -1)
    if fast:
        shared = tensor_gather(jnp.concatenate([state_weight, small], axis=0))
        beside = jnp.concatenate([piece[:share] for piece in shared], axis=1)
        small = shared[0][share:] + shared[1][share:] + shared[2][share:] + shared[3][share:]
        tail = jnp.concatenate([small, step_rows], axis=1)
        tail = jnp.pad(tail, ((0, 0), (0, depth - tail.shape[1])))
        msg = ring_gather(jnp.concatenate([input_flat, beside, tail], axis=0))
        out_msg = ring_gather(output_weight)
        row_pieces = tensor_gather(tokens)
        grad_pieces = tensor_gather(cotangent)
        weight_pieces = [piece for piece, _ in msg]
        out_pieces = [piece for piece, _ in out_msg]
        place = jnp.stack([me, me ^ 1, me ^ 2, me ^ 3] + [index for _, index in msg])
    else:
        row_pieces = [lax.all_gather(tokens, "tensor", axis=0, tiled=True)]
        grad_pieces = [lax.all_gather(cotangent, "tensor", axis=0, tiled=True)]
        weight_pieces = [
            lax.all_gather(input_flat, "dp", axis=0, tiled=True),
            lax.all_gather(state_weight, ("dp", "tensor"), axis=0, tiled=True),
            lax.all_gather(step_rows, "dp", axis=1, tiled=True),
            lax.psum(small, ("dp", "tensor")),
        ]
        out_pieces = [lax.all_gather(output_weight, "dp", axis=1, tiled=True)]
        place = jnp.zeros((12,), jnp.int32)
    place = place.astype(jnp.int32)

    def row(value):
        return value.astype(f32).reshape(1, -1)

    def head(value):
        return jnp.pad(value.astype(f32), (0, head_rows - heads))

    taps_float = conv_inner.astype(f32)
    scan_params = [
        taps_float,
        row(conv_inner_bias),
        head(step_bias)[None, :],
        head(step_bias)[:, None],
        head(decay_log)[None, :],
        head(decay_log)[:, None],
        row(jnp.repeat(skip_gain, channels // heads)),
    ]
    masks = ((taps - 1, total + pad, 128), f32)
    state_taps = [((taps, states), f32), ((1, states), f32)]
    (
        rows,
        normed,
        weight_full,
        state_full,
        step_full,
        small_full,
        gate,
        raw,
        state_raw,
        step_col,
        step_row,
        act,
        state_act,
        mixed,
    ) = call(
        functools.partial(forward_kernel, fast),
        [place, lengths],
        row_pieces + weight_pieces + scan_params,
        [
            ((total, depth), bf16),
            ((total, depth), bf16),
            ((depth, 2 * channels), bf16),
            ((depth, states), bf16),
            ((head_rows, depth), bf16),
            ((16, states), f32),
            ((total, channels), f32),
            ((total + pad, channels), f32),
            ((total + pad, states), f32),
            ((total, head_rows), f32),
            ((head_rows, total), f32),
            ((total, channels), f32),
            ((total, states), f32),
            ((total, channels), f32),
        ],
        [masks] + state_taps,
    )
    norm_row = row(norm_gain)
    grad_rows, output_full, grad_normalized, sums = call(
        functools.partial(grad_in_kernel, fast),
        [place, lengths],
        grad_pieces + out_pieces + [gate, mixed, norm_row],
        [
            ((total, depth), bf16),
            ((channels, depth), bf16),
            ((total, channels), f32),
            ((8, total), f32),
        ],
        [((total, 128), f32)],
    )
    if fast:
        sums = sums + tensor_swap(sums, 1)
        sums = sums + tensor_swap(sums, 2)
    else:
        sums = lax.psum(sums, "tensor")
    chunks = 8
    tall = depth // chunks
    partial_out, gate_msg, grad_gate, grad_mixed, norm_grad = call(
        functools.partial(norm_kernel, inner_total),
        [lengths],
        [sums, gate, mixed, grad_normalized, norm_row, output_full, grad_rows, normed],
        [
            ((total, depth), bf16),
            ((chunks, 2 * tall, channels), bf16),
            ((total, channels), bf16),
            ((total, channels), f32),
            ((1, channels), f32),
        ],
        [((total, 128), f32), ((total, channels), bf16)],
    )
    (
        inner_msg,
        state_part,
        step_part,
        gain_part,
        grad_normed,
        inner_sums,
        head_sums,
        state_sums,
    ) = call(
        backward_kernel,
        [lengths],
        [
            grad_mixed,
            act,
            state_act,
            raw,
            state_raw,
            step_col,
            step_row,
            grad_gate,
            normed,
            rows,
            weight_full,
            state_full,
            step_full,
            small_full,
        ]
        + scan_params,
        [
            ((chunks, tall, channels), bf16),
            ((depth, states), bf16),
            ((head_rows, depth), f32),
            ((1, depth), f32),
            ((total, depth), bf16),
            ((8, channels), f32),
            ((head_rows, 128), f32),
            ((8, states), f32),
        ],
        [
            masks,
            *state_taps,
            ((span, span), f32),
            ((total, channels), f32),
            ((total, states), f32),
            ((total + pad, channels), f32),
            ((total + pad, states), f32),
            ((total, channels), bf16),
            ((total, states), bf16),
        ],
    )

    token_float = tokens.astype(f32)
    gain_full = small_full[: depth // states].reshape(1, depth)

    def lay(value):
        value = value.reshape(owners, -1)
        return jnp.pad(value, ((0, 0), (0, states - value.shape[1])))[:, None, :].astype(bf16)

    conv_state_owned = state_sums[:taps].reshape(taps, owners, -1).transpose(1, 0, 2)
    shared_part = jnp.concatenate(
        [
            state_part.reshape(owners, share, states),
            lay(gain_part),
            lay(conv_state_owned),
            lay(state_sums[taps]),
        ],
        axis=1,
    )
    shared_part = jnp.pad(shared_part, ((0, 0), (0, -shared_part.shape[1] % 8), (0, 0)))
    if fast:
        mixed_rows = tensor_scatter(partial_out.reshape((n_tensor, -1, depth)))
        grad_local = tensor_scatter(grad_normed.reshape((n_tensor, -1, depth)))
        by_tensor = shared_part.reshape((n_dp, n_tensor) + shared_part.shape[1:])
        shared_mine = ring_scatter(tensor_scatter(by_tensor.transpose(1, 0, 2, 3)))
        gate_out = ring_scatter(gate_msg)
        gate_grad, output_grad = gate_out[:tall], gate_out[tall:].T
        inner_grad = ring_scatter(inner_msg)
        step_chunks = step_part[:heads].reshape(heads, n_dp, tall).transpose(1, 0, 2)
        step_grad = ring_scatter(step_chunks).T
    else:
        mixed_rows = lax.psum_scatter(
            partial_out, "tensor", scatter_dimension=0, tiled=True
        ).astype(f32)
        grad_local = lax.psum_scatter(
            grad_normed, "tensor", scatter_dimension=0, tiled=True
        ).astype(f32)
        shared_mine = lax.psum_scatter(
            shared_part.astype(f32), ("dp", "tensor"), scatter_dimension=0, tiled=True
        )[0]
        both = gate_msg.astype(f32)
        gate_grad, output_grad, inner_grad = (
            lax.psum_scatter(part.reshape(depth, channels), "dp", scatter_dimension=0, tiled=True)
            for part in (both[:, :tall], both[:, tall:], inner_msg.astype(f32))
        )
        output_grad = output_grad.T
        step_grad = lax.psum_scatter(step_part[:heads].T, "dp", scatter_dimension=0, tiled=True)
    input_grad = jnp.stack([gate_grad, inner_grad], axis=1)
    block_out = (token_float + mixed_rows).astype(bf16)
    scale = lax.rsqrt(jnp.mean(token_float * token_float, axis=1, keepdims=True) + epsilon)
    grad_scaled = grad_local * gain_full
    along = jnp.sum(grad_scaled * token_float, axis=1, keepdims=True) / depth
    tokens_grad = (
        scale * grad_scaled
        - token_float * (scale * scale * scale * along)
        + cotangent.astype(f32)
    )
    state_grad = shared_mine[:share]
    pre_gain_grad = shared_mine[share, : depth // owners]
    conv_state_grad = shared_mine[share + 1, : taps * (states // owners)].reshape(taps, -1)
    conv_state_bias_grad = shared_mine[share + 2, : states // owners]

    head_part = jnp.pad(head_sums[:, :2].T, ((0, 0), (0, channels - head_rows)))
    sums = jnp.concatenate([inner_sums, norm_grad, head_part], axis=0)
    if fast:
        for other in dp_others(sums):
            sums = sums + other
    else:
        sums = lax.psum(sums, "dp")
    skip_grad = sums[taps + 1].reshape(heads, -1).sum(axis=1)
    return (
        block_out,
        tokens_grad,
        pre_gain_grad,
        input_grad,
        step_grad,
        state_grad,
        sums[:taps],
        sums[taps],
        conv_state_grad,
        conv_state_bias_grad,
        sums[9, :heads],
        sums[10, :heads],
        skip_grad,
        sums[8],
        output_grad,
    )


def solution(mesh):
    in_specs = (
        P(("dp", "tensor"), None),
        P("dp", None),
        P(("dp", "tensor"), None),
        P(("dp", "tensor")),
        P("dp", None, "tensor"),
        P("dp", "tensor"),
        P(("dp", "tensor"), None),
        P(None, "tensor"),
        P("tensor"),
        P(None, ("dp", "tensor")),
        P(("dp", "tensor")),
        P("tensor"),
        P("tensor"),
        P("tensor"),
        P("tensor"),
        P("tensor", "dp"),
    )
    out_specs = (
        P(("dp", "tensor"), None),
        P(("dp", "tensor"), None),
        P(("dp", "tensor")),
        P("dp", None, "tensor"),
        P("dp", "tensor"),
        P(("dp", "tensor"), None),
        P(None, "tensor"),
        P("tensor"),
        P(None, ("dp", "tensor")),
        P(("dp", "tensor")),
        P("tensor"),
        P("tensor"),
        P("tensor"),
        P("tensor"),
        P("tensor", "dp"),
    )
    return jax.shard_map(body, mesh=mesh, in_specs=in_specs, out_specs=out_specs, check_vma=False)
```

```python
import functools

import jax
import jax.numpy as jnp
from jax import lax
from jax.experimental import pallas as pl
from jax.experimental.pallas import tpu as pltpu
from jax.sharding import PartitionSpec as P

epsilon = 1e-05
highest = lax.Precision.HIGHEST
f32 = jnp.float32
bf16 = jnp.bfloat16
span = 256
pad = 8
head_rows = 16
head_width = 64
vmem_bytes = 32 * 1024 * 1024


def mm(a, b, over=(1, 0)):
    dims = (((over[0],), (over[1],)), ((), ()))
    return lax.dot_general(a, b, dims, preferred_element_type=f32)


def mm_exact(a, b, over=(1, 0)):
    dims = (((over[0],), (over[1],)), ((), ()))
    return lax.dot_general(a, b, dims, preferred_element_type=f32, precision=highest)


def sigmoid(v):
    return 1.0 / (1.0 + jnp.exp(-v))


def ends_of(lengths_ref):
    ends, total = [], None
    for slot in range(lengths_ref.shape[1]):
        here = lengths_ref[0, slot]
        total = here if total is None else total + here
        ends.append(total)
    return ends


def segment_of(places, ends):
    segment = jnp.zeros(places.shape, jnp.int32)
    for end in ends:
        segment = segment + jnp.where(places >= end, 1, 0)
    return segment


def iota(shape, dim):
    return lax.broadcasted_iota(jnp.int32, shape, dim)


def write_masks(mask_ref, ends):
    rows = mask_ref.shape[1] - pad
    places = iota((rows, 128), 0)
    segment = segment_of(places, ends)
    for shift in range(1, mask_ref.shape[0] + 1):
        same = (segment_of(places - shift, ends) == segment) & (places >= shift)
        mask_ref[shift - 1, :rows, :] = jnp.where(same, 1.0, 0.0)
        mask_ref[shift - 1, rows:, :] = jnp.zeros((pad, 128), f32)


def shifted_rows(x_ref, mask_ref, at, cols, shift, tall):
    part = x_ref[pad + at - shift : pad + at - shift + tall, cols]
    if shift == 0:
        return part
    return part * mask_ref[shift - 1, at : at + tall, :]


def conv_pre(x_ref, mask_ref, taps_ref, bias_ref, at, cols, tall):
    taps = taps_ref.shape[0]
    shifted = [shifted_rows(x_ref, mask_ref, at, cols, s, tall) for s in range(taps)]
    total = bias_ref[:, cols]
    for s in range(taps):
        total = total + taps_ref[taps - 1 - s : taps - s, cols] * shifted[s]
    return total, shifted


def column_loop(width, step):
    def one(c, carry):
        step(pl.ds(pl.multiple_of(c * 128, 128), 128))
        return carry

    lax.fori_loop(0, width // 128, one, 0)


def row_loop(rows, tall, step):
    def one(r, carry):
        step(pl.multiple_of(r * tall, tall))
        return carry

    lax.fori_loop(0, rows // tall, one, 0)


class Block:
    def __init__(self, b, ends, step_col, step_row, rate_col, rate_row, state_ref):
        low, top = b * span, (b + 1) * span
        states = state_ref.shape[1] // 2
        lower = jnp.where(iota((span, span), 0) >= iota((span, span), 1), 1.0, 0.0)
        self.rows = slice(low, top)
        self.step = step_col[low:top]
        self.step_row = step_row[:, low:top]
        self.cum = mm_exact(lower, rate_col[low:top])
        self.cum_row = mm_exact(rate_row[:, low:top], lower, (1, 1))
        self.inputs = state_ref[low:top, :states].astype(bf16)
        self.outputs = state_ref[low:top, states:].astype(bf16)
        segment = segment_of(iota((span, 1), 0) + low, ends)
        segment_row = segment_of(iota((1, span), 1) + low, ends)
        edge = sum(jnp.where(span - 1 >= end, 1, 0) for end in ends)
        self.near_edge = jnp.where(segment == edge, 1.0, 0.0)
        self.mask = jnp.where(segment == segment_row, lower, 0.0)
        self.contact = mm(self.outputs, self.inputs, (1, 1)) * self.mask

    def decay(self, h):
        gap = self.cum[:, h : h + 1] - self.cum_row[h : h + 1, :]
        return jnp.exp(jnp.minimum(gap, 0.0))

    def from_edge(self, h):
        return jnp.exp(self.cum[:, h : h + 1]) * self.near_edge

    def to_edge(self, h):
        last = self.cum[span - 1 : span, h : h + 1]
        return jnp.exp(last - self.cum[:, h : h + 1]) * self.near_edge


def wide(low_half, left, right):
    return jnp.where(low_half, left, right)


def step_sizes(raw_col, raw_row, bias_ref, bias_col_ref, log_ref, log_col_ref):
    def soft(v):
        return jnp.maximum(v, 0.0) + jnp.log1p(jnp.exp(-jnp.abs(v)))

    step_col = soft(raw_col + bias_ref[...])
    step_row = soft(raw_row + bias_col_ref[...])
    rate_col = -step_col * jnp.exp(log_ref[...])
    rate_row = -step_row * jnp.exp(log_col_ref[...])
    return step_col, step_row, rate_col, rate_row


def forward_kernel(fast, place_ref, lengths_ref, *refs):
    n_rows = 4 if fast else 1
    n_msg = 8 if fast else 4
    row_refs, msg_refs, refs = refs[:n_rows], refs[n_rows : n_rows + n_msg], refs[n_rows + n_msg :]
    (taps_ref, bias_ref, step_bias_ref, step_bias_col_ref, log_ref, log_col_ref, skip_ref) = refs[:7]
    (
        rows_ref,
        normed_ref,
        weight_ref,
        state_weight_ref,
        step_weight_ref,
        small_ref,
        raw_ref,
        state_raw_ref,
        step_col_ref,
        step_row_ref,
        act_ref,
        state_ref,
        mixed_ref,
    ) = refs[7:20]
    mask_ref, state_taps_ref, state_bias_ref = refs[20:]
    total = rows_ref.shape[0]
    channels = act_ref.shape[1]
    ends = ends_of(lengths_ref)

    if fast:
        depth_part = 128
        small = jnp.zeros(small_ref.shape, f32)
        share = state_weight_ref.shape[0] // 32
        for slot in range(8):
            msg = msg_refs[slot]
            index = place_ref[4 + slot]
            at = pl.multiple_of(index * depth_part, depth_part)
            weight_ref[pl.ds(at, depth_part), :] = msg[:depth_part, :]
            for member in range(4):
                inner = pl.multiple_of(at + member * share, share)
                high, low = depth_part + share * (member // 2), 256 * (member % 2)
                state_weight_ref[pl.ds(inner, share), :] = msg[
                    high : high + share, low : low + 256
                ]
            tail = depth_part + 2 * share
            small = small + msg[tail : tail + 16, :256].astype(f32)
            step_weight_ref[:, pl.ds(at, depth_part)] = msg[tail : tail + 16, 256:384]
        small_ref[...] = small
    else:
        weight_ref[...] = msg_refs[0][...]
        state_weight_ref[...] = msg_refs[1][...]
        step_weight_ref[...] = msg_refs[2][...]
        small_ref[...] = msg_refs[3][...].astype(f32)
    gain = jnp.concatenate([small_ref[i : i + 1, :] for i in range(4)], axis=1)
    taps = taps_ref.shape[0]
    state_taps_ref[...] = small_ref[4 : 4 + taps, :]
    state_bias_ref[...] = small_ref[4 + taps : 5 + taps, :]

    tall = total // n_rows
    for member in range(n_rows):
        at = pl.multiple_of(place_ref[member] * tall, tall) if fast else 0
        own = row_refs[member][:tall, :]
        rows_ref[pl.ds(at, tall), :] = own
        value = own.astype(f32)
        scale = lax.rsqrt(jnp.mean(value * value, axis=1, keepdims=True) + epsilon)
        normed_ref[pl.ds(at, tall), :] = (value * scale * gain).astype(bf16)

    raw_ref[:pad, :] = jnp.zeros((pad, channels), f32)
    state_raw_ref[:pad, :] = jnp.zeros((pad, state_raw_ref.shape[1]), f32)

    def project(at):
        part = normed_ref[pl.ds(at, 128), :]
        raw_ref[pl.ds(at + pad, 128), :] = mm(part, weight_ref[...])
        state_raw_ref[pl.ds(at + pad, 128), :] = mm(part, state_weight_ref[...])
        step_col_ref[pl.ds(at, 128), :] = mm(part, step_weight_ref[...], (1, 1))

    row_loop(total, 128, project)
    step_row_ref[...] = mm(step_weight_ref[...], normed_ref[...], (1, 1))

    write_masks(mask_ref, ends)

    def activate(x_ref, out_ref, own_taps, own_bias):
        def column(cols):
            for at in range(0, total, 128):
                pre, _ = conv_pre(x_ref, mask_ref, own_taps, own_bias, at, cols, 128)
                out_ref[at : at + 128, cols] = pre * sigmoid(pre)

        column_loop(out_ref.shape[1], column)

    activate(raw_ref, act_ref, taps_ref, bias_ref)
    activate(state_raw_ref, state_ref, state_taps_ref, state_bias_ref)

    steps = step_sizes(
        step_col_ref[...],
        step_row_ref[...],
        step_bias_ref,
        step_bias_col_ref,
        log_ref,
        log_col_ref,
    )
    low_half = iota((span, 128), 1) < head_width
    held = []
    for b in range(total // span):
        block = Block(b, ends, *steps, state_ref)
        for i in range(channels // 128):
            cols = slice(128 * i, 128 * (i + 1))
            pair = (2 * i, 2 * i + 1)
            x = act_ref[block.rows, cols]
            step_wide = wide(low_half, *(block.step[:, h : h + 1] for h in pair))
            x_step = (x * step_wide).astype(bf16)
            y = [mm((block.decay(h) * block.contact).astype(bf16), x_step) for h in pair]
            y = wide(low_half, *y) + skip_ref[:, cols] * x
            if b == 0:
                reach = wide(low_half, *(block.to_edge(h) for h in pair))
                weighted = (x * step_wide * reach).astype(bf16)
                held.append(mm(block.inputs, weighted, (0, 0)).astype(bf16))
            else:
                reach = wide(low_half, *(block.from_edge(h) for h in pair))
                y = y + reach * mm(block.outputs, held[i])
            mixed_ref[block.rows, cols] = y


def grad_in_kernel(fast, place_ref, lengths_ref, *refs):
    n_rows = 4 if fast else 1
    n_msg = 8 if fast else 2
    row_refs, msg_refs, refs = refs[:n_rows], refs[n_rows : n_rows + n_msg], refs[n_rows + n_msg :]
    normed_ref, mixed_ref, norm_ref = refs[:3]
    rows_ref, gate_weight_ref, out_weight_ref, gate_ref, grad_ref, sums_ref, wide_ref = refs[3:]
    total = rows_ref.shape[0]
    ends = ends_of(lengths_ref)
    tall = total // n_rows
    for member in range(n_rows):
        at = pl.multiple_of(place_ref[member] * tall, tall) if fast else 0
        rows_ref[pl.ds(at, tall), :] = row_refs[member][-tall:, :]
    if fast:
        for slot in range(8):
            at = pl.multiple_of(place_ref[4 + slot] * 128, 128)
            gate_weight_ref[pl.ds(at, 128), :] = msg_refs[slot][:128, :]
            out_weight_ref[pl.ds(at, 128), :] = msg_refs[slot][128:, :]
    else:
        gate_weight_ref[...] = msg_refs[0][...]
        out_weight_ref[...] = msg_refs[1][...]

    def part(at):
        rows = pl.ds(at, 128)
        valid = jnp.where(iota((128, 1), 0) + at < ends[-1], 1.0, 0.0)
        grad = mm(rows_ref[rows, :], out_weight_ref[...]) * valid
        grad_ref[rows, :] = grad
        gate = mm(normed_ref[rows, :], gate_weight_ref[...])
        gate_ref[rows, :] = gate
        gated = mixed_ref[rows, :] * (gate * sigmoid(gate))
        square = jnp.sum(gated * gated, axis=1, keepdims=True)
        cross = jnp.sum(grad * norm_ref[...] * gated, axis=1, keepdims=True)
        lane = iota((128, 128), 1)
        wide_ref[rows, :] = jnp.where(lane == 0, square, jnp.where(lane == 1, cross, 0.0))

    row_loop(total, 128, part)
    for at in range(0, total, 128):
        sums_ref[:, at : at + 128] = wide_ref[at : at + 128, :].T[:8, :]


def norm_kernel(inner_total, lengths_ref, *refs):
    (sums_ref, gate_ref, mixed_ref, grad_ref, norm_ref, weight_ref, rows_ref, normed_ref) = refs[:8]
    partial_ref, msg_ref, grad_gate_ref, grad_mixed_ref, norm_grad_ref = refs[8:13]
    wide_ref, out_rows_ref = refs[13:]
    total, channels = gate_ref.shape
    ends = ends_of(lengths_ref)
    for at in range(0, total, 128):
        tile = jnp.concatenate([sums_ref[:, at : at + 128]] * 16, axis=0)
        wide_ref[at : at + 128, :] = tile.T
    norm_grad_ref[...] = jnp.zeros(norm_grad_ref.shape, f32)

    def part(at):
        rows = pl.ds(at, 128)
        valid = jnp.where(iota((128, 1), 0) + at < ends[-1], 1.0, 0.0)
        scale = lax.rsqrt(wide_ref[rows, 0:1] / inner_total + epsilon)
        cross = wide_ref[rows, 1:2]
        gate = gate_ref[rows, :]
        mixed = mixed_ref[rows, :]
        sig = sigmoid(gate)
        gate_act = gate * sig
        gated = mixed * gate_act
        grad = grad_ref[rows, :]
        norm = norm_ref[...]
        hat = gated * scale
        out_rows_ref[rows, :] = (hat * norm * valid).astype(bf16)
        norm_grad_ref[...] += jnp.sum(grad * hat, axis=0, keepdims=True)
        grad_gated = scale * (grad * norm) - gated * (scale * scale * scale * cross / inner_total)
        grad_mixed_ref[rows, :] = grad_gated * gate_act
        grad_gate = grad_gated * mixed * sig * (1.0 + gate * (1.0 - sig))
        grad_gate_ref[rows, :] = grad_gate.astype(bf16)
        partial_ref[rows, :] = mm(out_rows_ref[rows, :], weight_ref[...], (1, 1)).astype(bf16)

    row_loop(total, 128, part)

    chunks, tall = msg_ref.shape[0], msg_ref.shape[1] // 2

    def chunk(c):
        cols = pl.ds(pl.multiple_of(c * tall, tall), tall)
        msg_ref[c, :tall, :] = mm(normed_ref[:, cols], grad_gate_ref[...], (0, 0)).astype(bf16)
        msg_ref[c, tall:, :] = mm(rows_ref[:, cols], out_rows_ref[...], (0, 0)).astype(bf16)

    def one(c, carry):
        chunk(c)
        return carry

    lax.fori_loop(0, chunks, one, 0)


def backward_kernel(lengths_ref, *refs):
    (
        grad_mixed_ref,
        act_ref,
        state_ref,
        raw_ref,
        state_raw_ref,
        step_col_ref,
        step_row_ref,
        grad_gate_ref,
        normed_ref,
        rows_ref,
        gate_weight_ref,
        weight_ref,
        state_weight_ref,
        step_weight_ref,
        small_ref,
        norm_grad_ref,
        taps_ref,
        bias_ref,
        step_bias_ref,
        step_bias_col_ref,
        log_ref,
        log_col_ref,
        skip_ref,
    ) = refs[:23]
    (
        msg_ref,
        state_part_ref,
        gain_part_ref,
        grad_normed_ref,
        inner_sums_ref,
        state_sums_ref,
    ) = refs[23:29]
    (
        mask_ref,
        state_taps_ref,
        state_bias_ref,
        acc_ref,
        grad_act_ref,
        grad_state_ref,
        pre_ref,
        state_pre_ref,
        grad_inner_ref,
        grad_state_low_ref,
    ) = refs[29:]
    total, channels = grad_mixed_ref.shape
    states = state_ref.shape[1] // 2
    ends = ends_of(lengths_ref)
    taps = taps_ref.shape[0]
    state_taps_ref[...] = small_ref[4 : 4 + taps, :]
    state_bias_ref[...] = small_ref[4 + taps : 5 + taps, :]
    write_masks(mask_ref, ends)
    raw_row = step_row_ref[...]
    steps = step_sizes(
        step_col_ref[...], raw_row, step_bias_ref, step_bias_col_ref, log_ref, log_col_ref
    )
    rate_row = steps[3]
    low_half = iota((span, 128), 1) < head_width
    lower = jnp.where(iota((span, span), 0) >= iota((span, span), 1), 1.0, 0.0)
    blocks = [Block(b, ends, *steps, state_ref) for b in range(total // span)]
    first, second = blocks
    row_sums, step_rows, out_sums, in_sums = [], [], None, None
    grad_out = jnp.zeros((span, states), f32)
    grad_in = jnp.zeros((span, states), f32)
    head_of = iota((head_rows, 128), 0)
    lane_head = iota((head_rows, 128), 1) // head_width

    for b, block in enumerate(blocks):
        acc_ref[...] = jnp.zeros((span, span), f32)
        row_sum = jnp.zeros((span, 128), f32)
        step_grad = jnp.zeros((head_rows, span), f32)
        lane = iota((span, 128), 1)
        head_row = iota((head_rows, span), 0)
        for i in range(channels // 128):
            cols = slice(128 * i, 128 * (i + 1))
            pair = (2 * i, 2 * i + 1)
            x = act_ref[block.rows, cols]
            x_low = x.astype(bf16)
            grad = grad_mixed_ref[block.rows, cols]
            grad_low = grad.astype(bf16)
            halves = (
                jnp.where(low_half, grad, 0.0).astype(bf16),
                jnp.where(low_half, 0.0, grad).astype(bf16),
            )
            step_wide = wide(low_half, *(block.step[:, h : h + 1] for h in pair))
            grads = []
            for h, half in zip(pair, halves):
                decay = block.decay(h)
                spread = mm(half, x_low, (1, 1)) * decay
                stepped = spread * block.step_row[h : h + 1, :]
                acc_ref[...] += stepped
                row_here = jnp.sum(stepped * block.contact, axis=1, keepdims=True)
                row_sum = jnp.where(lane == h, row_here, row_sum)
                step_here = jnp.sum(spread * block.contact, axis=0, keepdims=True)
                step_grad = jnp.where(head_row == h, step_here, step_grad)
                grads.append(mm((decay * block.contact).astype(bf16), grad_low, (0, 0)))
            grad_act = wide(low_half, *grads) * step_wide + skip_ref[:, cols] * grad
            picks = jnp.where(lane_head + 2 * i == head_of, 1.0, 0.0)
            if b == 0:
                reach = wide(low_half, *(second.from_edge(h) for h in pair))
                lead = (grad_mixed_ref[second.rows, cols] * reach).astype(bf16)
                edge = wide(low_half, *(block.to_edge(h) for h in pair))
                weighted = (x * step_wide * edge).astype(bf16)
                held = mm(block.inputs, weighted, (0, 0)).astype(bf16)
                held_grad = mm(second.outputs, lead, (0, 0)).astype(bf16)
                grad_out = grad_out + mm(lead, held, (1, 1))
                grad_in = grad_in + mm(weighted, held_grad, (1, 1))
                back = mm(block.inputs, held_grad) * edge
                grad_act = grad_act + back * step_wide
                ahead = mm(second.outputs, held)
                out_here = mm_exact(picks, lead.astype(f32) * ahead, (1, 1))
                in_here = mm_exact(picks, x * back, (1, 1))
                out_sums = out_here if out_sums is None else out_sums + out_here
                in_sums = in_here if in_sums is None else in_sums + in_here
            grad_act_ref[block.rows, cols] = grad_act
        table = (acc_ref[...] * block.mask).astype(bf16)
        grad_c = mm(table, block.inputs)
        grad_b = mm(table, block.outputs, (0, 0))
        if b == 0:
            grad_b = grad_b + grad_in
        else:
            grad_c = grad_c + grad_out
        grad_state_ref[block.rows, :states] = grad_b
        grad_state_ref[block.rows, states:] = grad_c
        row_sums.append(row_sum)
        step_rows.append(step_grad)

    rate_grads = []
    for b, block in enumerate(blocks):
        column = step_rows[b] * block.step_row
        crossing = mm_exact(row_sums[b], lower, (0, 0))[:head_rows] - mm_exact(column, lower)
        if b == 0:
            crossing = crossing + mm_exact(in_sums * block.step_row, 1.0 - lower)
        else:
            crossing = crossing + mm_exact(out_sums, lower)
        rate_grads.append(crossing)
    step_rows[0] = step_rows[0] + in_sums
    rate_grad = jnp.concatenate(rate_grads, axis=1)
    step_grad = jnp.concatenate(step_rows, axis=1) - rate_grad * jnp.exp(log_col_ref[...])
    step_grad = step_grad * sigmoid(raw_row + step_bias_col_ref[...])
    decay_sum = jnp.sum(rate_grad * rate_row, axis=1, keepdims=True)
    bias_sum = jnp.sum(step_grad, axis=1, keepdims=True)
    lane = iota((head_rows, 128), 1)
    head_sums = jnp.where(lane == 0, bias_sum, jnp.where(lane == 1, decay_sum, 0.0))
    head_sums = jnp.concatenate([head_sums] * (128 // head_rows), axis=0).T
    step_grad_low = step_grad.astype(bf16)

    def conv_back(x_ref, grad_ref, held_ref, out_ref, sums_ref, own_taps, own_bias, skips):
        held_ref[total:, :] = jnp.zeros((pad, held_ref.shape[1]), f32)

        def column(cols):
            sums = [jnp.zeros((1, 128), f32) for _ in range(taps + 2)]
            for at in range(0, total, 128):
                pre, shifted = conv_pre(x_ref, mask_ref, own_taps, own_bias, at, cols, 128)
                sig = sigmoid(pre)
                grad = grad_ref[at : at + 128, cols] * sig * (1.0 + pre * (1.0 - sig))
                held_ref[at : at + 128, cols] = grad
                for s in range(taps):
                    sums[taps - 1 - s] += jnp.sum(grad * shifted[s], axis=0, keepdims=True)
                sums[taps] += jnp.sum(grad, axis=0, keepdims=True)
                if skips:
                    act = act_ref[at : at + 128, cols]
                    over = grad_mixed_ref[at : at + 128, cols] * act
                    sums[taps + 1] += jnp.sum(over, axis=0, keepdims=True)
            for t, value in enumerate(sums):
                sums_ref[t : t + 1, cols] = value
            for at in range(0, total, 128):
                back = own_taps[taps - 1 : taps, cols] * held_ref[at : at + 128, cols]
                for s in range(1, taps):
                    part = held_ref[at + s : at + s + 128, cols]
                    part = part * mask_ref[s - 1, at + s : at + s + 128, :]
                    back = back + own_taps[taps - 1 - s : taps - s, cols] * part
                out_ref[at : at + 128, cols] = back.astype(bf16)

        column_loop(out_ref.shape[1], column)

    inner_sums_ref[...] = jnp.zeros(inner_sums_ref.shape, f32)
    inner_sums_ref[6:7, :] = norm_grad_ref[...]
    inner_sums_ref[8:10, :128] = head_sums[:2, :]
    state_sums_ref[...] = jnp.zeros(state_sums_ref.shape, f32)
    conv_back(
        raw_ref, grad_act_ref, pre_ref, grad_inner_ref, inner_sums_ref, taps_ref, bias_ref, True
    )
    conv_back(
        state_raw_ref,
        grad_state_ref,
        state_pre_ref,
        grad_state_low_ref,
        state_sums_ref,
        state_taps_ref,
        state_bias_ref,
        False,
    )

    chunks, tall = msg_ref.shape[0], msg_ref.shape[1] - head_rows
    msg_ref[...] = jnp.zeros(msg_ref.shape, bf16)

    def chunk(c, carry):
        at = pl.multiple_of(c * tall, tall)
        part = normed_ref[:, pl.ds(at, tall)]
        msg_ref[c, :tall, :] = mm(part, grad_inner_ref[...], (0, 0)).astype(bf16)
        msg_ref[c, tall:, :tall] = mm(step_grad_low, part).astype(bf16)
        state_part_ref[pl.ds(at, tall), :] = mm(part, grad_state_low_ref[...], (0, 0)).astype(bf16)
        return carry

    lax.fori_loop(0, chunks, chunk, 0)
    step_back = step_grad.T.astype(bf16)
    gain_part_ref[...] = jnp.zeros(gain_part_ref.shape, f32)
    for at in range(0, total, 128):
        rows = slice(at, at + 128)
        grad = mm(grad_gate_ref[rows, :], gate_weight_ref[...], (1, 1))
        grad = grad + mm(grad_inner_ref[rows, :], weight_ref[...], (1, 1))
        grad = grad + mm(grad_state_low_ref[rows, :], state_weight_ref[...], (1, 1))
        grad = grad + mm(step_back[rows, :], step_weight_ref[...])
        grad_normed_ref[rows, :] = grad.astype(bf16)
        value = rows_ref[rows, :].astype(f32)
        scale = lax.rsqrt(jnp.mean(value * value, axis=1, keepdims=True) + epsilon)
        gain_part_ref[...] += jnp.sum(grad * (value * scale), axis=0, keepdims=True)


def call(kernel, micros, scalars, arrays, outs, scratch):
    smem = pl.BlockSpec(memory_space=pltpu.SMEM)
    vmem = pl.BlockSpec(memory_space=pltpu.VMEM)
    return pl.pallas_call(
        kernel,
        out_shape=[jax.ShapeDtypeStruct(shape, kind) for shape, kind in outs],
        in_specs=[smem] * len(scalars) + [vmem] * len(arrays),
        out_specs=[vmem] * len(outs),
        scratch_shapes=[pltpu.VMEM(shape, kind) for shape, kind in scratch],
        compiler_params=pltpu.CompilerParams(vmem_limit_bytes=vmem_bytes),
        cost_estimate=pl.CostEstimate(
            flops=int(micros * 1.1e9), bytes_accessed=1 << 20, transcendentals=0
        ),
    )(*scalars, *arrays)


def ring_ok(n_dp, n_tensor):
    return n_dp == 8 and n_tensor == 4


ring_order = (0, 2, 4, 6, 7, 5, 3, 1)


def ring_place(index):
    high, low = index // 2, index % 2
    return jnp.where(low == 0, high, 7 - high)


def ring_index(place):
    place = lax.rem(place + 16, 8)
    return jnp.where(place < 4, 2 * place, 2 * (7 - place) + 1)


def ring_send(value, forward):
    pairs = []
    for place in range(8):
        other = (place + (1 if forward else 7)) % 8
        pairs.append((ring_order[place], ring_order[other]))
    return lax.ppermute(value, "dp", pairs)


def ring_gather(value):
    me = ring_place(lax.axis_index("dp"))
    pieces = [(value, ring_index(me))]
    ahead, back = value, value
    for step in range(1, 5):
        ahead = ring_send(ahead, True)
        pieces.append((ahead, ring_index(me - step)))
        if step < 4:
            back = ring_send(back, False)
            pieces.append((back, ring_index(me + step)))
    return pieces


def ring_scatter(parts):
    me = ring_place(lax.axis_index("dp"))

    def own(place):
        return lax.dynamic_index_in_dim(parts, ring_index(place), 0, keepdims=False).astype(f32)

    total = own(me)
    for forward, steps in ((True, 4), (False, 3)):
        sign = 1 if forward else -1
        held = own(me + sign * steps)
        for step in range(1, steps + 1):
            got = ring_send(held.astype(bf16), forward).astype(f32)
            if step < steps:
                held = got + own(me + sign * (steps - step))
            else:
                total = total + got
    return total


def tensor_swap(value, bit):
    return lax.ppermute(value, "tensor", [(i, i ^ bit) for i in range(4)])


def tensor_gather(value):
    near = tensor_swap(value, 1)
    far = tensor_swap(value, 2)
    return [value, near, far, tensor_swap(far, 1)]


def tensor_scatter(parts):
    me = lax.axis_index("tensor")
    core, across = me % 2, me // 2
    split = parts.reshape((2, 2) + parts.shape[1:])
    give = lax.dynamic_index_in_dim(split, 1 - core, 1, keepdims=False)
    keep = lax.dynamic_index_in_dim(split, core, 1, keepdims=False)
    got = tensor_swap(give, 1)
    half = keep.astype(f32) + got.astype(f32)
    give = lax.dynamic_index_in_dim(half, 1 - across, 0, keepdims=False)
    keep = lax.dynamic_index_in_dim(half, across, 0, keepdims=False)
    got = tensor_swap(give.astype(bf16), 2)
    return keep + got.astype(f32)


def body(
    tokens,
    lengths,
    cotangent,
    pre_gain,
    input_weight,
    step_weight,
    state_weight,
    conv_inner,
    conv_inner_bias,
    conv_state,
    conv_state_bias,
    step_bias,
    decay_log,
    skip_gain,
    norm_gain,
    output_weight,
):
    n_dp, n_tensor = lax.axis_size("dp"), lax.axis_size("tensor")
    fast = ring_ok(n_dp, n_tensor)
    owners = n_dp * n_tensor
    me = lax.axis_index("tensor")
    owner = lax.axis_index("dp") * n_tensor + me
    own_rows, depth = tokens.shape
    total = own_rows * n_tensor
    states = state_weight.shape[1]
    heads = step_weight.shape[1]
    share = state_weight.shape[0]
    taps = conv_state.shape[0]
    channels = input_weight.shape[2]
    inner_total = channels * n_tensor

    def placed(value, whole):
        zeros = jnp.zeros(value.shape[:-1] + (whole,), value.dtype)
        start = (0,) * (value.ndim - 1) + (owner * value.shape[-1],)
        return lax.dynamic_update_slice(zeros, value, start)

    small = jnp.concatenate(
        [
            placed(pre_gain, depth).reshape(-1, states),
            placed(conv_state, states),
            placed(conv_state_bias[None], states),
        ],
        axis=0,
    )
    small = jnp.pad(small, ((0, 16 - small.shape[0]), (0, 0)))
    step_rows = jnp.pad(step_weight.T, ((0, head_rows - heads), (0, 0)))
    gate_weight, inner_weight = input_weight[:, 0], input_weight[:, 1]
    if fast:
        late = ring_gather(jnp.concatenate([gate_weight, output_weight.T], axis=0))
        shared = jnp.concatenate([state_weight, small], axis=0)
        shared = lax.all_to_all(
            jnp.broadcast_to(shared, (4,) + shared.shape), "tensor", 0, 0, tiled=True
        )
        small = shared[0, share:] + shared[1, share:] + shared[2, share:] + shared[3, share:]
        tail = jnp.concatenate([small, step_rows], axis=1)
        tail = jnp.pad(tail, ((0, 0), (0, channels - tail.shape[1])))
        beside = [
            jnp.concatenate([shared[i, :share], shared[i + 1, :share]], axis=1) for i in (0, 2)
        ]
        msg = ring_gather(jnp.concatenate([inner_weight, *beside, tail], axis=0))
        row_pieces = tensor_gather(jnp.concatenate([tokens, cotangent], axis=0))
        grad_pieces = row_pieces
        weight_pieces = [piece for piece, _ in msg]
        late_pieces = [piece for piece, _ in late]
        place = jnp.stack([me, me ^ 1, me ^ 2, me ^ 3] + [index for _, index in msg])
    else:
        row_pieces = [lax.all_gather(tokens, "tensor", axis=0, tiled=True)]
        grad_pieces = [lax.all_gather(cotangent, "tensor", axis=0, tiled=True)]
        weight_pieces = [
            lax.all_gather(inner_weight, "dp", axis=0, tiled=True),
            lax.all_gather(state_weight, ("dp", "tensor"), axis=0, tiled=True),
            lax.all_gather(step_rows, "dp", axis=1, tiled=True),
            lax.psum(small, ("dp", "tensor")),
        ]
        late_pieces = [
            lax.all_gather(gate_weight, "dp", axis=0, tiled=True),
            lax.all_gather(output_weight.T, "dp", axis=0, tiled=True),
        ]
        place = jnp.zeros((12,), jnp.int32)
    place = place.astype(jnp.int32)

    def row(value):
        return value.astype(f32).reshape(1, -1)

    def head(value):
        return jnp.pad(value.astype(f32), (0, head_rows - heads))

    taps_float = conv_inner.astype(f32)
    scan_params = [
        taps_float,
        row(conv_inner_bias),
        head(step_bias)[None, :],
        head(step_bias)[:, None],
        head(decay_log)[None, :],
        head(decay_log)[:, None],
        row(jnp.repeat(skip_gain, channels // heads)),
    ]
    masks = ((taps - 1, total + pad, 128), f32)
    state_taps = [((taps, states), f32), ((1, states), f32)]
    (
        rows,
        normed,
        inner_full,
        state_full,
        step_full,
        small_full,
        raw,
        state_raw,
        step_col,
        step_row,
        act,
        state_act,
        mixed,
    ) = call(
        functools.partial(forward_kernel, fast),
        12,
        [place, lengths],
        row_pieces + weight_pieces + scan_params,
        [
            ((total, depth), bf16),
            ((total, depth), bf16),
            ((depth, channels), bf16),
            ((depth, states), bf16),
            ((head_rows, depth), bf16),
            ((16, states), f32),
            ((total + pad, channels), f32),
            ((total + pad, states), f32),
            ((total, head_rows), f32),
            ((head_rows, total), f32),
            ((total, channels), f32),
            ((total, states), f32),
            ((total, channels), f32),
        ],
        [masks] + state_taps,
    )
    norm_row = row(norm_gain)
    grad_rows, gate_full, output_full, gate, grad_normalized, sums = call(
        functools.partial(grad_in_kernel, fast),
        5,
        [place, lengths],
        grad_pieces + late_pieces + [normed, mixed, norm_row],
        [
            ((total, depth), bf16),
            ((depth, channels), bf16),
            ((depth, channels), bf16),
            ((total, channels), f32),
            ((total, channels), f32),
            ((8, total), f32),
        ],
        [((total, 128), f32)],
    )
    if fast:
        sums = sums + tensor_swap(sums, 1)
        sums = sums + tensor_swap(sums, 2)
    else:
        sums = lax.psum(sums, "tensor")
    chunks = 8
    tall = depth // chunks
    partial_out, gate_msg, grad_gate, grad_mixed, norm_grad = call(
        functools.partial(norm_kernel, inner_total),
        9,
        [lengths],
        [sums, gate, mixed, grad_normalized, norm_row, output_full, grad_rows, normed],
        [
            ((total, depth), bf16),
            ((chunks, 2 * tall, channels), bf16),
            ((total, channels), bf16),
            ((total, channels), f32),
            ((1, channels), f32),
        ],
        [((total, 128), f32), ((total, channels), bf16)],
    )
    (
        inner_msg,
        state_part,
        gain_part,
        grad_normed,
        sums,
        state_sums,
    ) = call(
        backward_kernel,
        23,
        [lengths],
        [
            grad_mixed,
            act,
            state_act,
            raw,
            state_raw,
            step_col,
            step_row,
            grad_gate,
            normed,
            rows,
            gate_full,
            inner_full,
            state_full,
            step_full,
            small_full,
            norm_grad,
        ]
        + scan_params,
        [
            ((chunks, tall + head_rows, channels), bf16),
            ((depth, states), bf16),
            ((1, depth), f32),
            ((total, depth), bf16),
            ((16, channels), f32),
            ((8, states), f32),
        ],
        [
            masks,
            *state_taps,
            ((span, span), f32),
            ((total, channels), f32),
            ((total, states), f32),
            ((total + pad, channels), f32),
            ((total + pad, states), f32),
            ((total, channels), bf16),
            ((total, states), bf16),
        ],
    )

    token_float = tokens.astype(f32)
    gain_full = small_full[: depth // states].reshape(1, depth)

    def lay(value):
        value = value.reshape(owners, -1)
        return jnp.pad(value, ((0, 0), (0, states - value.shape[1])))[:, None, :].astype(bf16)

    conv_state_owned = state_sums[:taps].reshape(taps, owners, -1).transpose(1, 0, 2)
    shared_part = jnp.concatenate(
        [
            state_part.reshape(owners, share, states),
            lay(gain_part),
            lay(conv_state_owned),
            lay(state_sums[taps]),
        ],
        axis=1,
    )
    shared_part = jnp.pad(shared_part, ((0, 0), (0, -shared_part.shape[1] % 8), (0, 0)))
    if fast:
        mixed_rows = tensor_scatter(partial_out.reshape((n_tensor, -1, depth)))
        grad_local = tensor_scatter(grad_normed.reshape((n_tensor, -1, depth)))
        shared_mine = lax.all_to_all(shared_part, ("dp", "tensor"), 0, 0, tiled=True)
        shared_mine = jnp.sum(shared_mine.astype(f32), axis=0)
        gate_out = ring_scatter(gate_msg)
        gate_grad, output_grad = gate_out[:tall], gate_out[tall:].T
        inner_out = ring_scatter(inner_msg)
        inner_grad, step_grad = inner_out[:tall], inner_out[tall : tall + heads, :tall].T
        sums = lax.all_to_all(
            jnp.broadcast_to(sums, (n_dp,) + sums.shape), "dp", 0, 0, tiled=True
        )
        sums = jnp.sum(sums, axis=0)
    else:
        mixed_rows = lax.psum_scatter(
            partial_out, "tensor", scatter_dimension=0, tiled=True
        ).astype(f32)
        grad_local = lax.psum_scatter(
            grad_normed, "tensor", scatter_dimension=0, tiled=True
        ).astype(f32)
        shared_mine = lax.psum_scatter(
            shared_part.astype(f32), ("dp", "tensor"), scatter_dimension=0, tiled=True
        )[0]
        both, inner_float = gate_msg.astype(f32), inner_msg.astype(f32)
        gate_grad, output_grad, inner_grad = (
            lax.psum_scatter(part.reshape(depth, channels), "dp", scatter_dimension=0, tiled=True)
            for part in (both[:, :tall], both[:, tall:], inner_float[:, :tall])
        )
        output_grad = output_grad.T
        step_part = inner_float[:, tall : tall + heads, :tall].transpose(0, 2, 1)
        step_part = step_part.reshape(depth, heads)
        step_grad = lax.psum_scatter(step_part, "dp", scatter_dimension=0, tiled=True)
        sums = lax.psum(sums, "dp")
    input_grad = jnp.stack([gate_grad, inner_grad], axis=1)
    block_out = (token_float + mixed_rows).astype(bf16)
    scale = lax.rsqrt(jnp.mean(token_float * token_float, axis=1, keepdims=True) + epsilon)
    grad_scaled = grad_local * gain_full
    along = jnp.sum(grad_scaled * token_float, axis=1, keepdims=True) / depth
    tokens_grad = (
        scale * grad_scaled
        - token_float * (scale * scale * scale * along)
        + cotangent.astype(f32)
    )
    state_grad = shared_mine[:share]
    pre_gain_grad = shared_mine[share, : depth // owners]
    conv_state_grad = shared_mine[share + 1, : taps * (states // owners)].reshape(taps, -1)
    conv_state_bias_grad = shared_mine[share + 2, : states // owners]

    skip_grad = sums[taps + 1].reshape(heads, -1).sum(axis=1)
    return (
        block_out,
        tokens_grad,
        pre_gain_grad,
        input_grad,
        step_grad,
        state_grad,
        sums[:taps],
        sums[taps],
        conv_state_grad,
        conv_state_bias_grad,
        sums[8, :heads],
        sums[9, :heads],
        skip_grad,
        sums[6],
        output_grad,
    )


def solution(mesh):
    in_specs = (
        P(("dp", "tensor"), None),
        P("dp", None),
        P(("dp", "tensor"), None),
        P(("dp", "tensor")),
        P("dp", None, "tensor"),
        P("dp", "tensor"),
        P(("dp", "tensor"), None),
        P(None, "tensor"),
        P("tensor"),
        P(None, ("dp", "tensor")),
        P(("dp", "tensor")),
        P("tensor"),
        P("tensor"),
        P("tensor"),
        P("tensor"),
        P("tensor", "dp"),
    )
    out_specs = (
        P(("dp", "tensor"), None),
        P(("dp", "tensor"), None),
        P(("dp", "tensor")),
        P("dp", None, "tensor"),
        P("dp", "tensor"),
        P(("dp", "tensor"), None),
        P(None, "tensor"),
        P("tensor"),
        P(None, ("dp", "tensor")),
        P(("dp", "tensor")),
        P("tensor"),
        P("tensor"),
        P("tensor"),
        P("tensor"),
        P("tensor", "dp"),
    )
    return jax.shard_map(body, mesh=mesh, in_specs=in_specs, out_specs=out_specs, check_vma=False)
```

```python
import functools

import jax
import jax.numpy as jnp
from jax import lax
from jax.experimental import pallas as pl
from jax.experimental.pallas import tpu as pltpu
from jax.sharding import PartitionSpec as P

epsilon = 1e-05
highest = lax.Precision.HIGHEST
f32 = jnp.float32
bf16 = jnp.bfloat16
span = 256
pad = 8
head_rows = 16
head_width = 64
vmem_bytes = 54 * 1024 * 1024


def mm(a, b, over=(1, 0)):
    dims = (((over[0],), (over[1],)), ((), ()))
    return lax.dot_general(a, b, dims, preferred_element_type=f32)


def mm_exact(a, b, over=(1, 0)):
    dims = (((over[0],), (over[1],)), ((), ()))
    return lax.dot_general(a, b, dims, preferred_element_type=f32, precision=highest)


def sigmoid(v):
    return 1.0 / (1.0 + jnp.exp(-v))


def ends_of(lengths_ref):
    ends, total = [], None
    for slot in range(lengths_ref.shape[1]):
        here = lengths_ref[0, slot]
        total = here if total is None else total + here
        ends.append(total)
    return ends


def segment_of(places, ends):
    segment = jnp.zeros(places.shape, jnp.int32)
    for end in ends:
        segment = segment + jnp.where(places >= end, 1, 0)
    return segment


def iota(shape, dim):
    return lax.broadcasted_iota(jnp.int32, shape, dim)


def write_masks(mask_ref, ends):
    rows = mask_ref.shape[1] - pad
    places = iota((rows, 128), 0)
    segment = segment_of(places, ends)
    for shift in range(1, mask_ref.shape[0] + 1):
        same = (segment_of(places - shift, ends) == segment) & (places >= shift)
        mask_ref[shift - 1, :rows, :] = jnp.where(same, 1.0, 0.0)
        mask_ref[shift - 1, rows:, :] = jnp.zeros((pad, 128), f32)


def shifted_rows(x_ref, mask_ref, at, cols, shift, tall):
    part = x_ref[pad + at - shift : pad + at - shift + tall, cols]
    if shift == 0:
        return part
    return part * mask_ref[shift - 1, at : at + tall, :]


def conv_pre(x_ref, mask_ref, taps_ref, bias_ref, at, cols, tall):
    taps = taps_ref.shape[0]
    shifted = [shifted_rows(x_ref, mask_ref, at, cols, s, tall) for s in range(taps)]
    total = bias_ref[:, cols]
    for s in range(taps):
        total = total + taps_ref[taps - 1 - s : taps - s, cols] * shifted[s]
    return total, shifted


def column_loop(width, step):
    def one(c, carry):
        step(pl.ds(pl.multiple_of(c * 128, 128), 128))
        return carry

    lax.fori_loop(0, width // 128, one, 0)


def row_loop(rows, tall, step):
    def one(r, carry):
        step(pl.multiple_of(r * tall, tall))
        return carry

    lax.fori_loop(0, rows // tall, one, 0)


def for_chunks(place_ref, give_ref, keep_ref, step):
    side = place_ref[8]

    def one(c, carry):
        step(c, 1 - side, give_ref)
        step(c, side, keep_ref)
        return carry

    lax.fori_loop(0, give_ref.shape[0], one, 0)


class Block:
    def __init__(self, b, ends, step_col, step_row, rate_col, rate_row, state_ref):
        low, top = b * span, (b + 1) * span
        states = state_ref.shape[1] // 2
        lower = jnp.where(iota((span, span), 0) >= iota((span, span), 1), 1.0, 0.0)
        self.rows = slice(low, top)
        self.step = step_col[low:top]
        self.step_row = step_row[:, low:top]
        self.cum = mm_exact(lower, rate_col[low:top])
        self.cum_row = mm_exact(rate_row[:, low:top], lower, (1, 1))
        self.inputs = state_ref[low:top, :states].astype(bf16)
        self.outputs = state_ref[low:top, states:].astype(bf16)
        segment = segment_of(iota((span, 1), 0) + low, ends)
        segment_row = segment_of(iota((1, span), 1) + low, ends)
        edge = sum(jnp.where(span - 1 >= end, 1, 0) for end in ends)
        self.near_edge = jnp.where(segment == edge, 1.0, 0.0)
        self.mask = jnp.where(segment == segment_row, lower, 0.0)
        self.contact = mm(self.outputs, self.inputs, (1, 1)) * self.mask

    def decay(self, h):
        gap = self.cum[:, h : h + 1] - self.cum_row[h : h + 1, :]
        return jnp.exp(jnp.minimum(gap, 0.0))

    def from_edge(self, h):
        return jnp.exp(self.cum[:, h : h + 1]) * self.near_edge

    def to_edge(self, h):
        last = self.cum[span - 1 : span, h : h + 1]
        return jnp.exp(last - self.cum[:, h : h + 1]) * self.near_edge


def wide(low_half, left, right):
    return jnp.where(low_half, left, right)


def step_sizes(raw_col, raw_row, bias_ref, bias_col_ref, log_ref, log_col_ref):
    def soft(v):
        return jnp.maximum(v, 0.0) + jnp.log1p(jnp.exp(-jnp.abs(v)))

    step_col = soft(raw_col + bias_ref[...])
    step_row = soft(raw_row + bias_col_ref[...])
    rate_col = -step_col * jnp.exp(log_ref[...])
    rate_row = -step_row * jnp.exp(log_col_ref[...])
    return step_col, step_row, rate_col, rate_row


def forward_kernel(fast, place_ref, lengths_ref, *refs):
    n_msg = 8 if fast else 4
    rows_ref, msg_refs, refs = refs[0], refs[1 : 1 + n_msg], refs[1 + n_msg :]
    (taps_ref, bias_ref, step_bias_ref, step_bias_col_ref, log_ref, log_col_ref, skip_ref) = refs[:7]
    (
        normed_ref,
        weight_ref,
        state_weight_ref,
        step_weight_ref,
        small_ref,
        raw_ref,
        state_raw_ref,
        step_col_ref,
        step_row_ref,
        act_ref,
        state_ref,
        mixed_ref,
    ) = refs[7:19]
    mask_ref, state_taps_ref, state_bias_ref = refs[19:]
    total = rows_ref.shape[0]
    channels = act_ref.shape[1]
    ends = ends_of(lengths_ref)

    if fast:
        depth_part = 128
        small = jnp.zeros(small_ref.shape, f32)
        share = state_weight_ref.shape[0] // 32
        for slot in range(8):
            msg = msg_refs[slot]
            index = place_ref[slot]
            at = pl.multiple_of(index * depth_part, depth_part)
            weight_ref[pl.ds(at, depth_part), :] = msg[:depth_part, :]
            for member in range(4):
                inner = pl.multiple_of(at + member * share, share)
                high, low = depth_part + share * (member // 2), 256 * (member % 2)
                state_weight_ref[pl.ds(inner, share), :] = msg[
                    high : high + share, low : low + 256
                ]
            tail = depth_part + 2 * share
            small = small + msg[tail : tail + 16, :256].astype(f32)
            step_weight_ref[:, pl.ds(at, depth_part)] = msg[tail : tail + 16, 256:384]
        small_ref[...] = small
    else:
        weight_ref[...] = msg_refs[0][...]
        state_weight_ref[...] = msg_refs[1][...]
        step_weight_ref[...] = msg_refs[2][...]
        small_ref[...] = msg_refs[3][...].astype(f32)
    gain = jnp.concatenate([small_ref[i : i + 1, :] for i in range(4)], axis=1)
    taps = taps_ref.shape[0]
    state_taps_ref[...] = small_ref[4 : 4 + taps, :]
    state_bias_ref[...] = small_ref[4 + taps : 5 + taps, :]

    def norm(at):
        value = rows_ref[pl.ds(at, 128), :].astype(f32)
        scale = lax.rsqrt(jnp.mean(value * value, axis=1, keepdims=True) + epsilon)
        normed_ref[pl.ds(at, 128), :] = (value * scale * gain).astype(bf16)

    row_loop(total, 128, norm)

    raw_ref[:pad, :] = jnp.zeros((pad, channels), f32)
    state_raw_ref[:pad, :] = jnp.zeros((pad, state_raw_ref.shape[1]), f32)

    def project(at):
        part = normed_ref[pl.ds(at, 128), :]
        raw_ref[pl.ds(at + pad, 128), :] = mm(part, weight_ref[...])
        state_raw_ref[pl.ds(at + pad, 128), :] = mm(part, state_weight_ref[...])
        step_col_ref[pl.ds(at, 128), :] = mm(part, step_weight_ref[...], (1, 1))

    row_loop(total, 128, project)
    step_row_ref[...] = mm(step_weight_ref[...], normed_ref[...], (1, 1))

    write_masks(mask_ref, ends)

    def activate(x_ref, out_ref, own_taps, own_bias):
        def column(cols):
            for at in range(0, total, 128):
                pre, _ = conv_pre(x_ref, mask_ref, own_taps, own_bias, at, cols, 128)
                out_ref[at : at + 128, cols] = pre * sigmoid(pre)

        column_loop(out_ref.shape[1], column)

    activate(raw_ref, act_ref, taps_ref, bias_ref)
    activate(state_raw_ref, state_ref, state_taps_ref, state_bias_ref)

    steps = step_sizes(
        step_col_ref[...],
        step_row_ref[...],
        step_bias_ref,
        step_bias_col_ref,
        log_ref,
        log_col_ref,
    )
    low_half = iota((span, 128), 1) < head_width
    held = []
    for b in range(total // span):
        block = Block(b, ends, *steps, state_ref)
        for i in range(channels // 128):
            cols = slice(128 * i, 128 * (i + 1))
            pair = (2 * i, 2 * i + 1)
            x = act_ref[block.rows, cols]
            step_wide = wide(low_half, *(block.step[:, h : h + 1] for h in pair))
            x_step = (x * step_wide).astype(bf16)
            y = [mm((block.decay(h) * block.contact).astype(bf16), x_step) for h in pair]
            y = wide(low_half, *y) + skip_ref[:, cols] * x
            if b == 0:
                reach = wide(low_half, *(block.to_edge(h) for h in pair))
                weighted = (x * step_wide * reach).astype(bf16)
                held.append(mm(block.inputs, weighted, (0, 0)).astype(bf16))
            else:
                reach = wide(low_half, *(block.from_edge(h) for h in pair))
                y = y + reach * mm(block.outputs, held[i])
            mixed_ref[block.rows, cols] = y


def grad_in_kernel(fast, place_ref, lengths_ref, *refs):
    n_msg = 8 if fast else 2
    rows_ref, msg_refs, refs = refs[0], refs[1 : 1 + n_msg], refs[1 + n_msg :]
    normed_ref, mixed_ref, norm_ref = refs[:3]
    gate_weight_ref, out_weight_ref, gate_ref, grad_ref, sums_ref, wide_ref = refs[3:]
    total = rows_ref.shape[0]
    ends = ends_of(lengths_ref)
    if fast:
        for slot in range(8):
            at = pl.multiple_of(place_ref[slot] * 128, 128)
            gate_weight_ref[pl.ds(at, 128), :] = msg_refs[slot][:128, :]
            out_weight_ref[pl.ds(at, 128), :] = msg_refs[slot][128:, :]
    else:
        gate_weight_ref[...] = msg_refs[0][...]
        out_weight_ref[...] = msg_refs[1][...]

    def part(at):
        rows = pl.ds(at, 128)
        valid = jnp.where(iota((128, 1), 0) + at < ends[-1], 1.0, 0.0)
        grad = mm(rows_ref[rows, :], out_weight_ref[...]) * valid
        grad_ref[rows, :] = grad
        gate = mm(normed_ref[rows, :], gate_weight_ref[...])
        gate_ref[rows, :] = gate
        gated = mixed_ref[rows, :] * (gate * sigmoid(gate))
        square = jnp.sum(gated * gated, axis=1, keepdims=True)
        cross = jnp.sum(grad * norm_ref[...] * gated, axis=1, keepdims=True)
        lane = iota((128, 128), 1)
        wide_ref[rows, :] = jnp.where(lane == 0, square, jnp.where(lane == 1, cross, 0.0))

    row_loop(total, 128, part)
    for at in range(0, total, 128):
        sums_ref[:, at : at + 128] = wide_ref[at : at + 128, :].T[:8, :]


def norm_kernel(inner_total, place_ref, lengths_ref, *refs):
    (sums_ref, gate_ref, mixed_ref, grad_ref, norm_ref, weight_ref, rows_ref, normed_ref) = refs[:8]
    partial_ref, give_ref, keep_ref, grad_gate_ref, grad_mixed_ref, norm_grad_ref = refs[8:14]
    wide_ref, out_rows_ref = refs[14:]
    total, channels = gate_ref.shape
    ends = ends_of(lengths_ref)
    for at in range(0, total, 128):
        tile = jnp.concatenate([sums_ref[:, at : at + 128]] * 16, axis=0)
        wide_ref[at : at + 128, :] = tile.T
    norm_grad_ref[...] = jnp.zeros(norm_grad_ref.shape, f32)

    def part(at):
        rows = pl.ds(at, 128)
        valid = jnp.where(iota((128, 1), 0) + at < ends[-1], 1.0, 0.0)
        scale = lax.rsqrt(wide_ref[rows, 0:1] / inner_total + epsilon)
        cross = wide_ref[rows, 1:2]
        gate = gate_ref[rows, :]
        mixed = mixed_ref[rows, :]
        sig = sigmoid(gate)
        gate_act = gate * sig
        gated = mixed * gate_act
        grad = grad_ref[rows, :]
        norm = norm_ref[...]
        hat = gated * scale
        out_rows_ref[rows, :] = (hat * norm * valid).astype(bf16)
        norm_grad_ref[...] += jnp.sum(grad * hat, axis=0, keepdims=True)
        grad_gated = scale * (grad * norm) - gated * (scale * scale * scale * cross / inner_total)
        grad_mixed_ref[rows, :] = grad_gated * gate_act
        grad_gate = grad_gated * mixed * sig * (1.0 + gate * (1.0 - sig))
        grad_gate_ref[rows, :] = grad_gate.astype(bf16)
        partial_ref[rows, :] = mm(out_rows_ref[rows, :], weight_ref[...], (1, 1)).astype(bf16)

    row_loop(total, 128, part)

    tall = give_ref.shape[1] // 2

    def chunk(c, side, msg_ref):
        cols = pl.ds(pl.multiple_of((2 * c + side) * tall, tall), tall)
        msg_ref[c, :tall, :] = mm(normed_ref[:, cols], grad_gate_ref[...], (0, 0)).astype(bf16)
        msg_ref[c, tall:, :] = mm(rows_ref[:, cols], out_rows_ref[...], (0, 0)).astype(bf16)

    for_chunks(place_ref, give_ref, keep_ref, chunk)


def scan_back_kernel(lengths_ref, *refs):
    grad_mixed_ref, act_ref, state_ref, step_col_ref, step_row_ref = refs[:5]
    step_bias_ref, step_bias_col_ref, log_ref, log_col_ref, skip_ref = refs[5:10]
    grad_act_ref, grad_state_ref, step_grad_ref, sums_ref, acc_ref = refs[10:]
    total, channels = grad_mixed_ref.shape
    states = state_ref.shape[1] // 2
    ends = ends_of(lengths_ref)
    sums_ref[...] = jnp.zeros(sums_ref.shape, f32)
    raw_row = step_row_ref[...]
    steps = step_sizes(
        step_col_ref[...], raw_row, step_bias_ref, step_bias_col_ref, log_ref, log_col_ref
    )
    rate_row = steps[3]
    low_half = iota((span, 128), 1) < head_width
    lower = jnp.where(iota((span, span), 0) >= iota((span, span), 1), 1.0, 0.0)
    blocks = [Block(b, ends, *steps, state_ref) for b in range(total // span)]
    first, second = blocks
    row_sums, step_rows, out_sums, in_sums = [], [], None, None
    grad_out = jnp.zeros((span, states), f32)
    grad_in = jnp.zeros((span, states), f32)
    head_of = iota((head_rows, 128), 0)
    lane_head = iota((head_rows, 128), 1) // head_width

    for b, block in enumerate(blocks):
        acc_ref[...] = jnp.zeros((span, span), f32)
        row_sum = jnp.zeros((span, 128), f32)
        step_grad = jnp.zeros((head_rows, span), f32)
        lane = iota((span, 128), 1)
        head_row = iota((head_rows, span), 0)
        for i in range(channels // 128):
            cols = slice(128 * i, 128 * (i + 1))
            pair = (2 * i, 2 * i + 1)
            x = act_ref[block.rows, cols]
            x_low = x.astype(bf16)
            grad = grad_mixed_ref[block.rows, cols]
            grad_low = grad.astype(bf16)
            halves = (
                jnp.where(low_half, grad, 0.0).astype(bf16),
                jnp.where(low_half, 0.0, grad).astype(bf16),
            )
            step_wide = wide(low_half, *(block.step[:, h : h + 1] for h in pair))
            grads = []
            for h, half in zip(pair, halves):
                decay = block.decay(h)
                spread = mm(half, x_low, (1, 1)) * decay
                stepped = spread * block.step_row[h : h + 1, :]
                acc_ref[...] += stepped
                row_here = jnp.sum(stepped * block.contact, axis=1, keepdims=True)
                row_sum = jnp.where(lane == h, row_here, row_sum)
                step_here = jnp.sum(spread * block.contact, axis=0, keepdims=True)
                step_grad = jnp.where(head_row == h, step_here, step_grad)
                grads.append(mm((decay * block.contact).astype(bf16), grad_low, (0, 0)))
            grad_act = wide(low_half, *grads) * step_wide + skip_ref[:, cols] * grad
            sums_ref[2:3, cols] += jnp.sum(grad * x, axis=0, keepdims=True)
            picks = jnp.where(lane_head + 2 * i == head_of, 1.0, 0.0)
            if b == 0:
                reach = wide(low_half, *(second.from_edge(h) for h in pair))
                lead = (grad_mixed_ref[second.rows, cols] * reach).astype(bf16)
                edge = wide(low_half, *(block.to_edge(h) for h in pair))
                weighted = (x * step_wide * edge).astype(bf16)
                held = mm(block.inputs, weighted, (0, 0)).astype(bf16)
                held_grad = mm(second.outputs, lead, (0, 0)).astype(bf16)
                grad_out = grad_out + mm(lead, held, (1, 1))
                grad_in = grad_in + mm(weighted, held_grad, (1, 1))
                back = mm(block.inputs, held_grad) * edge
                grad_act = grad_act + back * step_wide
                ahead = mm(second.outputs, held)
                out_here = mm_exact(picks, lead.astype(f32) * ahead, (1, 1))
                in_here = mm_exact(picks, x * back, (1, 1))
                out_sums = out_here if out_sums is None else out_sums + out_here
                in_sums = in_here if in_sums is None else in_sums + in_here
            grad_act_ref[block.rows, cols] = grad_act
        table = (acc_ref[...] * block.mask).astype(bf16)
        grad_c = mm(table, block.inputs)
        grad_b = mm(table, block.outputs, (0, 0))
        if b == 0:
            grad_b = grad_b + grad_in
        else:
            grad_c = grad_c + grad_out
        grad_state_ref[block.rows, :states] = grad_b
        grad_state_ref[block.rows, states:] = grad_c
        row_sums.append(row_sum)
        step_rows.append(step_grad)

    rate_grads = []
    for b, block in enumerate(blocks):
        column = step_rows[b] * block.step_row
        crossing = mm_exact(row_sums[b], lower, (0, 0))[:head_rows] - mm_exact(column, lower)
        if b == 0:
            crossing = crossing + mm_exact(in_sums * block.step_row, 1.0 - lower)
        else:
            crossing = crossing + mm_exact(out_sums, lower)
        rate_grads.append(crossing)
    step_rows[0] = step_rows[0] + in_sums
    rate_grad = jnp.concatenate(rate_grads, axis=1)
    step_grad = jnp.concatenate(step_rows, axis=1) - rate_grad * jnp.exp(log_col_ref[...])
    step_grad = step_grad * sigmoid(raw_row + step_bias_col_ref[...])
    decay_sum = jnp.sum(rate_grad * rate_row, axis=1, keepdims=True)
    bias_sum = jnp.sum(step_grad, axis=1, keepdims=True)
    lane = iota((head_rows, 128), 1)
    head_sums = jnp.where(lane == 0, bias_sum, jnp.where(lane == 1, decay_sum, 0.0))
    head_sums = jnp.concatenate([head_sums] * (128 // head_rows), axis=0).T
    sums_ref[0:2, :128] = head_sums[:2, :]
    step_grad_ref[...] = step_grad


def backward_kernel(place_ref, lengths_ref, *refs):
    (
        grad_act_ref,
        grad_state_ref,
        step_grad_ref,
        head_sums_ref,
        raw_ref,
        state_raw_ref,
        grad_gate_ref,
        normed_ref,
        rows_ref,
        gate_weight_ref,
        weight_ref,
        state_weight_ref,
        step_weight_ref,
        small_ref,
        norm_grad_ref,
        taps_ref,
        bias_ref,
    ) = refs[:17]
    (
        give_ref,
        keep_ref,
        state_part_ref,
        gain_part_ref,
        grad_normed_ref,
        inner_sums_ref,
        state_sums_ref,
    ) = refs[17:24]
    (
        mask_ref,
        state_taps_ref,
        state_bias_ref,
        pre_ref,
        state_pre_ref,
        grad_inner_ref,
        grad_state_low_ref,
    ) = refs[24:]
    total = grad_act_ref.shape[0]
    ends = ends_of(lengths_ref)
    taps = taps_ref.shape[0]
    state_taps_ref[...] = small_ref[4 : 4 + taps, :]
    state_bias_ref[...] = small_ref[4 + taps : 5 + taps, :]
    write_masks(mask_ref, ends)
    step_grad = step_grad_ref[...]
    step_grad_low = step_grad.astype(bf16)

    def conv_back(x_ref, grad_ref, held_ref, out_ref, sums_ref, own_taps, own_bias):
        held_ref[total:, :] = jnp.zeros((pad, held_ref.shape[1]), f32)

        def column(cols):
            sums = [jnp.zeros((1, 128), f32) for _ in range(taps + 1)]
            for at in range(0, total, 128):
                pre, shifted = conv_pre(x_ref, mask_ref, own_taps, own_bias, at, cols, 128)
                sig = sigmoid(pre)
                grad = grad_ref[at : at + 128, cols] * sig * (1.0 + pre * (1.0 - sig))
                held_ref[at : at + 128, cols] = grad
                for s in range(taps):
                    sums[taps - 1 - s] += jnp.sum(grad * shifted[s], axis=0, keepdims=True)
                sums[taps] += jnp.sum(grad, axis=0, keepdims=True)
            for t, value in enumerate(sums):
                sums_ref[t : t + 1, cols] = value
            for at in range(0, total, 128):
                back = own_taps[taps - 1 : taps, cols] * held_ref[at : at + 128, cols]
                for s in range(1, taps):
                    part = held_ref[at + s : at + s + 128, cols]
                    part = part * mask_ref[s - 1, at + s : at + s + 128, :]
                    back = back + own_taps[taps - 1 - s : taps - s, cols] * part
                out_ref[at : at + 128, cols] = back.astype(bf16)

        column_loop(out_ref.shape[1], column)

    inner_sums_ref[...] = jnp.zeros(inner_sums_ref.shape, f32)
    inner_sums_ref[6:7, :] = norm_grad_ref[...]
    inner_sums_ref[7:10, :] = head_sums_ref[:3, :]
    state_sums_ref[...] = jnp.zeros(state_sums_ref.shape, f32)
    conv_back(
        raw_ref, grad_act_ref, pre_ref, grad_inner_ref, inner_sums_ref, taps_ref, bias_ref
    )
    conv_back(
        state_raw_ref,
        grad_state_ref,
        state_pre_ref,
        grad_state_low_ref,
        state_sums_ref,
        state_taps_ref,
        state_bias_ref,
    )

    tall = give_ref.shape[1] - head_rows
    give_ref[...] = jnp.zeros(give_ref.shape, bf16)
    keep_ref[...] = jnp.zeros(keep_ref.shape, bf16)

    def chunk(c, side, msg_ref):
        at = pl.multiple_of((2 * c + side) * tall, tall)
        part = normed_ref[:, pl.ds(at, tall)]
        msg_ref[c, :tall, :] = mm(part, grad_inner_ref[...], (0, 0)).astype(bf16)
        msg_ref[c, tall:, :tall] = mm(step_grad_low, part).astype(bf16)
        state_part_ref[pl.ds(at, tall), :] = mm(part, grad_state_low_ref[...], (0, 0)).astype(bf16)

    for_chunks(place_ref, give_ref, keep_ref, chunk)
    step_back = step_grad.T.astype(bf16)
    gain_part_ref[...] = jnp.zeros(gain_part_ref.shape, f32)
    for at in range(0, total, 128):
        rows = slice(at, at + 128)
        grad = mm(grad_gate_ref[rows, :], gate_weight_ref[...], (1, 1))
        grad = grad + mm(grad_inner_ref[rows, :], weight_ref[...], (1, 1))
        grad = grad + mm(grad_state_low_ref[rows, :], state_weight_ref[...], (1, 1))
        grad = grad + mm(step_back[rows, :], step_weight_ref[...])
        grad_normed_ref[rows, :] = grad.astype(bf16)
        value = rows_ref[rows, :].astype(f32)
        scale = lax.rsqrt(jnp.mean(value * value, axis=1, keepdims=True) + epsilon)
        gain_part_ref[...] += jnp.sum(grad * (value * scale), axis=0, keepdims=True)


def call(kernel, micros, scalars, arrays, outs, scratch):
    smem = pl.BlockSpec(memory_space=pltpu.SMEM)
    vmem = pl.BlockSpec(memory_space=pltpu.VMEM)
    return pl.pallas_call(
        kernel,
        out_shape=[jax.ShapeDtypeStruct(shape, kind) for shape, kind in outs],
        in_specs=[smem] * len(scalars) + [vmem] * len(arrays),
        out_specs=[vmem] * len(outs),
        scratch_shapes=[pltpu.VMEM(shape, kind) for shape, kind in scratch],
        compiler_params=pltpu.CompilerParams(vmem_limit_bytes=vmem_bytes),
        cost_estimate=pl.CostEstimate(
            flops=int(micros * 1.1e9), bytes_accessed=1 << 20, transcendentals=0
        ),
    )(*scalars, *arrays)


def ring_ok(n_dp, n_tensor):
    return n_dp == 8 and n_tensor == 4


ring_order = (0, 2, 4, 6, 7, 5, 3, 1)


def ring_place(index):
    high, low = index // 2, index % 2
    return jnp.where(low == 0, high, 7 - high)


def ring_index(place):
    place = lax.rem(place + 16, 8)
    return jnp.where(place < 4, 2 * place, 2 * (7 - place) + 1)


def ring_send(value, forward):
    pairs = []
    for place in range(8):
        other = (place + (1 if forward else 7)) % 8
        pairs.append((ring_order[place], ring_order[other]))
    return lax.ppermute(value, "dp", pairs)


def ring_gather(value):
    me = ring_place(lax.axis_index("dp"))
    pieces = [(value, ring_index(me))]
    ahead, back = value, value
    for step in range(1, 5):
        ahead = ring_send(ahead, True)
        pieces.append((ahead, ring_index(me - step)))
        if step < 4:
            back = ring_send(back, False)
            pieces.append((back, ring_index(me + step)))
    return pieces


def side_sum(give, keep):
    got = lax.ppermute(give, "dp", [(i, i ^ 1) for i in range(8)])
    return (keep.astype(f32) + got.astype(f32)).astype(bf16)


def line_blocks(half):
    lines = [[0, 2, 4, 6], [1, 3, 5, 7]]
    return lax.all_to_all(half, "dp", 0, 0, axis_index_groups=lines, tiled=True)


def tensor_swap(value, bit):
    return lax.ppermute(value, "tensor", [(i, i ^ bit) for i in range(4)])


def body(
    tokens,
    lengths,
    cotangent,
    pre_gain,
    input_weight,
    step_weight,
    state_weight,
    conv_inner,
    conv_inner_bias,
    conv_state,
    conv_state_bias,
    step_bias,
    decay_log,
    skip_gain,
    norm_gain,
    output_weight,
):
    n_dp, n_tensor = lax.axis_size("dp"), lax.axis_size("tensor")
    fast = ring_ok(n_dp, n_tensor)
    owners = n_dp * n_tensor
    me = lax.axis_index("tensor")
    owner = lax.axis_index("dp") * n_tensor + me
    own_rows, depth = tokens.shape
    total = own_rows * n_tensor
    states = state_weight.shape[1]
    heads = step_weight.shape[1]
    share = state_weight.shape[0]
    taps = conv_state.shape[0]
    channels = input_weight.shape[2]
    inner_total = channels * n_tensor

    def placed(value, whole):
        width = value.shape[-1]
        mine = jnp.arange(whole, dtype=jnp.int32) // width == owner
        spread = jnp.tile(value, (1,) * (value.ndim - 1) + (whole // width,))
        return jnp.where(mine, spread, jnp.zeros((), value.dtype))

    small = jnp.concatenate(
        [
            placed(pre_gain, depth).reshape(-1, states),
            placed(conv_state, states),
            placed(conv_state_bias[None], states),
        ],
        axis=0,
    )
    small = jnp.pad(small, ((0, 16 - small.shape[0]), (0, 0)))
    step_rows = jnp.pad(step_weight.T, ((0, head_rows - heads), (0, 0)))
    gate_weight, inner_weight = input_weight[:, 0], input_weight[:, 1]
    rows = lax.all_gather(tokens, "tensor", axis=0, tiled=True)
    grad_rows = lax.all_gather(cotangent, "tensor", axis=0, tiled=True)
    if fast:
        late = jnp.concatenate([gate_weight, output_weight.T], axis=0)
        shared = jnp.concatenate([state_weight, small], axis=0)
        late, shared = lax.optimization_barrier((late, shared))
        late = ring_gather(late)
        shared = lax.all_to_all(
            jnp.broadcast_to(shared, (4,) + shared.shape), "tensor", 0, 0, tiled=True
        )
        small = shared[0, share:] + shared[1, share:] + shared[2, share:] + shared[3, share:]
        tail = jnp.concatenate([small, step_rows], axis=1)
        tail = jnp.pad(tail, ((0, 0), (0, channels - tail.shape[1])))
        beside = [
            jnp.concatenate([shared[i, :share], shared[i + 1, :share]], axis=1) for i in (0, 2)
        ]
        msg = ring_gather(jnp.concatenate([inner_weight, *beside, tail], axis=0))
        weight_pieces = [piece for piece, _ in msg]
        late_pieces = [piece for piece, _ in late]
        place = jnp.stack([index for _, index in msg] + [lax.axis_index("dp") % 2])
    else:
        weight_pieces = [
            lax.all_gather(inner_weight, "dp", axis=0, tiled=True),
            lax.all_gather(state_weight, ("dp", "tensor"), axis=0, tiled=True),
            lax.all_gather(step_rows, "dp", axis=1, tiled=True),
            lax.psum(small, ("dp", "tensor")),
        ]
        late_pieces = [
            lax.all_gather(gate_weight, "dp", axis=0, tiled=True),
            lax.all_gather(output_weight.T, "dp", axis=0, tiled=True),
        ]
        place = jnp.zeros((9,), jnp.int32)
    place = place.astype(jnp.int32)

    def row(value):
        return value.astype(f32).reshape(1, -1)

    def head(value):
        return jnp.pad(value.astype(f32), (0, head_rows - heads))

    taps_float = conv_inner.astype(f32)
    scan_params = [
        taps_float,
        row(conv_inner_bias),
        head(step_bias)[None, :],
        head(step_bias)[:, None],
        head(decay_log)[None, :],
        head(decay_log)[:, None],
        row(jnp.repeat(skip_gain, channels // heads)),
    ]
    masks = ((taps - 1, total + pad, 128), f32)
    state_taps = [((taps, states), f32), ((1, states), f32)]
    rows, grad_rows = lax.optimization_barrier((rows, grad_rows))
    (
        normed,
        inner_full,
        state_full,
        step_full,
        small_full,
        raw,
        state_raw,
        step_col,
        step_row,
        act,
        state_act,
        mixed,
    ) = call(
        functools.partial(forward_kernel, fast),
        12,
        [place, lengths],
        [rows] + weight_pieces + scan_params,
        [
            ((total, depth), bf16),
            ((depth, channels), bf16),
            ((depth, states), bf16),
            ((head_rows, depth), bf16),
            ((16, states), f32),
            ((total + pad, channels), f32),
            ((total + pad, states), f32),
            ((total, head_rows), f32),
            ((head_rows, total), f32),
            ((total, channels), f32),
            ((total, states), f32),
            ((total, channels), f32),
        ],
        [masks] + state_taps,
    )
    norm_row = row(norm_gain)
    gate_full, output_full, gate, grad_normalized, sums = call(
        functools.partial(grad_in_kernel, fast),
        5,
        [place, lengths],
        [grad_rows] + late_pieces + [normed, mixed, norm_row],
        [
            ((depth, channels), bf16),
            ((depth, channels), bf16),
            ((total, channels), f32),
            ((total, channels), f32),
            ((8, total), f32),
        ],
        [((total, 128), f32)],
    )
    if fast:
        sums = sums + tensor_swap(sums, 1)
        sums = sums + tensor_swap(sums, 2)
    else:
        sums = lax.psum(sums, "tensor")
    chunks = 8
    tall = depth // chunks
    partial_out, gate_give, gate_keep, grad_gate, grad_mixed, norm_grad = call(
        functools.partial(norm_kernel, inner_total),
        9,
        [place, lengths],
        [sums, gate, mixed, grad_normalized, norm_row, output_full, grad_rows, normed],
        [
            ((total, depth), bf16),
            ((chunks // 2, 2 * tall, channels), bf16),
            ((chunks // 2, 2 * tall, channels), bf16),
            ((total, channels), bf16),
            ((total, channels), f32),
            ((1, channels), f32),
        ],
        [((total, 128), f32), ((total, channels), bf16)],
    )
    grad_act, grad_state, step_grad, head_sums = call(
        scan_back_kernel,
        13,
        [lengths],
        [grad_mixed, act, state_act, step_col, step_row] + scan_params[2:],
        [
            ((total, channels), f32),
            ((total, states), f32),
            ((head_rows, total), f32),
            ((8, channels), f32),
        ],
        [((span, span), f32)],
    )
    if fast:
        gate_half = side_sum(gate_give, gate_keep)
        grad_act, gate_half = lax.optimization_barrier((grad_act, gate_half))
        gate_blocks = line_blocks(gate_half)
    (
        inner_give,
        inner_keep,
        state_part,
        gain_part,
        grad_normed,
        sums,
        state_sums,
    ) = call(
        backward_kernel,
        9,
        [place, lengths],
        [
            grad_act,
            grad_state,
            step_grad,
            head_sums,
            raw,
            state_raw,
            grad_gate,
            normed,
            rows,
            gate_full,
            inner_full,
            state_full,
            step_full,
            small_full,
            norm_grad,
        ]
        + scan_params[:2],
        [
            ((chunks // 2, tall + head_rows, channels), bf16),
            ((chunks // 2, tall + head_rows, channels), bf16),
            ((depth, states), bf16),
            ((1, depth), f32),
            ((total, depth), bf16),
            ((16, channels), f32),
            ((8, states), f32),
        ],
        [
            masks,
            *state_taps,
            ((total + pad, channels), f32),
            ((total + pad, states), f32),
            ((total, channels), bf16),
            ((total, states), bf16),
        ],
    )

    token_float = tokens.astype(f32)
    gain_full = small_full[: depth // states].reshape(1, depth)

    def lay(value):
        value = value.reshape(owners, -1)
        return jnp.pad(value, ((0, 0), (0, states - value.shape[1])))[:, None, :].astype(bf16)

    conv_state_owned = state_sums[:taps].reshape(taps, owners, -1).transpose(1, 0, 2)
    shared_part = jnp.concatenate(
        [
            state_part.reshape(owners, share, states),
            lay(gain_part),
            lay(conv_state_owned),
            lay(state_sums[taps]),
        ],
        axis=1,
    )
    shared_part = jnp.pad(shared_part, ((0, 0), (0, -shared_part.shape[1] % 8), (0, 0)))
    mixed_rows = lax.psum_scatter(partial_out, "tensor", scatter_dimension=0, tiled=True)
    grad_normed, mixed_rows = lax.optimization_barrier((grad_normed, mixed_rows))
    grad_local = lax.psum_scatter(grad_normed, "tensor", scatter_dimension=0, tiled=True)
    mixed_rows, grad_local = mixed_rows.astype(f32), grad_local.astype(f32)
    if fast:
        shared_mine = lax.all_to_all(shared_part, ("dp", "tensor"), 0, 0, tiled=True)
        shared_mine = jnp.sum(shared_mine.astype(f32), axis=0)
        inner_half = side_sum(inner_give, inner_keep)
        inner_half, gate_blocks = lax.optimization_barrier((inner_half, gate_blocks))
        gate_out = jnp.sum(gate_blocks.astype(f32), axis=0)
        gate_grad, output_grad = gate_out[:tall], gate_out[tall:].T
        inner_out = jnp.sum(line_blocks(inner_half).astype(f32), axis=0)
        inner_grad, step_grad = inner_out[:tall], inner_out[tall : tall + heads, :tall].T
        sums = lax.all_to_all(
            jnp.broadcast_to(sums, (n_dp,) + sums.shape), "dp", 0, 0, tiled=True
        )
        sums = jnp.sum(sums, axis=0)
    else:
        shared_mine = lax.psum_scatter(
            shared_part.astype(f32), ("dp", "tensor"), scatter_dimension=0, tiled=True
        )[0]
        both, inner_float = (
            jnp.stack([keep, give], axis=1).reshape((chunks,) + keep.shape[1:]).astype(f32)
            for keep, give in ((gate_keep, gate_give), (inner_keep, inner_give))
        )
        gate_grad, output_grad, inner_grad = (
            lax.psum_scatter(part.reshape(depth, channels), "dp", scatter_dimension=0, tiled=True)
            for part in (both[:, :tall], both[:, tall:], inner_float[:, :tall])
        )
        output_grad = output_grad.T
        step_part = inner_float[:, tall : tall + heads, :tall].transpose(0, 2, 1)
        step_part = step_part.reshape(depth, heads)
        step_grad = lax.psum_scatter(step_part, "dp", scatter_dimension=0, tiled=True)
        sums = lax.psum(sums, "dp")
    input_grad = jnp.stack([gate_grad, inner_grad], axis=1)
    block_out = (token_float + mixed_rows).astype(bf16)
    scale = lax.rsqrt(jnp.mean(token_float * token_float, axis=1, keepdims=True) + epsilon)
    grad_scaled = grad_local * gain_full
    along = jnp.sum(grad_scaled * token_float, axis=1, keepdims=True) / depth
    tokens_grad = (
        scale * grad_scaled
        - token_float * (scale * scale * scale * along)
        + cotangent.astype(f32)
    )
    state_grad = shared_mine[:share]
    pre_gain_grad = shared_mine[share, : depth // owners]
    conv_state_grad = shared_mine[share + 1, : taps * (states // owners)].reshape(taps, -1)
    conv_state_bias_grad = shared_mine[share + 2, : states // owners]

    skip_grad = sums[9].reshape(heads, -1).sum(axis=1)
    return (
        block_out,
        tokens_grad,
        pre_gain_grad,
        input_grad,
        step_grad,
        state_grad,
        sums[:taps],
        sums[taps],
        conv_state_grad,
        conv_state_bias_grad,
        sums[7, :heads],
        sums[8, :heads],
        skip_grad,
        sums[6],
        output_grad,
    )


def solution(mesh):
    in_specs = (
        P(("dp", "tensor"), None),
        P("dp", None),
        P(("dp", "tensor"), None),
        P(("dp", "tensor")),
        P("dp", None, "tensor"),
        P("dp", "tensor"),
        P(("dp", "tensor"), None),
        P(None, "tensor"),
        P("tensor"),
        P(None, ("dp", "tensor")),
        P(("dp", "tensor")),
        P("tensor"),
        P("tensor"),
        P("tensor"),
        P("tensor"),
        P("tensor", "dp"),
    )
    out_specs = (
        P(("dp", "tensor"), None),
        P(("dp", "tensor"), None),
        P(("dp", "tensor")),
        P("dp", None, "tensor"),
        P("dp", "tensor"),
        P(("dp", "tensor"), None),
        P(None, "tensor"),
        P("tensor"),
        P(None, ("dp", "tensor")),
        P(("dp", "tensor")),
        P("tensor"),
        P("tensor"),
        P("tensor"),
        P("tensor"),
        P("tensor", "dp"),
    )
    return jax.shard_map(body, mesh=mesh, in_specs=in_specs, out_specs=out_specs, check_vma=False)
```

```python
import functools

import jax
import jax.numpy as jnp
from jax import lax
from jax.experimental import pallas as pl
from jax.experimental.pallas import tpu as pltpu
from jax.sharding import PartitionSpec as P

epsilon = 1e-05
highest = lax.Precision.HIGHEST
f32 = jnp.float32
bf16 = jnp.bfloat16
span = 256
pad = 8
head_rows = 16
head_width = 64
vmem_bytes = 54 * 1024 * 1024


def mm(a, b, over=(1, 0)):
    dims = (((over[0],), (over[1],)), ((), ()))
    return lax.dot_general(a, b, dims, preferred_element_type=f32)


def mm_exact(a, b, over=(1, 0)):
    dims = (((over[0],), (over[1],)), ((), ()))
    return lax.dot_general(a, b, dims, preferred_element_type=f32, precision=highest)


def sigmoid(v):
    return 1.0 / (1.0 + jnp.exp(-v))


def ends_of(lengths_ref):
    ends, total = [], None
    for slot in range(lengths_ref.shape[1]):
        here = lengths_ref[0, slot]
        total = here if total is None else total + here
        ends.append(total)
    return ends


def segment_of(places, ends):
    segment = jnp.zeros(places.shape, jnp.int32)
    for end in ends:
        segment = segment + jnp.where(places >= end, 1, 0)
    return segment


def iota(shape, dim):
    return lax.broadcasted_iota(jnp.int32, shape, dim)


def write_masks(mask_ref, ends):
    rows = mask_ref.shape[1] - pad
    places = iota((rows, 128), 0)
    segment = segment_of(places, ends)
    for shift in range(1, mask_ref.shape[0] + 1):
        same = (segment_of(places - shift, ends) == segment) & (places >= shift)
        mask_ref[shift - 1, :rows, :] = jnp.where(same, 1.0, 0.0)
        mask_ref[shift - 1, rows:, :] = jnp.zeros((pad, 128), f32)


def shifted_rows(x_ref, mask_ref, at, cols, shift, tall):
    part = x_ref[pad + at - shift : pad + at - shift + tall, cols]
    if shift == 0:
        return part
    return part * mask_ref[shift - 1, at : at + tall, :]


def conv_pre(x_ref, mask_ref, taps_ref, bias_ref, at, cols, tall):
    taps = taps_ref.shape[0]
    shifted = [shifted_rows(x_ref, mask_ref, at, cols, s, tall) for s in range(taps)]
    total = bias_ref[:, cols]
    for s in range(taps):
        total = total + taps_ref[taps - 1 - s : taps - s, cols] * shifted[s]
    return total, shifted


def column_loop(width, step):
    def one(c, carry):
        step(pl.ds(pl.multiple_of(c * 128, 128), 128))
        return carry

    lax.fori_loop(0, width // 128, one, 0)


def row_loop(rows, tall, step):
    def one(r, carry):
        step(pl.multiple_of(r * tall, tall))
        return carry

    lax.fori_loop(0, rows // tall, one, 0)


class Block:
    def __init__(self, b, ends, step_col, step_row, rate_col, rate_row, state_ref):
        low, top = b * span, (b + 1) * span
        states = state_ref.shape[1] // 2
        lower = jnp.where(iota((span, span), 0) >= iota((span, span), 1), 1.0, 0.0)
        self.rows = slice(low, top)
        self.step = step_col[low:top]
        self.step_row = step_row[:, low:top]
        self.cum = mm_exact(lower, rate_col[low:top])
        self.cum_row = mm_exact(rate_row[:, low:top], lower, (1, 1))
        self.inputs = state_ref[low:top, :states].astype(bf16)
        self.outputs = state_ref[low:top, states:].astype(bf16)
        segment = segment_of(iota((span, 1), 0) + low, ends)
        segment_row = segment_of(iota((1, span), 1) + low, ends)
        edge = sum(jnp.where(span - 1 >= end, 1, 0) for end in ends)
        self.near_edge = jnp.where(segment == edge, 1.0, 0.0)
        self.mask = jnp.where(segment == segment_row, lower, 0.0)
        self.contact = mm(self.outputs, self.inputs, (1, 1)) * self.mask

    def decay(self, h):
        gap = self.cum[:, h : h + 1] - self.cum_row[h : h + 1, :]
        return jnp.exp(jnp.minimum(gap, 0.0))

    def from_edge(self, h):
        return jnp.exp(self.cum[:, h : h + 1]) * self.near_edge

    def to_edge(self, h):
        last = self.cum[span - 1 : span, h : h + 1]
        return jnp.exp(last - self.cum[:, h : h + 1]) * self.near_edge


def wide(low_half, left, right):
    return jnp.where(low_half, left, right)


def step_sizes(raw_col, raw_row, bias_ref, bias_col_ref, log_ref, log_col_ref):
    def soft(v):
        return jnp.maximum(v, 0.0) + jnp.log1p(jnp.exp(-jnp.abs(v)))

    step_col = soft(raw_col + bias_ref[...])
    step_row = soft(raw_row + bias_col_ref[...])
    rate_col = -step_col * jnp.exp(log_ref[...])
    rate_row = -step_row * jnp.exp(log_col_ref[...])
    return step_col, step_row, rate_col, rate_row


def forward_kernel(fast, place_ref, lengths_ref, *refs):
    n_msg = 8 if fast else 4
    n_rows = 4 if fast else 1
    row_refs, msg_refs, refs = refs[:n_rows], refs[n_rows : n_rows + n_msg], refs[n_rows + n_msg :]
    (taps_ref, bias_ref, step_bias_ref, step_bias_col_ref, log_ref, log_col_ref, skip_ref) = refs[:7]
    (
        rows_ref,
        normed_ref,
        weight_ref,
        state_weight_ref,
        step_weight_ref,
        small_ref,
        raw_ref,
        state_raw_ref,
        step_col_ref,
        step_row_ref,
        act_ref,
        state_ref,
        mixed_ref,
    ) = refs[7:20]
    mask_ref, state_taps_ref, state_bias_ref = refs[20:]
    total = rows_ref.shape[0]
    channels = act_ref.shape[1]
    ends = ends_of(lengths_ref)

    if fast:
        depth_part = 128
        small = jnp.zeros(small_ref.shape, f32)
        share = state_weight_ref.shape[0] // 32
        for slot in range(8):
            msg = msg_refs[slot]
            index = place_ref[slot]
            at = pl.multiple_of(index * depth_part, depth_part)
            weight_ref[pl.ds(at, depth_part), :] = msg[:depth_part, :]
            for member in range(4):
                inner = pl.multiple_of(at + member * share, share)
                high, low = depth_part + share * (member // 2), 256 * (member % 2)
                state_weight_ref[pl.ds(inner, share), :] = msg[
                    high : high + share, low : low + 256
                ]
            tail = depth_part + 2 * share
            small = small + msg[tail : tail + 16, :256].astype(f32)
            step_weight_ref[:, pl.ds(at, depth_part)] = msg[tail : tail + 16, 256:384]
        small_ref[...] = small
    else:
        weight_ref[...] = msg_refs[0][...]
        state_weight_ref[...] = msg_refs[1][...]
        step_weight_ref[...] = msg_refs[2][...]
        small_ref[...] = msg_refs[3][...].astype(f32)
    gain = jnp.concatenate([small_ref[i : i + 1, :] for i in range(4)], axis=1)
    taps = taps_ref.shape[0]
    state_taps_ref[...] = small_ref[4 : 4 + taps, :]
    state_bias_ref[...] = small_ref[4 + taps : 5 + taps, :]

    tall = total // n_rows
    for member in range(n_rows):
        at = pl.multiple_of(place_ref[8 + member] * tall, tall) if fast else 0
        own = row_refs[member][:tall, :]
        rows_ref[pl.ds(at, tall), :] = own
        value = own.astype(f32)
        scale = lax.rsqrt(jnp.mean(value * value, axis=1, keepdims=True) + epsilon)
        normed_ref[pl.ds(at, tall), :] = (value * scale * gain).astype(bf16)

    raw_ref[:pad, :] = jnp.zeros((pad, channels), f32)
    state_raw_ref[:pad, :] = jnp.zeros((pad, state_raw_ref.shape[1]), f32)

    def project(at):
        part = normed_ref[pl.ds(at, 128), :]
        raw_ref[pl.ds(at + pad, 128), :] = mm(part, weight_ref[...])
        state_raw_ref[pl.ds(at + pad, 128), :] = mm(part, state_weight_ref[...])
        step_col_ref[pl.ds(at, 128), :] = mm(part, step_weight_ref[...], (1, 1))

    row_loop(total, 128, project)
    step_row_ref[...] = mm(step_weight_ref[...], normed_ref[...], (1, 1))

    write_masks(mask_ref, ends)

    def activate(x_ref, out_ref, own_taps, own_bias):
        def column(cols):
            for at in range(0, total, 128):
                pre, _ = conv_pre(x_ref, mask_ref, own_taps, own_bias, at, cols, 128)
                out_ref[at : at + 128, cols] = pre * sigmoid(pre)

        column_loop(out_ref.shape[1], column)

    activate(raw_ref, act_ref, taps_ref, bias_ref)
    activate(state_raw_ref, state_ref, state_taps_ref, state_bias_ref)

    steps = step_sizes(
        step_col_ref[...],
        step_row_ref[...],
        step_bias_ref,
        step_bias_col_ref,
        log_ref,
        log_col_ref,
    )
    low_half = iota((span, 128), 1) < head_width
    held = []
    for b in range(total // span):
        block = Block(b, ends, *steps, state_ref)
        for i in range(channels // 128):
            cols = slice(128 * i, 128 * (i + 1))
            pair = (2 * i, 2 * i + 1)
            x = act_ref[block.rows, cols]
            step_wide = wide(low_half, *(block.step[:, h : h + 1] for h in pair))
            x_step = (x * step_wide).astype(bf16)
            y = [mm((block.decay(h) * block.contact).astype(bf16), x_step) for h in pair]
            y = wide(low_half, *y) + skip_ref[:, cols] * x
            if b == 0:
                reach = wide(low_half, *(block.to_edge(h) for h in pair))
                weighted = (x * step_wide * reach).astype(bf16)
                held.append(mm(block.inputs, weighted, (0, 0)).astype(bf16))
            else:
                reach = wide(low_half, *(block.from_edge(h) for h in pair))
                y = y + reach * mm(block.outputs, held[i])
            mixed_ref[block.rows, cols] = y


def grad_in_kernel(fast, place_ref, lengths_ref, *refs):
    n_rows = 4 if fast else 1
    n_msg = 8 if fast else 2
    row_refs, msg_refs, refs = refs[:n_rows], refs[n_rows : n_rows + n_msg], refs[n_rows + n_msg :]
    normed_ref, mixed_ref, norm_ref = refs[:3]
    rows_ref, gate_weight_ref, out_weight_ref, gate_ref, grad_ref, sums_ref, wide_ref = refs[3:]
    total = rows_ref.shape[0]
    ends = ends_of(lengths_ref)
    tall = total // n_rows
    for member in range(n_rows):
        at = pl.multiple_of(place_ref[8 + member] * tall, tall) if fast else 0
        rows_ref[pl.ds(at, tall), :] = row_refs[member][-tall:, :]
    if fast:
        for slot in range(8):
            at = pl.multiple_of(place_ref[slot] * 128, 128)
            gate_weight_ref[pl.ds(at, 128), :] = msg_refs[slot][:128, :]
            out_weight_ref[pl.ds(at, 128), :] = msg_refs[slot][128:, :]
    else:
        gate_weight_ref[...] = msg_refs[0][...]
        out_weight_ref[...] = msg_refs[1][...]

    def part(at):
        rows = pl.ds(at, 128)
        valid = jnp.where(iota((128, 1), 0) + at < ends[-1], 1.0, 0.0)
        grad = mm(rows_ref[rows, :], out_weight_ref[...]) * valid
        grad_ref[rows, :] = grad
        gate = mm(normed_ref[rows, :], gate_weight_ref[...])
        gate_ref[rows, :] = gate
        gated = mixed_ref[rows, :] * (gate * sigmoid(gate))
        square = jnp.sum(gated * gated, axis=1, keepdims=True)
        cross = jnp.sum(grad * norm_ref[...] * gated, axis=1, keepdims=True)
        lane = iota((128, 128), 1)
        wide_ref[rows, :] = jnp.where(lane == 0, square, jnp.where(lane == 1, cross, 0.0))

    row_loop(total, 128, part)
    for at in range(0, total, 128):
        sums_ref[:, at : at + 128] = wide_ref[at : at + 128, :].T[:8, :]


def norm_kernel(inner_total, place_ref, lengths_ref, *refs):
    (sums_ref, gate_ref, mixed_ref, grad_ref, norm_ref, weight_ref, rows_ref, normed_ref) = refs[:8]
    chunk_refs = refs[8:16]
    partial_ref, grad_gate_ref, grad_mixed_ref, norm_grad_ref = refs[16:20]
    wide_ref, out_rows_ref = refs[20:]
    total, channels = gate_ref.shape
    ends = ends_of(lengths_ref)
    for at in range(0, total, 128):
        tile = jnp.concatenate([sums_ref[:, at : at + 128]] * 16, axis=0)
        wide_ref[at : at + 128, :] = tile.T
    norm_grad_ref[...] = jnp.zeros(norm_grad_ref.shape, f32)

    def part(at):
        rows = pl.ds(at, 128)
        valid = jnp.where(iota((128, 1), 0) + at < ends[-1], 1.0, 0.0)
        scale = lax.rsqrt(wide_ref[rows, 0:1] / inner_total + epsilon)
        cross = wide_ref[rows, 1:2]
        gate = gate_ref[rows, :]
        mixed = mixed_ref[rows, :]
        sig = sigmoid(gate)
        gate_act = gate * sig
        gated = mixed * gate_act
        grad = grad_ref[rows, :]
        norm = norm_ref[...]
        hat = gated * scale
        out_rows_ref[rows, :] = (hat * norm * valid).astype(bf16)
        norm_grad_ref[...] += jnp.sum(grad * hat, axis=0, keepdims=True)
        grad_gated = scale * (grad * norm) - gated * (scale * scale * scale * cross / inner_total)
        grad_mixed_ref[rows, :] = grad_gated * gate_act
        grad_gate = grad_gated * mixed * sig * (1.0 + gate * (1.0 - sig))
        grad_gate_ref[rows, :] = grad_gate.astype(bf16)
        partial_ref[rows, :] = mm(out_rows_ref[rows, :], weight_ref[...], (1, 1)).astype(bf16)

    row_loop(total, 128, part)

    tall = chunk_refs[0].shape[0] // 2
    for slot, chunk_ref in enumerate(chunk_refs):
        cols = pl.ds(pl.multiple_of(place_ref[slot] * tall, tall), tall)
        chunk_ref[:tall, :] = mm(normed_ref[:, cols], grad_gate_ref[...], (0, 0)).astype(bf16)
        chunk_ref[tall:, :] = mm(rows_ref[:, cols], out_rows_ref[...], (0, 0)).astype(bf16)


def scan_back_kernel(first_pair, lengths_ref, *refs):
    grad_mixed_ref, act_ref, state_ref, step_col_ref, step_row_ref = refs[:5]
    step_bias_ref, step_bias_col_ref, log_ref, log_col_ref, skip_ref = refs[5:10]
    grad_act_ref, grad_state_ref, step_grad_ref, sums_ref, acc_ref = refs[10:]
    total, own_width = grad_act_ref.shape
    states = state_ref.shape[1] // 2
    ends = ends_of(lengths_ref)
    sums_ref[...] = jnp.zeros(sums_ref.shape, f32)
    raw_row = step_row_ref[...]
    steps = step_sizes(
        step_col_ref[...], raw_row, step_bias_ref, step_bias_col_ref, log_ref, log_col_ref
    )
    rate_row = steps[3]
    low_half = iota((span, 128), 1) < head_width
    lower = jnp.where(iota((span, span), 0) >= iota((span, span), 1), 1.0, 0.0)
    blocks = [Block(b, ends, *steps, state_ref) for b in range(total // span)]
    first, second = blocks
    row_sums, step_rows, out_sums, in_sums = [], [], None, None
    grad_out = jnp.zeros((span, states), f32)
    grad_in = jnp.zeros((span, states), f32)
    head_of = iota((head_rows, 128), 0)
    lane_head = iota((head_rows, 128), 1) // head_width

    for b, block in enumerate(blocks):
        acc_ref[...] = jnp.zeros((span, span), f32)
        row_sum = jnp.zeros((span, 128), f32)
        step_grad = jnp.zeros((head_rows, span), f32)
        lane = iota((span, 128), 1)
        head_row = iota((head_rows, span), 0)
        for i in range(first_pair, first_pair + own_width // 128):
            cols = slice(128 * i, 128 * (i + 1))
            own_cols = slice(128 * (i - first_pair), 128 * (i - first_pair + 1))
            pair = (2 * i, 2 * i + 1)
            x = act_ref[block.rows, cols]
            x_low = x.astype(bf16)
            grad = grad_mixed_ref[block.rows, cols]
            grad_low = grad.astype(bf16)
            halves = (
                jnp.where(low_half, grad, 0.0).astype(bf16),
                jnp.where(low_half, 0.0, grad).astype(bf16),
            )
            step_wide = wide(low_half, *(block.step[:, h : h + 1] for h in pair))
            grads = []
            for h, half in zip(pair, halves):
                decay = block.decay(h)
                spread = mm(half, x_low, (1, 1)) * decay
                stepped = spread * block.step_row[h : h + 1, :]
                acc_ref[...] += stepped
                row_here = jnp.sum(stepped * block.contact, axis=1, keepdims=True)
                row_sum = jnp.where(lane == h, row_here, row_sum)
                step_here = jnp.sum(spread * block.contact, axis=0, keepdims=True)
                step_grad = jnp.where(head_row == h, step_here, step_grad)
                grads.append(mm((decay * block.contact).astype(bf16), grad_low, (0, 0)))
            grad_act = wide(low_half, *grads) * step_wide + skip_ref[:, cols] * grad
            sums_ref[2:3, own_cols] += jnp.sum(grad * x, axis=0, keepdims=True)
            picks = jnp.where(lane_head + 2 * i == head_of, 1.0, 0.0)
            if b == 0:
                reach = wide(low_half, *(second.from_edge(h) for h in pair))
                lead = (grad_mixed_ref[second.rows, cols] * reach).astype(bf16)
                edge = wide(low_half, *(block.to_edge(h) for h in pair))
                weighted = (x * step_wide * edge).astype(bf16)
                held = mm(block.inputs, weighted, (0, 0)).astype(bf16)
                held_grad = mm(second.outputs, lead, (0, 0)).astype(bf16)
                grad_out = grad_out + mm(lead, held, (1, 1))
                grad_in = grad_in + mm(weighted, held_grad, (1, 1))
                back = mm(block.inputs, held_grad) * edge
                grad_act = grad_act + back * step_wide
                ahead = mm(second.outputs, held)
                out_here = mm_exact(picks, lead.astype(f32) * ahead, (1, 1))
                in_here = mm_exact(picks, x * back, (1, 1))
                out_sums = out_here if out_sums is None else out_sums + out_here
                in_sums = in_here if in_sums is None else in_sums + in_here
            grad_act_ref[block.rows, own_cols] = grad_act
        table = (acc_ref[...] * block.mask).astype(bf16)
        grad_c = mm(table, block.inputs)
        grad_b = mm(table, block.outputs, (0, 0))
        if b == 0:
            grad_b = grad_b + grad_in
        else:
            grad_c = grad_c + grad_out
        grad_state_ref[block.rows, :states] = grad_b
        grad_state_ref[block.rows, states:] = grad_c
        row_sums.append(row_sum)
        step_rows.append(step_grad)

    rate_grads = []
    for b, block in enumerate(blocks):
        column = step_rows[b] * block.step_row
        crossing = mm_exact(row_sums[b], lower, (0, 0))[:head_rows] - mm_exact(column, lower)
        if b == 0:
            crossing = crossing + mm_exact(in_sums * block.step_row, 1.0 - lower)
        else:
            crossing = crossing + mm_exact(out_sums, lower)
        rate_grads.append(crossing)
    step_rows[0] = step_rows[0] + in_sums
    rate_grad = jnp.concatenate(rate_grads, axis=1)
    step_grad = jnp.concatenate(step_rows, axis=1) - rate_grad * jnp.exp(log_col_ref[...])
    step_grad = step_grad * sigmoid(raw_row + step_bias_col_ref[...])
    decay_sum = jnp.sum(rate_grad * rate_row, axis=1, keepdims=True)
    bias_sum = jnp.sum(step_grad, axis=1, keepdims=True)
    lane = iota((head_rows, 128), 1)
    head_sums = jnp.where(lane == 0, bias_sum, jnp.where(lane == 1, decay_sum, 0.0))
    head_sums = jnp.concatenate([head_sums] * (128 // head_rows), axis=0).T
    sums_ref[0:2, :128] = head_sums[:2, :]
    step_grad_ref[...] = step_grad


def conv_back_kernel(lengths_ref, *refs):
    act_refs, state_refs, step_refs, head_refs, refs = (
        refs[0:2],
        refs[2:4],
        refs[4:6],
        refs[6:8],
        refs[8:],
    )
    raw_ref, state_raw_ref, normed_ref, small_ref, norm_grad_ref, taps_ref, bias_ref = refs[:7]
    (
        grad_inner_ref,
        grad_state_low_ref,
        step_low_ref,
        state_part_ref,
        inner_sums_ref,
        state_sums_ref,
    ) = refs[7:13]
    (
        mask_ref,
        state_taps_ref,
        state_bias_ref,
        grad_act_ref,
        grad_state_ref,
        pre_ref,
        state_pre_ref,
    ) = refs[13:]
    total, channels = grad_inner_ref.shape
    ends = ends_of(lengths_ref)
    taps = taps_ref.shape[0]
    half = channels // 2
    state_taps_ref[...] = small_ref[4 : 4 + taps, :]
    state_bias_ref[...] = small_ref[4 + taps : 5 + taps, :]
    write_masks(mask_ref, ends)
    grad_act_ref[:, :half] = act_refs[0][...]
    grad_act_ref[:, half:] = act_refs[1][...]
    grad_state_ref[...] = state_refs[0][...] + state_refs[1][...]
    step_low_ref[...] = (step_refs[0][...] + step_refs[1][...]).astype(bf16)

    def conv_back(x_ref, grad_ref, held_ref, out_ref, sums_ref, own_taps, own_bias):
        held_ref[total:, :] = jnp.zeros((pad, held_ref.shape[1]), f32)

        def column(cols):
            sums = [jnp.zeros((1, 128), f32) for _ in range(taps + 1)]
            for at in range(0, total, 128):
                pre, shifted = conv_pre(x_ref, mask_ref, own_taps, own_bias, at, cols, 128)
                sig = sigmoid(pre)
                grad = grad_ref[at : at + 128, cols] * sig * (1.0 + pre * (1.0 - sig))
                held_ref[at : at + 128, cols] = grad
                for s in range(taps):
                    sums[taps - 1 - s] += jnp.sum(grad * shifted[s], axis=0, keepdims=True)
                sums[taps] += jnp.sum(grad, axis=0, keepdims=True)
            for t, value in enumerate(sums):
                sums_ref[t : t + 1, cols] = value
            for at in range(0, total, 128):
                back = own_taps[taps - 1 : taps, cols] * held_ref[at : at + 128, cols]
                for s in range(1, taps):
                    part = held_ref[at + s : at + s + 128, cols]
                    part = part * mask_ref[s - 1, at + s : at + s + 128, :]
                    back = back + own_taps[taps - 1 - s : taps - s, cols] * part
                out_ref[at : at + 128, cols] = back.astype(bf16)

        column_loop(out_ref.shape[1], column)

    inner_sums_ref[...] = jnp.zeros(inner_sums_ref.shape, f32)
    inner_sums_ref[6:7, :] = norm_grad_ref[...]
    inner_sums_ref[7:9, :half] = head_refs[0][:2, :] + head_refs[1][:2, :]
    inner_sums_ref[9:10, :half] = head_refs[0][2:3, :]
    inner_sums_ref[9:10, half:] = head_refs[1][2:3, :]
    state_sums_ref[...] = jnp.zeros(state_sums_ref.shape, f32)
    conv_back(
        raw_ref, grad_act_ref, pre_ref, grad_inner_ref, inner_sums_ref, taps_ref, bias_ref
    )
    conv_back(
        state_raw_ref,
        grad_state_ref,
        state_pre_ref,
        grad_state_low_ref,
        state_sums_ref,
        state_taps_ref,
        state_bias_ref,
    )

    def chunk(at):
        part = normed_ref[:, pl.ds(at, 256)]
        state_part_ref[pl.ds(at, 256), :] = mm(part, grad_state_low_ref[...], (0, 0)).astype(bf16)

    row_loop(normed_ref.shape[1], 256, chunk)


def project_back_kernel(*refs):
    (
        grad_gate_ref,
        grad_inner_ref,
        grad_state_low_ref,
        step_low_ref,
        normed_ref,
        rows_ref,
        gate_weight_ref,
        weight_ref,
        state_weight_ref,
        step_weight_ref,
        msg_ref,
        gain_part_ref,
        grad_normed_ref,
    ) = refs
    total = rows_ref.shape[0]
    tall = msg_ref.shape[1] - head_rows
    step_low = step_low_ref[...]

    def chunk(c, carry):
        part = normed_ref[:, pl.ds(pl.multiple_of(c * tall, tall), tall)]
        msg_ref[c, :tall, :] = mm(part, grad_inner_ref[...], (0, 0)).astype(bf16)
        msg_ref[c, tall:, :tall] = mm(step_low, part).astype(bf16)
        msg_ref[c, tall:, tall:] = jnp.zeros((head_rows, msg_ref.shape[2] - tall), bf16)
        return carry

    lax.fori_loop(0, msg_ref.shape[0], chunk, 0)
    gain_part_ref[...] = jnp.zeros(gain_part_ref.shape, f32)

    def back(at):
        rows = pl.ds(at, 128)
        grad = mm(grad_gate_ref[rows, :], gate_weight_ref[...], (1, 1))
        grad = grad + mm(grad_inner_ref[rows, :], weight_ref[...], (1, 1))
        grad = grad + mm(grad_state_low_ref[rows, :], state_weight_ref[...], (1, 1))
        grad = grad + mm(step_low_ref[:, rows], step_weight_ref[...], (0, 0))
        grad_normed_ref[rows, :] = grad.astype(bf16)
        value = rows_ref[rows, :].astype(f32)
        scale = lax.rsqrt(jnp.mean(value * value, axis=1, keepdims=True) + epsilon)
        gain_part_ref[...] += jnp.sum(grad * (value * scale), axis=0, keepdims=True)

    row_loop(total, 128, back)


def prepare_kernel(place_ref, *refs):
    (gain_ref, taps_ref, bias_ref, state_ref, step_ref, input_ref, out_ref) = refs[:7]
    shared_ref, step_rows_ref, inner_ref, late_ref = refs[7:]
    owner = place_ref[0]
    share, states = state_ref.shape
    depth_part = input_ref.shape[0]
    channels = out_ref.shape[0]
    shared_ref[...] = jnp.zeros(shared_ref.shape, bf16)
    shared_ref[:share, :] = state_ref[...]

    def placed(value, at):
        width = value.shape[1]
        pick = iota((width, states), 1) - at == iota((width, states), 0)
        return mm(value, jnp.where(pick, 1.0, 0.0).astype(bf16))

    start = owner * gain_ref.shape[1]
    gain = jnp.concatenate(
        [placed(gain_ref[...], start - states * i) for i in range(4)]
        + [placed(taps_ref[...], owner * taps_ref.shape[1])]
        + [placed(bias_ref[...], owner * bias_ref.shape[1])]
        + [jnp.zeros((7, states), f32)],
        axis=0,
    )
    shared_ref[share:, :] = gain.astype(bf16)
    step_rows_ref[...] = jnp.zeros(step_rows_ref.shape, bf16)
    step_rows_ref[: step_ref.shape[0], :] = step_ref[...]
    late_ref[:depth_part, :] = input_ref[:, :channels]
    late_ref[depth_part:, :] = out_ref[...].astype(f32).T.astype(bf16)
    inner_ref[...] = input_ref[:, channels:]


def call(kernel, micros, scalars, arrays, outs, scratch):
    smem = pl.BlockSpec(memory_space=pltpu.SMEM)
    vmem = pl.BlockSpec(memory_space=pltpu.VMEM)
    return pl.pallas_call(
        kernel,
        out_shape=[jax.ShapeDtypeStruct(shape, kind) for shape, kind in outs],
        in_specs=[smem] * len(scalars) + [vmem] * len(arrays),
        out_specs=[vmem] * len(outs),
        scratch_shapes=[pltpu.VMEM(shape, kind) for shape, kind in scratch],
        compiler_params=pltpu.CompilerParams(vmem_limit_bytes=vmem_bytes),
        cost_estimate=pl.CostEstimate(
            flops=int(micros * 1.1e9), bytes_accessed=1 << 20, transcendentals=0
        ),
    )(*scalars, *arrays)


def ring_ok(n_dp, n_tensor):
    return n_dp == 8 and n_tensor == 4


ring_order = (0, 2, 4, 6, 7, 5, 3, 1)


def ring_place(index):
    high, low = index // 2, index % 2
    return jnp.where(low == 0, high, 7 - high)


def ring_index(place):
    place = lax.rem(place + 16, 8)
    return jnp.where(place < 4, 2 * place, 2 * (7 - place) + 1)


def ring_send(value, forward):
    pairs = []
    for place in range(8):
        other = (place + (1 if forward else 7)) % 8
        pairs.append((ring_order[place], ring_order[other]))
    return lax.ppermute(value, "dp", pairs)


def ring_gather(value):
    me = ring_place(lax.axis_index("dp"))
    pieces = [(value, ring_index(me))]
    ahead, back = value, value
    for step in range(1, 5):
        ahead = ring_send(ahead, True)
        pieces.append((ahead, ring_index(me - step)))
        if step < 4:
            back = ring_send(back, False)
            pieces.append((back, ring_index(me + step)))
    return pieces


def ring_step(held):
    return ring_send(held[0], True), ring_send(held[1], False)


def add_low(got, own):
    return (got.astype(f32) + own.astype(f32)).astype(bf16)


def ordered(first, then):
    return lax.optimization_barrier((first, then))


def tensor_gather(value):
    near = tensor_swap(value, 1)
    far = tensor_swap(value, 2)
    return [value, near, far, tensor_swap(far, 1)]


def tensor_sum(value, depth):
    parts = value.reshape(4, -1, depth)
    parts = lax.all_to_all(parts, "tensor", 0, 0, tiled=True)
    return jnp.sum(parts.astype(f32), axis=0)


def tensor_swap(value, bit):
    return lax.ppermute(value, "tensor", [(i, i ^ bit) for i in range(4)])


def body(
    tokens,
    lengths,
    cotangent,
    pre_gain,
    input_weight,
    step_weight,
    state_weight,
    conv_inner,
    conv_inner_bias,
    conv_state,
    conv_state_bias,
    step_bias,
    decay_log,
    skip_gain,
    norm_gain,
    output_weight,
):
    n_dp, n_tensor = lax.axis_size("dp"), lax.axis_size("tensor")
    fast = ring_ok(n_dp, n_tensor)
    owners = n_dp * n_tensor
    me = lax.axis_index("tensor")
    owner = lax.axis_index("dp") * n_tensor + me
    own_rows, depth = tokens.shape
    total = own_rows * n_tensor
    states = state_weight.shape[1]
    heads = step_weight.shape[1]
    share = state_weight.shape[0]
    taps = conv_state.shape[0]
    channels = input_weight.shape[2]
    inner_total = channels * n_tensor

    input_flat = input_weight.reshape(input_weight.shape[0], -1)
    owner_place = jnp.stack([owner, owners]).astype(jnp.int32)
    shared, step_rows, inner_weight, late = call(
        prepare_kernel,
        2,
        [owner_place],
        [
            pre_gain[None, :],
            conv_state,
            conv_state_bias[None, :],
            state_weight,
            step_weight.T,
            input_flat,
            output_weight,
        ],
        [
            ((share + 16, states), bf16),
            ((head_rows, step_weight.shape[0]), bf16),
            ((input_weight.shape[0], channels), bf16),
            ((input_weight.shape[0] + output_weight.shape[1], channels), bf16),
        ],
        [],
    )
    if fast:
        late_one = ring_step((late, late))
        shared = lax.all_to_all(
            jnp.broadcast_to(shared, (4,) + shared.shape), "tensor", 0, 0, tiled=True
        )
        small = shared[0, share:] + shared[1, share:] + shared[2, share:] + shared[3, share:]
        tail = jnp.concatenate([small, step_rows], axis=1)
        tail = jnp.pad(tail, ((0, 0), (0, channels - tail.shape[1])))
        beside = [
            jnp.concatenate([shared[i, :share], shared[i + 1, :share]], axis=1) for i in (0, 2)
        ]
        msg = jnp.concatenate([inner_weight, *beside, tail], axis=0)
        late_one, msg = ordered(late_one, msg)
        msg = ring_gather(msg)
        late_pieces = [late, *late_one]
        held = late_one
        for step in range(2, 5):
            if step < 4:
                held = ring_step(held)
                late_pieces += held
            else:
                late_pieces.append(ring_send(held[0], True))
        row_pieces = tensor_gather(jnp.concatenate([tokens, cotangent], axis=0))
        grad_pieces = row_pieces
        weight_pieces = [piece for piece, _ in msg]
        place = jnp.stack([index for _, index in msg] + [me, me ^ 1, me ^ 2, me ^ 3])
    else:
        row_pieces = [lax.all_gather(tokens, "tensor", axis=0, tiled=True)]
        grad_pieces = [lax.all_gather(cotangent, "tensor", axis=0, tiled=True)]
        gate_weight = late[: input_weight.shape[0]]
        weight_pieces = [
            lax.all_gather(inner_weight, "dp", axis=0, tiled=True),
            lax.all_gather(state_weight, ("dp", "tensor"), axis=0, tiled=True),
            lax.all_gather(step_rows, "dp", axis=1, tiled=True),
            lax.psum(shared[share:], ("dp", "tensor")),
        ]
        late_pieces = [
            lax.all_gather(gate_weight, "dp", axis=0, tiled=True),
            lax.all_gather(late[input_weight.shape[0] :], "dp", axis=0, tiled=True),
        ]
        place = jnp.arange(12)
    place = place.astype(jnp.int32)

    def row(value):
        return value.astype(f32).reshape(1, -1)

    def head(value):
        return jnp.pad(value.astype(f32), (0, head_rows - heads))

    taps_float = conv_inner.astype(f32)
    scan_params = [
        taps_float,
        row(conv_inner_bias),
        head(step_bias)[None, :],
        head(step_bias)[:, None],
        head(decay_log)[None, :],
        head(decay_log)[:, None],
        row(jnp.repeat(skip_gain, channels // heads)),
    ]
    masks = ((taps - 1, total + pad, 128), f32)
    state_taps = [((taps, states), f32), ((1, states), f32)]
    (
        rows,
        normed,
        inner_full,
        state_full,
        step_full,
        small_full,
        raw,
        state_raw,
        step_col,
        step_row,
        act,
        state_act,
        mixed,
    ) = call(
        functools.partial(forward_kernel, fast),
        12,
        [place, lengths],
        row_pieces + weight_pieces + scan_params,
        [
            ((total, depth), bf16),
            ((total, depth), bf16),
            ((depth, channels), bf16),
            ((depth, states), bf16),
            ((head_rows, depth), bf16),
            ((16, states), f32),
            ((total + pad, channels), f32),
            ((total + pad, states), f32),
            ((total, head_rows), f32),
            ((head_rows, total), f32),
            ((total, channels), f32),
            ((total, states), f32),
            ((total, channels), f32),
        ],
        [masks] + state_taps,
    )
    norm_row = row(norm_gain)
    grad_rows, gate_full, output_full, gate, grad_normalized, sums = call(
        functools.partial(grad_in_kernel, fast),
        5,
        [place, lengths],
        grad_pieces + late_pieces + [normed, mixed, norm_row],
        [
            ((total, depth), bf16),
            ((depth, channels), bf16),
            ((depth, channels), bf16),
            ((total, channels), f32),
            ((total, channels), f32),
            ((8, total), f32),
        ],
        [((total, 128), f32)],
    )
    if fast:
        sums = sums + tensor_swap(sums, 1)
        sums = sums + tensor_swap(sums, 2)
    else:
        sums = lax.psum(sums, "tensor")
    chunks = 8
    tall = depth // chunks
    norm_outs = call(
        functools.partial(norm_kernel, inner_total),
        9,
        [place, lengths],
        [sums, gate, mixed, grad_normalized, norm_row, output_full, grad_rows, normed],
        [((2 * tall, channels), bf16)] * chunks
        + [
            ((total, depth), bf16),
            ((total, channels), bf16),
            ((total, channels), f32),
            ((1, channels), f32),
        ],
        [((total, 128), f32), ((total, channels), bf16)],
    )
    gate_chunks = norm_outs[:chunks]
    partial_out, grad_gate, grad_mixed, norm_grad = norm_outs[chunks:]

    def scan_back(first_pair, grad):
        return call(
            functools.partial(scan_back_kernel, first_pair),
            6,
            [lengths],
            [grad, act, state_act, step_col, step_row] + scan_params[2:],
            [
                ((total, channels // 2), f32),
                ((total, states), f32),
                ((head_rows, total), f32),
                ((8, channels // 2), f32),
            ],
            [((span, span), f32)],
        )

    if fast:
        got = ring_step((gate_chunks[7], gate_chunks[5]))
        held = add_low(got[0], gate_chunks[6]), add_low(got[1], gate_chunks[3])
    first = scan_back(0, grad_mixed)
    if fast:
        held, grad_mixed = ordered(held, grad_mixed)
        got = ring_step(held)
        held = add_low(got[0], gate_chunks[4]), add_low(got[1], gate_chunks[1])
    second = scan_back(channels // 256, grad_mixed)
    if fast:
        held, raw = ordered(held, raw)
        got = ring_step(held)
        held, last = add_low(got[0], gate_chunks[2]), got[1]
    backs = [part for pair in zip(first, second) for part in pair]
    grad_inner, grad_state_low, step_low, state_part, sums, state_sums = call(
        conv_back_kernel,
        7,
        [lengths],
        backs + [raw, state_raw, normed, small_full, norm_grad] + scan_params[:2],
        [
            ((total, channels), bf16),
            ((total, states), bf16),
            ((head_rows, total), bf16),
            ((depth, states), bf16),
            ((16, channels), f32),
            ((8, states), f32),
        ],
        [
            masks,
            *state_taps,
            ((total, channels), f32),
            ((total, states), f32),
            ((total + pad, channels), f32),
            ((total + pad, states), f32),
        ],
    )
    if fast:
        mixed_rows = tensor_sum(partial_out, depth)
        (held, mixed_rows), grad_inner = ordered((held, mixed_rows), grad_inner)
        gate_out = gate_chunks[0].astype(f32) + last.astype(f32)
        gate_out = gate_out + ring_send(held, True).astype(f32)
    inner_msg, gain_part, grad_normed = call(
        project_back_kernel,
        6,
        [],
        [
            grad_gate,
            grad_inner,
            grad_state_low,
            step_low,
            normed,
            rows,
            gate_full,
            inner_full,
            state_full,
            step_full,
        ],
        [
            ((chunks, tall + head_rows, channels), bf16),
            ((1, depth), f32),
            ((total, depth), bf16),
        ],
        [],
    )

    if fast:
        inner_msg, sums = ordered(inner_msg, sums)
    token_float = tokens.astype(f32)
    gain_full = small_full[: depth // states].reshape(1, depth)

    def lay(value):
        value = value.reshape(owners, -1)
        return jnp.pad(value, ((0, 0), (0, states - value.shape[1])))[:, None, :].astype(bf16)

    conv_state_owned = state_sums[:taps].reshape(taps, owners, -1).transpose(1, 0, 2)
    shared_part = jnp.concatenate(
        [
            state_part.reshape(owners, share, states),
            lay(gain_part),
            lay(conv_state_owned),
            lay(state_sums[taps]),
        ],
        axis=1,
    )
    shared_part = jnp.pad(shared_part, ((0, 0), (0, -shared_part.shape[1] % 8), (0, 0)))
    if fast:
        shared_mine = lax.all_to_all(shared_part, ("dp", "tensor"), 0, 0, tiled=True)
        shared_mine = jnp.sum(shared_mine.astype(f32), axis=0)
        gate_grad, output_grad = gate_out[:tall], gate_out[tall:].T
        inner_out = lax.all_to_all(inner_msg, "dp", 0, 0, tiled=True)
        inner_out = jnp.sum(inner_out.astype(f32), axis=0)
        grad_local = tensor_sum(grad_normed, depth)
        inner_grad, step_grad = inner_out[:tall], inner_out[tall : tall + heads, :tall].T
        sums = lax.all_to_all(
            jnp.broadcast_to(sums, (n_dp,) + sums.shape), "dp", 0, 0, tiled=True
        )
        sums = jnp.sum(sums, axis=0)
    else:
        shared_mine = lax.psum_scatter(
            shared_part.astype(f32), ("dp", "tensor"), scatter_dimension=0, tiled=True
        )[0]
        mixed_rows, grad_local = (
            lax.psum_scatter(part, "tensor", scatter_dimension=0, tiled=True).astype(f32)
            for part in (partial_out, grad_normed)
        )
        both, inner_float = jnp.stack(gate_chunks).astype(f32), inner_msg.astype(f32)
        gate_grad, output_grad, inner_grad = (
            lax.psum_scatter(part.reshape(depth, channels), "dp", scatter_dimension=0, tiled=True)
            for part in (both[:, :tall], both[:, tall:], inner_float[:, :tall])
        )
        output_grad = output_grad.T
        step_part = inner_float[:, tall : tall + heads, :tall].transpose(0, 2, 1)
        step_part = step_part.reshape(depth, heads)
        step_grad = lax.psum_scatter(step_part, "dp", scatter_dimension=0, tiled=True)
        sums = lax.psum(sums, "dp")
    input_grad = jnp.stack([gate_grad, inner_grad], axis=1)
    block_out = (token_float + mixed_rows).astype(bf16)
    scale = lax.rsqrt(jnp.mean(token_float * token_float, axis=1, keepdims=True) + epsilon)
    grad_scaled = grad_local * gain_full
    along = jnp.sum(grad_scaled * token_float, axis=1, keepdims=True) / depth
    tokens_grad = (
        scale * grad_scaled
        - token_float * (scale * scale * scale * along)
        + cotangent.astype(f32)
    )
    state_grad = shared_mine[:share]
    pre_gain_grad = shared_mine[share, : depth // owners]
    conv_state_grad = shared_mine[share + 1, : taps * (states // owners)].reshape(taps, -1)
    conv_state_bias_grad = shared_mine[share + 2, : states // owners]

    skip_grad = sums[9].reshape(heads, -1).sum(axis=1)
    return (
        block_out,
        tokens_grad,
        pre_gain_grad,
        input_grad,
        step_grad,
        state_grad,
        sums[:taps],
        sums[taps],
        conv_state_grad,
        conv_state_bias_grad,
        sums[7, :heads],
        sums[8, :heads],
        skip_grad,
        sums[6],
        output_grad,
    )


def solution(mesh):
    in_specs = (
        P(("dp", "tensor"), None),
        P("dp", None),
        P(("dp", "tensor"), None),
        P(("dp", "tensor")),
        P("dp", None, "tensor"),
        P("dp", "tensor"),
        P(("dp", "tensor"), None),
        P(None, "tensor"),
        P("tensor"),
        P(None, ("dp", "tensor")),
        P(("dp", "tensor")),
        P("tensor"),
        P("tensor"),
        P("tensor"),
        P("tensor"),
        P("tensor", "dp"),
    )
    out_specs = (
        P(("dp", "tensor"), None),
        P(("dp", "tensor"), None),
        P(("dp", "tensor")),
        P("dp", None, "tensor"),
        P("dp", "tensor"),
        P(("dp", "tensor"), None),
        P(None, "tensor"),
        P("tensor"),
        P(None, ("dp", "tensor")),
        P(("dp", "tensor")),
        P("tensor"),
        P("tensor"),
        P("tensor"),
        P("tensor"),
        P("tensor", "dp"),
    )
    return jax.shard_map(body, mesh=mesh, in_specs=in_specs, out_specs=out_specs, check_vma=False)
```

```python
import functools

import jax
import jax.numpy as jnp
from jax import lax
from jax.experimental import pallas as pl
from jax.experimental.pallas import tpu as pltpu
from jax.sharding import PartitionSpec as P

epsilon = 1e-05
highest = lax.Precision.HIGHEST
f32 = jnp.float32
bf16 = jnp.bfloat16
span = 256
pad = 8
head_rows = 16
head_width = 64
vmem_bytes = 54 * 1024 * 1024


def mm(a, b, over=(1, 0)):
    dims = (((over[0],), (over[1],)), ((), ()))
    return lax.dot_general(a, b, dims, preferred_element_type=f32)


def mm_exact(a, b, over=(1, 0)):
    dims = (((over[0],), (over[1],)), ((), ()))
    return lax.dot_general(a, b, dims, preferred_element_type=f32, precision=highest)


def sigmoid(v):
    return 1.0 / (1.0 + jnp.exp(-v))


def ends_of(lengths_ref):
    ends, total = [], None
    for slot in range(lengths_ref.shape[1]):
        here = lengths_ref[0, slot]
        total = here if total is None else total + here
        ends.append(total)
    return ends


def segment_of(places, ends):
    segment = jnp.zeros(places.shape, jnp.int32)
    for end in ends:
        segment = segment + jnp.where(places >= end, 1, 0)
    return segment


def iota(shape, dim):
    return lax.broadcasted_iota(jnp.int32, shape, dim)


def write_masks(mask_ref, ends):
    rows = mask_ref.shape[1] - pad
    places = iota((rows, 128), 0)
    segment = segment_of(places, ends)
    for shift in range(1, mask_ref.shape[0] + 1):
        same = (segment_of(places - shift, ends) == segment) & (places >= shift)
        mask_ref[shift - 1, :rows, :] = jnp.where(same, 1.0, 0.0)
        mask_ref[shift - 1, rows:, :] = jnp.zeros((pad, 128), f32)


def shifted_rows(x_ref, mask_ref, at, cols, shift, tall):
    part = x_ref[pad + at - shift : pad + at - shift + tall, cols]
    if shift == 0:
        return part
    return part * mask_ref[shift - 1, at : at + tall, :]


def conv_pre(x_ref, mask_ref, taps_ref, bias_ref, at, cols, tall):
    taps = taps_ref.shape[0]
    shifted = [shifted_rows(x_ref, mask_ref, at, cols, s, tall) for s in range(taps)]
    total = bias_ref[:, cols]
    for s in range(taps):
        total = total + taps_ref[taps - 1 - s : taps - s, cols] * shifted[s]
    return total, shifted


def column_loop(width, step):
    def one(c, carry):
        step(pl.ds(pl.multiple_of(c * 128, 128), 128))
        return carry

    lax.fori_loop(0, width // 128, one, 0)


def row_loop(rows, tall, step):
    def one(r, carry):
        step(pl.multiple_of(r * tall, tall))
        return carry

    lax.fori_loop(0, rows // tall, one, 0)


class Block:
    def __init__(self, b, ends, step_col, step_row, rate_col, rate_row, state_ref):
        low, top = b * span, (b + 1) * span
        states = state_ref.shape[1] // 2
        lower = jnp.where(iota((span, span), 0) >= iota((span, span), 1), 1.0, 0.0)
        self.rows = slice(low, top)
        self.step = step_col[low:top]
        self.step_row = step_row[:, low:top]
        self.cum = mm_exact(lower, rate_col[low:top])
        self.cum_row = mm_exact(rate_row[:, low:top], lower, (1, 1))
        self.inputs = state_ref[low:top, :states].astype(bf16)
        self.outputs = state_ref[low:top, states:].astype(bf16)
        segment = segment_of(iota((span, 1), 0) + low, ends)
        segment_row = segment_of(iota((1, span), 1) + low, ends)
        edge = sum(jnp.where(span - 1 >= end, 1, 0) for end in ends)
        self.near_edge = jnp.where(segment == edge, 1.0, 0.0)
        self.mask = jnp.where(segment == segment_row, lower, 0.0)
        self.contact = mm(self.outputs, self.inputs, (1, 1)) * self.mask

    def decay(self, h):
        gap = self.cum[:, h : h + 1] - self.cum_row[h : h + 1, :]
        return jnp.exp(jnp.minimum(gap, 0.0))

    def from_edge(self, h):
        return jnp.exp(self.cum[:, h : h + 1]) * self.near_edge

    def to_edge(self, h):
        last = self.cum[span - 1 : span, h : h + 1]
        return jnp.exp(last - self.cum[:, h : h + 1]) * self.near_edge


def wide(low_half, left, right):
    return jnp.where(low_half, left, right)


def step_sizes(raw_col, raw_row, bias_ref, bias_col_ref, log_ref, log_col_ref):
    def soft(v):
        return jnp.maximum(v, 0.0) + jnp.log1p(jnp.exp(-jnp.abs(v)))

    step_col = soft(raw_col + bias_ref[...])
    step_row = soft(raw_row + bias_col_ref[...])
    rate_col = -step_col * jnp.exp(log_ref[...])
    rate_row = -step_row * jnp.exp(log_col_ref[...])
    return step_col, step_row, rate_col, rate_row


def forward_kernel(fast, place_ref, lengths_ref, *refs):
    n_msg = 8 if fast else 4
    n_rows = 4 if fast else 1
    row_refs, msg_refs, refs = refs[:n_rows], refs[n_rows : n_rows + n_msg], refs[n_rows + n_msg :]
    taps_ref, bias_ref = refs[:2]
    (
        rows_ref,
        normed_ref,
        weight_ref,
        state_weight_ref,
        step_weight_ref,
        small_ref,
        raw_ref,
        state_raw_ref,
        step_col_ref,
        step_row_ref,
        act_ref,
        state_ref,
    ) = refs[2:14]
    mask_ref, state_taps_ref, state_bias_ref = refs[14:]
    total = rows_ref.shape[0]
    channels = act_ref.shape[1]
    ends = ends_of(lengths_ref)

    if fast:
        depth_part = 128
        small = jnp.zeros(small_ref.shape, f32)
        share = state_weight_ref.shape[0] // 32
        for slot in range(8):
            msg = msg_refs[slot]
            index = place_ref[slot]
            at = pl.multiple_of(index * depth_part, depth_part)
            weight_ref[pl.ds(at, depth_part), :] = msg[:depth_part, :]
            for member in range(4):
                inner = pl.multiple_of(at + place_ref[8 + member] * share, share)
                high, low = depth_part + share * (member // 2), 256 * (member % 2)
                state_weight_ref[pl.ds(inner, share), :] = msg[
                    high : high + share, low : low + 256
                ]
            tail = depth_part + 2 * share
            small = small + msg[tail : tail + 16, :256].astype(f32)
            step_weight_ref[:, pl.ds(at, depth_part)] = msg[tail : tail + 16, 256:384]
        small_ref[...] = small
    else:
        weight_ref[...] = msg_refs[0][...]
        state_weight_ref[...] = msg_refs[1][...]
        step_weight_ref[...] = msg_refs[2][...]
        small_ref[...] = msg_refs[3][...].astype(f32)
    gain = jnp.concatenate([small_ref[i : i + 1, :] for i in range(4)], axis=1)
    taps = taps_ref.shape[0]
    state_taps_ref[...] = small_ref[4 : 4 + taps, :]
    state_bias_ref[...] = small_ref[4 + taps : 5 + taps, :]

    tall = total // n_rows
    for member in range(n_rows):
        at = pl.multiple_of(place_ref[8 + member] * tall, tall) if fast else 0
        own = row_refs[member][:tall, :]
        rows_ref[pl.ds(at, tall), :] = own
        value = own.astype(f32)
        scale = lax.rsqrt(jnp.mean(value * value, axis=1, keepdims=True) + epsilon)
        normed_ref[pl.ds(at, tall), :] = (value * scale * gain).astype(bf16)

    raw_ref[:pad, :] = jnp.zeros((pad, channels), f32)
    state_raw_ref[:pad, :] = jnp.zeros((pad, state_raw_ref.shape[1]), f32)

    def project(at):
        part = normed_ref[pl.ds(at, 128), :]
        raw_ref[pl.ds(at + pad, 128), :] = mm(part, weight_ref[...])
        state_raw_ref[pl.ds(at + pad, 128), :] = mm(part, state_weight_ref[...])
        step_col_ref[pl.ds(at, 128), :] = mm(part, step_weight_ref[...], (1, 1))

    row_loop(total, 128, project)
    step_row_ref[...] = mm(step_weight_ref[...], normed_ref[...], (1, 1))

    write_masks(mask_ref, ends)

    def activate(x_ref, out_ref, own_taps, own_bias):
        def column(cols):
            for at in range(0, total, 128):
                pre, _ = conv_pre(x_ref, mask_ref, own_taps, own_bias, at, cols, 128)
                out_ref[at : at + 128, cols] = pre * sigmoid(pre)

        column_loop(out_ref.shape[1], column)

    activate(raw_ref, act_ref, taps_ref, bias_ref)
    activate(state_raw_ref, state_ref, state_taps_ref, state_bias_ref)


def scan_kernel(lengths_ref, *refs):
    act_ref, state_ref, step_col_ref, step_row_ref = refs[:4]
    step_bias_ref, step_bias_col_ref, log_ref, log_col_ref, skip_ref, mixed_ref = refs[4:]
    total, channels = act_ref.shape
    ends = ends_of(lengths_ref)
    steps = step_sizes(
        step_col_ref[...],
        step_row_ref[...],
        step_bias_ref,
        step_bias_col_ref,
        log_ref,
        log_col_ref,
    )
    low_half = iota((span, 128), 1) < head_width
    held = []
    for b in range(total // span):
        block = Block(b, ends, *steps, state_ref)
        for i in range(channels // 128):
            cols = slice(128 * i, 128 * (i + 1))
            pair = (2 * i, 2 * i + 1)
            x = act_ref[block.rows, cols]
            step_wide = wide(low_half, *(block.step[:, h : h + 1] for h in pair))
            x_step = (x * step_wide).astype(bf16)
            y = [mm((block.decay(h) * block.contact).astype(bf16), x_step) for h in pair]
            y = wide(low_half, *y) + skip_ref[:, cols] * x
            if b == 0:
                reach = wide(low_half, *(block.to_edge(h) for h in pair))
                weighted = (x * step_wide * reach).astype(bf16)
                held.append(mm(block.inputs, weighted, (0, 0)).astype(bf16))
            else:
                reach = wide(low_half, *(block.from_edge(h) for h in pair))
                y = y + reach * mm(block.outputs, held[i])
            mixed_ref[block.rows, cols] = y


def grad_in_kernel(fast, place_ref, lengths_ref, *refs):
    n_rows = 4 if fast else 1
    n_msg = 8 if fast else 2
    row_refs, msg_refs, refs = refs[:n_rows], refs[n_rows : n_rows + n_msg], refs[n_rows + n_msg :]
    normed_ref, mixed_ref, norm_ref = refs[:3]
    rows_ref, gate_weight_ref, out_weight_ref, gate_ref, grad_ref, sums_ref, wide_ref = refs[3:]
    total = rows_ref.shape[0]
    ends = ends_of(lengths_ref)
    tall = total // n_rows
    for member in range(n_rows):
        at = pl.multiple_of(place_ref[8 + member] * tall, tall) if fast else 0
        rows_ref[pl.ds(at, tall), :] = row_refs[member][-tall:, :]
    if fast:
        for slot in range(8):
            at = pl.multiple_of(place_ref[slot] * 128, 128)
            gate_weight_ref[pl.ds(at, 128), :] = msg_refs[slot][:128, :]
            out_weight_ref[pl.ds(at, 128), :] = msg_refs[slot][128:, :]
    else:
        gate_weight_ref[...] = msg_refs[0][...]
        out_weight_ref[...] = msg_refs[1][...]

    def part(at):
        rows = pl.ds(at, 128)
        valid = jnp.where(iota((128, 1), 0) + at < ends[-1], 1.0, 0.0)
        grad = mm(rows_ref[rows, :], out_weight_ref[...]) * valid
        grad_ref[rows, :] = grad
        gate = mm(normed_ref[rows, :], gate_weight_ref[...])
        gate_ref[rows, :] = gate
        gated = mixed_ref[rows, :] * (gate * sigmoid(gate))
        square = jnp.sum(gated * gated, axis=1, keepdims=True)
        cross = jnp.sum(grad * norm_ref[...] * gated, axis=1, keepdims=True)
        lane = iota((128, 128), 1)
        wide_ref[rows, :] = jnp.where(lane == 0, square, jnp.where(lane == 1, cross, 0.0))

    row_loop(total, 128, part)
    for at in range(0, total, 128):
        sums_ref[:, at : at + 128] = wide_ref[at : at + 128, :].T[:8, :]


def norm_kernel(inner_total, place_ref, lengths_ref, *refs):
    n_sums = len(refs) - 21
    sums_refs, refs = refs[:n_sums], refs[n_sums:]
    gate_ref, mixed_ref, grad_ref, norm_ref, weight_ref, rows_ref, normed_ref = refs[:7]
    chunk_refs = refs[7:15]
    partial_ref, grad_gate_ref, grad_mixed_ref, norm_grad_ref = refs[15:19]
    wide_ref, out_rows_ref = refs[19:]
    total, channels = gate_ref.shape
    ends = ends_of(lengths_ref)
    for at in range(0, total, 128):
        tile = sum(ref[:, at : at + 128] for ref in sums_refs)
        tile = jnp.concatenate([tile] * 16, axis=0)
        wide_ref[at : at + 128, :] = tile.T
    norm_grad_ref[...] = jnp.zeros(norm_grad_ref.shape, f32)

    def part(at):
        rows = pl.ds(at, 128)
        valid = jnp.where(iota((128, 1), 0) + at < ends[-1], 1.0, 0.0)
        scale = lax.rsqrt(wide_ref[rows, 0:1] / inner_total + epsilon)
        cross = wide_ref[rows, 1:2]
        gate = gate_ref[rows, :]
        mixed = mixed_ref[rows, :]
        sig = sigmoid(gate)
        gate_act = gate * sig
        gated = mixed * gate_act
        grad = grad_ref[rows, :]
        norm = norm_ref[...]
        hat = gated * scale
        out_rows_ref[rows, :] = (hat * norm * valid).astype(bf16)
        norm_grad_ref[...] += jnp.sum(grad * hat, axis=0, keepdims=True)
        grad_gated = scale * (grad * norm) - gated * (scale * scale * scale * cross / inner_total)
        grad_mixed_ref[rows, :] = grad_gated * gate_act
        grad_gate = grad_gated * mixed * sig * (1.0 + gate * (1.0 - sig))
        grad_gate_ref[rows, :] = grad_gate.astype(bf16)
        partial_ref[rows, :] = mm(out_rows_ref[rows, :], weight_ref[...], (1, 1)).astype(bf16)

    row_loop(total, 128, part)

    tall = chunk_refs[0].shape[0] // 2
    for slot, chunk_ref in enumerate(chunk_refs):
        cols = pl.ds(pl.multiple_of(place_ref[slot] * tall, tall), tall)
        chunk_ref[:tall, :] = mm(normed_ref[:, cols], grad_gate_ref[...], (0, 0)).astype(bf16)
        chunk_ref[tall:, :] = mm(rows_ref[:, cols], out_rows_ref[...], (0, 0)).astype(bf16)


def scan_back_kernel(first_pair, lengths_ref, *refs):
    grad_mixed_ref, act_ref, state_ref, step_col_ref, step_row_ref = refs[:5]
    step_bias_ref, step_bias_col_ref, log_ref, log_col_ref, skip_ref = refs[5:10]
    grad_act_ref, grad_state_ref, step_grad_ref, sums_ref, acc_ref = refs[10:]
    total, own_width = grad_act_ref.shape
    states = state_ref.shape[1] // 2
    ends = ends_of(lengths_ref)
    sums_ref[...] = jnp.zeros(sums_ref.shape, f32)
    raw_row = step_row_ref[...]
    steps = step_sizes(
        step_col_ref[...], raw_row, step_bias_ref, step_bias_col_ref, log_ref, log_col_ref
    )
    rate_row = steps[3]
    low_half = iota((span, 128), 1) < head_width
    lower = jnp.where(iota((span, span), 0) >= iota((span, span), 1), 1.0, 0.0)
    blocks = [Block(b, ends, *steps, state_ref) for b in range(total // span)]
    first, second = blocks
    row_sums, step_rows, out_sums, in_sums = [], [], None, None
    grad_out = jnp.zeros((span, states), f32)
    grad_in = jnp.zeros((span, states), f32)
    head_of = iota((head_rows, 128), 0)
    lane_head = iota((head_rows, 128), 1) // head_width

    for b, block in enumerate(blocks):
        acc_ref[...] = jnp.zeros((span, span), f32)
        row_sum = jnp.zeros((span, 128), f32)
        step_grad = jnp.zeros((head_rows, span), f32)
        lane = iota((span, 128), 1)
        head_row = iota((head_rows, span), 0)
        for i in range(first_pair, first_pair + own_width // 128):
            cols = slice(128 * i, 128 * (i + 1))
            own_cols = slice(128 * (i - first_pair), 128 * (i - first_pair + 1))
            pair = (2 * i, 2 * i + 1)
            x = act_ref[block.rows, cols]
            x_low = x.astype(bf16)
            grad = grad_mixed_ref[block.rows, cols]
            grad_low = grad.astype(bf16)
            halves = (
                jnp.where(low_half, grad, 0.0).astype(bf16),
                jnp.where(low_half, 0.0, grad).astype(bf16),
            )
            step_wide = wide(low_half, *(block.step[:, h : h + 1] for h in pair))
            grads = []
            for h, half in zip(pair, halves):
                decay = block.decay(h)
                spread = mm(half, x_low, (1, 1)) * decay
                stepped = spread * block.step_row[h : h + 1, :]
                acc_ref[...] += stepped
                row_here = jnp.sum(stepped * block.contact, axis=1, keepdims=True)
                row_sum = jnp.where(lane == h, row_here, row_sum)
                step_here = jnp.sum(spread * block.contact, axis=0, keepdims=True)
                step_grad = jnp.where(head_row == h, step_here, step_grad)
                grads.append(mm((decay * block.contact).astype(bf16), grad_low, (0, 0)))
            grad_act = wide(low_half, *grads) * step_wide + skip_ref[:, cols] * grad
            sums_ref[2:3, own_cols] += jnp.sum(grad * x, axis=0, keepdims=True)
            picks = jnp.where(lane_head + 2 * i == head_of, 1.0, 0.0)
            if b == 0:
                reach = wide(low_half, *(second.from_edge(h) for h in pair))
                lead = (grad_mixed_ref[second.rows, cols] * reach).astype(bf16)
                edge = wide(low_half, *(block.to_edge(h) for h in pair))
                weighted = (x * step_wide * edge).astype(bf16)
                held = mm(block.inputs, weighted, (0, 0)).astype(bf16)
                held_grad = mm(second.outputs, lead, (0, 0)).astype(bf16)
                grad_out = grad_out + mm(lead, held, (1, 1))
                grad_in = grad_in + mm(weighted, held_grad, (1, 1))
                back = mm(block.inputs, held_grad) * edge
                grad_act = grad_act + back * step_wide
                ahead = mm(second.outputs, held)
                out_here = mm_exact(picks, lead.astype(f32) * ahead, (1, 1))
                in_here = mm_exact(picks, x * back, (1, 1))
                out_sums = out_here if out_sums is None else out_sums + out_here
                in_sums = in_here if in_sums is None else in_sums + in_here
            grad_act_ref[block.rows, own_cols] = grad_act
        table = (acc_ref[...] * block.mask).astype(bf16)
        grad_c = mm(table, block.inputs)
        grad_b = mm(table, block.outputs, (0, 0))
        if b == 0:
            grad_b = grad_b + grad_in
        else:
            grad_c = grad_c + grad_out
        grad_state_ref[block.rows, :states] = grad_b
        grad_state_ref[block.rows, states:] = grad_c
        row_sums.append(row_sum)
        step_rows.append(step_grad)

    rate_grads = []
    for b, block in enumerate(blocks):
        column = step_rows[b] * block.step_row
        crossing = mm_exact(row_sums[b], lower, (0, 0))[:head_rows] - mm_exact(column, lower)
        if b == 0:
            crossing = crossing + mm_exact(in_sums * block.step_row, 1.0 - lower)
        else:
            crossing = crossing + mm_exact(out_sums, lower)
        rate_grads.append(crossing)
    step_rows[0] = step_rows[0] + in_sums
    rate_grad = jnp.concatenate(rate_grads, axis=1)
    step_grad = jnp.concatenate(step_rows, axis=1) - rate_grad * jnp.exp(log_col_ref[...])
    step_grad = step_grad * sigmoid(raw_row + step_bias_col_ref[...])
    decay_sum = jnp.sum(rate_grad * rate_row, axis=1, keepdims=True)
    bias_sum = jnp.sum(step_grad, axis=1, keepdims=True)
    lane = iota((head_rows, 128), 1)
    head_sums = jnp.where(lane == 0, bias_sum, jnp.where(lane == 1, decay_sum, 0.0))
    head_sums = jnp.concatenate([head_sums] * (128 // head_rows), axis=0).T
    sums_ref[0:2, :128] = head_sums[:2, :]
    step_grad_ref[...] = step_grad


def conv_back(x_ref, mask_ref, grad_ref, held_ref, out_ref, sums_ref, own_taps, own_bias):
    total, taps = out_ref.shape[0], own_taps.shape[0]
    held_ref[total:, :] = jnp.zeros((pad, held_ref.shape[1]), f32)

    def column(cols):
        sums = [jnp.zeros((1, 128), f32) for _ in range(taps + 1)]
        for at in range(0, total, 128):
            pre, shifted = conv_pre(x_ref, mask_ref, own_taps, own_bias, at, cols, 128)
            sig = sigmoid(pre)
            grad = grad_ref[at : at + 128, cols] * sig * (1.0 + pre * (1.0 - sig))
            held_ref[at : at + 128, cols] = grad
            for s in range(taps):
                sums[taps - 1 - s] += jnp.sum(grad * shifted[s], axis=0, keepdims=True)
            sums[taps] += jnp.sum(grad, axis=0, keepdims=True)
        for t, value in enumerate(sums):
            sums_ref[t : t + 1, cols] = value
        for at in range(0, total, 128):
            back = own_taps[taps - 1 : taps, cols] * held_ref[at : at + 128, cols]
            for s in range(1, taps):
                part = held_ref[at + s : at + s + 128, cols]
                part = part * mask_ref[s - 1, at + s : at + s + 128, :]
                back = back + own_taps[taps - 1 - s : taps - s, cols] * part
            out_ref[at : at + 128, cols] = back.astype(bf16)

    column_loop(out_ref.shape[1], column)


def state_back_kernel(fast, place_ref, lengths_ref, *refs):
    state_refs, step_refs, refs = refs[0:2], refs[2:4], refs[4:]
    state_raw_ref, normed_ref, small_ref, grad_state_low_ref, step_low_ref = refs[:5]
    n_out = 4 if fast else 2
    out_refs, refs = refs[5 : 5 + n_out], refs[5 + n_out :]
    mask_ref, taps_ref, bias_ref, grad_state_ref, pre_ref, part_ref, sums_ref = refs
    taps = taps_ref.shape[0]
    taps_ref[...] = small_ref[4 : 4 + taps, :]
    bias_ref[...] = small_ref[4 + taps : 5 + taps, :]
    write_masks(mask_ref, ends_of(lengths_ref))
    grad_state_ref[...] = state_refs[0][...] + state_refs[1][...]
    step_low_ref[...] = (step_refs[0][...] + step_refs[1][...]).astype(bf16)
    sums_ref[...] = jnp.zeros(sums_ref.shape, f32)
    conv_back(
        state_raw_ref,
        mask_ref,
        grad_state_ref,
        pre_ref,
        grad_state_low_ref,
        sums_ref,
        taps_ref,
        bias_ref,
    )

    def chunk(at):
        part = normed_ref[:, pl.ds(at, 256)]
        part_ref[pl.ds(at, 256), :] = mm(part, grad_state_low_ref[...], (0, 0)).astype(bf16)

    depth = normed_ref.shape[1]
    row_loop(depth, 256, chunk)
    if fast:
        share = depth // 32
        for member, out_ref in enumerate(out_refs):
            for c in range(8):
                at = pl.multiple_of((4 * c + place_ref[8 + member]) * share, share)
                out_ref[share * c : share * (c + 1), :] = part_ref[pl.ds(at, share), :]
            out_ref[8 * share :, :] = sums_ref[...].astype(bf16)
    else:
        out_refs[0][...] = part_ref[...]
        out_refs[1][...] = sums_ref[...]


def inner_back_kernel(lengths_ref, *refs):
    act_refs, head_refs, refs = refs[0:2], refs[2:4], refs[4:]
    raw_ref, norm_grad_ref, taps_ref, bias_ref, grad_inner_ref, sums_ref = refs[:6]
    mask_ref, grad_act_ref, pre_ref = refs[6:]
    half = grad_inner_ref.shape[1] // 2
    write_masks(mask_ref, ends_of(lengths_ref))
    grad_act_ref[:, :half] = act_refs[0][...]
    grad_act_ref[:, half:] = act_refs[1][...]
    sums_ref[...] = jnp.zeros(sums_ref.shape, f32)
    sums_ref[6:7, :] = norm_grad_ref[...]
    sums_ref[7:9, :half] = head_refs[0][:2, :] + head_refs[1][:2, :]
    sums_ref[9:10, :half] = head_refs[0][2:3, :]
    sums_ref[9:10, half:] = head_refs[1][2:3, :]
    conv_back(
        raw_ref,
        mask_ref,
        grad_act_ref,
        pre_ref,
        grad_inner_ref,
        sums_ref,
        taps_ref,
        bias_ref,
    )


def message_kernel(fast, *refs):
    grad_inner_ref, step_low_ref, normed_ref = refs[:3]
    msg_ref = refs[-1]
    chunks = msg_ref.shape[0]
    tall = normed_ref.shape[1] // chunks
    step_low = step_low_ref[...]
    tail = tall + head_rows

    def chunk(c, carry):
        part = normed_ref[:, pl.ds(pl.multiple_of(c * tall, tall), tall)]
        msg_ref[c, :tall, :] = mm(part, grad_inner_ref[...], (0, 0)).astype(bf16)
        msg_ref[c, tall:tail, :tall] = mm(step_low, part).astype(bf16)
        msg_ref[c, tall:tail, tall:] = jnp.zeros((head_rows, msg_ref.shape[2] - tall), bf16)
        return carry

    lax.fori_loop(0, chunks, chunk, 0)
    if fast:
        sums_ref, state_refs = refs[3], refs[4:8]

        def state_rows(low, high):
            return sum(ref[low:high, :].astype(f32) for ref in state_refs)

        states = state_refs[0].shape[1]
        share = (state_refs[0].shape[0] - 16) // chunks
        shared = state_rows(share * chunks, share * chunks + 5)
        shared = jnp.concatenate([shared, jnp.zeros((5, states), f32)], axis=1)
        sums = jnp.concatenate([sums_ref[:10, :], shared, jnp.zeros((1, 2 * states), f32)], axis=0)
        sums = sums.astype(bf16)
        for c in range(chunks):
            low = share * c
            part = jnp.concatenate(
                [state_rows(low, low + 16), state_rows(low + 16, low + 32)], axis=1
            )
            msg_ref[c, tail : tail + 16, :] = part.astype(bf16)
            msg_ref[c, tail + 16 :, :] = sums


def project_back_kernel(fast, place_ref, *refs):
    (
        grad_gate_ref,
        grad_inner_ref,
        grad_state_low_ref,
        step_low_ref,
        gate_weight_ref,
        weight_ref,
        state_weight_ref,
        step_weight_ref,
    ) = refs[:8]
    out_refs = refs[8:]
    for member in range(4):
        at = pl.multiple_of(place_ref[8 + member] * 128, 128) if fast else 128 * member
        rows = pl.ds(at, 128)
        grad = mm(grad_gate_ref[rows, :], gate_weight_ref[...], (1, 1))
        grad = grad + mm(grad_inner_ref[rows, :], weight_ref[...], (1, 1))
        grad = grad + mm(grad_state_low_ref[rows, :], state_weight_ref[...], (1, 1))
        grad = grad + mm(step_low_ref[:, rows], step_weight_ref[...], (0, 0))
        out_refs[member % 2][member // 2] = grad.astype(bf16)


def prepare_kernel(place_ref, gain_ref, taps_ref, bias_ref, state_ref, shared_ref):
    owner = place_ref[0]
    share, states = state_ref.shape
    shared_ref[:share, :] = state_ref[...]

    def placed(value, at):
        width = value.shape[1]
        pick = iota((width, states), 1) - at == iota((width, states), 0)
        return mm(value, jnp.where(pick, 1.0, 0.0).astype(bf16))

    start = owner * gain_ref.shape[1]
    small = jnp.concatenate(
        [placed(gain_ref[...], start - states * i) for i in range(4)]
        + [placed(taps_ref[...], owner * taps_ref.shape[1])]
        + [placed(bias_ref[...], owner * bias_ref.shape[1])]
        + [jnp.zeros((7, states), f32)],
        axis=0,
    )
    shared_ref[share:, :] = small.astype(bf16)


def prepare_late_kernel(*refs):
    input_ref, out_ref, taps_ref, bias_ref, step_bias_ref, log_ref, skip_ref, norm_ref = refs[:8]
    late_ref, outs = refs[8], refs[9:]
    depth_part = input_ref.shape[0]
    late_ref[:depth_part, :] = input_ref[:, 0, :]
    late_ref[depth_part:, :] = out_ref[...].astype(f32).T.astype(bf16)
    heads = step_bias_ref.shape[1]
    pick = jnp.where(iota((heads, head_rows), 0) == iota((heads, head_rows), 1), 1.0, 0.0)
    square = iota((head_rows, head_rows), 0) == iota((head_rows, head_rows), 1)

    def both(value_ref, row_ref, col_ref):
        row = mm_exact(value_ref[...].astype(f32), pick)
        row_ref[...] = row
        col_ref[...] = jnp.sum(jnp.where(square, row, 0.0), axis=1, keepdims=True)

    outs[0][...] = taps_ref[...].astype(f32)
    outs[1][...] = bias_ref[...].astype(f32)
    both(step_bias_ref, outs[2], outs[3])
    both(log_ref, outs[4], outs[5])
    channels = norm_ref.shape[1]
    own = iota((heads, channels), 1) // (channels // heads) == iota((heads, channels), 0)
    outs[6][...] = mm_exact(skip_ref[...].astype(f32), jnp.where(own, 1.0, 0.0))
    outs[7][...] = norm_ref[...].astype(f32)


def assemble_kernel(input_ref, step_ref, *refs):
    shared_refs, msg_ref = refs[:4], refs[4]
    depth_part, _, channels = input_ref.shape
    share = shared_refs[0].shape[0] - 16
    tail = depth_part + 2 * share
    msg_ref[:depth_part, :] = input_ref[:, 1, :]
    for member, ref in enumerate(shared_refs):
        high, low = depth_part + share * (member // 2), 256 * (member % 2)
        msg_ref[high : high + share, low : low + 256] = ref[:share, :]
    small = sum(ref[share:, :].astype(f32) for ref in shared_refs)
    msg_ref[tail:, :256] = small.astype(bf16)
    msg_ref[tail:, 256:384] = step_ref[...]
    msg_ref[tail:, 384:] = jnp.zeros((16, channels - 384), bf16)


def call(kernel, micros, scalars, arrays, outs, scratch):
    smem = pl.BlockSpec(memory_space=pltpu.SMEM)
    vmem = pl.BlockSpec(memory_space=pltpu.VMEM)
    return pl.pallas_call(
        kernel,
        out_shape=[jax.ShapeDtypeStruct(shape, kind) for shape, kind in outs],
        in_specs=[smem] * len(scalars) + [vmem] * len(arrays),
        out_specs=[vmem] * len(outs),
        scratch_shapes=[pltpu.VMEM(shape, kind) for shape, kind in scratch],
        compiler_params=pltpu.CompilerParams(vmem_limit_bytes=vmem_bytes),
        cost_estimate=pl.CostEstimate(
            flops=int(micros * 1.1e9), bytes_accessed=1 << 20, transcendentals=0
        ),
    )(*scalars, *arrays)


def ring_ok(n_dp, n_tensor):
    return n_dp == 8 and n_tensor == 4


ring_order = (0, 2, 4, 6, 7, 5, 3, 1)


def ring_place(index):
    high, low = index // 2, index % 2
    return jnp.where(low == 0, high, 7 - high)


def ring_index(place):
    place = lax.rem(place + 16, 8)
    return jnp.where(place < 4, 2 * place, 2 * (7 - place) + 1)


def ring_send(value, forward):
    pairs = []
    for place in range(8):
        other = (place + (1 if forward else 7)) % 8
        pairs.append((ring_order[place], ring_order[other]))
    return lax.ppermute(value, "dp", pairs)


def ring_gather(value):
    me = ring_place(lax.axis_index("dp"))
    pieces = [(value, ring_index(me))]
    ahead, back = value, value
    for step in range(1, 5):
        ahead = ring_send(ahead, True)
        pieces.append((ahead, ring_index(me - step)))
        if step < 4:
            back = ring_send(back, False)
            pieces.append((back, ring_index(me + step)))
    return pieces


def dp_swap(value, bit):
    return lax.ppermute(value, "dp", [(i, i ^ bit) for i in range(8)])


def ring_step(held):
    return ring_send(held[0], True), ring_send(held[1], False)


def add_low(got, own):
    return (got.astype(f32) + own.astype(f32)).astype(bf16)


def ordered(first, then):
    return lax.optimization_barrier((first, then))


def tensor_gather(value):
    near = tensor_swap(value, 1)
    far = tensor_swap(value, 2)
    return [value, near, far, tensor_swap(far, 1)]


def tensor_direct(value):
    return [value] + [tensor_swap(value, bit) for bit in range(1, 4)]


def tensor_sum(value, depth):
    parts = value.reshape(4, -1, depth)
    parts = lax.all_to_all(parts, "tensor", 0, 0, tiled=True)
    return jnp.sum(parts.astype(f32), axis=0)


def tensor_swap(value, bit):
    return lax.ppermute(value, "tensor", [(i, i ^ bit) for i in range(4)])


def body(
    tokens,
    lengths,
    cotangent,
    pre_gain,
    input_weight,
    step_weight,
    state_weight,
    conv_inner,
    conv_inner_bias,
    conv_state,
    conv_state_bias,
    step_bias,
    decay_log,
    skip_gain,
    norm_gain,
    output_weight,
):
    n_dp, n_tensor = lax.axis_size("dp"), lax.axis_size("tensor")
    fast = ring_ok(n_dp, n_tensor)
    owners = n_dp * n_tensor
    me = lax.axis_index("tensor")
    owner = lax.axis_index("dp") * n_tensor + me
    own_rows, depth = tokens.shape
    total = own_rows * n_tensor
    states = state_weight.shape[1]
    heads = step_weight.shape[1]
    share = state_weight.shape[0]
    taps = conv_state.shape[0]
    channels = input_weight.shape[2]
    inner_total = channels * n_tensor

    owner_place = jnp.stack([owner, owners]).astype(jnp.int32)
    (shared,) = call(
        prepare_kernel,
        1,
        [owner_place],
        [pre_gain[None, :], conv_state, conv_state_bias[None, :], state_weight],
        [((share + 16, states), bf16)],
        [],
    )
    step_rows = jnp.pad(step_weight.T, ((0, head_rows - heads), (0, 0)))
    late, *params = call(
        prepare_late_kernel,
        2,
        [],
        [
            input_weight,
            output_weight,
            conv_inner,
            conv_inner_bias[None, :],
            step_bias[None, :],
            decay_log[None, :],
            skip_gain[None, :],
            norm_gain[None, :],
        ],
        [
            ((input_weight.shape[0] + output_weight.shape[1], channels), bf16),
            ((taps, channels), f32),
            ((1, channels), f32),
            ((1, head_rows), f32),
            ((head_rows, 1), f32),
            ((1, head_rows), f32),
            ((head_rows, 1), f32),
            ((1, channels), f32),
            ((1, channels), f32),
        ],
        [],
    )
    conv_params, head_params, norm_row = params[:2], params[2:7], params[7]
    if fast:
        shared = tensor_direct(shared)
        late_one = ring_step((late, late))
        (msg,) = call(
            assemble_kernel,
            1,
            [],
            [input_weight, step_rows, *shared],
            [((input_weight.shape[0] + 2 * share + 16, channels), bf16)],
            [],
        )
        late_one, msg = ordered(late_one, msg)
        msg = ring_gather(msg)
        weight_pieces, late_one = ordered([piece for piece, _ in msg], late_one)
        late_two = ring_step(late_one)
        late_three = ring_step(late_two)
        late_pieces = [late, *late_one, *late_two, *late_three, ring_send(late_three[0], True)]
        row_pieces = tensor_gather(jnp.concatenate([tokens, cotangent], axis=0))
        grad_pieces = row_pieces
        place = jnp.stack([index for _, index in msg] + [me, me ^ 1, me ^ 2, me ^ 3])
    else:
        row_pieces = [lax.all_gather(tokens, "tensor", axis=0, tiled=True)]
        grad_pieces = [lax.all_gather(cotangent, "tensor", axis=0, tiled=True)]
        gate_weight, inner_weight = late[: input_weight.shape[0]], input_weight[:, 1]
        weight_pieces = [
            lax.all_gather(inner_weight, "dp", axis=0, tiled=True),
            lax.all_gather(state_weight, ("dp", "tensor"), axis=0, tiled=True),
            lax.all_gather(step_rows, "dp", axis=1, tiled=True),
            lax.psum(shared[share:], ("dp", "tensor")),
        ]
        late_pieces = [
            lax.all_gather(gate_weight, "dp", axis=0, tiled=True),
            lax.all_gather(late[input_weight.shape[0] :], "dp", axis=0, tiled=True),
        ]
        place = jnp.concatenate([jnp.arange(8), jnp.arange(4)])
    place = place.astype(jnp.int32)

    masks = ((taps - 1, total + pad, 128), f32)
    state_taps = [((taps, states), f32), ((1, states), f32)]
    (
        rows,
        normed,
        inner_full,
        state_full,
        step_full,
        small_full,
        raw,
        state_raw,
        step_col,
        step_row,
        act,
        state_act,
    ) = call(
        functools.partial(forward_kernel, fast),
        6,
        [place, lengths],
        row_pieces + weight_pieces + conv_params,
        [
            ((total, depth), bf16),
            ((total, depth), bf16),
            ((depth, channels), bf16),
            ((depth, states), bf16),
            ((head_rows, depth), bf16),
            ((16, states), f32),
            ((total + pad, channels), f32),
            ((total + pad, states), f32),
            ((total, head_rows), f32),
            ((head_rows, total), f32),
            ((total, channels), f32),
            ((total, states), f32),
        ],
        [masks] + state_taps,
    )
    if fast:
        late_two, act = ordered(late_two, act)
        late_pieces[3:5] = late_two
    (mixed,) = call(
        scan_kernel,
        5,
        [lengths],
        [act, state_act, step_col, step_row] + head_params,
        [((total, channels), f32)],
        [],
    )
    grad_rows, gate_full, output_full, gate, grad_normalized, sums = call(
        functools.partial(grad_in_kernel, fast),
        5,
        [place, lengths],
        grad_pieces + late_pieces + [normed, mixed, norm_row],
        [
            ((total, depth), bf16),
            ((depth, channels), bf16),
            ((depth, channels), bf16),
            ((total, channels), f32),
            ((total, channels), f32),
            ((8, total), f32),
        ],
        [((total, 128), f32)],
    )
    if fast:
        sums = tensor_direct(sums)
    else:
        sums = [lax.psum(sums, "tensor")]
    chunks = 8
    tall = depth // chunks
    norm_outs = call(
        functools.partial(norm_kernel, inner_total),
        9,
        [place, lengths],
        [*sums, gate, mixed, grad_normalized, norm_row, output_full, grad_rows, normed],
        [((2 * tall, channels), bf16)] * chunks
        + [
            ((total, depth), bf16),
            ((total, channels), bf16),
            ((total, channels), f32),
            ((1, channels), f32),
        ],
        [((total, 128), f32), ((total, channels), bf16)],
    )
    gate_chunks = norm_outs[:chunks]
    partial_out, grad_gate, grad_mixed, norm_grad = norm_outs[chunks:]

    def scan_back(first_pair, grad):
        return call(
            functools.partial(scan_back_kernel, first_pair),
            6,
            [lengths],
            [grad, act, state_act, step_col, step_row] + head_params,
            [
                ((total, channels // 2), f32),
                ((total, states), f32),
                ((head_rows, total), f32),
                ((8, channels // 2), f32),
            ],
            [((span, span), f32)],
        )

    if fast:
        got = ring_step((gate_chunks[7], gate_chunks[5]))
        held = add_low(got[0], gate_chunks[6]), add_low(got[1], gate_chunks[3])
    first = scan_back(0, grad_mixed)
    if fast:
        held, grad_mixed = ordered(held, grad_mixed)
        got = ring_step(held)
        held = add_low(got[0], gate_chunks[4]), add_low(got[1], gate_chunks[1])
    second = scan_back(channels // 256, grad_mixed)
    if fast:
        held, state_raw = ordered(held, state_raw)
        got = ring_step(held)
        held, last = add_low(got[0], gate_chunks[2]), got[1]
    share_rows = depth // 4 + 16
    state_outs = call(
        functools.partial(state_back_kernel, fast),
        4,
        [place, lengths],
        [first[1], second[1], first[2], second[2], state_raw, normed, small_full],
        [((total, states), bf16), ((head_rows, total), bf16)]
        + (
            [((share_rows, states), bf16)] * 4
            if fast
            else [((depth, states), bf16), ((16, states), f32)]
        ),
        [
            masks,
            *state_taps,
            ((total, states), f32),
            ((total + pad, states), f32),
            ((depth, states), bf16),
            ((16, states), f32),
        ],
    )
    grad_state_low, step_low = state_outs[:2]
    state_parts = state_outs[2:]
    if fast:
        state_parts = [state_parts[0]] + [tensor_swap(state_parts[i], i) for i in range(1, 4)]
    if fast:
        (held, last), raw = ordered((held, last), raw)
        gate_out = gate_chunks[0].astype(f32) + last.astype(f32)
        gate_out = gate_out + ring_send(held, True).astype(f32)
    grad_inner, sums = call(
        inner_back_kernel,
        6,
        [lengths],
        [first[0], second[0], first[3], second[3], raw, norm_grad] + conv_params,
        [((total, channels), bf16), ((16, channels), f32)],
        [masks, ((total, channels), f32), ((total + pad, channels), f32)],
    )
    if fast:
        mixed_rows = tensor_sum(partial_out, depth)
        (gate_out, mixed_rows), grad_inner = ordered((gate_out, mixed_rows), grad_inner)
    msg_rows = tall + head_rows + (32 if fast else 0)
    (inner_msg,) = call(
        functools.partial(message_kernel, fast),
        5,
        [],
        [grad_inner, step_low, normed] + ([sums, *state_parts] if fast else []),
        [((chunks, msg_rows, channels), bf16)],
        [],
    )
    if fast:
        inner_msg, grad_inner = ordered(inner_msg, grad_inner)
    keep_rows, give_rows = call(
        functools.partial(project_back_kernel, fast),
        6,
        [place],
        [
            grad_gate,
            grad_inner,
            grad_state_low,
            step_low,
            gate_full,
            inner_full,
            state_full,
            step_full,
        ],
        [((2, 128, depth), bf16)] * 2,
        [],
    )

    token_float = tokens.astype(f32)
    gain_full = small_full[: depth // states].reshape(1, depth)

    if fast:
        got = tensor_swap(give_rows, 1)
        far = tensor_swap(add_low(keep_rows[1], got[1]), 2)
        grad_local = keep_rows[0].astype(f32) + got[0].astype(f32) + far.astype(f32)
        gate_grad, output_grad = gate_out[:tall], gate_out[tall:].T
        inner_out = lax.all_to_all(inner_msg, "dp", 0, 0, tiled=True)
        inner_out = jnp.sum(inner_out.astype(f32), axis=0)
        tail = tall + head_rows
        state_grad = inner_out[tail : tail + 16]
        state_grad = jnp.concatenate([state_grad[:, :states], state_grad[:, states:]], axis=0)
        sums = inner_out[tail + 16 :]
        width = states // owners
        conv_state_sum = lax.dynamic_slice(
            sums, (10, owner * width), (taps + 1, width)
        )
        conv_state_grad, conv_state_bias_grad = conv_state_sum[:taps], conv_state_sum[taps]
        inner_grad, step_grad = inner_out[:tall], inner_out[tall : tall + heads, :tall].T
    else:
        state_part, state_sums = state_parts
        state_grad = lax.psum_scatter(
            state_part.astype(f32), ("dp", "tensor"), scatter_dimension=0, tiled=True
        )
        conv_state_sum = lax.psum_scatter(
            state_sums[: taps + 1], ("dp", "tensor"), scatter_dimension=1, tiled=True
        )
        conv_state_grad, conv_state_bias_grad = conv_state_sum[:taps], conv_state_sum[taps]
        grad_normed = jnp.stack([keep_rows, give_rows], axis=1).reshape(total, depth)
        mixed_rows, grad_local = (
            lax.psum_scatter(part, "tensor", scatter_dimension=0, tiled=True).astype(f32)
            for part in (partial_out, grad_normed)
        )
        both, inner_float = jnp.stack(gate_chunks).astype(f32), inner_msg.astype(f32)
        gate_grad, output_grad, inner_grad = (
            lax.psum_scatter(part.reshape(depth, channels), "dp", scatter_dimension=0, tiled=True)
            for part in (both[:, :tall], both[:, tall:], inner_float[:, :tall])
        )
        output_grad = output_grad.T
        step_part = inner_float[:, tall : tall + heads, :tall].transpose(0, 2, 1)
        step_part = step_part.reshape(depth, heads)
        step_grad = lax.psum_scatter(step_part, "dp", scatter_dimension=0, tiled=True)
        sums = lax.psum(sums, "dp")
    input_grad = jnp.stack([gate_grad, inner_grad], axis=1)
    own_gain = jnp.sum(input_weight.astype(f32) * input_grad, axis=(1, 2))
    own_gain = own_gain + jnp.sum(step_weight.astype(f32) * step_grad, axis=1)
    state_gain = jnp.sum(state_weight.astype(f32) * state_grad, axis=1)
    if fast:
        own_gain = sum(tensor_direct(own_gain))
        own_gain = lax.dynamic_slice(own_gain, (me * share,), (share,))
    else:
        own_gain = lax.psum_scatter(own_gain, "tensor", scatter_dimension=0, tiled=True)
    pre_gain_grad = (own_gain + state_gain) / pre_gain.astype(f32)
    block_out = (token_float + mixed_rows).astype(bf16)
    scale = lax.rsqrt(jnp.mean(token_float * token_float, axis=1, keepdims=True) + epsilon)
    grad_scaled = grad_local * gain_full
    along = jnp.sum(grad_scaled * token_float, axis=1, keepdims=True) / depth
    tokens_grad = (
        scale * grad_scaled
        - token_float * (scale * scale * scale * along)
        + cotangent.astype(f32)
    )
    skip_grad = sums[9].reshape(heads, -1).sum(axis=1)
    return (
        block_out,
        tokens_grad,
        pre_gain_grad,
        input_grad,
        step_grad,
        state_grad,
        sums[:taps],
        sums[taps],
        conv_state_grad,
        conv_state_bias_grad,
        sums[7, :heads],
        sums[8, :heads],
        skip_grad,
        sums[6],
        output_grad,
    )


def solution(mesh):
    in_specs = (
        P(("dp", "tensor"), None),
        P("dp", None),
        P(("dp", "tensor"), None),
        P(("dp", "tensor")),
        P("dp", None, "tensor"),
        P("dp", "tensor"),
        P(("dp", "tensor"), None),
        P(None, "tensor"),
        P("tensor"),
        P(None, ("dp", "tensor")),
        P(("dp", "tensor")),
        P("tensor"),
        P("tensor"),
        P("tensor"),
        P("tensor"),
        P("tensor", "dp"),
    )
    out_specs = (
        P(("dp", "tensor"), None),
        P(("dp", "tensor"), None),
        P(("dp", "tensor")),
        P("dp", None, "tensor"),
        P("dp", "tensor"),
        P(("dp", "tensor"), None),
        P(None, "tensor"),
        P("tensor"),
        P(None, ("dp", "tensor")),
        P(("dp", "tensor")),
        P("tensor"),
        P("tensor"),
        P("tensor"),
        P("tensor"),
        P("tensor", "dp"),
    )
    return jax.shard_map(body, mesh=mesh, in_specs=in_specs, out_specs=out_specs, check_vma=False)
```

```python
import functools

import jax
import jax.numpy as jnp
from jax import lax
from jax.experimental import pallas as pl
from jax.experimental.pallas import tpu as pltpu
from jax.sharding import PartitionSpec as P

epsilon = 1e-05
highest = lax.Precision.HIGHEST
f32 = jnp.float32
bf16 = jnp.bfloat16
span = 256
pad = 8
head_rows = 16
head_width = 64
vmem_bytes = 61 * 1024 * 1024


def mm(a, b, over=(1, 0)):
    dims = (((over[0],), (over[1],)), ((), ()))
    return lax.dot_general(a, b, dims, preferred_element_type=f32)


def mm_exact(a, b, over=(1, 0)):
    dims = (((over[0],), (over[1],)), ((), ()))
    return lax.dot_general(a, b, dims, preferred_element_type=f32, precision=highest)


def sigmoid(v):
    return 1.0 / (1.0 + jnp.exp(-v))


def ends_of(lengths_ref):
    ends, total = [], None
    for slot in range(lengths_ref.shape[1]):
        here = lengths_ref[0, slot]
        total = here if total is None else total + here
        ends.append(total)
    return ends


def segment_of(places, ends):
    segment = jnp.zeros(places.shape, jnp.int32)
    for end in ends:
        segment = segment + jnp.where(places >= end, 1, 0)
    return segment


def iota(shape, dim):
    return lax.broadcasted_iota(jnp.int32, shape, dim)


def write_masks(mask_ref, ends):
    rows = mask_ref.shape[1] - pad
    places = iota((rows, 128), 0)
    segment = segment_of(places, ends)
    for shift in range(1, mask_ref.shape[0] + 1):
        same = (segment_of(places - shift, ends) == segment) & (places >= shift)
        mask_ref[shift - 1, :rows, :] = jnp.where(same, 1.0, 0.0)
        mask_ref[shift - 1, rows:, :] = jnp.zeros((pad, 128), f32)


def shifted_rows(x_ref, mask_ref, at, cols, shift, tall):
    part = x_ref[pad + at - shift : pad + at - shift + tall, cols]
    if shift == 0:
        return part
    return part * mask_ref[shift - 1, at : at + tall, :]


def conv_pre(x_ref, mask_ref, taps_ref, bias_ref, at, cols, tall):
    taps = taps_ref.shape[0]
    shifted = [shifted_rows(x_ref, mask_ref, at, cols, s, tall) for s in range(taps)]
    total = bias_ref[:, cols]
    for s in range(taps):
        total = total + taps_ref[taps - 1 - s : taps - s, cols] * shifted[s]
    return total, shifted


def column_loop(width, step):
    def one(c, carry):
        step(pl.ds(pl.multiple_of(c * 128, 128), 128))
        return carry

    lax.fori_loop(0, width // 128, one, 0)


def row_loop(rows, tall, step):
    def one(r, carry):
        step(pl.multiple_of(r * tall, tall))
        return carry

    lax.fori_loop(0, rows // tall, one, 0)


class Block:
    def __init__(self, b, ends, step_col, step_row, rate_col, rate_row, state_ref):
        low, top = b * span, (b + 1) * span
        states = state_ref.shape[1] // 2
        lower = jnp.where(iota((span, span), 0) >= iota((span, span), 1), 1.0, 0.0)
        self.rows = slice(low, top)
        self.step = step_col[low:top]
        self.step_row = step_row[:, low:top]
        self.cum = mm_exact(lower, rate_col[low:top])
        self.cum_row = mm_exact(rate_row[:, low:top], lower, (1, 1))
        self.inputs = state_ref[low:top, :states].astype(bf16)
        self.outputs = state_ref[low:top, states:].astype(bf16)
        segment = segment_of(iota((span, 1), 0) + low, ends)
        segment_row = segment_of(iota((1, span), 1) + low, ends)
        edge = sum(jnp.where(span - 1 >= end, 1, 0) for end in ends)
        self.near_edge = jnp.where(segment == edge, 1.0, 0.0)
        self.mask = jnp.where(segment == segment_row, lower, 0.0)
        self.contact = mm(self.outputs, self.inputs, (1, 1)) * self.mask

    def decay(self, h):
        gap = self.cum[:, h : h + 1] - self.cum_row[h : h + 1, :]
        return jnp.exp(jnp.minimum(gap, 0.0))

    def from_edge(self, h):
        return jnp.exp(self.cum[:, h : h + 1]) * self.near_edge

    def to_edge(self, h):
        last = self.cum[span - 1 : span, h : h + 1]
        return jnp.exp(last - self.cum[:, h : h + 1]) * self.near_edge


def wide(low_half, left, right):
    return jnp.where(low_half, left, right)


def step_sizes(raw_col, raw_row, bias_ref, bias_col_ref, log_ref, log_col_ref):
    def soft(v):
        return jnp.maximum(v, 0.0) + jnp.log1p(jnp.exp(-jnp.abs(v)))

    step_col = soft(raw_col + bias_ref[...])
    step_row = soft(raw_row + bias_col_ref[...])
    rate_col = -step_col * jnp.exp(log_ref[...])
    rate_row = -step_row * jnp.exp(log_col_ref[...])
    return step_col, step_row, rate_col, rate_row


def forward_kernel(fast, place_ref, lengths_ref, *refs):
    n_msg = 8 if fast else 4
    n_rows = 4 if fast else 1
    row_refs, msg_refs, refs = refs[:n_rows], refs[n_rows : n_rows + n_msg], refs[n_rows + n_msg :]
    (taps_ref, bias_ref, step_bias_ref, step_bias_col_ref, log_ref, log_col_ref, skip_ref) = refs[:7]
    (
        normed_ref,
        turned_ref,
        weight_ref,
        state_weight_ref,
        step_weight_ref,
        small_ref,
        raw_ref,
        state_raw_ref,
        step_col_ref,
        step_row_ref,
        act_ref,
        state_ref,
        mixed_ref,
    ) = refs[7:20]
    mask_ref, state_taps_ref, state_bias_ref = refs[20:]
    total, channels = act_ref.shape
    ends = ends_of(lengths_ref)

    if fast:
        depth_part = 128
        small = jnp.zeros(small_ref.shape, f32)
        share = state_weight_ref.shape[0] // 32
        for slot in range(8):
            msg = msg_refs[slot]
            index = place_ref[slot]
            at = pl.multiple_of(index * depth_part, depth_part)
            weight_ref[pl.ds(at, depth_part), :] = msg[:depth_part, :]
            for member in range(4):
                inner = pl.multiple_of(at + place_ref[8 + member] * share, share)
                high, low = depth_part + share * (member // 2), 256 * (member % 2)
                state_weight_ref[pl.ds(inner, share), :] = msg[
                    high : high + share, low : low + 256
                ]
            tail = depth_part + 2 * share
            small = small + msg[tail : tail + 16, :256].astype(f32)
            step_weight_ref[:, pl.ds(at, depth_part)] = msg[tail : tail + 16, 256:384]
        small_ref[...] = small
    else:
        weight_ref[...] = msg_refs[0][...]
        state_weight_ref[...] = msg_refs[1][...]
        step_weight_ref[...] = msg_refs[2][...]
        small_ref[...] = msg_refs[3][...].astype(f32)
    gain = jnp.concatenate([small_ref[i : i + 1, :] for i in range(4)], axis=1)
    taps = taps_ref.shape[0]
    state_taps_ref[...] = small_ref[4 : 4 + taps, :]
    state_bias_ref[...] = small_ref[4 + taps : 5 + taps, :]

    tall = total // n_rows
    for member in range(n_rows):
        at = pl.multiple_of(place_ref[8 + member] * tall, tall) if fast else 0
        value = row_refs[member][:tall, :].astype(f32)
        scale = lax.rsqrt(jnp.mean(value * value, axis=1, keepdims=True) + epsilon)
        normed = (value * scale * gain).astype(bf16)
        normed_ref[pl.ds(at, tall), :] = normed
        turned_ref[:, pl.ds(at, tall)] = normed.astype(f32).T.astype(bf16)

    raw_ref[:pad, :] = jnp.zeros((pad, channels), f32)
    state_raw_ref[:pad, :] = jnp.zeros((pad, state_raw_ref.shape[1]), f32)

    def project(at):
        part = normed_ref[pl.ds(at, 128), :]
        raw_ref[pl.ds(at + pad, 128), :] = mm(part, weight_ref[...])
        state_raw_ref[pl.ds(at + pad, 128), :] = mm(part, state_weight_ref[...])
        step_col_ref[pl.ds(at, 128), :] = mm(part, step_weight_ref[...], (1, 1))

    row_loop(total, 128, project)
    step_row_ref[...] = mm(step_weight_ref[...], normed_ref[...], (1, 1))

    write_masks(mask_ref, ends)

    def activate(x_ref, out_ref, own_taps, own_bias):
        def column(cols):
            for at in range(0, total, 128):
                pre, _ = conv_pre(x_ref, mask_ref, own_taps, own_bias, at, cols, 128)
                out_ref[at : at + 128, cols] = pre * sigmoid(pre)

        column_loop(out_ref.shape[1], column)

    activate(raw_ref, act_ref, taps_ref, bias_ref)
    activate(state_raw_ref, state_ref, state_taps_ref, state_bias_ref)

    steps = step_sizes(
        step_col_ref[...],
        step_row_ref[...],
        step_bias_ref,
        step_bias_col_ref,
        log_ref,
        log_col_ref,
    )
    low_half = iota((span, 128), 1) < head_width
    held = []
    for b in range(total // span):
        block = Block(b, ends, *steps, state_ref)
        for i in range(channels // 128):
            cols = slice(128 * i, 128 * (i + 1))
            pair = (2 * i, 2 * i + 1)
            x = act_ref[block.rows, cols]
            step_wide = wide(low_half, *(block.step[:, h : h + 1] for h in pair))
            x_step = (x * step_wide).astype(bf16)
            y = [mm((block.decay(h) * block.contact).astype(bf16), x_step) for h in pair]
            y = wide(low_half, *y) + skip_ref[:, cols] * x
            if b == 0:
                reach = wide(low_half, *(block.to_edge(h) for h in pair))
                weighted = (x * step_wide * reach).astype(bf16)
                held.append(mm(block.inputs, weighted, (0, 0)).astype(bf16))
            else:
                reach = wide(low_half, *(block.from_edge(h) for h in pair))
                y = y + reach * mm(block.outputs, held[i])
            mixed_ref[block.rows, cols] = y


def grad_in_kernel(fast, place_ref, lengths_ref, *refs):
    n_rows = 4 if fast else 1
    n_msg = 8 if fast else 2
    row_refs, msg_refs, refs = refs[:n_rows], refs[n_rows : n_rows + n_msg], refs[n_rows + n_msg :]
    normed_ref, mixed_ref, norm_ref = refs[:3]
    rows_ref, gate_weight_ref, out_weight_ref, gate_ref, grad_ref, sums_ref, wide_ref = refs[3:]
    total = rows_ref.shape[0]
    ends = ends_of(lengths_ref)
    tall = total // n_rows
    for member in range(n_rows):
        at = pl.multiple_of(place_ref[8 + member] * tall, tall) if fast else 0
        rows_ref[pl.ds(at, tall), :] = row_refs[member][-tall:, :]
    if fast:
        for slot in range(8):
            at = pl.multiple_of(place_ref[slot] * 128, 128)
            gate_weight_ref[pl.ds(at, 128), :] = msg_refs[slot][:128, :]
            out_weight_ref[pl.ds(at, 128), :] = msg_refs[slot][128:, :]
    else:
        gate_weight_ref[...] = msg_refs[0][...]
        out_weight_ref[...] = msg_refs[1][...]

    def part(at):
        rows = pl.ds(at, 128)
        valid = jnp.where(iota((128, 1), 0) + at < ends[-1], 1.0, 0.0)
        grad = mm(rows_ref[rows, :], out_weight_ref[...]) * valid
        grad_ref[rows, :] = grad
        gate = mm(normed_ref[rows, :], gate_weight_ref[...])
        gate_ref[rows, :] = gate
        gated = mixed_ref[rows, :] * (gate * sigmoid(gate))
        square = jnp.sum(gated * gated, axis=1, keepdims=True)
        cross = jnp.sum(grad * norm_ref[...] * gated, axis=1, keepdims=True)
        lane = iota((128, 128), 1)
        wide_ref[rows, :] = jnp.where(lane == 0, square, jnp.where(lane == 1, cross, 0.0))

    row_loop(total, 128, part)
    for at in range(0, total, 128):
        sums_ref[:, at : at + 128] = wide_ref[at : at + 128, :].T[:8, :]


def norm_kernel(inner_total, place_ref, lengths_ref, *refs):
    n_sums = len(refs) - 21
    sums_refs, refs = refs[:n_sums], refs[n_sums:]
    gate_ref, mixed_ref, grad_ref, norm_ref, weight_ref, rows_ref, turned_ref = refs[:7]
    chunk_refs = refs[7:15]
    partial_ref, grad_gate_ref, grad_mixed_ref, norm_grad_ref = refs[15:19]
    wide_ref, out_rows_ref = refs[19:]
    total, channels = gate_ref.shape
    ends = ends_of(lengths_ref)
    for at in range(0, total, 128):
        tile = sum(ref[:, at : at + 128] for ref in sums_refs)
        tile = jnp.concatenate([tile] * 16, axis=0)
        wide_ref[at : at + 128, :] = tile.T
    norm_grad_ref[...] = jnp.zeros(norm_grad_ref.shape, f32)

    def part(at):
        rows = pl.ds(at, 128)
        valid = jnp.where(iota((128, 1), 0) + at < ends[-1], 1.0, 0.0)
        scale = lax.rsqrt(wide_ref[rows, 0:1] / inner_total + epsilon)
        cross = wide_ref[rows, 1:2]
        gate = gate_ref[rows, :]
        mixed = mixed_ref[rows, :]
        sig = sigmoid(gate)
        gate_act = gate * sig
        gated = mixed * gate_act
        grad = grad_ref[rows, :]
        norm = norm_ref[...]
        hat = gated * scale
        out_rows_ref[rows, :] = (hat * norm * valid).astype(bf16)
        norm_grad_ref[...] += jnp.sum(grad * hat, axis=0, keepdims=True)
        grad_gated = scale * (grad * norm) - gated * (scale * scale * scale * cross / inner_total)
        grad_mixed_ref[rows, :] = grad_gated * gate_act
        grad_gate = grad_gated * mixed * sig * (1.0 + gate * (1.0 - sig))
        grad_gate_ref[rows, :] = grad_gate.astype(bf16)

    row_loop(total, 128, part)

    def back(at):
        cols = pl.ds(at, 256)
        partial_ref[:, cols] = mm(out_rows_ref[...], weight_ref[cols, :], (1, 1)).astype(bf16)

    row_loop(weight_ref.shape[0], 256, back)
    tall = chunk_refs[0].shape[0] // 2
    for slot, chunk_ref in enumerate(chunk_refs):
        cols = pl.ds(pl.multiple_of(place_ref[slot] * tall, tall), tall)
        chunk_ref[:tall, :] = mm(turned_ref[cols, :], grad_gate_ref[...]).astype(bf16)
        chunk_ref[tall:, :] = mm(rows_ref[:, cols], out_rows_ref[...], (0, 0)).astype(bf16)


def scan_back_kernel(first_pair, lengths_ref, *refs):
    grad_mixed_ref, act_ref, state_ref, step_col_ref, step_row_ref = refs[:5]
    step_bias_ref, step_bias_col_ref, log_ref, log_col_ref, skip_ref = refs[5:10]
    grad_act_ref, grad_state_ref, step_grad_ref, sums_ref, acc_ref = refs[10:]
    total, own_width = grad_act_ref.shape
    states = state_ref.shape[1] // 2
    ends = ends_of(lengths_ref)
    sums_ref[...] = jnp.zeros(sums_ref.shape, f32)
    raw_row = step_row_ref[...]
    steps = step_sizes(
        step_col_ref[...], raw_row, step_bias_ref, step_bias_col_ref, log_ref, log_col_ref
    )
    rate_row = steps[3]
    low_half = iota((span, 128), 1) < head_width
    lower = jnp.where(iota((span, span), 0) >= iota((span, span), 1), 1.0, 0.0)
    blocks = [Block(b, ends, *steps, state_ref) for b in range(total // span)]
    first, second = blocks
    row_sums, step_rows, out_sums, in_sums = [], [], None, None
    grad_out = jnp.zeros((span, states), f32)
    grad_in = jnp.zeros((span, states), f32)
    head_of = iota((head_rows, 128), 0)
    lane_head = iota((head_rows, 128), 1) // head_width

    for b, block in enumerate(blocks):
        acc_ref[...] = jnp.zeros((span, span), f32)
        row_sum = jnp.zeros((span, 128), f32)
        step_grad = jnp.zeros((head_rows, span), f32)
        lane = iota((span, 128), 1)
        head_row = iota((head_rows, span), 0)
        for i in range(first_pair, first_pair + own_width // 128):
            cols = slice(128 * i, 128 * (i + 1))
            own_cols = slice(128 * (i - first_pair), 128 * (i - first_pair + 1))
            pair = (2 * i, 2 * i + 1)
            x = act_ref[block.rows, cols]
            x_low = x.astype(bf16)
            grad = grad_mixed_ref[block.rows, cols]
            grad_low = grad.astype(bf16)
            halves = (
                jnp.where(low_half, grad, 0.0).astype(bf16),
                jnp.where(low_half, 0.0, grad).astype(bf16),
            )
            step_wide = wide(low_half, *(block.step[:, h : h + 1] for h in pair))
            grads = []
            for h, half in zip(pair, halves):
                decay = block.decay(h)
                spread = mm(half, x_low, (1, 1)) * decay
                stepped = spread * block.step_row[h : h + 1, :]
                acc_ref[...] += stepped
                row_here = jnp.sum(stepped * block.contact, axis=1, keepdims=True)
                row_sum = jnp.where(lane == h, row_here, row_sum)
                step_here = jnp.sum(spread * block.contact, axis=0, keepdims=True)
                step_grad = jnp.where(head_row == h, step_here, step_grad)
                grads.append(mm((decay * block.contact).astype(bf16), grad_low, (0, 0)))
            grad_act = wide(low_half, *grads) * step_wide + skip_ref[:, cols] * grad
            sums_ref[2:3, own_cols] += jnp.sum(grad * x, axis=0, keepdims=True)
            picks = jnp.where(lane_head + 2 * i == head_of, 1.0, 0.0)
            if b == 0:
                reach = wide(low_half, *(second.from_edge(h) for h in pair))
                lead = (grad_mixed_ref[second.rows, cols] * reach).astype(bf16)
                edge = wide(low_half, *(block.to_edge(h) for h in pair))
                weighted = (x * step_wide * edge).astype(bf16)
                held = mm(block.inputs, weighted, (0, 0)).astype(bf16)
                held_grad = mm(second.outputs, lead, (0, 0)).astype(bf16)
                grad_out = grad_out + mm(lead, held, (1, 1))
                grad_in = grad_in + mm(weighted, held_grad, (1, 1))
                back = mm(block.inputs, held_grad) * edge
                grad_act = grad_act + back * step_wide
                ahead = mm(second.outputs, held)
                out_here = mm_exact(picks, lead.astype(f32) * ahead, (1, 1))
                in_here = mm_exact(picks, x * back, (1, 1))
                out_sums = out_here if out_sums is None else out_sums + out_here
                in_sums = in_here if in_sums is None else in_sums + in_here
            grad_act_ref[block.rows, own_cols] = grad_act
        table = (acc_ref[...] * block.mask).astype(bf16)
        grad_c = mm(table, block.inputs)
        grad_b = mm(table, block.outputs, (0, 0))
        if b == 0:
            grad_b = grad_b + grad_in
        else:
            grad_c = grad_c + grad_out
        grad_state_ref[block.rows, :states] = grad_b
        grad_state_ref[block.rows, states:] = grad_c
        row_sums.append(row_sum)
        step_rows.append(step_grad)

    rate_grads = []
    for b, block in enumerate(blocks):
        column = step_rows[b] * block.step_row
        crossing = mm_exact(row_sums[b], lower, (0, 0))[:head_rows] - mm_exact(column, lower)
        if b == 0:
            crossing = crossing + mm_exact(in_sums * block.step_row, 1.0 - lower)
        else:
            crossing = crossing + mm_exact(out_sums, lower)
        rate_grads.append(crossing)
    step_rows[0] = step_rows[0] + in_sums
    rate_grad = jnp.concatenate(rate_grads, axis=1)
    step_grad = jnp.concatenate(step_rows, axis=1) - rate_grad * jnp.exp(log_col_ref[...])
    step_grad = step_grad * sigmoid(raw_row + step_bias_col_ref[...])
    decay_sum = jnp.sum(rate_grad * rate_row, axis=1, keepdims=True)
    bias_sum = jnp.sum(step_grad, axis=1, keepdims=True)
    lane = iota((head_rows, 128), 1)
    head_sums = jnp.where(lane == 0, bias_sum, jnp.where(lane == 1, decay_sum, 0.0))
    head_sums = jnp.concatenate([head_sums] * (128 // head_rows), axis=0).T
    sums_ref[0:2, :128] = head_sums[:2, :]
    step_grad_ref[...] = step_grad


def conv_back(x_ref, mask_ref, grad_ref, held_ref, out_ref, sums_ref, own_taps, own_bias):
    total, taps = out_ref.shape[0], own_taps.shape[0]
    held_ref[total:, :] = jnp.zeros((pad, held_ref.shape[1]), f32)

    def column(cols):
        sums = [jnp.zeros((1, 128), f32) for _ in range(taps + 1)]
        for at in range(0, total, 128):
            pre, shifted = conv_pre(x_ref, mask_ref, own_taps, own_bias, at, cols, 128)
            sig = sigmoid(pre)
            grad = grad_ref[at : at + 128, cols] * sig * (1.0 + pre * (1.0 - sig))
            held_ref[at : at + 128, cols] = grad
            for s in range(taps):
                sums[taps - 1 - s] += jnp.sum(grad * shifted[s], axis=0, keepdims=True)
            sums[taps] += jnp.sum(grad, axis=0, keepdims=True)
        for t, value in enumerate(sums):
            sums_ref[t : t + 1, cols] = value
        for at in range(0, total, 128):
            back = own_taps[taps - 1 : taps, cols] * held_ref[at : at + 128, cols]
            for s in range(1, taps):
                part = held_ref[at + s : at + s + 128, cols]
                part = part * mask_ref[s - 1, at + s : at + s + 128, :]
                back = back + own_taps[taps - 1 - s : taps - s, cols] * part
            out_ref[at : at + 128, cols] = back.astype(bf16)

    column_loop(out_ref.shape[1], column)


def state_back_kernel(fast, place_ref, lengths_ref, *refs):
    state_refs, step_refs, refs = refs[0:2], refs[2:4], refs[4:]
    state_raw_ref, turned_ref, small_ref, grad_state_low_ref, step_low_ref = refs[:5]
    n_out = 4 if fast else 2
    out_refs, refs = refs[5 : 5 + n_out], refs[5 + n_out :]
    mask_ref, taps_ref, bias_ref, grad_state_ref, pre_ref, part_ref, sums_ref = refs
    taps = taps_ref.shape[0]
    taps_ref[...] = small_ref[4 : 4 + taps, :]
    bias_ref[...] = small_ref[4 + taps : 5 + taps, :]
    write_masks(mask_ref, ends_of(lengths_ref))
    grad_state_ref[...] = state_refs[0][...] + state_refs[1][...]
    step_low_ref[...] = (step_refs[0][...] + step_refs[1][...]).astype(bf16)
    sums_ref[...] = jnp.zeros(sums_ref.shape, f32)
    conv_back(
        state_raw_ref,
        mask_ref,
        grad_state_ref,
        pre_ref,
        grad_state_low_ref,
        sums_ref,
        taps_ref,
        bias_ref,
    )

    def chunk(at):
        part = turned_ref[pl.ds(at, 256), :]
        part_ref[pl.ds(at, 256), :] = mm(part, grad_state_low_ref[...]).astype(bf16)

    depth = turned_ref.shape[0]
    row_loop(depth, 256, chunk)
    if fast:
        share = depth // 32
        for member, out_ref in enumerate(out_refs):
            for c in range(8):
                at = pl.multiple_of((4 * c + place_ref[8 + member]) * share, share)
                out_ref[share * c : share * (c + 1), :] = part_ref[pl.ds(at, share), :]
            out_ref[8 * share :, :] = sums_ref[...].astype(bf16)
    else:
        out_refs[0][...] = part_ref[...]
        out_refs[1][...] = sums_ref[...]


def inner_back_kernel(lengths_ref, *refs):
    act_refs, head_refs, refs = refs[0:2], refs[2:4], refs[4:]
    raw_ref, norm_grad_ref, taps_ref, bias_ref, grad_inner_ref, sums_ref = refs[:6]
    mask_ref, grad_act_ref, pre_ref = refs[6:]
    half = grad_inner_ref.shape[1] // 2
    write_masks(mask_ref, ends_of(lengths_ref))
    grad_act_ref[:, :half] = act_refs[0][...]
    grad_act_ref[:, half:] = act_refs[1][...]
    sums_ref[...] = jnp.zeros(sums_ref.shape, f32)
    heads = head_refs[0][:2, :128] + head_refs[1][:2, :128]
    sums_ref[5:6, :] = norm_grad_ref[...]
    sums_ref[6:7, :half] = head_refs[0][2:3, :]
    sums_ref[6:7, half:] = head_refs[1][2:3, :]
    sums_ref[9:10, half : half + 128] = heads[0:1, :]
    sums_ref[9:10, half + 128 :] = heads[1:2, :]
    conv_back(
        raw_ref,
        mask_ref,
        grad_act_ref,
        pre_ref,
        grad_inner_ref,
        sums_ref,
        taps_ref,
        bias_ref,
    )


def message_kernel(grad_inner_ref, step_low_ref, turned_ref, msg_ref):
    chunks = msg_ref.shape[0]
    tall = turned_ref.shape[0] // chunks
    step_low = step_low_ref[...]

    def chunk(c, carry):
        part = turned_ref[pl.ds(pl.multiple_of(c * tall, tall), tall), :]
        msg_ref[c, :tall, :] = mm(part, grad_inner_ref[...]).astype(bf16)
        msg_ref[c, tall:, :tall] = mm(step_low, part, (1, 1)).astype(bf16)
        msg_ref[c, tall:, tall:] = jnp.zeros((head_rows, msg_ref.shape[2] - tall), bf16)
        return carry

    lax.fori_loop(0, chunks, chunk, 0)


def chunk_kernel(slots, n_got, place_ref, *refs):
    grad_inner_ref, step_low_ref, sums_ref = refs[:3]
    state_refs, turned_refs, got_refs = refs[3:7], refs[7:9], refs[9 : 9 + n_got]
    out_refs = refs[9 + n_got :]
    states = state_refs[0].shape[1]
    share = (state_refs[0].shape[0] - 16) // 8

    def state_rows(low, tall):
        return sum(ref[pl.ds(low, tall), :].astype(f32) for ref in state_refs)

    shared = state_rows(8 * share, 16)
    sums = [
        sums_ref[:7, :],
        jnp.concatenate([shared[0:1, :], shared[1:2, :]], axis=1),
        jnp.concatenate([shared[2:3, :], shared[3:4, :]], axis=1),
        jnp.concatenate([shared[4:5, :], sums_ref[9:10, states:]], axis=1),
    ]
    for n, (slot, out_ref) in enumerate(zip(slots, out_refs)):
        index = place_ref[slot]
        part = turned_refs[n][...]
        step = mm(step_low_ref[...], part, (1, 1))
        step = [
            jnp.concatenate([step[4 * k + i : 4 * k + i + 1, :] for i in range(4)], axis=1)
            for k in range(2)
        ]
        state = state_rows(pl.multiple_of(index * share, share), share)
        value = jnp.concatenate(
            [
                mm(part, grad_inner_ref[...]),
                jnp.concatenate([state[:16, :], state[16:, :]], axis=1),
                *sums,
                *step,
                jnp.zeros((4, 2 * states), f32),
            ],
            axis=0,
        )
        tail = value.shape[0] - 16
        main, sums_here = value[:tail, :], value[tail:, :]
        if n < n_got:
            got = got_refs[n]
            main = main + got[:tail, :].astype(f32)
            sums_here = sums_here + got[tail : tail + 16, :].astype(f32)
            sums_here = sums_here + got[tail + 16 :, :].astype(f32)
        out_ref[:tail, :] = main.astype(out_ref.dtype)
        high = sums_here.astype(bf16)
        out_ref[tail : tail + 16, :] = high.astype(out_ref.dtype)
        out_ref[tail + 16 :, :] = (sums_here - high.astype(f32)).astype(out_ref.dtype)


def project_back_kernel(fast, place_ref, *refs):
    grad_refs, step_low_ref, weight_refs, step_weight_ref = refs[:3], refs[3], refs[4:7], refs[7]
    out_refs, held_refs, step_ref = refs[8:10], refs[10:13], refs[13]
    for n, member in enumerate((0, 2, 1, 3)):
        at = pl.multiple_of(place_ref[8 + member] * 128, 128) if fast else 128 * member
        for held_ref, grad_ref in zip(held_refs, grad_refs):
            held_ref[128 * n : 128 * (n + 1), :] = grad_ref[pl.ds(at, 128), :]
        step_ref[:, 128 * n : 128 * (n + 1)] = step_low_ref[:, pl.ds(at, 128)]

    def back(at):
        cols = pl.ds(at, 256)
        grad = mm(step_ref[...], step_weight_ref[:, cols], (0, 0))
        for held_ref, weight_ref in zip(held_refs, weight_refs):
            grad = grad + mm(held_ref[...], weight_ref[cols, :], (1, 1))
        grad = grad.astype(bf16)
        for n in range(4):
            out_refs[n // 2][n % 2, :, cols] = grad[128 * n : 128 * (n + 1), :]

    row_loop(step_weight_ref.shape[1], 256, back)


def prepare_kernel(place_ref, gain_ref, taps_ref, bias_ref, state_ref, shared_ref):
    owner = place_ref[0]
    share, states = state_ref.shape
    shared_ref[:share, :] = state_ref[...]

    def placed(value, at):
        width = value.shape[1]
        pick = iota((width, states), 1) - at == iota((width, states), 0)
        return mm(value, jnp.where(pick, 1.0, 0.0).astype(bf16))

    start = owner * gain_ref.shape[1]
    small = jnp.concatenate(
        [placed(gain_ref[...], start - states * i) for i in range(4)]
        + [placed(taps_ref[...], owner * taps_ref.shape[1])]
        + [placed(bias_ref[...], owner * bias_ref.shape[1])]
        + [jnp.zeros((7, states), f32)],
        axis=0,
    )
    shared_ref[share:, :] = small.astype(bf16)


def prepare_late_kernel(input_ref, out_ref, late_ref):
    depth_part = input_ref.shape[0]
    late_ref[:depth_part, :] = input_ref[:, 0, :]
    late_ref[depth_part:, :] = out_ref[...].astype(f32).T.astype(bf16)


def params_kernel(*refs):
    taps_ref, bias_ref, step_bias_ref, log_ref, skip_ref, norm_ref = refs[:6]
    outs = refs[6:]
    heads = step_bias_ref.shape[1]
    pick = jnp.where(iota((heads, head_rows), 0) == iota((heads, head_rows), 1), 1.0, 0.0)
    square = iota((head_rows, head_rows), 0) == iota((head_rows, head_rows), 1)

    def both(value_ref, row_ref, col_ref):
        row = mm_exact(value_ref[...].astype(f32), pick)
        row_ref[...] = row
        col_ref[...] = jnp.sum(jnp.where(square, row, 0.0), axis=1, keepdims=True)

    outs[0][...] = taps_ref[...].astype(f32)
    outs[1][...] = bias_ref[...].astype(f32)
    both(step_bias_ref, outs[2], outs[3])
    both(log_ref, outs[4], outs[5])
    channels = norm_ref.shape[1]
    own = iota((heads, channels), 1) // (channels // heads) == iota((heads, channels), 0)
    outs[6][...] = mm_exact(skip_ref[...].astype(f32), jnp.where(own, 1.0, 0.0))
    outs[7][...] = norm_ref[...].astype(f32)


def assemble_kernel(input_ref, step_ref, *refs):
    shared_refs, msg_ref = refs[:4], refs[4]
    depth_part, _, channels = input_ref.shape
    share = shared_refs[0].shape[0] - 16
    tail = depth_part + 2 * share
    msg_ref[:depth_part, :] = input_ref[:, 1, :]
    for member, ref in enumerate(shared_refs):
        high, low = depth_part + share * (member // 2), 256 * (member % 2)
        msg_ref[high : high + share, low : low + 256] = ref[:share, :]
    small = sum(ref[share:, :].astype(f32) for ref in shared_refs)
    msg_ref[tail:, :256] = small.astype(bf16)
    msg_ref[tail:, 256:384] = step_ref[...]
    msg_ref[tail:, 384:] = jnp.zeros((16, channels - 384), bf16)


def call(kernel, micros, scalars, arrays, outs, scratch):
    smem = pl.BlockSpec(memory_space=pltpu.SMEM)
    vmem = pl.BlockSpec(memory_space=pltpu.VMEM)
    return pl.pallas_call(
        kernel,
        out_shape=[jax.ShapeDtypeStruct(shape, kind) for shape, kind in outs],
        in_specs=[smem] * len(scalars) + [vmem] * len(arrays),
        out_specs=[vmem] * len(outs),
        scratch_shapes=[pltpu.VMEM(shape, kind) for shape, kind in scratch],
        compiler_params=pltpu.CompilerParams(vmem_limit_bytes=vmem_bytes),
        cost_estimate=pl.CostEstimate(
            flops=int(micros * 1.1e9), bytes_accessed=1 << 20, transcendentals=0
        ),
    )(*scalars, *arrays)


def ring_ok(n_dp, n_tensor):
    return n_dp == 8 and n_tensor == 4


ring_order = (0, 2, 4, 6, 7, 5, 3, 1)


def ring_place(index):
    high, low = index // 2, index % 2
    return jnp.where(low == 0, high, 7 - high)


def ring_index(place):
    place = lax.rem(place + 16, 8)
    return jnp.where(place < 4, 2 * place, 2 * (7 - place) + 1)


def ring_send(value, forward):
    pairs = []
    for place in range(8):
        other = (place + (1 if forward else 7)) % 8
        pairs.append((ring_order[place], ring_order[other]))
    return lax.ppermute(value, "dp", pairs)


def ring_gather(value):
    me = ring_place(lax.axis_index("dp"))
    pieces = [(value, ring_index(me))]
    ahead, back = value, value
    for step in range(1, 5):
        ahead = ring_send(ahead, True)
        pieces.append((ahead, ring_index(me - step)))
        if step < 4:
            back = ring_send(back, False)
            pieces.append((back, ring_index(me + step)))
    return pieces


def dp_swap(value, bit):
    return lax.ppermute(value, "dp", [(i, i ^ bit) for i in range(8)])


def ring_step(held):
    return ring_send(held[0], True), ring_send(held[1], False)


def add_low(got, own):
    return (got.astype(f32) + own.astype(f32)).astype(bf16)


def ordered(first, then):
    return lax.optimization_barrier((first, then))


def tensor_gather(value):
    near = tensor_swap(value, 1)
    far = tensor_swap(value, 2)
    return [value, near, far, tensor_swap(far, 1)]


def tensor_direct(value):
    return [value] + [tensor_swap(value, bit) for bit in range(1, 4)]


def tensor_sum(value, depth):
    parts = value.reshape(4, -1, depth)
    parts = lax.all_to_all(parts, "tensor", 0, 0, tiled=True)
    return jnp.sum(parts.astype(f32), axis=0)


def tensor_swap(value, bit):
    return lax.ppermute(value, "tensor", [(i, i ^ bit) for i in range(4)])


def body(
    tokens,
    lengths,
    cotangent,
    pre_gain,
    input_weight,
    step_weight,
    state_weight,
    conv_inner,
    conv_inner_bias,
    conv_state,
    conv_state_bias,
    step_bias,
    decay_log,
    skip_gain,
    norm_gain,
    output_weight,
):
    n_dp, n_tensor = lax.axis_size("dp"), lax.axis_size("tensor")
    fast = ring_ok(n_dp, n_tensor)
    owners = n_dp * n_tensor
    me = lax.axis_index("tensor")
    owner = lax.axis_index("dp") * n_tensor + me
    own_rows, depth = tokens.shape
    total = own_rows * n_tensor
    states = state_weight.shape[1]
    heads = step_weight.shape[1]
    share = state_weight.shape[0]
    taps = conv_state.shape[0]
    channels = input_weight.shape[2]
    inner_total = channels * n_tensor

    owner_place = jnp.stack([owner, owners]).astype(jnp.int32)
    (shared,) = call(
        prepare_kernel,
        1,
        [owner_place],
        [pre_gain[None, :], conv_state, conv_state_bias[None, :], state_weight],
        [((share + 16, states), bf16)],
        [],
    )
    step_rows = jnp.pad(step_weight.T, ((0, head_rows - heads), (0, 0)))
    shared, out_shard = ordered(shared, output_weight)
    (late,) = call(
        prepare_late_kernel,
        2,
        [],
        [input_weight, out_shard],
        [((input_weight.shape[0] + output_weight.shape[1], channels), bf16)],
        [],
    )
    params = call(
        params_kernel,
        1,
        [],
        [
            conv_inner,
            conv_inner_bias[None, :],
            step_bias[None, :],
            decay_log[None, :],
            skip_gain[None, :],
            norm_gain[None, :],
        ],
        [
            ((taps, channels), f32),
            ((1, channels), f32),
            ((1, head_rows), f32),
            ((head_rows, 1), f32),
            ((1, head_rows), f32),
            ((head_rows, 1), f32),
            ((1, channels), f32),
            ((1, channels), f32),
        ],
        [],
    )
    params = list(params)
    conv_params, head_params, norm_row = params[:2], params[2:7], params[7]
    if fast:
        shared = tensor_direct(shared)
        late_one = ring_step((late, late))
        (msg,) = call(
            assemble_kernel,
            1,
            [],
            [input_weight, step_rows, *shared],
            [((input_weight.shape[0] + 2 * share + 16, channels), bf16)],
            [],
        )
        late_one, msg = ordered(late_one, msg)
        msg = ring_gather(msg)
        weight_pieces = [piece for piece, _ in msg]
        late_two = ring_step(late_one)
        late_three = ring_step(late_two)
        late_pieces = [late, *late_one, *late_two, *late_three, ring_send(late_three[0], True)]
        own_rows_both = jnp.concatenate([tokens, cotangent], axis=0)
        row_pieces = tensor_gather(ordered(shared, own_rows_both)[1])
        grad_pieces = row_pieces
        place = jnp.stack([index for _, index in msg] + [me, me ^ 1, me ^ 2, me ^ 3])
    else:
        row_pieces = [lax.all_gather(tokens, "tensor", axis=0, tiled=True)]
        grad_pieces = [lax.all_gather(cotangent, "tensor", axis=0, tiled=True)]
        gate_weight, inner_weight = late[: input_weight.shape[0]], input_weight[:, 1]
        weight_pieces = [
            lax.all_gather(inner_weight, "dp", axis=0, tiled=True),
            lax.all_gather(state_weight, ("dp", "tensor"), axis=0, tiled=True),
            lax.all_gather(step_rows, "dp", axis=1, tiled=True),
            lax.psum(shared[share:], ("dp", "tensor")),
        ]
        late_pieces = [
            lax.all_gather(gate_weight, "dp", axis=0, tiled=True),
            lax.all_gather(late[input_weight.shape[0] :], "dp", axis=0, tiled=True),
        ]
        place = jnp.concatenate([jnp.arange(8), jnp.arange(4)])
    place = place.astype(jnp.int32)

    masks = ((taps - 1, total + pad, 128), f32)
    state_taps = [((taps, states), f32), ((1, states), f32)]
    (
        normed,
        turned,
        inner_full,
        state_full,
        step_full,
        small_full,
        raw,
        state_raw,
        step_col,
        step_row,
        act,
        state_act,
        mixed,
    ) = call(
        functools.partial(forward_kernel, fast),
        11,
        [place, lengths],
        row_pieces + weight_pieces + conv_params + head_params,
        [
            ((total, depth), bf16),
            ((depth, total), bf16),
            ((depth, channels), bf16),
            ((depth, states), bf16),
            ((head_rows, depth), bf16),
            ((16, states), f32),
            ((total + pad, channels), f32),
            ((total + pad, states), f32),
            ((total, head_rows), f32),
            ((head_rows, total), f32),
            ((total, channels), f32),
            ((total, states), f32),
            ((total, channels), f32),
        ],
        [masks] + state_taps,
    )
    grad_rows, gate_full, output_full, gate, grad_normalized, sums = call(
        functools.partial(grad_in_kernel, fast),
        5,
        [place, lengths],
        grad_pieces + late_pieces + [normed, mixed, norm_row],
        [
            ((total, depth), bf16),
            ((depth, channels), bf16),
            ((depth, channels), bf16),
            ((total, channels), f32),
            ((total, channels), f32),
            ((8, total), f32),
        ],
        [((total, 128), f32)],
    )
    if fast:
        sums = tensor_direct(sums)
    else:
        sums = [lax.psum(sums, "tensor")]
    chunks = 8
    tall = depth // chunks
    norm_outs = call(
        functools.partial(norm_kernel, inner_total),
        9,
        [place, lengths],
        [*sums, gate, mixed, grad_normalized, norm_row, output_full, grad_rows, turned],
        [((2 * tall, channels), bf16)] * chunks
        + [
            ((total, depth), bf16),
            ((total, channels), bf16),
            ((total, channels), f32),
            ((1, channels), f32),
        ],
        [((total, 128), f32), ((total, channels), bf16)],
    )
    gate_chunks = norm_outs[:chunks]
    partial_out, grad_gate, grad_mixed, norm_grad = norm_outs[chunks:]

    def scan_back(first_pair, grad):
        return call(
            functools.partial(scan_back_kernel, first_pair),
            6,
            [lengths],
            [grad, act, state_act, step_col, step_row] + head_params,
            [
                ((total, channels // 2), f32),
                ((total, states), f32),
                ((head_rows, total), f32),
                ((8, channels // 2), f32),
            ],
            [((span, span), f32)],
        )

    if fast:
        got = ring_step((gate_chunks[7], gate_chunks[5]))
        held = add_low(got[0], gate_chunks[6]), add_low(got[1], gate_chunks[3])
    first = scan_back(0, grad_mixed)
    if fast:
        held, grad_mixed = ordered(held, grad_mixed)
        got = ring_step(held)
        held = add_low(got[0], gate_chunks[4]), add_low(got[1], gate_chunks[1])
    second = scan_back(channels // 256, grad_mixed)
    if fast:
        held, state_raw = ordered(held, state_raw)
        got = ring_step(held)
        held, last = add_low(got[0], gate_chunks[2]), got[1]
    share_rows = depth // 4 + 16
    state_outs = call(
        functools.partial(state_back_kernel, fast),
        4,
        [place, lengths],
        [first[1], second[1], first[2], second[2], state_raw, turned, small_full],
        [((total, states), bf16), ((head_rows, total), bf16)]
        + (
            [((share_rows, states), bf16)] * 4
            if fast
            else [((depth, states), bf16), ((16, states), f32)]
        ),
        [
            masks,
            *state_taps,
            ((total, states), f32),
            ((total + pad, states), f32),
            ((depth, states), bf16),
            ((16, states), f32),
        ],
    )
    grad_state_low, step_low = state_outs[:2]
    state_parts = state_outs[2:]
    if fast:
        state_parts = [state_parts[0]] + [tensor_swap(state_parts[i], i) for i in range(1, 4)]
    if fast:
        (held, last), raw = ordered((held, last), raw)
        gate_out = gate_chunks[0].astype(f32) + last.astype(f32)
        gate_out = gate_out + ring_send(held, True).astype(f32)
    grad_inner, sums = call(
        inner_back_kernel,
        6,
        [lengths],
        [first[0], second[0], first[3], second[3], raw, norm_grad] + conv_params,
        [((total, channels), bf16), ((16, channels), f32)],
        [masks, ((total, channels), f32), ((total + pad, channels), f32)],
    )
    if fast:
        mixed_rows = tensor_sum(partial_out, depth)
        (gate_out, mixed_rows), grad_inner = ordered((gate_out, mixed_rows), grad_inner)

    def project_back():
        return call(
            functools.partial(project_back_kernel, fast),
            6,
            [place],
            [
                grad_gate,
                grad_inner,
                grad_state_low,
                step_low,
                gate_full,
                inner_full,
                state_full,
                step_full,
            ],
            [((2, 128, depth), bf16)] * 2,
            [
                ((total, channels), bf16),
                ((total, channels), bf16),
                ((total, states), bf16),
                ((head_rows, total), bf16),
            ],
        )

    def chunk_pair(slots, got, after=None, last=bf16):
        grad = grad_inner if after is None else ordered(after, grad_inner)[1]
        arrays = [grad, step_low, sums, *state_parts, turned, turned, *got]

        def whole(array):
            return pl.BlockSpec(array.shape, lambda i, place: (0, 0))

        def block(slot):
            return pl.BlockSpec((tall, total), lambda i, place: (place[slot], 0))

        specs = [whole(array) for array in arrays]
        specs[7:9] = [block(slot) for slot in slots]
        out = pl.BlockSpec((tall + 48, channels), lambda i, place: (0, 0))
        return pl.pallas_call(
            functools.partial(chunk_kernel, slots, len(got)),
            grid_spec=pltpu.PrefetchScalarGridSpec(
                num_scalar_prefetch=1, grid=(1,), in_specs=specs, out_specs=[out, out]
            ),
            out_shape=[
                jax.ShapeDtypeStruct((tall + 48, channels), kind) for kind in (bf16, last)
            ],
            compiler_params=pltpu.CompilerParams(vmem_limit_bytes=vmem_bytes),
            cost_estimate=pl.CostEstimate(
                flops=2_000_000_000, bytes_accessed=1 << 20, transcendentals=0
            ),
        )(place, *arrays)

    if fast:
        got = ring_step(chunk_pair((7, 5), ()))
        keep_rows, give_rows = project_back()
        got = ring_step(chunk_pair((6, 3), got, give_rows))
        got = ring_step(chunk_pair((4, 1), got))
        held, inner_own = chunk_pair((2, 0), got, last=f32)
        inner_out = inner_own + ring_send(held, True).astype(f32)
    else:
        (inner_msg,) = call(
            message_kernel,
            5,
            [],
            [grad_inner, step_low, turned],
            [((chunks, tall + head_rows, channels), bf16)],
            [],
        )
        keep_rows, give_rows = project_back()

    token_float = tokens.astype(f32)
    gain_full = small_full[: depth // states].reshape(1, depth)

    if fast:
        got = tensor_swap(give_rows, 1)
        far = tensor_swap(add_low(keep_rows[1], got[1]), 2)
        grad_local = keep_rows[0].astype(f32) + got[0].astype(f32) + far.astype(f32)
        gate_grad, output_grad = gate_out[:tall], gate_out[tall:].T
        inner_grad = inner_out[:tall]
        state_grad = inner_out[tall : tall + 16]
        state_grad = jnp.concatenate([state_grad[:, :states], state_grad[:, states:]], axis=0)
        sums = inner_out[tall + 16 : tall + 32] + inner_out[tall + 32 :]
        step_grad = sums[10:12].reshape(heads, tall).T
        width = states // owners
        conv_state_sum = lax.dynamic_slice(
            sums[7:10].reshape(6, states), (0, owner * width), (taps + 1, width)
        )
        conv_state_grad, conv_state_bias_grad = conv_state_sum[:taps], conv_state_sum[taps]
    else:
        state_part, state_sums = state_parts
        state_grad = lax.psum_scatter(
            state_part.astype(f32), ("dp", "tensor"), scatter_dimension=0, tiled=True
        )
        conv_state_sum = lax.psum_scatter(
            state_sums[: taps + 1], ("dp", "tensor"), scatter_dimension=1, tiled=True
        )
        conv_state_grad, conv_state_bias_grad = conv_state_sum[:taps], conv_state_sum[taps]
        grad_normed = jnp.stack([keep_rows, give_rows], axis=1).reshape(total, depth)
        mixed_rows, grad_local = (
            lax.psum_scatter(part, "tensor", scatter_dimension=0, tiled=True).astype(f32)
            for part in (partial_out, grad_normed)
        )
        both, inner_float = jnp.stack(gate_chunks).astype(f32), inner_msg.astype(f32)
        gate_grad, output_grad, inner_grad = (
            lax.psum_scatter(part.reshape(depth, channels), "dp", scatter_dimension=0, tiled=True)
            for part in (both[:, :tall], both[:, tall:], inner_float[:, :tall])
        )
        output_grad = output_grad.T
        step_part = inner_float[:, tall : tall + heads, :tall].transpose(0, 2, 1)
        step_part = step_part.reshape(depth, heads)
        step_grad = lax.psum_scatter(step_part, "dp", scatter_dimension=0, tiled=True)
        sums = lax.psum(sums, "dp")
    input_grad = jnp.stack([gate_grad, inner_grad], axis=1)
    own_gain = jnp.sum(input_weight.astype(f32) * input_grad, axis=(1, 2))
    own_gain = own_gain + jnp.sum(step_weight.astype(f32) * step_grad, axis=1)
    state_gain = jnp.sum(state_weight.astype(f32) * state_grad, axis=1)
    if fast:
        own_gain = sum(tensor_direct(own_gain))
        own_gain = lax.dynamic_slice(own_gain, (me * share,), (share,))
    else:
        own_gain = lax.psum_scatter(own_gain, "tensor", scatter_dimension=0, tiled=True)
    pre_gain_grad = (own_gain + state_gain) / pre_gain.astype(f32)
    block_out = (token_float + mixed_rows).astype(bf16)
    scale = lax.rsqrt(jnp.mean(token_float * token_float, axis=1, keepdims=True) + epsilon)
    grad_scaled = grad_local * gain_full
    along = jnp.sum(grad_scaled * token_float, axis=1, keepdims=True) / depth
    tokens_grad = (
        scale * grad_scaled
        - token_float * (scale * scale * scale * along)
        + cotangent.astype(f32)
    )
    skip_grad = sums[6].reshape(heads, -1).sum(axis=1)
    return (
        block_out,
        tokens_grad,
        pre_gain_grad,
        input_grad,
        step_grad,
        state_grad,
        sums[:taps],
        sums[taps],
        conv_state_grad,
        conv_state_bias_grad,
        sums[9, states : states + heads],
        sums[9, states + 128 : states + 128 + heads],
        skip_grad,
        sums[5],
        output_grad,
    )


def solution(mesh):
    in_specs = (
        P(("dp", "tensor"), None),
        P("dp", None),
        P(("dp", "tensor"), None),
        P(("dp", "tensor")),
        P("dp", None, "tensor"),
        P("dp", "tensor"),
        P(("dp", "tensor"), None),
        P(None, "tensor"),
        P("tensor"),
        P(None, ("dp", "tensor")),
        P(("dp", "tensor")),
        P("tensor"),
        P("tensor"),
        P("tensor"),
        P("tensor"),
        P("tensor", "dp"),
    )
    out_specs = (
        P(("dp", "tensor"), None),
        P(("dp", "tensor"), None),
        P(("dp", "tensor")),
        P("dp", None, "tensor"),
        P("dp", "tensor"),
        P(("dp", "tensor"), None),
        P(None, "tensor"),
        P("tensor"),
        P(None, ("dp", "tensor")),
        P(("dp", "tensor")),
        P("tensor"),
        P("tensor"),
        P("tensor"),
        P("tensor"),
        P("tensor", "dp"),
    )
    return jax.shard_map(body, mesh=mesh, in_specs=in_specs, out_specs=out_specs, check_vma=False)
```

```python
import functools

import jax
import jax.numpy as jnp
from jax import lax
from jax.experimental import pallas as pl
from jax.experimental.pallas import tpu as pltpu
from jax.sharding import PartitionSpec as P

epsilon = 1e-05
highest = lax.Precision.HIGHEST
f32 = jnp.float32
bf16 = jnp.bfloat16
span = 256
pad = 8
head_rows = 16
head_width = 64
vmem_bytes = 63 * 1024 * 1024


def mm(a, b, over=(1, 0)):
    dims = (((over[0],), (over[1],)), ((), ()))
    return lax.dot_general(a, b, dims, preferred_element_type=f32)


def mm_exact(a, b, over=(1, 0)):
    dims = (((over[0],), (over[1],)), ((), ()))
    return lax.dot_general(a, b, dims, preferred_element_type=f32, precision=highest)


def sigmoid(v):
    return 1.0 / (1.0 + jnp.exp(-v))


def ends_of(lengths_ref):
    ends, total = [], None
    for slot in range(lengths_ref.shape[1]):
        here = lengths_ref[0, slot]
        total = here if total is None else total + here
        ends.append(total)
    return ends


def segment_of(places, ends):
    segment = jnp.zeros(places.shape, jnp.int32)
    for end in ends:
        segment = segment + jnp.where(places >= end, 1, 0)
    return segment


def iota(shape, dim):
    return lax.broadcasted_iota(jnp.int32, shape, dim)


def write_masks(mask_ref, ends):
    rows = mask_ref.shape[1] - pad
    places = iota((rows, 128), 0)
    segment = segment_of(places, ends)
    for shift in range(1, mask_ref.shape[0] + 1):
        same = (segment_of(places - shift, ends) == segment) & (places >= shift)
        mask_ref[shift - 1, :rows, :] = jnp.where(same, 1.0, 0.0)
        mask_ref[shift - 1, rows:, :] = jnp.zeros((pad, 128), f32)


def shifted_rows(x_ref, mask_ref, at, cols, shift, tall):
    part = x_ref[pad + at - shift : pad + at - shift + tall, cols]
    if shift == 0:
        return part
    return part * mask_ref[shift - 1, at : at + tall, :]


def conv_pre(x_ref, mask_ref, taps_ref, bias_ref, at, cols, tall):
    taps = taps_ref.shape[0]
    shifted = [shifted_rows(x_ref, mask_ref, at, cols, s, tall) for s in range(taps)]
    total = bias_ref[:, cols]
    for s in range(taps):
        total = total + taps_ref[taps - 1 - s : taps - s, cols] * shifted[s]
    return total, shifted


def column_loop(width, step):
    def one(c, carry):
        step(pl.ds(pl.multiple_of(c * 128, 128), 128))
        return carry

    lax.fori_loop(0, width // 128, one, 0)


def row_loop(rows, tall, step):
    def one(r, carry):
        step(pl.multiple_of(r * tall, tall))
        return carry

    lax.fori_loop(0, rows // tall, one, 0)


class Block:
    def __init__(self, b, ends, step_col, step_row, rate_col, rate_row, state_ref):
        low, top = b * span, (b + 1) * span
        states = state_ref.shape[1] // 2
        lower = jnp.where(iota((span, span), 0) >= iota((span, span), 1), 1.0, 0.0)
        self.rows = slice(low, top)
        self.step = step_col[low:top]
        self.step_row = step_row[:, low:top]
        self.cum = mm_exact(lower, rate_col[low:top])
        self.cum_row = mm_exact(rate_row[:, low:top], lower, (1, 1))
        self.inputs = state_ref[low:top, :states].astype(bf16)
        self.outputs = state_ref[low:top, states:].astype(bf16)
        segment = segment_of(iota((span, 1), 0) + low, ends)
        segment_row = segment_of(iota((1, span), 1) + low, ends)
        edge = sum(jnp.where(span - 1 >= end, 1, 0) for end in ends)
        self.near_edge = jnp.where(segment == edge, 1.0, 0.0)
        self.mask = jnp.where(segment == segment_row, lower, 0.0)
        self.contact = mm(self.outputs, self.inputs, (1, 1)) * self.mask

    def decay(self, h):
        gap = self.cum[:, h : h + 1] - self.cum_row[h : h + 1, :]
        return jnp.exp(jnp.minimum(gap, 0.0))

    def from_edge(self, h):
        return jnp.exp(self.cum[:, h : h + 1]) * self.near_edge

    def to_edge(self, h):
        last = self.cum[span - 1 : span, h : h + 1]
        return jnp.exp(last - self.cum[:, h : h + 1]) * self.near_edge


def wide(low_half, left, right):
    return jnp.where(low_half, left, right)


def step_sizes(raw_col, raw_row, bias_ref, bias_col_ref, log_ref, log_col_ref):
    def soft(v):
        return jnp.maximum(v, 0.0) + jnp.log1p(jnp.exp(-jnp.abs(v)))

    step_col = soft(raw_col + bias_ref[...])
    step_row = soft(raw_row + bias_col_ref[...])
    rate_col = -step_col * jnp.exp(log_ref[...])
    rate_row = -step_row * jnp.exp(log_col_ref[...])
    return step_col, step_row, rate_col, rate_row


def forward_kernel(fast, place_ref, lengths_ref, *refs):
    n_msg = 8 if fast else 4
    n_rows = 4 if fast else 1
    row_refs, msg_refs, refs = refs[:n_rows], refs[n_rows : n_rows + n_msg], refs[n_rows + n_msg :]
    (taps_ref, bias_ref, step_bias_ref, step_bias_col_ref, log_ref, log_col_ref, skip_ref) = refs[:7]
    (
        normed_ref,
        turned_ref,
        weight_ref,
        state_weight_ref,
        step_weight_ref,
        small_ref,
        raw_ref,
        state_raw_ref,
        step_col_ref,
        step_row_ref,
        act_ref,
        state_ref,
        mixed_ref,
    ) = refs[7:20]
    mask_ref, state_taps_ref, state_bias_ref = refs[20:]
    total, channels = act_ref.shape
    ends = ends_of(lengths_ref)

    if fast:
        depth_part = 128
        small = jnp.zeros(small_ref.shape, f32)
        share = state_weight_ref.shape[0] // 32
        for slot in range(8):
            msg = msg_refs[slot]
            index = place_ref[slot]
            at = pl.multiple_of(index * depth_part, depth_part)
            weight_ref[pl.ds(at, depth_part), :] = msg[:depth_part, :]
            for member in range(4):
                inner = pl.multiple_of(at + place_ref[8 + member] * share, share)
                high, low = depth_part + share * (member // 2), 256 * (member % 2)
                state_weight_ref[pl.ds(inner, share), :] = msg[
                    high : high + share, low : low + 256
                ]
            tail = depth_part + 2 * share
            small = small + msg[tail : tail + 16, :256].astype(f32)
            step_weight_ref[:, pl.ds(at, depth_part)] = msg[tail : tail + 16, 256:384]
        small_ref[...] = small
    else:
        weight_ref[...] = msg_refs[0][...]
        state_weight_ref[...] = msg_refs[1][...]
        step_weight_ref[...] = msg_refs[2][...]
        small_ref[...] = msg_refs[3][...].astype(f32)
    gain = jnp.concatenate([small_ref[i : i + 1, :] for i in range(4)], axis=1)
    taps = taps_ref.shape[0]
    state_taps_ref[...] = small_ref[4 : 4 + taps, :]
    state_bias_ref[...] = small_ref[4 + taps : 5 + taps, :]

    tall = total // n_rows
    for member in range(n_rows):
        at = pl.multiple_of(place_ref[8 + member] * tall, tall) if fast else 0
        value = row_refs[member][:tall, :].astype(f32)
        scale = lax.rsqrt(jnp.mean(value * value, axis=1, keepdims=True) + epsilon)
        normed = (value * scale * gain).astype(bf16)
        normed_ref[pl.ds(at, tall), :] = normed
        turned_ref[:, pl.ds(at, tall)] = normed.astype(f32).T.astype(bf16)

    raw_ref[:pad, :] = jnp.zeros((pad, channels), f32)
    state_raw_ref[:pad, :] = jnp.zeros((pad, state_raw_ref.shape[1]), f32)

    def project(at):
        part = normed_ref[pl.ds(at, 128), :]
        raw_ref[pl.ds(at + pad, 128), :] = mm(part, weight_ref[...])
        state_raw_ref[pl.ds(at + pad, 128), :] = mm(part, state_weight_ref[...])
        step_col_ref[pl.ds(at, 128), :] = mm(part, step_weight_ref[...], (1, 1))

    row_loop(total, 128, project)
    step_row_ref[...] = mm(step_weight_ref[...], normed_ref[...], (1, 1))

    write_masks(mask_ref, ends)

    def activate(x_ref, out_ref, own_taps, own_bias):
        def column(cols):
            for at in range(0, total, 128):
                pre, _ = conv_pre(x_ref, mask_ref, own_taps, own_bias, at, cols, 128)
                out_ref[at : at + 128, cols] = pre * sigmoid(pre)

        column_loop(out_ref.shape[1], column)

    activate(raw_ref, act_ref, taps_ref, bias_ref)
    activate(state_raw_ref, state_ref, state_taps_ref, state_bias_ref)

    steps = step_sizes(
        step_col_ref[...],
        step_row_ref[...],
        step_bias_ref,
        step_bias_col_ref,
        log_ref,
        log_col_ref,
    )
    low_half = iota((span, 128), 1) < head_width
    held = []
    for b in range(total // span):
        block = Block(b, ends, *steps, state_ref)
        for i in range(channels // 128):
            cols = slice(128 * i, 128 * (i + 1))
            pair = (2 * i, 2 * i + 1)
            x = act_ref[block.rows, cols]
            step_wide = wide(low_half, *(block.step[:, h : h + 1] for h in pair))
            x_step = (x * step_wide).astype(bf16)
            y = [mm((block.decay(h) * block.contact).astype(bf16), x_step) for h in pair]
            y = wide(low_half, *y) + skip_ref[:, cols] * x
            if b == 0:
                reach = wide(low_half, *(block.to_edge(h) for h in pair))
                weighted = (x * step_wide * reach).astype(bf16)
                held.append(mm(block.inputs, weighted, (0, 0)).astype(bf16))
            else:
                reach = wide(low_half, *(block.from_edge(h) for h in pair))
                y = y + reach * mm(block.outputs, held[i])
            mixed_ref[block.rows, cols] = y


def grad_in_kernel(fast, place_ref, lengths_ref, *refs):
    n_rows = 4 if fast else 1
    n_msg = 8 if fast else 2
    row_refs, msg_refs, refs = refs[:n_rows], refs[n_rows : n_rows + n_msg], refs[n_rows + n_msg :]
    normed_ref, mixed_ref, norm_ref = refs[:3]
    rows_ref, gate_weight_ref, out_weight_ref, gate_ref, grad_ref, sums_ref, wide_ref = refs[3:]
    total = rows_ref.shape[0]
    ends = ends_of(lengths_ref)
    tall = total // n_rows
    for member in range(n_rows):
        at = pl.multiple_of(place_ref[8 + member] * tall, tall) if fast else 0
        rows_ref[pl.ds(at, tall), :] = row_refs[member][-tall:, :]
    if fast:
        for slot in range(8):
            at = pl.multiple_of(place_ref[slot] * 128, 128)
            gate_weight_ref[pl.ds(at, 128), :] = msg_refs[slot][:128, :]
            out_weight_ref[pl.ds(at, 128), :] = msg_refs[slot][128:, :]
    else:
        gate_weight_ref[...] = msg_refs[0][...]
        out_weight_ref[...] = msg_refs[1][...]

    def part(at):
        rows = pl.ds(at, 128)
        valid = jnp.where(iota((128, 1), 0) + at < ends[-1], 1.0, 0.0)
        grad = mm(rows_ref[rows, :], out_weight_ref[...]) * valid
        grad_ref[rows, :] = grad
        gate = mm(normed_ref[rows, :], gate_weight_ref[...])
        gate_ref[rows, :] = gate
        gated = mixed_ref[rows, :] * (gate * sigmoid(gate))
        square = jnp.sum(gated * gated, axis=1, keepdims=True)
        cross = jnp.sum(grad * norm_ref[...] * gated, axis=1, keepdims=True)
        lane = iota((128, 128), 1)
        wide_ref[rows, :] = jnp.where(lane == 0, square, jnp.where(lane == 1, cross, 0.0))

    row_loop(total, 128, part)
    for at in range(0, total, 128):
        sums_ref[:, at : at + 128] = wide_ref[at : at + 128, :].T[:8, :]


def norm_kernel(inner_total, place_ref, lengths_ref, *refs):
    n_sums = len(refs) - 21
    sums_refs, refs = refs[:n_sums], refs[n_sums:]
    gate_ref, mixed_ref, grad_ref, norm_ref, weight_ref, rows_ref, turned_ref = refs[:7]
    chunk_refs = refs[7:15]
    partial_ref, grad_gate_ref, grad_mixed_ref, norm_grad_ref = refs[15:19]
    wide_ref, out_rows_ref = refs[19:]
    total, channels = gate_ref.shape
    ends = ends_of(lengths_ref)
    for at in range(0, total, 128):
        tile = sum(ref[:, at : at + 128] for ref in sums_refs)
        tile = jnp.concatenate([tile] * 16, axis=0)
        wide_ref[at : at + 128, :] = tile.T
    norm_grad_ref[...] = jnp.zeros(norm_grad_ref.shape, f32)

    def part(at):
        rows = pl.ds(at, 128)
        valid = jnp.where(iota((128, 1), 0) + at < ends[-1], 1.0, 0.0)
        scale = lax.rsqrt(wide_ref[rows, 0:1] / inner_total + epsilon)
        cross = wide_ref[rows, 1:2]
        gate = gate_ref[rows, :]
        mixed = mixed_ref[rows, :]
        sig = sigmoid(gate)
        gate_act = gate * sig
        gated = mixed * gate_act
        grad = grad_ref[rows, :]
        norm = norm_ref[...]
        hat = gated * scale
        out_rows_ref[rows, :] = (hat * norm * valid).astype(bf16)
        norm_grad_ref[...] += jnp.sum(grad * hat, axis=0, keepdims=True)
        grad_gated = scale * (grad * norm) - gated * (scale * scale * scale * cross / inner_total)
        grad_mixed_ref[rows, :] = grad_gated * gate_act
        grad_gate = grad_gated * mixed * sig * (1.0 + gate * (1.0 - sig))
        grad_gate_ref[rows, :] = grad_gate.astype(bf16)

    row_loop(total, 128, part)

    def back(at):
        cols = pl.ds(at, 256)
        partial_ref[:, cols] = mm(out_rows_ref[...], weight_ref[cols, :], (1, 1)).astype(bf16)

    row_loop(weight_ref.shape[0], 256, back)
    tall = chunk_refs[0].shape[0] // 2
    for slot, chunk_ref in enumerate(chunk_refs):
        cols = pl.ds(pl.multiple_of(place_ref[slot] * tall, tall), tall)
        chunk_ref[:tall, :] = mm(turned_ref[cols, :], grad_gate_ref[...]).astype(bf16)
        chunk_ref[tall:, :] = mm(rows_ref[:, cols], out_rows_ref[...], (0, 0)).astype(bf16)


def scan_back_kernel(first_pair, lengths_ref, *refs):
    grad_mixed_ref, act_ref, state_ref, step_col_ref, step_row_ref = refs[:5]
    step_bias_ref, step_bias_col_ref, log_ref, log_col_ref, skip_ref = refs[5:10]
    grad_act_ref, grad_state_ref, step_grad_ref, sums_ref, acc_ref = refs[10:]
    total, own_width = grad_act_ref.shape
    states = state_ref.shape[1] // 2
    ends = ends_of(lengths_ref)
    sums_ref[...] = jnp.zeros(sums_ref.shape, f32)
    raw_row = step_row_ref[...]
    steps = step_sizes(
        step_col_ref[...], raw_row, step_bias_ref, step_bias_col_ref, log_ref, log_col_ref
    )
    rate_row = steps[3]
    low_half = iota((span, 128), 1) < head_width
    lower = jnp.where(iota((span, span), 0) >= iota((span, span), 1), 1.0, 0.0)
    blocks = [Block(b, ends, *steps, state_ref) for b in range(total // span)]
    first, second = blocks
    row_sums, step_rows, out_sums, in_sums = [], [], None, None
    grad_out = jnp.zeros((span, states), f32)
    grad_in = jnp.zeros((span, states), f32)
    head_of = iota((head_rows, 128), 0)
    lane_head = iota((head_rows, 128), 1) // head_width

    for b, block in enumerate(blocks):
        acc_ref[...] = jnp.zeros((span, span), f32)
        row_sum = jnp.zeros((span, 128), f32)
        step_grad = jnp.zeros((head_rows, span), f32)
        lane = iota((span, 128), 1)
        head_row = iota((head_rows, span), 0)
        for i in range(first_pair, first_pair + own_width // 128):
            cols = slice(128 * i, 128 * (i + 1))
            own_cols = slice(128 * (i - first_pair), 128 * (i - first_pair + 1))
            pair = (2 * i, 2 * i + 1)
            x = act_ref[block.rows, cols]
            x_low = x.astype(bf16)
            grad = grad_mixed_ref[block.rows, cols]
            grad_low = grad.astype(bf16)
            halves = (
                jnp.where(low_half, grad, 0.0).astype(bf16),
                jnp.where(low_half, 0.0, grad).astype(bf16),
            )
            step_wide = wide(low_half, *(block.step[:, h : h + 1] for h in pair))
            grads = []
            for h, half in zip(pair, halves):
                decay = block.decay(h)
                spread = mm(half, x_low, (1, 1)) * decay
                stepped = spread * block.step_row[h : h + 1, :]
                acc_ref[...] += stepped
                row_here = jnp.sum(stepped * block.contact, axis=1, keepdims=True)
                row_sum = jnp.where(lane == h, row_here, row_sum)
                step_here = jnp.sum(spread * block.contact, axis=0, keepdims=True)
                step_grad = jnp.where(head_row == h, step_here, step_grad)
                grads.append(mm((decay * block.contact).astype(bf16), grad_low, (0, 0)))
            grad_act = wide(low_half, *grads) * step_wide + skip_ref[:, cols] * grad
            sums_ref[2:3, own_cols] += jnp.sum(grad * x, axis=0, keepdims=True)
            picks = jnp.where(lane_head + 2 * i == head_of, 1.0, 0.0)
            if b == 0:
                reach = wide(low_half, *(second.from_edge(h) for h in pair))
                lead = (grad_mixed_ref[second.rows, cols] * reach).astype(bf16)
                edge = wide(low_half, *(block.to_edge(h) for h in pair))
                weighted = (x * step_wide * edge).astype(bf16)
                held = mm(block.inputs, weighted, (0, 0)).astype(bf16)
                held_grad = mm(second.outputs, lead, (0, 0)).astype(bf16)
                grad_out = grad_out + mm(lead, held, (1, 1))
                grad_in = grad_in + mm(weighted, held_grad, (1, 1))
                back = mm(block.inputs, held_grad) * edge
                grad_act = grad_act + back * step_wide
                ahead = mm(second.outputs, held)
                out_here = mm_exact(picks, lead.astype(f32) * ahead, (1, 1))
                in_here = mm_exact(picks, x * back, (1, 1))
                out_sums = out_here if out_sums is None else out_sums + out_here
                in_sums = in_here if in_sums is None else in_sums + in_here
            grad_act_ref[block.rows, own_cols] = grad_act
        table = (acc_ref[...] * block.mask).astype(bf16)
        grad_c = mm(table, block.inputs)
        grad_b = mm(table, block.outputs, (0, 0))
        if b == 0:
            grad_b = grad_b + grad_in
        else:
            grad_c = grad_c + grad_out
        grad_state_ref[block.rows, :states] = grad_b
        grad_state_ref[block.rows, states:] = grad_c
        row_sums.append(row_sum)
        step_rows.append(step_grad)

    rate_grads = []
    for b, block in enumerate(blocks):
        column = step_rows[b] * block.step_row
        crossing = mm_exact(row_sums[b], lower, (0, 0))[:head_rows] - mm_exact(column, lower)
        if b == 0:
            crossing = crossing + mm_exact(in_sums * block.step_row, 1.0 - lower)
        else:
            crossing = crossing + mm_exact(out_sums, lower)
        rate_grads.append(crossing)
    step_rows[0] = step_rows[0] + in_sums
    rate_grad = jnp.concatenate(rate_grads, axis=1)
    step_grad = jnp.concatenate(step_rows, axis=1) - rate_grad * jnp.exp(log_col_ref[...])
    step_grad = step_grad * sigmoid(raw_row + step_bias_col_ref[...])
    decay_sum = jnp.sum(rate_grad * rate_row, axis=1, keepdims=True)
    bias_sum = jnp.sum(step_grad, axis=1, keepdims=True)
    lane = iota((head_rows, 128), 1)
    head_sums = jnp.where(lane == 0, bias_sum, jnp.where(lane == 1, decay_sum, 0.0))
    head_sums = jnp.concatenate([head_sums] * (128 // head_rows), axis=0).T
    sums_ref[0:2, :128] = head_sums[:2, :]
    step_grad_ref[...] = step_grad


def conv_back(x_ref, mask_ref, grad_ref, held_ref, out_ref, sums_ref, own_taps, own_bias):
    total, taps = out_ref.shape[0], own_taps.shape[0]
    held_ref[total:, :] = jnp.zeros((pad, held_ref.shape[1]), f32)

    def column(cols):
        sums = [jnp.zeros((1, 128), f32) for _ in range(taps + 1)]
        for at in range(0, total, 128):
            pre, shifted = conv_pre(x_ref, mask_ref, own_taps, own_bias, at, cols, 128)
            sig = sigmoid(pre)
            grad = grad_ref[at : at + 128, cols] * sig * (1.0 + pre * (1.0 - sig))
            held_ref[at : at + 128, cols] = grad
            for s in range(taps):
                sums[taps - 1 - s] += jnp.sum(grad * shifted[s], axis=0, keepdims=True)
            sums[taps] += jnp.sum(grad, axis=0, keepdims=True)
        for t, value in enumerate(sums):
            sums_ref[t : t + 1, cols] = value
        for at in range(0, total, 128):
            back = own_taps[taps - 1 : taps, cols] * held_ref[at : at + 128, cols]
            for s in range(1, taps):
                part = held_ref[at + s : at + s + 128, cols]
                part = part * mask_ref[s - 1, at + s : at + s + 128, :]
                back = back + own_taps[taps - 1 - s : taps - s, cols] * part
            out_ref[at : at + 128, cols] = back.astype(bf16)

    column_loop(out_ref.shape[1], column)


def state_back_kernel(fast, place_ref, lengths_ref, *refs):
    state_refs, step_refs, refs = refs[0:2], refs[2:4], refs[4:]
    state_raw_ref, turned_ref, small_ref, grad_state_low_ref, step_low_ref = refs[:5]
    n_out = 4 if fast else 2
    out_refs, refs = refs[5 : 5 + n_out], refs[5 + n_out :]
    mask_ref, taps_ref, bias_ref, grad_state_ref, pre_ref, part_ref, sums_ref = refs
    taps = taps_ref.shape[0]
    taps_ref[...] = small_ref[4 : 4 + taps, :]
    bias_ref[...] = small_ref[4 + taps : 5 + taps, :]
    write_masks(mask_ref, ends_of(lengths_ref))
    grad_state_ref[...] = state_refs[0][...] + state_refs[1][...]
    step_low_ref[...] = (step_refs[0][...] + step_refs[1][...]).astype(bf16)
    sums_ref[...] = jnp.zeros(sums_ref.shape, f32)
    conv_back(
        state_raw_ref,
        mask_ref,
        grad_state_ref,
        pre_ref,
        grad_state_low_ref,
        sums_ref,
        taps_ref,
        bias_ref,
    )

    def chunk(at):
        part = turned_ref[pl.ds(at, 256), :]
        part_ref[pl.ds(at, 256), :] = mm(part, grad_state_low_ref[...]).astype(bf16)

    depth = turned_ref.shape[0]
    row_loop(depth, 256, chunk)
    if fast:
        share = depth // 32
        for member, out_ref in enumerate(out_refs):
            for c in range(8):
                at = pl.multiple_of((4 * c + place_ref[8 + member]) * share, share)
                out_ref[share * c : share * (c + 1), :] = part_ref[pl.ds(at, share), :]
            out_ref[8 * share :, :] = sums_ref[...].astype(bf16)
    else:
        out_refs[0][...] = part_ref[...]
        out_refs[1][...] = sums_ref[...]


def inner_back_kernel(lengths_ref, *refs):
    act_refs, head_refs, refs = refs[0:2], refs[2:4], refs[4:]
    raw_ref, norm_grad_ref, taps_ref, bias_ref, grad_inner_ref, sums_ref = refs[:6]
    mask_ref, grad_act_ref, pre_ref = refs[6:]
    half = grad_inner_ref.shape[1] // 2
    write_masks(mask_ref, ends_of(lengths_ref))
    grad_act_ref[:, :half] = act_refs[0][...]
    grad_act_ref[:, half:] = act_refs[1][...]
    sums_ref[...] = jnp.zeros(sums_ref.shape, f32)
    heads = head_refs[0][:2, :128] + head_refs[1][:2, :128]
    sums_ref[5:6, :] = norm_grad_ref[...]
    sums_ref[6:7, :half] = head_refs[0][2:3, :]
    sums_ref[6:7, half:] = head_refs[1][2:3, :]
    sums_ref[9:10, half : half + 128] = heads[0:1, :]
    sums_ref[9:10, half + 128 :] = heads[1:2, :]
    conv_back(
        raw_ref,
        mask_ref,
        grad_act_ref,
        pre_ref,
        grad_inner_ref,
        sums_ref,
        taps_ref,
        bias_ref,
    )


def message_kernel(grad_inner_ref, step_low_ref, turned_ref, msg_ref):
    chunks = msg_ref.shape[0]
    tall = turned_ref.shape[0] // chunks
    step_low = step_low_ref[...]

    def chunk(c, carry):
        part = turned_ref[pl.ds(pl.multiple_of(c * tall, tall), tall), :]
        msg_ref[c, :tall, :] = mm(part, grad_inner_ref[...]).astype(bf16)
        msg_ref[c, tall:, :tall] = mm(step_low, part, (1, 1)).astype(bf16)
        msg_ref[c, tall:, tall:] = jnp.zeros((head_rows, msg_ref.shape[2] - tall), bf16)
        return carry

    lax.fori_loop(0, chunks, chunk, 0)


def chunk_kernel(slots, n_got, place_ref, *refs):
    grad_inner_ref, step_low_ref, sums_ref = refs[:3]
    state_refs, turned_refs, got_refs = refs[3:7], refs[7:9], refs[9 : 9 + n_got]
    out_refs = refs[9 + n_got :]
    states = state_refs[0].shape[1]
    share = (state_refs[0].shape[0] - 16) // 8

    def state_rows(low, tall):
        return sum(ref[pl.ds(low, tall), :].astype(f32) for ref in state_refs)

    shared = state_rows(8 * share, 16)
    sums = [
        sums_ref[:7, :],
        jnp.concatenate([shared[0:1, :], shared[1:2, :]], axis=1),
        jnp.concatenate([shared[2:3, :], shared[3:4, :]], axis=1),
        jnp.concatenate([shared[4:5, :], sums_ref[9:10, states:]], axis=1),
    ]
    tall = turned_refs[0].shape[0]
    parts = jnp.concatenate([ref[...] for ref in turned_refs], axis=0)
    products = mm(parts, grad_inner_ref[...])
    for n, (slot, out_ref) in enumerate(zip(slots, out_refs)):
        index = place_ref[slot]
        part = parts[tall * n : tall * (n + 1), :]
        step = mm(step_low_ref[...], part, (1, 1))
        step = [
            jnp.concatenate([step[4 * k + i : 4 * k + i + 1, :] for i in range(4)], axis=1)
            for k in range(2)
        ]
        state = state_rows(pl.multiple_of(index * share, share), share)
        value = jnp.concatenate(
            [
                products[tall * n : tall * (n + 1), :],
                jnp.concatenate([state[:16, :], state[16:, :]], axis=1),
                *sums,
                *step,
                jnp.zeros((4, 2 * states), f32),
            ],
            axis=0,
        )
        tail = value.shape[0] - 16
        main, sums_here = value[:tail, :], value[tail:, :]
        if n < n_got:
            got = got_refs[n]
            main = main + got[:tail, :].astype(f32)
            sums_here = sums_here + got[tail : tail + 16, :].astype(f32)
            sums_here = sums_here + got[tail + 16 :, :].astype(f32)
        out_ref[:tail, :] = main.astype(out_ref.dtype)
        high = sums_here.astype(bf16)
        out_ref[tail : tail + 16, :] = high.astype(out_ref.dtype)
        out_ref[tail + 16 :, :] = (sums_here - high.astype(f32)).astype(out_ref.dtype)


def finish_kernel(*refs):
    own_ref, got_ref, gate_ref, input_ref, step_rows_ref, state_ref = refs[:6]
    input_grad_ref, step_grad_ref, state_grad_ref, sums_ref, gain_ref, state_gain_ref = refs[6:]
    tall = input_ref.shape[0]
    states = state_ref.shape[1]
    heads = step_grad_ref.shape[1]
    inner = own_ref[:tall, :] + got_ref[:tall, :].astype(f32)
    gate = gate_ref[...]
    input_grad_ref[:, 0, :] = gate
    input_grad_ref[:, 1, :] = inner
    state = own_ref[tall : tall + 16, :] + got_ref[tall : tall + 16, :].astype(f32)
    state = jnp.concatenate([state[:, :states], state[:, states:]], axis=0)
    state_grad_ref[...] = state
    sums = own_ref[tall + 16 : tall + 32, :] + own_ref[tall + 32 :, :]
    sums = sums + got_ref[tall + 16 : tall + 32, :].astype(f32)
    sums = sums + got_ref[tall + 32 :, :].astype(f32)
    sums_ref[...] = sums
    step = [sums[10 + h // 4 : 11 + h // 4, 128 * (h % 4) : 128 * (h % 4 + 1)] for h in range(heads)]
    step = jnp.concatenate(step, axis=0)
    along = input_ref[:, 0, :].astype(f32) * gate + input_ref[:, 1, :].astype(f32) * inner
    gain = mm_exact(jnp.ones((8, along.shape[1]), f32), along, (1, 1))
    over = jnp.sum(step_rows_ref[:heads, :].astype(f32) * step, axis=0, keepdims=True)
    gain_ref[...] = gain + over
    along = state_ref[...].astype(f32) * state
    state_gain_ref[...] = mm_exact(jnp.ones((8, states), f32), along, (1, 1))
    step = jnp.concatenate([step, jnp.zeros((128 - heads, 128), f32)], axis=0).T
    step_grad_ref[...] = step[:, :heads]


def project_back_kernel(fast, place_ref, *refs):
    grad_refs, step_low_ref, weight_refs, step_weight_ref = refs[:3], refs[3], refs[4:7], refs[7]
    out_refs, held_refs, step_ref = refs[8:10], refs[10:13], refs[13]
    for n, member in enumerate((0, 2, 1, 3)):
        at = pl.multiple_of(place_ref[8 + member] * 128, 128) if fast else 128 * member
        for held_ref, grad_ref in zip(held_refs, grad_refs):
            held_ref[128 * n : 128 * (n + 1), :] = grad_ref[pl.ds(at, 128), :]
        step_ref[:, 128 * n : 128 * (n + 1)] = step_low_ref[:, pl.ds(at, 128)]

    def back(at):
        cols = pl.ds(at, 256)
        grad = mm(step_ref[...], step_weight_ref[:, cols], (0, 0))
        for held_ref, weight_ref in zip(held_refs, weight_refs):
            grad = grad + mm(held_ref[...], weight_ref[cols, :], (1, 1))
        grad = grad.astype(bf16)
        for n in range(4):
            out_refs[n // 2][n % 2, :, cols] = grad[128 * n : 128 * (n + 1), :]

    row_loop(step_weight_ref.shape[1], 256, back)


def prepare_kernel(place_ref, *refs):
    gain_ref, taps_ref, bias_ref, state_ref, step_ref, input_ref, out_ref = refs[:7]
    shared_ref, step_rows_ref, late_ref = refs[7:]
    owner = place_ref[0]
    share, states = state_ref.shape
    shared_ref[:share, :] = state_ref[...]

    def placed(value, at):
        width = value.shape[1]
        pick = iota((width, states), 1) - at == iota((width, states), 0)
        return mm(value, jnp.where(pick, 1.0, 0.0).astype(bf16))

    start = owner * gain_ref.shape[1]
    small = jnp.concatenate(
        [placed(gain_ref[...], start - states * i) for i in range(4)]
        + [placed(taps_ref[...], owner * taps_ref.shape[1])]
        + [placed(bias_ref[...], owner * bias_ref.shape[1])]
        + [jnp.zeros((7, states), f32)],
        axis=0,
    )
    shared_ref[share:, :] = small.astype(bf16)
    depth_part, heads = step_ref.shape
    step = step_ref[...].astype(f32)
    step = jnp.concatenate([step, jnp.zeros((depth_part, 128 - heads), f32)], axis=1).T
    step_rows_ref[...] = step[:head_rows, :].astype(bf16)
    late_ref[:depth_part, :] = input_ref[:, 0, :]
    late_ref[depth_part:, :] = out_ref[...].astype(f32).T.astype(bf16)


def params_kernel(*refs):
    taps_ref, bias_ref, step_bias_ref, log_ref, skip_ref, norm_ref = refs[:6]
    outs = refs[6:]
    heads = step_bias_ref.shape[1]
    pick = jnp.where(iota((heads, head_rows), 0) == iota((heads, head_rows), 1), 1.0, 0.0)
    square = iota((head_rows, head_rows), 0) == iota((head_rows, head_rows), 1)

    def both(value_ref, row_ref, col_ref):
        row = mm_exact(value_ref[...].astype(f32), pick)
        row_ref[...] = row
        col_ref[...] = jnp.sum(jnp.where(square, row, 0.0), axis=1, keepdims=True)

    outs[0][...] = taps_ref[...].astype(f32)
    outs[1][...] = bias_ref[...].astype(f32)
    both(step_bias_ref, outs[2], outs[3])
    both(log_ref, outs[4], outs[5])
    channels = norm_ref.shape[1]
    own = iota((heads, channels), 1) // (channels // heads) == iota((heads, channels), 0)
    outs[6][...] = mm_exact(skip_ref[...].astype(f32), jnp.where(own, 1.0, 0.0))
    outs[7][...] = norm_ref[...].astype(f32)


def assemble_kernel(input_ref, step_ref, *refs):
    shared_refs, msg_ref = refs[:4], refs[4]
    depth_part, _, channels = input_ref.shape
    share = shared_refs[0].shape[0] - 16
    tail = depth_part + 2 * share
    msg_ref[:depth_part, :] = input_ref[:, 1, :]
    for member, ref in enumerate(shared_refs):
        high, low = depth_part + share * (member // 2), 256 * (member % 2)
        msg_ref[high : high + share, low : low + 256] = ref[:share, :]
    small = sum(ref[share:, :].astype(f32) for ref in shared_refs)
    msg_ref[tail:, :256] = small.astype(bf16)
    msg_ref[tail:, 256:384] = step_ref[...]
    msg_ref[tail:, 384:] = jnp.zeros((16, channels - 384), bf16)


def call(kernel, micros, scalars, arrays, outs, scratch):
    smem = pl.BlockSpec(memory_space=pltpu.SMEM)
    vmem = pl.BlockSpec(memory_space=pltpu.VMEM)
    return pl.pallas_call(
        kernel,
        out_shape=[jax.ShapeDtypeStruct(shape, kind) for shape, kind in outs],
        in_specs=[smem] * len(scalars) + [vmem] * len(arrays),
        out_specs=[vmem] * len(outs),
        scratch_shapes=[pltpu.VMEM(shape, kind) for shape, kind in scratch],
        compiler_params=pltpu.CompilerParams(vmem_limit_bytes=vmem_bytes),
        cost_estimate=pl.CostEstimate(
            flops=int(micros * 1.1e9), bytes_accessed=1 << 20, transcendentals=0
        ),
    )(*scalars, *arrays)


def ring_ok(n_dp, n_tensor):
    return n_dp == 8 and n_tensor == 4


ring_order = (0, 2, 4, 6, 7, 5, 3, 1)


def ring_place(index):
    high, low = index // 2, index % 2
    return jnp.where(low == 0, high, 7 - high)


def ring_index(place):
    place = lax.rem(place + 16, 8)
    return jnp.where(place < 4, 2 * place, 2 * (7 - place) + 1)


def ring_send(value, forward):
    pairs = []
    for place in range(8):
        other = (place + (1 if forward else 7)) % 8
        pairs.append((ring_order[place], ring_order[other]))
    return lax.ppermute(value, "dp", pairs)


def ring_gather(value):
    me = ring_place(lax.axis_index("dp"))
    pieces = [(value, ring_index(me))]
    ahead, back = value, value
    for step in range(1, 5):
        ahead = ring_send(ahead, True)
        pieces.append((ahead, ring_index(me - step)))
        if step < 4:
            back = ring_send(back, False)
            pieces.append((back, ring_index(me + step)))
    return pieces


def dp_swap(value, bit):
    return lax.ppermute(value, "dp", [(i, i ^ bit) for i in range(8)])


def ring_step(held):
    return ring_send(held[0], True), ring_send(held[1], False)


def add_low(got, own):
    return (got.astype(f32) + own.astype(f32)).astype(bf16)


def ordered(first, then):
    return lax.optimization_barrier((first, then))


def tensor_gather(value):
    near = tensor_swap(value, 1)
    far = tensor_swap(value, 2)
    return [value, near, far, tensor_swap(far, 1)]


def tensor_direct(value):
    return [value] + [tensor_swap(value, bit) for bit in range(1, 4)]


def tensor_sum(value, depth):
    parts = value.reshape(4, -1, depth)
    parts = lax.all_to_all(parts, "tensor", 0, 0, tiled=True)
    return jnp.sum(parts.astype(f32), axis=0)


def tensor_swap(value, bit):
    return lax.ppermute(value, "tensor", [(i, i ^ bit) for i in range(4)])


def body(
    tokens,
    lengths,
    cotangent,
    pre_gain,
    input_weight,
    step_weight,
    state_weight,
    conv_inner,
    conv_inner_bias,
    conv_state,
    conv_state_bias,
    step_bias,
    decay_log,
    skip_gain,
    norm_gain,
    output_weight,
):
    n_dp, n_tensor = lax.axis_size("dp"), lax.axis_size("tensor")
    fast = ring_ok(n_dp, n_tensor)
    owners = n_dp * n_tensor
    me = lax.axis_index("tensor")
    owner = lax.axis_index("dp") * n_tensor + me
    own_rows, depth = tokens.shape
    total = own_rows * n_tensor
    states = state_weight.shape[1]
    heads = step_weight.shape[1]
    share = state_weight.shape[0]
    taps = conv_state.shape[0]
    channels = input_weight.shape[2]
    inner_total = channels * n_tensor

    owner_place = jnp.stack([owner, owners]).astype(jnp.int32)
    shared, step_rows, late = call(
        prepare_kernel,
        3,
        [owner_place],
        [
            pre_gain[None, :],
            conv_state,
            conv_state_bias[None, :],
            state_weight,
            step_weight,
            input_weight,
            output_weight,
        ],
        [
            ((share + 16, states), bf16),
            ((head_rows, step_weight.shape[0]), bf16),
            ((input_weight.shape[0] + output_weight.shape[1], channels), bf16),
        ],
        [],
    )
    params = call(
        params_kernel,
        1,
        [],
        [
            conv_inner,
            conv_inner_bias[None, :],
            step_bias[None, :],
            decay_log[None, :],
            skip_gain[None, :],
            norm_gain[None, :],
        ],
        [
            ((taps, channels), f32),
            ((1, channels), f32),
            ((1, head_rows), f32),
            ((head_rows, 1), f32),
            ((1, head_rows), f32),
            ((head_rows, 1), f32),
            ((1, channels), f32),
            ((1, channels), f32),
        ],
        [],
    )
    params = list(params)
    conv_params, head_params, norm_row = params[:2], params[2:7], params[7]
    if fast:
        shared = tensor_direct(shared)
        late_one = ring_step((late, late))
        (msg,) = call(
            assemble_kernel,
            1,
            [],
            [input_weight, step_rows, *shared],
            [((input_weight.shape[0] + 2 * share + 16, channels), bf16)],
            [],
        )
        msg = ring_gather(msg)
        weight_pieces = [piece for piece, _ in msg]
        late_two = ring_step(late_one)
        late_three = ring_step(late_two)
        late_pieces = [late, *late_one, *late_two, *late_three, ring_send(late_three[0], True)]
        own_rows_both = jnp.concatenate([tokens, cotangent], axis=0)
        row_pieces = tensor_gather(ordered(shared, own_rows_both)[1])
        grad_pieces = row_pieces
        place = jnp.stack([index for _, index in msg] + [me, me ^ 1, me ^ 2, me ^ 3])
    else:
        row_pieces = [lax.all_gather(tokens, "tensor", axis=0, tiled=True)]
        grad_pieces = [lax.all_gather(cotangent, "tensor", axis=0, tiled=True)]
        gate_weight, inner_weight = late[: input_weight.shape[0]], input_weight[:, 1]
        weight_pieces = [
            lax.all_gather(inner_weight, "dp", axis=0, tiled=True),
            lax.all_gather(state_weight, ("dp", "tensor"), axis=0, tiled=True),
            lax.all_gather(step_rows, "dp", axis=1, tiled=True),
            lax.psum(shared[share:], ("dp", "tensor")),
        ]
        late_pieces = [
            lax.all_gather(gate_weight, "dp", axis=0, tiled=True),
            lax.all_gather(late[input_weight.shape[0] :], "dp", axis=0, tiled=True),
        ]
        place = jnp.concatenate([jnp.arange(8), jnp.arange(4)])
    place = place.astype(jnp.int32)

    masks = ((taps - 1, total + pad, 128), f32)
    state_taps = [((taps, states), f32), ((1, states), f32)]
    (
        normed,
        turned,
        inner_full,
        state_full,
        step_full,
        small_full,
        raw,
        state_raw,
        step_col,
        step_row,
        act,
        state_act,
        mixed,
    ) = call(
        functools.partial(forward_kernel, fast),
        11,
        [place, lengths],
        row_pieces + weight_pieces + conv_params + head_params,
        [
            ((total, depth), bf16),
            ((depth, total), bf16),
            ((depth, channels), bf16),
            ((depth, states), bf16),
            ((head_rows, depth), bf16),
            ((16, states), f32),
            ((total + pad, channels), f32),
            ((total + pad, states), f32),
            ((total, head_rows), f32),
            ((head_rows, total), f32),
            ((total, channels), f32),
            ((total, states), f32),
            ((total, channels), f32),
        ],
        [masks] + state_taps,
    )
    grad_rows, gate_full, output_full, gate, grad_normalized, sums = call(
        functools.partial(grad_in_kernel, fast),
        5,
        [place, lengths],
        grad_pieces + late_pieces + [normed, mixed, norm_row],
        [
            ((total, depth), bf16),
            ((depth, channels), bf16),
            ((depth, channels), bf16),
            ((total, channels), f32),
            ((total, channels), f32),
            ((8, total), f32),
        ],
        [((total, 128), f32)],
    )
    if fast:
        sums = tensor_direct(sums)
    else:
        sums = [lax.psum(sums, "tensor")]
    chunks = 8
    tall = depth // chunks
    norm_outs = call(
        functools.partial(norm_kernel, inner_total),
        9,
        [place, lengths],
        [*sums, gate, mixed, grad_normalized, norm_row, output_full, grad_rows, turned],
        [((2 * tall, channels), bf16)] * chunks
        + [
            ((total, depth), bf16),
            ((total, channels), bf16),
            ((total, channels), f32),
            ((1, channels), f32),
        ],
        [((total, 128), f32), ((total, channels), bf16)],
    )
    gate_chunks = norm_outs[:chunks]
    partial_out, grad_gate, grad_mixed, norm_grad = norm_outs[chunks:]

    def scan_back(first_pair, grad):
        return call(
            functools.partial(scan_back_kernel, first_pair),
            6,
            [lengths],
            [grad, act, state_act, step_col, step_row] + head_params,
            [
                ((total, channels // 2), f32),
                ((total, states), f32),
                ((head_rows, total), f32),
                ((8, channels // 2), f32),
            ],
            [((span, span), f32)],
        )

    if fast:
        got = ring_step((gate_chunks[7], gate_chunks[5]))
        held = add_low(got[0], gate_chunks[6]), add_low(got[1], gate_chunks[3])
    first = scan_back(0, grad_mixed)
    if fast:
        held, grad_mixed = ordered(held, grad_mixed)
        got = ring_step(held)
        held = add_low(got[0], gate_chunks[4]), add_low(got[1], gate_chunks[1])
    second = scan_back(channels // 256, grad_mixed)
    if fast:
        held, state_raw = ordered(held, state_raw)
        got = ring_step(held)
        held, last = add_low(got[0], gate_chunks[2]), got[1]
    share_rows = depth // 4 + 16
    state_outs = call(
        functools.partial(state_back_kernel, fast),
        4,
        [place, lengths],
        [first[1], second[1], first[2], second[2], state_raw, turned, small_full],
        [((total, states), bf16), ((head_rows, total), bf16)]
        + (
            [((share_rows, states), bf16)] * 4
            if fast
            else [((depth, states), bf16), ((16, states), f32)]
        ),
        [
            masks,
            *state_taps,
            ((total, states), f32),
            ((total + pad, states), f32),
            ((depth, states), bf16),
            ((16, states), f32),
        ],
    )
    grad_state_low, step_low = state_outs[:2]
    state_parts = state_outs[2:]
    if fast:
        state_parts = [state_parts[0]] + [tensor_swap(state_parts[i], i) for i in range(1, 4)]
    if fast:
        (held, last), raw = ordered((held, last), raw)
        gate_out = gate_chunks[0].astype(f32) + last.astype(f32)
        gate_out = gate_out + ring_send(held, True).astype(f32)
    grad_inner, sums = call(
        inner_back_kernel,
        6,
        [lengths],
        [first[0], second[0], first[3], second[3], raw, norm_grad] + conv_params,
        [((total, channels), bf16), ((16, channels), f32)],
        [masks, ((total, channels), f32), ((total + pad, channels), f32)],
    )
    if fast:
        mixed_rows = tensor_sum(partial_out, depth)
        (gate_out, mixed_rows), grad_inner = ordered((gate_out, mixed_rows), grad_inner)

    def project_back():
        return call(
            functools.partial(project_back_kernel, fast),
            6,
            [place],
            [
                grad_gate,
                grad_inner,
                grad_state_low,
                step_low,
                gate_full,
                inner_full,
                state_full,
                step_full,
            ],
            [((2, 128, depth), bf16)] * 2,
            [
                ((total, channels), bf16),
                ((total, channels), bf16),
                ((total, states), bf16),
                ((head_rows, total), bf16),
            ],
        )

    def chunk_pair(slots, got, after=None, last=bf16):
        grad = grad_inner if after is None else ordered(after, grad_inner)[1]
        arrays = [grad, step_low, sums, *state_parts, turned, turned, *got]

        def whole(array):
            return pl.BlockSpec(array.shape, lambda i, place: (0, 0))

        def block(slot):
            return pl.BlockSpec((tall, total), lambda i, place: (place[slot], 0))

        specs = [whole(array) for array in arrays]
        specs[7:9] = [block(slot) for slot in slots]
        out = pl.BlockSpec((tall + 48, channels), lambda i, place: (0, 0))
        return pl.pallas_call(
            functools.partial(chunk_kernel, slots, len(got)),
            grid_spec=pltpu.PrefetchScalarGridSpec(
                num_scalar_prefetch=1, grid=(1,), in_specs=specs, out_specs=[out, out]
            ),
            out_shape=[
                jax.ShapeDtypeStruct((tall + 48, channels), kind) for kind in (bf16, last)
            ],
            compiler_params=pltpu.CompilerParams(vmem_limit_bytes=vmem_bytes),
            cost_estimate=pl.CostEstimate(
                flops=2_000_000_000, bytes_accessed=1 << 20, transcendentals=0
            ),
        )(place, *arrays)

    if fast:
        got = ring_step(chunk_pair((7, 5), ()))
        keep_rows, give_rows = project_back()
        got = ring_step(chunk_pair((6, 3), got, give_rows))
        got = ring_step(chunk_pair((4, 1), got))
        held, inner_own = chunk_pair((2, 0), got, last=f32)
        inner_got = ring_send(held, True)
    else:
        (inner_msg,) = call(
            message_kernel,
            5,
            [],
            [grad_inner, step_low, turned],
            [((chunks, tall + head_rows, channels), bf16)],
            [],
        )
        keep_rows, give_rows = project_back()

    token_float = tokens.astype(f32)
    gain_full = small_full[: depth // states].reshape(1, depth)

    if fast:
        got = tensor_swap(give_rows, 1)
        far = tensor_swap(add_low(keep_rows[1], got[1]), 2)
        grad_local = keep_rows[0].astype(f32) + got[0].astype(f32) + far.astype(f32)
        gate_grad, output_grad = gate_out[:tall], gate_out[tall:].T
        input_grad, step_grad, state_grad, sums, own_gain, state_gain = call(
            finish_kernel,
            2,
            [],
            [inner_own, inner_got, gate_grad, input_weight, step_rows, state_weight],
            [
                (input_weight.shape, f32),
                (step_weight.shape, f32),
                (state_weight.shape, f32),
                ((16, channels), f32),
                ((8, tall), f32),
                ((8, share), f32),
            ],
            [],
        )
        own_gain, state_gain = sum(tensor_direct(own_gain))[0], state_gain[0]
        own_gain = lax.dynamic_slice(own_gain, (me * share,), (share,))
        width = states // owners
        conv_state_sum = lax.dynamic_slice(
            sums[7:10].reshape(6, states), (0, owner * width), (taps + 1, width)
        )
        conv_state_grad, conv_state_bias_grad = conv_state_sum[:taps], conv_state_sum[taps]
    else:
        state_part, state_sums = state_parts
        state_grad = lax.psum_scatter(
            state_part.astype(f32), ("dp", "tensor"), scatter_dimension=0, tiled=True
        )
        conv_state_sum = lax.psum_scatter(
            state_sums[: taps + 1], ("dp", "tensor"), scatter_dimension=1, tiled=True
        )
        conv_state_grad, conv_state_bias_grad = conv_state_sum[:taps], conv_state_sum[taps]
        grad_normed = jnp.stack([keep_rows, give_rows], axis=1).reshape(total, depth)
        mixed_rows, grad_local = (
            lax.psum_scatter(part, "tensor", scatter_dimension=0, tiled=True).astype(f32)
            for part in (partial_out, grad_normed)
        )
        both, inner_float = jnp.stack(gate_chunks).astype(f32), inner_msg.astype(f32)
        gate_grad, output_grad, inner_grad = (
            lax.psum_scatter(part.reshape(depth, channels), "dp", scatter_dimension=0, tiled=True)
            for part in (both[:, :tall], both[:, tall:], inner_float[:, :tall])
        )
        output_grad = output_grad.T
        step_part = inner_float[:, tall : tall + heads, :tall].transpose(0, 2, 1)
        step_part = step_part.reshape(depth, heads)
        step_grad = lax.psum_scatter(step_part, "dp", scatter_dimension=0, tiled=True)
        sums = lax.psum(sums, "dp")
        input_grad = jnp.stack([gate_grad, inner_grad], axis=1)
        own_gain = jnp.sum(input_weight.astype(f32) * input_grad, axis=(1, 2))
        own_gain = own_gain + jnp.sum(step_weight.astype(f32) * step_grad, axis=1)
        own_gain = lax.psum_scatter(own_gain, "tensor", scatter_dimension=0, tiled=True)
        state_gain = jnp.sum(state_weight.astype(f32) * state_grad, axis=1)
    pre_gain_grad = (own_gain + state_gain) / pre_gain.astype(f32)
    block_out = (token_float + mixed_rows).astype(bf16)
    scale = lax.rsqrt(jnp.mean(token_float * token_float, axis=1, keepdims=True) + epsilon)
    grad_scaled = grad_local * gain_full
    along = jnp.sum(grad_scaled * token_float, axis=1, keepdims=True) / depth
    tokens_grad = (
        scale * grad_scaled
        - token_float * (scale * scale * scale * along)
        + cotangent.astype(f32)
    )
    skip_grad = sums[6].reshape(heads, -1).sum(axis=1)
    return (
        block_out,
        tokens_grad,
        pre_gain_grad,
        input_grad,
        step_grad,
        state_grad,
        sums[:taps],
        sums[taps],
        conv_state_grad,
        conv_state_bias_grad,
        sums[9, states : states + heads],
        sums[9, states + 128 : states + 128 + heads],
        skip_grad,
        sums[5],
        output_grad,
    )


def solution(mesh):
    in_specs = (
        P(("dp", "tensor"), None),
        P("dp", None),
        P(("dp", "tensor"), None),
        P(("dp", "tensor")),
        P("dp", None, "tensor"),
        P("dp", "tensor"),
        P(("dp", "tensor"), None),
        P(None, "tensor"),
        P("tensor"),
        P(None, ("dp", "tensor")),
        P(("dp", "tensor")),
        P("tensor"),
        P("tensor"),
        P("tensor"),
        P("tensor"),
        P("tensor", "dp"),
    )
    out_specs = (
        P(("dp", "tensor"), None),
        P(("dp", "tensor"), None),
        P(("dp", "tensor")),
        P("dp", None, "tensor"),
        P("dp", "tensor"),
        P(("dp", "tensor"), None),
        P(None, "tensor"),
        P("tensor"),
        P(None, ("dp", "tensor")),
        P(("dp", "tensor")),
        P("tensor"),
        P("tensor"),
        P("tensor"),
        P("tensor"),
        P("tensor", "dp"),
    )
    return jax.shard_map(body, mesh=mesh, in_specs=in_specs, out_specs=out_specs, check_vma=False)
```

```python
import functools

import jax
import jax.numpy as jnp
from jax import lax
from jax.experimental import pallas as pl
from jax.experimental.pallas import tpu as pltpu
from jax.sharding import PartitionSpec as P

epsilon = 1e-05
highest = lax.Precision.HIGHEST
f32 = jnp.float32
bf16 = jnp.bfloat16
span = 256
pad = 8
head_rows = 16
head_width = 64
vmem_bytes = 61 * 1024 * 1024


def mm(a, b, over=(1, 0)):
    dims = (((over[0],), (over[1],)), ((), ()))
    return lax.dot_general(a, b, dims, preferred_element_type=f32)


def mm_exact(a, b, over=(1, 0)):
    dims = (((over[0],), (over[1],)), ((), ()))
    return lax.dot_general(a, b, dims, preferred_element_type=f32, precision=highest)


def sigmoid(v):
    return 1.0 / (1.0 + jnp.exp(-v))


def ends_of(lengths_ref):
    ends, total = [], None
    for slot in range(lengths_ref.shape[1]):
        here = lengths_ref[0, slot]
        total = here if total is None else total + here
        ends.append(total)
    return ends


def segment_of(places, ends):
    segment = jnp.zeros(places.shape, jnp.int32)
    for end in ends:
        segment = segment + jnp.where(places >= end, 1, 0)
    return segment


def iota(shape, dim):
    return lax.broadcasted_iota(jnp.int32, shape, dim)


def write_masks(mask_ref, ends):
    rows = mask_ref.shape[1] - pad
    places = iota((rows, 128), 0)
    segment = segment_of(places, ends)
    for shift in range(1, mask_ref.shape[0] + 1):
        same = (segment_of(places - shift, ends) == segment) & (places >= shift)
        mask_ref[shift - 1, :rows, :] = jnp.where(same, 1.0, 0.0)
        mask_ref[shift - 1, rows:, :] = jnp.zeros((pad, 128), f32)


def shifted_rows(x_ref, mask_ref, at, cols, shift, tall):
    part = x_ref[pad + at - shift : pad + at - shift + tall, cols]
    if shift == 0:
        return part
    return part * mask_ref[shift - 1, at : at + tall, :]


def conv_pre(x_ref, mask_ref, taps_ref, bias_ref, at, cols, tall):
    taps = taps_ref.shape[0]
    shifted = [shifted_rows(x_ref, mask_ref, at, cols, s, tall) for s in range(taps)]
    total = bias_ref[:, cols]
    for s in range(taps):
        total = total + taps_ref[taps - 1 - s : taps - s, cols] * shifted[s]
    return total, shifted


def column_loop(width, step):
    def one(c, carry):
        step(pl.ds(pl.multiple_of(c * 128, 128), 128))
        return carry

    lax.fori_loop(0, width // 128, one, 0)


def row_loop(rows, tall, step):
    def one(r, carry):
        step(pl.multiple_of(r * tall, tall))
        return carry

    lax.fori_loop(0, rows // tall, one, 0)


class Block:
    def __init__(self, b, ends, step_col, step_row, rate_col, rate_row, state_ref):
        low, top = b * span, (b + 1) * span
        states = state_ref.shape[1] // 2
        lower = jnp.where(iota((span, span), 0) >= iota((span, span), 1), 1.0, 0.0)
        self.rows = slice(low, top)
        self.step = step_col[low:top]
        self.step_row = step_row[:, low:top]
        self.cum = mm_exact(lower, rate_col[low:top])
        self.cum_row = mm_exact(rate_row[:, low:top], lower, (1, 1))
        self.inputs = state_ref[low:top, :states].astype(bf16)
        self.outputs = state_ref[low:top, states:].astype(bf16)
        segment = segment_of(iota((span, 1), 0) + low, ends)
        segment_row = segment_of(iota((1, span), 1) + low, ends)
        edge = sum(jnp.where(span - 1 >= end, 1, 0) for end in ends)
        self.near_edge = jnp.where(segment == edge, 1.0, 0.0)
        self.mask = jnp.where(segment == segment_row, lower, 0.0)
        self.contact = mm(self.outputs, self.inputs, (1, 1)) * self.mask

    def decay(self, h, at):
        end = at + span // 2
        gap = self.cum[at:end, h : h + 1] - self.cum_row[h : h + 1, :end]
        return jnp.exp(jnp.minimum(gap, 0.0)), self.contact[at:end, :end]

    def mix(self, h, x_step):
        parts = []
        for at in (0, span // 2):
            decay, contact = self.decay(h, at)
            parts.append(mm((decay * contact).astype(bf16), x_step[: at + span // 2]))
        return jnp.concatenate(parts, axis=0)

    def from_edge(self, h):
        return jnp.exp(self.cum[:, h : h + 1]) * self.near_edge

    def to_edge(self, h):
        last = self.cum[span - 1 : span, h : h + 1]
        return jnp.exp(last - self.cum[:, h : h + 1]) * self.near_edge


def wide(low_half, left, right):
    return jnp.where(low_half, left, right)


def step_sizes(raw_col, raw_row, bias_ref, bias_col_ref, log_ref, log_col_ref):
    def soft(v):
        return jnp.maximum(v, 0.0) + jnp.log1p(jnp.exp(-jnp.abs(v)))

    step_col = soft(raw_col + bias_ref[...])
    step_row = soft(raw_row + bias_col_ref[...])
    rate_col = -step_col * jnp.exp(log_ref[...])
    rate_row = -step_row * jnp.exp(log_col_ref[...])
    return step_col, step_row, rate_col, rate_row


def forward_kernel(fast, place_ref, lengths_ref, *refs):
    n_msg = 8 if fast else 4
    n_rows = 4 if fast else 1
    row_refs, msg_refs, refs = refs[:n_rows], refs[n_rows : n_rows + n_msg], refs[n_rows + n_msg :]
    taps_ref, bias_ref = refs[:2]
    (
        normed_ref,
        turned_ref,
        weight_ref,
        state_weight_ref,
        step_weight_ref,
        small_ref,
        raw_ref,
        state_raw_ref,
        step_col_ref,
        step_row_ref,
        act_ref,
        state_ref,
    ) = refs[2:14]
    mask_ref, state_taps_ref, state_bias_ref = refs[14:]
    total, channels = act_ref.shape
    ends = ends_of(lengths_ref)

    if fast:
        depth_part = 128
        small = jnp.zeros(small_ref.shape, f32)
        share = state_weight_ref.shape[0] // 32
        for slot in range(8):
            msg = msg_refs[slot]
            index = place_ref[slot]
            at = pl.multiple_of(index * depth_part, depth_part)
            weight_ref[pl.ds(at, depth_part), :] = msg[:depth_part, :]
            for member in range(4):
                inner = pl.multiple_of(at + place_ref[8 + member] * share, share)
                high, low = depth_part + share * (member // 2), 256 * (member % 2)
                state_weight_ref[pl.ds(inner, share), :] = msg[
                    high : high + share, low : low + 256
                ]
            tail = depth_part + 2 * share
            small = small + msg[tail : tail + 16, :256].astype(f32)
            step_weight_ref[:, pl.ds(at, depth_part)] = msg[tail : tail + 16, 256:384]
        small_ref[...] = small
    else:
        weight_ref[...] = msg_refs[0][...]
        state_weight_ref[...] = msg_refs[1][...]
        step_weight_ref[...] = msg_refs[2][...]
        small_ref[...] = msg_refs[3][...].astype(f32)
    gain = jnp.concatenate([small_ref[i : i + 1, :] for i in range(4)], axis=1)
    taps = taps_ref.shape[0]
    state_taps_ref[...] = small_ref[4 : 4 + taps, :]
    state_bias_ref[...] = small_ref[4 + taps : 5 + taps, :]

    tall = total // n_rows
    for member in range(n_rows):
        at = pl.multiple_of(place_ref[8 + member] * tall, tall) if fast else 0
        value = row_refs[member][:tall, :].astype(f32)
        scale = lax.rsqrt(jnp.mean(value * value, axis=1, keepdims=True) + epsilon)
        normed = (value * scale * gain).astype(bf16)
        normed_ref[pl.ds(at, tall), :] = normed
        turned_ref[:, pl.ds(at, tall)] = normed.astype(f32).T.astype(bf16)

    raw_ref[:pad, :] = jnp.zeros((pad, channels), f32)
    state_raw_ref[:pad, :] = jnp.zeros((pad, state_raw_ref.shape[1]), f32)

    def project(at):
        part = normed_ref[pl.ds(at, 128), :]
        raw_ref[pl.ds(at + pad, 128), :] = mm(part, weight_ref[...])
        state_raw_ref[pl.ds(at + pad, 128), :] = mm(part, state_weight_ref[...])
        step_col_ref[pl.ds(at, 128), :] = mm(part, step_weight_ref[...], (1, 1))

    row_loop(total, 128, project)
    step_row_ref[...] = mm(step_weight_ref[...], normed_ref[...], (1, 1))

    write_masks(mask_ref, ends)

    def activate(x_ref, out_ref, own_taps, own_bias):
        def column(cols):
            for at in range(0, total, 128):
                pre, _ = conv_pre(x_ref, mask_ref, own_taps, own_bias, at, cols, 128)
                out_ref[at : at + 128, cols] = pre * sigmoid(pre)

        column_loop(out_ref.shape[1], column)

    activate(raw_ref, act_ref, taps_ref, bias_ref)
    activate(state_raw_ref, state_ref, state_taps_ref, state_bias_ref)


def scan_kernel(lengths_ref, *refs):
    act_ref, state_ref, step_col_ref, step_row_ref = refs[:4]
    step_bias_ref, step_bias_col_ref, log_ref, log_col_ref, skip_ref, mixed_ref = refs[4:]
    total, channels = act_ref.shape
    ends = ends_of(lengths_ref)
    steps = step_sizes(
        step_col_ref[...],
        step_row_ref[...],
        step_bias_ref,
        step_bias_col_ref,
        log_ref,
        log_col_ref,
    )
    low_half = iota((span, 128), 1) < head_width
    held = []
    for b in range(total // span):
        block = Block(b, ends, *steps, state_ref)
        for i in range(channels // 128):
            cols = slice(128 * i, 128 * (i + 1))
            pair = (2 * i, 2 * i + 1)
            x = act_ref[block.rows, cols]
            step_wide = wide(low_half, *(block.step[:, h : h + 1] for h in pair))
            x_step = (x * step_wide).astype(bf16)
            y = [block.mix(h, x_step) for h in pair]
            y = wide(low_half, *y) + skip_ref[:, cols] * x
            if b == 0:
                reach = wide(low_half, *(block.to_edge(h) for h in pair))
                weighted = (x * step_wide * reach).astype(bf16)
                held.append(mm(block.inputs, weighted, (0, 0)).astype(bf16))
            else:
                reach = wide(low_half, *(block.from_edge(h) for h in pair))
                y = y + reach * mm(block.outputs, held[i])
            mixed_ref[block.rows, cols] = y


def grad_in_kernel(fast, place_ref, lengths_ref, *refs):
    n_rows = 4 if fast else 1
    n_msg = 8 if fast else 2
    row_refs, msg_refs, refs = refs[:n_rows], refs[n_rows : n_rows + n_msg], refs[n_rows + n_msg :]
    normed_ref, mixed_ref, norm_ref = refs[:3]
    rows_ref, gate_weight_ref, out_weight_ref, gate_ref, grad_ref, sums_ref, wide_ref = refs[3:]
    total = rows_ref.shape[0]
    ends = ends_of(lengths_ref)
    tall = total // n_rows
    for member in range(n_rows):
        at = pl.multiple_of(place_ref[8 + member] * tall, tall) if fast else 0
        rows_ref[pl.ds(at, tall), :] = row_refs[member][-tall:, :]
    if fast:
        for slot in range(8):
            at = pl.multiple_of(place_ref[slot] * 128, 128)
            gate_weight_ref[pl.ds(at, 128), :] = msg_refs[slot][:128, :]
            out_weight_ref[pl.ds(at, 128), :] = msg_refs[slot][128:, :]
    else:
        gate_weight_ref[...] = msg_refs[0][...]
        out_weight_ref[...] = msg_refs[1][...]

    def part(at):
        rows = pl.ds(at, 128)
        valid = jnp.where(iota((128, 1), 0) + at < ends[-1], 1.0, 0.0)
        grad = mm(rows_ref[rows, :], out_weight_ref[...]) * valid
        grad_ref[rows, :] = grad
        gate = mm(normed_ref[rows, :], gate_weight_ref[...])
        gate_ref[rows, :] = gate
        gated = mixed_ref[rows, :] * (gate * sigmoid(gate))
        square = jnp.sum(gated * gated, axis=1, keepdims=True)
        cross = jnp.sum(grad * norm_ref[...] * gated, axis=1, keepdims=True)
        lane = iota((128, 128), 1)
        wide_ref[rows, :] = jnp.where(lane == 0, square, jnp.where(lane == 1, cross, 0.0))

    row_loop(total, 128, part)
    for at in range(0, total, 128):
        sums_ref[:, at : at + 128] = wide_ref[at : at + 128, :].T[:8, :]


def norm_kernel(inner_total, place_ref, lengths_ref, *refs):
    n_sums = len(refs) - 21
    sums_refs, refs = refs[:n_sums], refs[n_sums:]
    gate_ref, mixed_ref, grad_ref, norm_ref, weight_ref, rows_ref, turned_ref = refs[:7]
    chunk_refs = refs[7:15]
    partial_ref, grad_gate_ref, grad_mixed_ref, norm_grad_ref = refs[15:19]
    wide_ref, out_rows_ref = refs[19:]
    total, channels = gate_ref.shape
    ends = ends_of(lengths_ref)
    for at in range(0, total, 128):
        tile = sum(ref[:, at : at + 128] for ref in sums_refs)
        tile = jnp.concatenate([tile] * 16, axis=0)
        wide_ref[at : at + 128, :] = tile.T
    norm_grad_ref[...] = jnp.zeros(norm_grad_ref.shape, f32)

    def part(at):
        rows = pl.ds(at, 128)
        valid = jnp.where(iota((128, 1), 0) + at < ends[-1], 1.0, 0.0)
        scale = lax.rsqrt(wide_ref[rows, 0:1] / inner_total + epsilon)
        cross = wide_ref[rows, 1:2]
        gate = gate_ref[rows, :]
        mixed = mixed_ref[rows, :]
        sig = sigmoid(gate)
        gate_act = gate * sig
        gated = mixed * gate_act
        grad = grad_ref[rows, :]
        norm = norm_ref[...]
        hat = gated * scale
        out_rows_ref[rows, :] = (hat * norm * valid).astype(bf16)
        norm_grad_ref[...] += jnp.sum(grad * hat, axis=0, keepdims=True)
        grad_gated = scale * (grad * norm) - gated * (scale * scale * scale * cross / inner_total)
        grad_mixed_ref[rows, :] = grad_gated * gate_act
        grad_gate = grad_gated * mixed * sig * (1.0 + gate * (1.0 - sig))
        grad_gate_ref[rows, :] = grad_gate.astype(bf16)

    row_loop(total, 128, part)

    def back(at):
        cols = pl.ds(at, 256)
        partial_ref[:, cols] = mm(out_rows_ref[...], weight_ref[cols, :], (1, 1)).astype(bf16)

    row_loop(weight_ref.shape[0], 256, back)
    tall = chunk_refs[0].shape[0] // 2
    for slot, chunk_ref in enumerate(chunk_refs):
        cols = pl.ds(pl.multiple_of(place_ref[slot] * tall, tall), tall)
        chunk_ref[:tall, :] = mm(turned_ref[cols, :], grad_gate_ref[...]).astype(bf16)
        chunk_ref[tall:, :] = mm(rows_ref[:, cols], out_rows_ref[...], (0, 0)).astype(bf16)


def scan_back_kernel(first_pair, lengths_ref, *refs):
    grad_mixed_ref, act_ref, state_ref, step_col_ref, step_row_ref = refs[:5]
    step_bias_ref, step_bias_col_ref, log_ref, log_col_ref, skip_ref = refs[5:10]
    grad_act_ref, grad_state_ref, step_grad_ref, sums_ref, acc_ref = refs[10:]
    total, own_width = grad_act_ref.shape
    states = state_ref.shape[1] // 2
    ends = ends_of(lengths_ref)
    sums_ref[...] = jnp.zeros(sums_ref.shape, f32)
    raw_row = step_row_ref[...]
    steps = step_sizes(
        step_col_ref[...], raw_row, step_bias_ref, step_bias_col_ref, log_ref, log_col_ref
    )
    rate_row = steps[3]
    low_half = iota((span, 128), 1) < head_width
    lower = jnp.where(iota((span, span), 0) >= iota((span, span), 1), 1.0, 0.0)
    blocks = [Block(b, ends, *steps, state_ref) for b in range(total // span)]
    first, second = blocks
    row_sums, step_rows, out_sums, in_sums = [], [], None, None
    grad_out = jnp.zeros((span, states), f32)
    grad_in = jnp.zeros((span, states), f32)
    head_of = iota((head_rows, 128), 0)
    lane_head = iota((head_rows, 128), 1) // head_width

    for b, block in enumerate(blocks):
        acc_ref[...] = jnp.zeros((span, span), f32)
        row_sum = jnp.zeros((span, 128), f32)
        step_grad = jnp.zeros((head_rows, span), f32)
        lane = iota((span, 128), 1)
        head_row = iota((head_rows, span), 0)
        for i in range(first_pair, first_pair + own_width // 128):
            cols = slice(128 * i, 128 * (i + 1))
            own_cols = slice(128 * (i - first_pair), 128 * (i - first_pair + 1))
            pair = (2 * i, 2 * i + 1)
            x = act_ref[block.rows, cols]
            x_low = x.astype(bf16)
            grad = grad_mixed_ref[block.rows, cols]
            grad_low = grad.astype(bf16)
            halves = (
                jnp.where(low_half, grad, 0.0).astype(bf16),
                jnp.where(low_half, 0.0, grad).astype(bf16),
            )
            step_wide = wide(low_half, *(block.step[:, h : h + 1] for h in pair))
            grads = []
            for h, half in zip(pair, halves):
                strips = []
                for at in (0, span // 2):
                    end = at + span // 2
                    decay, contact = block.decay(h, at)
                    spread = mm(half[at:end], x_low[:end], (1, 1)) * decay
                    stepped = spread * block.step_row[h : h + 1, :end]
                    acc_ref[at:end, :end] += stepped
                    row_here = jnp.sum(stepped * contact, axis=1, keepdims=True)
                    step_here = jnp.sum(spread * contact, axis=0, keepdims=True)
                    back = mm((decay * contact).astype(bf16), grad_low[at:end], (0, 0))
                    strips.append((row_here, step_here, back))
                (row_a, step_a, back_a), (row_b, step_b, back_b) = strips
                mid = span // 2
                row_sum = jnp.where(lane == h, jnp.concatenate([row_a, row_b], axis=0), row_sum)
                step_here = [step_a + step_b[:, :mid], step_b[:, mid:]]
                step_here = jnp.concatenate(step_here, axis=1)
                step_grad = jnp.where(head_row == h, step_here, step_grad)
                grads.append(jnp.concatenate([back_a + back_b[:mid], back_b[mid:]], axis=0))
            grad_act = wide(low_half, *grads) * step_wide + skip_ref[:, cols] * grad
            sums_ref[2:3, own_cols] += jnp.sum(grad * x, axis=0, keepdims=True)
            picks = jnp.where(lane_head + 2 * i == head_of, 1.0, 0.0)
            if b == 0:
                reach = wide(low_half, *(second.from_edge(h) for h in pair))
                lead = (grad_mixed_ref[second.rows, cols] * reach).astype(bf16)
                edge = wide(low_half, *(block.to_edge(h) for h in pair))
                weighted = (x * step_wide * edge).astype(bf16)
                held = mm(block.inputs, weighted, (0, 0)).astype(bf16)
                held_grad = mm(second.outputs, lead, (0, 0)).astype(bf16)
                grad_out = grad_out + mm(lead, held, (1, 1))
                grad_in = grad_in + mm(weighted, held_grad, (1, 1))
                back = mm(block.inputs, held_grad) * edge
                grad_act = grad_act + back * step_wide
                ahead = mm(second.outputs, held)
                out_here = mm_exact(picks, lead.astype(f32) * ahead, (1, 1))
                in_here = mm_exact(picks, x * back, (1, 1))
                out_sums = out_here if out_sums is None else out_sums + out_here
                in_sums = in_here if in_sums is None else in_sums + in_here
            grad_act_ref[block.rows, own_cols] = grad_act
        table = (acc_ref[...] * block.mask).astype(bf16)
        grad_c = mm(table, block.inputs)
        grad_b = mm(table, block.outputs, (0, 0))
        if b == 0:
            grad_b = grad_b + grad_in
        else:
            grad_c = grad_c + grad_out
        grad_state_ref[block.rows, :states] = grad_b
        grad_state_ref[block.rows, states:] = grad_c
        row_sums.append(row_sum)
        step_rows.append(step_grad)

    rate_grads = []
    for b, block in enumerate(blocks):
        column = step_rows[b] * block.step_row
        crossing = mm_exact(row_sums[b], lower, (0, 0))[:head_rows] - mm_exact(column, lower)
        if b == 0:
            crossing = crossing + mm_exact(in_sums * block.step_row, 1.0 - lower)
        else:
            crossing = crossing + mm_exact(out_sums, lower)
        rate_grads.append(crossing)
    step_rows[0] = step_rows[0] + in_sums
    rate_grad = jnp.concatenate(rate_grads, axis=1)
    step_grad = jnp.concatenate(step_rows, axis=1) - rate_grad * jnp.exp(log_col_ref[...])
    step_grad = step_grad * sigmoid(raw_row + step_bias_col_ref[...])
    decay_sum = jnp.sum(rate_grad * rate_row, axis=1, keepdims=True)
    bias_sum = jnp.sum(step_grad, axis=1, keepdims=True)
    lane = iota((head_rows, 128), 1)
    head_sums = jnp.where(lane == 0, bias_sum, jnp.where(lane == 1, decay_sum, 0.0))
    head_sums = jnp.concatenate([head_sums] * (128 // head_rows), axis=0).T
    sums_ref[0:2, :128] = head_sums[:2, :]
    step_grad_ref[...] = step_grad


def conv_back(x_ref, mask_ref, grad_ref, held_ref, out_ref, sums_ref, own_taps, own_bias):
    total, taps = out_ref.shape[0], own_taps.shape[0]
    held_ref[total:, :] = jnp.zeros((pad, held_ref.shape[1]), f32)

    def column(cols):
        sums = [jnp.zeros((1, 128), f32) for _ in range(taps + 1)]
        for at in range(0, total, 128):
            pre, shifted = conv_pre(x_ref, mask_ref, own_taps, own_bias, at, cols, 128)
            sig = sigmoid(pre)
            grad = grad_ref[at : at + 128, cols] * sig * (1.0 + pre * (1.0 - sig))
            held_ref[at : at + 128, cols] = grad
            for s in range(taps):
                sums[taps - 1 - s] += jnp.sum(grad * shifted[s], axis=0, keepdims=True)
            sums[taps] += jnp.sum(grad, axis=0, keepdims=True)
        for t, value in enumerate(sums):
            sums_ref[t : t + 1, cols] = value
        for at in range(0, total, 128):
            back = own_taps[taps - 1 : taps, cols] * held_ref[at : at + 128, cols]
            for s in range(1, taps):
                part = held_ref[at + s : at + s + 128, cols]
                part = part * mask_ref[s - 1, at + s : at + s + 128, :]
                back = back + own_taps[taps - 1 - s : taps - s, cols] * part
            out_ref[at : at + 128, cols] = back.astype(bf16)

    column_loop(out_ref.shape[1], column)


def state_back_kernel(fast, place_ref, lengths_ref, *refs):
    state_refs, step_refs, refs = refs[0:2], refs[2:4], refs[4:]
    state_raw_ref, turned_ref, small_ref, grad_state_low_ref, step_low_ref = refs[:5]
    n_out = 4 if fast else 2
    out_refs, refs = refs[5 : 5 + n_out], refs[5 + n_out :]
    mask_ref, taps_ref, bias_ref, grad_state_ref, pre_ref, part_ref, sums_ref = refs
    taps = taps_ref.shape[0]
    taps_ref[...] = small_ref[4 : 4 + taps, :]
    bias_ref[...] = small_ref[4 + taps : 5 + taps, :]
    write_masks(mask_ref, ends_of(lengths_ref))
    grad_state_ref[...] = state_refs[0][...] + state_refs[1][...]
    step_low_ref[...] = (step_refs[0][...] + step_refs[1][...]).astype(bf16)
    sums_ref[...] = jnp.zeros(sums_ref.shape, f32)
    conv_back(
        state_raw_ref,
        mask_ref,
        grad_state_ref,
        pre_ref,
        grad_state_low_ref,
        sums_ref,
        taps_ref,
        bias_ref,
    )

    def chunk(at):
        part = turned_ref[pl.ds(at, 256), :]
        part_ref[pl.ds(at, 256), :] = mm(part, grad_state_low_ref[...]).astype(bf16)

    depth = turned_ref.shape[0]
    row_loop(depth, 256, chunk)
    if fast:
        share = depth // 32
        for member, out_ref in enumerate(out_refs):
            for c in range(8):
                at = pl.multiple_of((4 * c + place_ref[8 + member]) * share, share)
                out_ref[share * c : share * (c + 1), :] = part_ref[pl.ds(at, share), :]
            out_ref[8 * share :, :] = sums_ref[...].astype(bf16)
    else:
        out_refs[0][...] = part_ref[...]
        out_refs[1][...] = sums_ref[...]


def inner_back_kernel(lengths_ref, *refs):
    act_refs, head_refs, refs = refs[0:2], refs[2:4], refs[4:]
    raw_ref, norm_grad_ref, taps_ref, bias_ref, grad_inner_ref, sums_ref = refs[:6]
    mask_ref, grad_act_ref, pre_ref = refs[6:]
    half = grad_inner_ref.shape[1] // 2
    write_masks(mask_ref, ends_of(lengths_ref))
    grad_act_ref[:, :half] = act_refs[0][...]
    grad_act_ref[:, half:] = act_refs[1][...]
    sums_ref[...] = jnp.zeros(sums_ref.shape, f32)
    heads = head_refs[0][:2, :128] + head_refs[1][:2, :128]
    sums_ref[5:6, :] = norm_grad_ref[...]
    sums_ref[6:7, :half] = head_refs[0][2:3, :]
    sums_ref[6:7, half:] = head_refs[1][2:3, :]
    sums_ref[9:10, half : half + 128] = heads[0:1, :]
    sums_ref[9:10, half + 128 :] = heads[1:2, :]
    conv_back(
        raw_ref,
        mask_ref,
        grad_act_ref,
        pre_ref,
        grad_inner_ref,
        sums_ref,
        taps_ref,
        bias_ref,
    )


def message_kernel(grad_inner_ref, step_low_ref, turned_ref, msg_ref):
    chunks = msg_ref.shape[0]
    tall = turned_ref.shape[0] // chunks
    step_low = step_low_ref[...]

    def chunk(c, carry):
        part = turned_ref[pl.ds(pl.multiple_of(c * tall, tall), tall), :]
        msg_ref[c, :tall, :] = mm(part, grad_inner_ref[...]).astype(bf16)
        msg_ref[c, tall:, :tall] = mm(step_low, part, (1, 1)).astype(bf16)
        msg_ref[c, tall:, tall:] = jnp.zeros((head_rows, msg_ref.shape[2] - tall), bf16)
        return carry

    lax.fori_loop(0, chunks, chunk, 0)


def chunk_kernel(slots, n_got, place_ref, *refs):
    grad_inner_ref, step_low_ref, sums_ref = refs[:3]
    state_refs, turned_refs, got_refs = refs[3:7], refs[7:9], refs[9 : 9 + n_got]
    out_refs = refs[9 + n_got :]
    states = state_refs[0].shape[1]
    share = (state_refs[0].shape[0] - 16) // 8

    def state_rows(low, tall):
        return sum(ref[pl.ds(low, tall), :].astype(f32) for ref in state_refs)

    shared = state_rows(8 * share, 16)
    sums = [
        sums_ref[:7, :],
        jnp.concatenate([shared[0:1, :], shared[1:2, :]], axis=1),
        jnp.concatenate([shared[2:3, :], shared[3:4, :]], axis=1),
        jnp.concatenate([shared[4:5, :], sums_ref[9:10, states:]], axis=1),
    ]
    tall = turned_refs[0].shape[0]
    parts = jnp.concatenate([ref[...] for ref in turned_refs], axis=0)
    products = mm(parts, grad_inner_ref[...])
    for n, (slot, out_ref) in enumerate(zip(slots, out_refs)):
        index = place_ref[slot]
        part = parts[tall * n : tall * (n + 1), :]
        step = mm(step_low_ref[...], part, (1, 1))
        step = [
            jnp.concatenate([step[4 * k + i : 4 * k + i + 1, :] for i in range(4)], axis=1)
            for k in range(2)
        ]
        state = state_rows(pl.multiple_of(index * share, share), share)
        value = jnp.concatenate(
            [
                products[tall * n : tall * (n + 1), :],
                jnp.concatenate([state[:16, :], state[16:, :]], axis=1),
                *sums,
                *step,
                jnp.zeros((4, 2 * states), f32),
            ],
            axis=0,
        )
        tail = value.shape[0] - 16
        main, sums_here = value[:tail, :], value[tail:, :]
        if n < n_got:
            got = got_refs[n]
            main = main + got[:tail, :].astype(f32)
            sums_here = sums_here + got[tail : tail + 16, :].astype(f32)
            sums_here = sums_here + got[tail + 16 :, :].astype(f32)
        out_ref[:tail, :] = main.astype(out_ref.dtype)
        high = sums_here.astype(bf16)
        out_ref[tail : tail + 16, :] = high.astype(out_ref.dtype)
        out_ref[tail + 16 :, :] = (sums_here - high.astype(f32)).astype(out_ref.dtype)


def finish_kernel(*refs):
    own_ref, got_ref, gate_ref, input_ref, step_rows_ref, state_ref = refs[:6]
    input_grad_ref, step_grad_ref, state_grad_ref, sums_ref, gain_ref, state_gain_ref = refs[6:]
    tall = input_ref.shape[0]
    states = state_ref.shape[1]
    heads = step_grad_ref.shape[1]
    inner = own_ref[:tall, :] + got_ref[:tall, :].astype(f32)
    gate = gate_ref[...]
    input_grad_ref[:, 0, :] = gate
    input_grad_ref[:, 1, :] = inner
    state = own_ref[tall : tall + 16, :] + got_ref[tall : tall + 16, :].astype(f32)
    state = jnp.concatenate([state[:, :states], state[:, states:]], axis=0)
    state_grad_ref[...] = state
    sums = own_ref[tall + 16 : tall + 32, :] + own_ref[tall + 32 :, :]
    sums = sums + got_ref[tall + 16 : tall + 32, :].astype(f32)
    sums = sums + got_ref[tall + 32 :, :].astype(f32)
    sums_ref[...] = sums
    step = [sums[10 + h // 4 : 11 + h // 4, 128 * (h % 4) : 128 * (h % 4 + 1)] for h in range(heads)]
    step = jnp.concatenate(step, axis=0)
    along = input_ref[:, 0, :].astype(f32) * gate + input_ref[:, 1, :].astype(f32) * inner
    gain = mm_exact(jnp.ones((8, along.shape[1]), f32), along, (1, 1))
    over = jnp.sum(step_rows_ref[:heads, :].astype(f32) * step, axis=0, keepdims=True)
    gain_ref[...] = gain + over
    along = state_ref[...].astype(f32) * state
    state_gain_ref[...] = mm_exact(jnp.ones((8, states), f32), along, (1, 1))
    step = jnp.concatenate([step, jnp.zeros((128 - heads, 128), f32)], axis=0).T
    step_grad_ref[...] = step[:, :heads]


def project_back_kernel(fast, place_ref, *refs):
    grad_refs, step_low_ref, weight_refs, step_weight_ref = refs[:3], refs[3], refs[4:7], refs[7]
    out_refs, held_refs, step_ref = refs[8:10], refs[10:13], refs[13]
    for n, member in enumerate((0, 2, 1, 3)):
        at = pl.multiple_of(place_ref[8 + member] * 128, 128) if fast else 128 * member
        for held_ref, grad_ref in zip(held_refs, grad_refs):
            held_ref[128 * n : 128 * (n + 1), :] = grad_ref[pl.ds(at, 128), :]
        step_ref[:, 128 * n : 128 * (n + 1)] = step_low_ref[:, pl.ds(at, 128)]

    def back(at):
        cols = pl.ds(at, 256)
        grad = mm(step_ref[...], step_weight_ref[:, cols], (0, 0))
        for held_ref, weight_ref in zip(held_refs, weight_refs):
            grad = grad + mm(held_ref[...], weight_ref[cols, :], (1, 1))
        grad = grad.astype(bf16)
        for n in range(4):
            out_refs[n // 2][n % 2, :, cols] = grad[128 * n : 128 * (n + 1), :]

    row_loop(step_weight_ref.shape[1], 256, back)


def prepare_kernel(place_ref, *refs):
    gain_ref, taps_ref, bias_ref, state_ref, step_ref, input_ref, out_ref = refs[:7]
    shared_ref, step_rows_ref, late_ref = refs[7:]
    owner = place_ref[0]
    share, states = state_ref.shape
    shared_ref[:share, :] = state_ref[...]

    def placed(value, at):
        width = value.shape[1]
        pick = iota((width, states), 1) - at == iota((width, states), 0)
        return mm(value, jnp.where(pick, 1.0, 0.0).astype(bf16))

    start = owner * gain_ref.shape[1]
    small = jnp.concatenate(
        [placed(gain_ref[...], start - states * i) for i in range(4)]
        + [placed(taps_ref[...], owner * taps_ref.shape[1])]
        + [placed(bias_ref[...], owner * bias_ref.shape[1])]
        + [jnp.zeros((7, states), f32)],
        axis=0,
    )
    shared_ref[share:, :] = small.astype(bf16)
    depth_part, heads = step_ref.shape
    step = step_ref[...].astype(f32)
    step = jnp.concatenate([step, jnp.zeros((depth_part, 128 - heads), f32)], axis=1).T
    step_rows_ref[...] = step[:head_rows, :].astype(bf16)
    late_ref[:depth_part, :] = input_ref[:, 0, :]
    late_ref[depth_part:, :] = out_ref[...].astype(f32).T.astype(bf16)


def params_kernel(*refs):
    taps_ref, bias_ref, step_bias_ref, log_ref, skip_ref, norm_ref = refs[:6]
    outs = refs[6:]
    heads = step_bias_ref.shape[1]
    pick = jnp.where(iota((heads, head_rows), 0) == iota((heads, head_rows), 1), 1.0, 0.0)
    square = iota((head_rows, head_rows), 0) == iota((head_rows, head_rows), 1)

    def both(value_ref, row_ref, col_ref):
        row = mm_exact(value_ref[...].astype(f32), pick)
        row_ref[...] = row
        col_ref[...] = jnp.sum(jnp.where(square, row, 0.0), axis=1, keepdims=True)

    outs[0][...] = taps_ref[...].astype(f32)
    outs[1][...] = bias_ref[...].astype(f32)
    both(step_bias_ref, outs[2], outs[3])
    both(log_ref, outs[4], outs[5])
    channels = norm_ref.shape[1]
    own = iota((heads, channels), 1) // (channels // heads) == iota((heads, channels), 0)
    outs[6][...] = mm_exact(skip_ref[...].astype(f32), jnp.where(own, 1.0, 0.0))
    outs[7][...] = norm_ref[...].astype(f32)


def assemble_kernel(input_ref, step_ref, *refs):
    shared_refs, msg_ref = refs[:4], refs[4]
    depth_part, _, channels = input_ref.shape
    share = shared_refs[0].shape[0] - 16
    tail = depth_part + 2 * share
    msg_ref[:depth_part, :] = input_ref[:, 1, :]
    for member, ref in enumerate(shared_refs):
        high, low = depth_part + share * (member // 2), 256 * (member % 2)
        msg_ref[high : high + share, low : low + 256] = ref[:share, :]
    small = sum(ref[share:, :].astype(f32) for ref in shared_refs)
    msg_ref[tail:, :256] = small.astype(bf16)
    msg_ref[tail:, 256:384] = step_ref[...]
    msg_ref[tail:, 384:] = jnp.zeros((16, channels - 384), bf16)


def call(kernel, micros, scalars, arrays, outs, scratch):
    smem = pl.BlockSpec(memory_space=pltpu.SMEM)
    vmem = pl.BlockSpec(memory_space=pltpu.VMEM)
    return pl.pallas_call(
        kernel,
        out_shape=[jax.ShapeDtypeStruct(shape, kind) for shape, kind in outs],
        in_specs=[smem] * len(scalars) + [vmem] * len(arrays),
        out_specs=[vmem] * len(outs),
        scratch_shapes=[pltpu.VMEM(shape, kind) for shape, kind in scratch],
        compiler_params=pltpu.CompilerParams(vmem_limit_bytes=vmem_bytes),
        cost_estimate=pl.CostEstimate(
            flops=int(micros * 1.1e9), bytes_accessed=1 << 20, transcendentals=0
        ),
    )(*scalars, *arrays)


def ring_ok(n_dp, n_tensor):
    return n_dp == 8 and n_tensor == 4


ring_order = (0, 2, 4, 6, 7, 5, 3, 1)


def ring_place(index):
    high, low = index // 2, index % 2
    return jnp.where(low == 0, high, 7 - high)


def ring_index(place):
    place = lax.rem(place + 16, 8)
    return jnp.where(place < 4, 2 * place, 2 * (7 - place) + 1)


def ring_send(value, forward):
    pairs = []
    for place in range(8):
        other = (place + (1 if forward else 7)) % 8
        pairs.append((ring_order[place], ring_order[other]))
    return lax.ppermute(value, "dp", pairs)


def ring_gather(value):
    me = ring_place(lax.axis_index("dp"))
    pieces = [(value, ring_index(me))]
    ahead, back = value, value
    for step in range(1, 5):
        ahead = ring_send(ahead, True)
        pieces.append((ahead, ring_index(me - step)))
        if step < 4:
            back = ring_send(back, False)
            pieces.append((back, ring_index(me + step)))
    return pieces


def dp_swap(value, bit):
    return lax.ppermute(value, "dp", [(i, i ^ bit) for i in range(8)])


def ring_step(held):
    return ring_send(held[0], True), ring_send(held[1], False)


def add_low(got, own):
    return (got.astype(f32) + own.astype(f32)).astype(bf16)


def ordered(first, then):
    return lax.optimization_barrier((first, then))


def tensor_gather(value):
    near = tensor_swap(value, 1)
    far = tensor_swap(value, 2)
    return [value, near, far, tensor_swap(far, 1)]


def tensor_direct(value):
    return [value] + [tensor_swap(value, bit) for bit in range(1, 4)]


def tensor_sum(value, depth):
    parts = value.reshape(4, -1, depth)
    parts = lax.all_to_all(parts, "tensor", 0, 0, tiled=True)
    return jnp.sum(parts.astype(f32), axis=0)


def tensor_swap(value, bit):
    return lax.ppermute(value, "tensor", [(i, i ^ bit) for i in range(4)])


def body(
    tokens,
    lengths,
    cotangent,
    pre_gain,
    input_weight,
    step_weight,
    state_weight,
    conv_inner,
    conv_inner_bias,
    conv_state,
    conv_state_bias,
    step_bias,
    decay_log,
    skip_gain,
    norm_gain,
    output_weight,
):
    n_dp, n_tensor = lax.axis_size("dp"), lax.axis_size("tensor")
    fast = ring_ok(n_dp, n_tensor)
    owners = n_dp * n_tensor
    me = lax.axis_index("tensor")
    owner = lax.axis_index("dp") * n_tensor + me
    own_rows, depth = tokens.shape
    total = own_rows * n_tensor
    states = state_weight.shape[1]
    heads = step_weight.shape[1]
    share = state_weight.shape[0]
    taps = conv_state.shape[0]
    channels = input_weight.shape[2]
    inner_total = channels * n_tensor

    owner_place = jnp.stack([owner, owners]).astype(jnp.int32)
    shared, step_rows, late = call(
        prepare_kernel,
        3,
        [owner_place],
        [
            pre_gain[None, :],
            conv_state,
            conv_state_bias[None, :],
            state_weight,
            step_weight,
            input_weight,
            output_weight,
        ],
        [
            ((share + 16, states), bf16),
            ((head_rows, step_weight.shape[0]), bf16),
            ((input_weight.shape[0] + output_weight.shape[1], channels), bf16),
        ],
        [],
    )
    params = call(
        params_kernel,
        1,
        [],
        [
            conv_inner,
            conv_inner_bias[None, :],
            step_bias[None, :],
            decay_log[None, :],
            skip_gain[None, :],
            norm_gain[None, :],
        ],
        [
            ((taps, channels), f32),
            ((1, channels), f32),
            ((1, head_rows), f32),
            ((head_rows, 1), f32),
            ((1, head_rows), f32),
            ((head_rows, 1), f32),
            ((1, channels), f32),
            ((1, channels), f32),
        ],
        [],
    )
    params = list(params)
    conv_params, head_params, norm_row = params[:2], params[2:7], params[7]
    if fast:
        shared = tensor_direct(shared)
        late_one = ring_step((late, late))
        (msg,) = call(
            assemble_kernel,
            1,
            [],
            [input_weight, step_rows, *shared],
            [((input_weight.shape[0] + 2 * share + 16, channels), bf16)],
            [],
        )
        msg = ring_gather(msg)
        weight_pieces = [piece for piece, _ in msg]
        late_two = ring_step(late_one)
        late_three = ring_step(late_two)
        late_pieces = [late, *late_one, *late_two, *late_three]
        own_rows_both = jnp.concatenate([tokens, cotangent], axis=0)
        row_pieces = tensor_gather(ordered(shared, own_rows_both)[1])
        grad_pieces = row_pieces
        place = jnp.stack([index for _, index in msg] + [me, me ^ 1, me ^ 2, me ^ 3])
    else:
        row_pieces = [lax.all_gather(tokens, "tensor", axis=0, tiled=True)]
        grad_pieces = [lax.all_gather(cotangent, "tensor", axis=0, tiled=True)]
        gate_weight, inner_weight = late[: input_weight.shape[0]], input_weight[:, 1]
        weight_pieces = [
            lax.all_gather(inner_weight, "dp", axis=0, tiled=True),
            lax.all_gather(state_weight, ("dp", "tensor"), axis=0, tiled=True),
            lax.all_gather(step_rows, "dp", axis=1, tiled=True),
            lax.psum(shared[share:], ("dp", "tensor")),
        ]
        late_pieces = [
            lax.all_gather(gate_weight, "dp", axis=0, tiled=True),
            lax.all_gather(late[input_weight.shape[0] :], "dp", axis=0, tiled=True),
        ]
        place = jnp.concatenate([jnp.arange(8), jnp.arange(4)])
    place = place.astype(jnp.int32)

    masks = ((taps - 1, total + pad, 128), f32)
    state_taps = [((taps, states), f32), ((1, states), f32)]
    (
        normed,
        turned,
        inner_full,
        state_full,
        step_full,
        small_full,
        raw,
        state_raw,
        step_col,
        step_row,
        act,
        state_act,
    ) = call(
        functools.partial(forward_kernel, fast),
        6,
        [place, lengths],
        row_pieces + weight_pieces + conv_params,
        [
            ((total, depth), bf16),
            ((depth, total), bf16),
            ((depth, channels), bf16),
            ((depth, states), bf16),
            ((head_rows, depth), bf16),
            ((16, states), f32),
            ((total + pad, channels), f32),
            ((total + pad, states), f32),
            ((total, head_rows), f32),
            ((head_rows, total), f32),
            ((total, channels), f32),
            ((total, states), f32),
        ],
        [masks] + state_taps,
    )
    if fast:
        late_three, act = ordered(late_three, act)
        late_pieces[5:7] = late_three
        late_pieces.append(ring_send(late_three[0], True))
    (mixed,) = call(
        scan_kernel,
        5,
        [lengths],
        [act, state_act, step_col, step_row] + head_params,
        [((total, channels), f32)],
        [],
    )
    grad_rows, gate_full, output_full, gate, grad_normalized, sums = call(
        functools.partial(grad_in_kernel, fast),
        5,
        [place, lengths],
        grad_pieces + late_pieces + [normed, mixed, norm_row],
        [
            ((total, depth), bf16),
            ((depth, channels), bf16),
            ((depth, channels), bf16),
            ((total, channels), f32),
            ((total, channels), f32),
            ((8, total), f32),
        ],
        [((total, 128), f32)],
    )
    if fast:
        sums = tensor_direct(sums)
    else:
        sums = [lax.psum(sums, "tensor")]
    chunks = 8
    tall = depth // chunks
    norm_outs = call(
        functools.partial(norm_kernel, inner_total),
        9,
        [place, lengths],
        [*sums, gate, mixed, grad_normalized, norm_row, output_full, grad_rows, turned],
        [((2 * tall, channels), bf16)] * chunks
        + [
            ((total, depth), bf16),
            ((total, channels), bf16),
            ((total, channels), f32),
            ((1, channels), f32),
        ],
        [((total, 128), f32), ((total, channels), bf16)],
    )
    gate_chunks = norm_outs[:chunks]
    partial_out, grad_gate, grad_mixed, norm_grad = norm_outs[chunks:]

    def scan_back(first_pair, grad):
        return call(
            functools.partial(scan_back_kernel, first_pair),
            6,
            [lengths],
            [grad, act, state_act, step_col, step_row] + head_params,
            [
                ((total, channels // 2), f32),
                ((total, states), f32),
                ((head_rows, total), f32),
                ((8, channels // 2), f32),
            ],
            [((span, span), f32)],
        )

    if fast:
        got = ring_step((gate_chunks[7], gate_chunks[5]))
        held = add_low(got[0], gate_chunks[6]), add_low(got[1], gate_chunks[3])
    first = scan_back(0, grad_mixed)
    if fast:
        held, grad_mixed = ordered(held, grad_mixed)
        got = ring_step(held)
        held = add_low(got[0], gate_chunks[4]), add_low(got[1], gate_chunks[1])
    second = scan_back(channels // 256, grad_mixed)
    if fast:
        held, state_raw = ordered(held, state_raw)
        got = ring_step(held)
        held, last = add_low(got[0], gate_chunks[2]), got[1]
    share_rows = depth // 4 + 16
    state_outs = call(
        functools.partial(state_back_kernel, fast),
        4,
        [place, lengths],
        [first[1], second[1], first[2], second[2], state_raw, turned, small_full],
        [((total, states), bf16), ((head_rows, total), bf16)]
        + (
            [((share_rows, states), bf16)] * 4
            if fast
            else [((depth, states), bf16), ((16, states), f32)]
        ),
        [
            masks,
            *state_taps,
            ((total, states), f32),
            ((total + pad, states), f32),
            ((depth, states), bf16),
            ((16, states), f32),
        ],
    )
    grad_state_low, step_low = state_outs[:2]
    state_parts = state_outs[2:]
    if fast:
        state_parts = [state_parts[0]] + [tensor_swap(state_parts[i], i) for i in range(1, 4)]
    if fast:
        (held, last), raw = ordered((held, last), raw)
        gate_out = gate_chunks[0].astype(f32) + last.astype(f32)
        gate_out = gate_out + ring_send(held, True).astype(f32)
    grad_inner, sums = call(
        inner_back_kernel,
        6,
        [lengths],
        [first[0], second[0], first[3], second[3], raw, norm_grad] + conv_params,
        [((total, channels), bf16), ((16, channels), f32)],
        [masks, ((total, channels), f32), ((total + pad, channels), f32)],
    )
    if fast:
        mixed_rows = tensor_sum(partial_out, depth)
        (gate_out, mixed_rows), grad_inner = ordered((gate_out, mixed_rows), grad_inner)

    def project_back():
        return call(
            functools.partial(project_back_kernel, fast),
            6,
            [place],
            [
                grad_gate,
                grad_inner,
                grad_state_low,
                step_low,
                gate_full,
                inner_full,
                state_full,
                step_full,
            ],
            [((2, 128, depth), bf16)] * 2,
            [
                ((total, channels), bf16),
                ((total, channels), bf16),
                ((total, states), bf16),
                ((head_rows, total), bf16),
            ],
        )

    def chunk_pair(slots, got, after=None, last=bf16):
        grad = grad_inner if after is None else ordered(after, grad_inner)[1]
        arrays = [grad, step_low, sums, *state_parts, turned, turned, *got]

        def whole(array):
            return pl.BlockSpec(array.shape, lambda i, place: (0, 0))

        def block(slot):
            return pl.BlockSpec((tall, total), lambda i, place: (place[slot], 0))

        specs = [whole(array) for array in arrays]
        specs[7:9] = [block(slot) for slot in slots]
        out = pl.BlockSpec((tall + 48, channels), lambda i, place: (0, 0))
        return pl.pallas_call(
            functools.partial(chunk_kernel, slots, len(got)),
            grid_spec=pltpu.PrefetchScalarGridSpec(
                num_scalar_prefetch=1, grid=(1,), in_specs=specs, out_specs=[out, out]
            ),
            out_shape=[
                jax.ShapeDtypeStruct((tall + 48, channels), kind) for kind in (bf16, last)
            ],
            compiler_params=pltpu.CompilerParams(vmem_limit_bytes=vmem_bytes),
            cost_estimate=pl.CostEstimate(
                flops=2_000_000_000, bytes_accessed=1 << 20, transcendentals=0
            ),
        )(place, *arrays)

    if fast:
        got = ring_step(chunk_pair((7, 5), ()))
        keep_rows, give_rows = project_back()
        got = ring_step(chunk_pair((6, 3), got, give_rows))
        got = ring_step(chunk_pair((4, 1), got))
        held, inner_own = chunk_pair((2, 0), got, last=f32)
        inner_got = ring_send(held, True)
    else:
        (inner_msg,) = call(
            message_kernel,
            5,
            [],
            [grad_inner, step_low, turned],
            [((chunks, tall + head_rows, channels), bf16)],
            [],
        )
        keep_rows, give_rows = project_back()

    token_float = tokens.astype(f32)
    gain_full = small_full[: depth // states].reshape(1, depth)

    if fast:
        got = tensor_swap(give_rows, 1)
        far = tensor_swap(add_low(keep_rows[1], got[1]), 2)
        grad_local = keep_rows[0].astype(f32) + got[0].astype(f32) + far.astype(f32)
        gate_grad, output_grad = gate_out[:tall], gate_out[tall:].T
        input_grad, step_grad, state_grad, sums, own_gain, state_gain = call(
            finish_kernel,
            2,
            [],
            [inner_own, inner_got, gate_grad, input_weight, step_rows, state_weight],
            [
                (input_weight.shape, f32),
                (step_weight.shape, f32),
                (state_weight.shape, f32),
                ((16, channels), f32),
                ((8, tall), f32),
                ((8, share), f32),
            ],
            [],
        )
        own_gain, state_gain = sum(tensor_direct(own_gain))[0], state_gain[0]
        own_gain = lax.dynamic_slice(own_gain, (me * share,), (share,))
        width = states // owners
        conv_state_sum = lax.dynamic_slice(
            sums[7:10].reshape(6, states), (0, owner * width), (taps + 1, width)
        )
        conv_state_grad, conv_state_bias_grad = conv_state_sum[:taps], conv_state_sum[taps]
    else:
        state_part, state_sums = state_parts
        state_grad = lax.psum_scatter(
            state_part.astype(f32), ("dp", "tensor"), scatter_dimension=0, tiled=True
        )
        conv_state_sum = lax.psum_scatter(
            state_sums[: taps + 1], ("dp", "tensor"), scatter_dimension=1, tiled=True
        )
        conv_state_grad, conv_state_bias_grad = conv_state_sum[:taps], conv_state_sum[taps]
        grad_normed = jnp.stack([keep_rows, give_rows], axis=1).reshape(total, depth)
        mixed_rows, grad_local = (
            lax.psum_scatter(part, "tensor", scatter_dimension=0, tiled=True).astype(f32)
            for part in (partial_out, grad_normed)
        )
        both, inner_float = jnp.stack(gate_chunks).astype(f32), inner_msg.astype(f32)
        gate_grad, output_grad, inner_grad = (
            lax.psum_scatter(part.reshape(depth, channels), "dp", scatter_dimension=0, tiled=True)
            for part in (both[:, :tall], both[:, tall:], inner_float[:, :tall])
        )
        output_grad = output_grad.T
        step_part = inner_float[:, tall : tall + heads, :tall].transpose(0, 2, 1)
        step_part = step_part.reshape(depth, heads)
        step_grad = lax.psum_scatter(step_part, "dp", scatter_dimension=0, tiled=True)
        sums = lax.psum(sums, "dp")
        input_grad = jnp.stack([gate_grad, inner_grad], axis=1)
        own_gain = jnp.sum(input_weight.astype(f32) * input_grad, axis=(1, 2))
        own_gain = own_gain + jnp.sum(step_weight.astype(f32) * step_grad, axis=1)
        own_gain = lax.psum_scatter(own_gain, "tensor", scatter_dimension=0, tiled=True)
        state_gain = jnp.sum(state_weight.astype(f32) * state_grad, axis=1)
    pre_gain_grad = (own_gain + state_gain) / pre_gain.astype(f32)
    block_out = (token_float + mixed_rows).astype(bf16)
    scale = lax.rsqrt(jnp.mean(token_float * token_float, axis=1, keepdims=True) + epsilon)
    grad_scaled = grad_local * gain_full
    along = jnp.sum(grad_scaled * token_float, axis=1, keepdims=True) / depth
    tokens_grad = (
        scale * grad_scaled
        - token_float * (scale * scale * scale * along)
        + cotangent.astype(f32)
    )
    skip_grad = sums[6].reshape(heads, -1).sum(axis=1)
    return (
        block_out,
        tokens_grad,
        pre_gain_grad,
        input_grad,
        step_grad,
        state_grad,
        sums[:taps],
        sums[taps],
        conv_state_grad,
        conv_state_bias_grad,
        sums[9, states : states + heads],
        sums[9, states + 128 : states + 128 + heads],
        skip_grad,
        sums[5],
        output_grad,
    )


def solution(mesh):
    in_specs = (
        P(("dp", "tensor"), None),
        P("dp", None),
        P(("dp", "tensor"), None),
        P(("dp", "tensor")),
        P("dp", None, "tensor"),
        P("dp", "tensor"),
        P(("dp", "tensor"), None),
        P(None, "tensor"),
        P("tensor"),
        P(None, ("dp", "tensor")),
        P(("dp", "tensor")),
        P("tensor"),
        P("tensor"),
        P("tensor"),
        P("tensor"),
        P("tensor", "dp"),
    )
    out_specs = (
        P(("dp", "tensor"), None),
        P(("dp", "tensor"), None),
        P(("dp", "tensor")),
        P("dp", None, "tensor"),
        P("dp", "tensor"),
        P(("dp", "tensor"), None),
        P(None, "tensor"),
        P("tensor"),
        P(None, ("dp", "tensor")),
        P(("dp", "tensor")),
        P("tensor"),
        P("tensor"),
        P("tensor"),
        P("tensor"),
        P("tensor", "dp"),
    )
    return jax.shard_map(body, mesh=mesh, in_specs=in_specs, out_specs=out_specs, check_vma=False)
```

```python
import functools

import jax
import jax.numpy as jnp
from jax import lax
from jax.experimental import pallas as pl
from jax.experimental.pallas import tpu as pltpu
from jax.sharding import PartitionSpec as P

epsilon = 1e-05
highest = lax.Precision.HIGHEST
f32 = jnp.float32
bf16 = jnp.bfloat16
span = 256
pad = 8
head_rows = 16
head_width = 64
vmem_bytes = 61 * 1024 * 1024


def mm(a, b, over=(1, 0)):
    dims = (((over[0],), (over[1],)), ((), ()))
    return lax.dot_general(a, b, dims, preferred_element_type=f32)


def mm_exact(a, b, over=(1, 0)):
    dims = (((over[0],), (over[1],)), ((), ()))
    return lax.dot_general(a, b, dims, preferred_element_type=f32, precision=highest)


def sigmoid(v):
    return 1.0 / (1.0 + jnp.exp(-v))


def ends_of(lengths_ref):
    ends, total = [], None
    for slot in range(lengths_ref.shape[1]):
        here = lengths_ref[0, slot]
        total = here if total is None else total + here
        ends.append(total)
    return ends


def segment_of(places, ends):
    segment = jnp.zeros(places.shape, jnp.int32)
    for end in ends:
        segment = segment + jnp.where(places >= end, 1, 0)
    return segment


def iota(shape, dim):
    return lax.broadcasted_iota(jnp.int32, shape, dim)


def write_masks(mask_ref, ends):
    rows = mask_ref.shape[1] - pad
    places = iota((rows, 128), 0)
    segment = segment_of(places, ends)
    for shift in range(1, mask_ref.shape[0] + 1):
        same = (segment_of(places - shift, ends) == segment) & (places >= shift)
        mask_ref[shift - 1, :rows, :] = jnp.where(same, 1.0, 0.0)
        mask_ref[shift - 1, rows:, :] = jnp.zeros((pad, 128), f32)


def shifted_rows(x_ref, mask_ref, at, cols, shift, tall):
    part = x_ref[pad + at - shift : pad + at - shift + tall, cols]
    if shift == 0:
        return part
    return part * mask_ref[shift - 1, at : at + tall, :]


def conv_pre(x_ref, mask_ref, taps_ref, bias_ref, at, cols, tall):
    taps = taps_ref.shape[0]
    shifted = [shifted_rows(x_ref, mask_ref, at, cols, s, tall) for s in range(taps)]
    total = bias_ref[:, cols]
    for s in range(taps):
        total = total + taps_ref[taps - 1 - s : taps - s, cols] * shifted[s]
    return total, shifted


def column_loop(width, step):
    def one(c, carry):
        step(pl.ds(pl.multiple_of(c * 128, 128), 128))
        return carry

    lax.fori_loop(0, width // 128, one, 0)


def row_loop(rows, tall, step):
    def one(r, carry):
        step(pl.multiple_of(r * tall, tall))
        return carry

    lax.fori_loop(0, rows // tall, one, 0)


class Block:
    def __init__(self, b, ends, step_col, step_row, rate_col, rate_row, state_ref):
        low, top = b * span, (b + 1) * span
        states = state_ref.shape[1] // 2
        lower = jnp.where(iota((span, span), 0) >= iota((span, span), 1), 1.0, 0.0)
        self.rows = slice(low, top)
        self.step = step_col[low:top]
        self.step_row = step_row[:, low:top]
        self.cum = mm_exact(lower, rate_col[low:top])
        self.cum_row = mm_exact(rate_row[:, low:top], lower, (1, 1))
        self.inputs = state_ref[low:top, :states].astype(bf16)
        self.outputs = state_ref[low:top, states:].astype(bf16)
        segment = segment_of(iota((span, 1), 0) + low, ends)
        segment_row = segment_of(iota((1, span), 1) + low, ends)
        edge = sum(jnp.where(span - 1 >= end, 1, 0) for end in ends)
        self.near_edge = jnp.where(segment == edge, 1.0, 0.0)
        self.mask = jnp.where(segment == segment_row, lower, 0.0)
        self.contact = mm(self.outputs, self.inputs, (1, 1)) * self.mask

    def decay(self, h):
        gap = self.cum[:, h : h + 1] - self.cum_row[h : h + 1, :]
        return jnp.exp(jnp.minimum(gap, 0.0))

    def from_edge(self, h):
        return jnp.exp(self.cum[:, h : h + 1]) * self.near_edge

    def to_edge(self, h):
        last = self.cum[span - 1 : span, h : h + 1]
        return jnp.exp(last - self.cum[:, h : h + 1]) * self.near_edge


def wide(low_half, left, right):
    return jnp.where(low_half, left, right)


def step_sizes(raw_col, raw_row, bias_ref, bias_col_ref, log_ref, log_col_ref):
    def soft(v):
        return jnp.maximum(v, 0.0) + jnp.log1p(jnp.exp(-jnp.abs(v)))

    step_col = soft(raw_col + bias_ref[...])
    step_row = soft(raw_row + bias_col_ref[...])
    rate_col = -step_col * jnp.exp(log_ref[...])
    rate_row = -step_row * jnp.exp(log_col_ref[...])
    return step_col, step_row, rate_col, rate_row


def forward_kernel(fast, place_ref, lengths_ref, *refs):
    n_msg = 8 if fast else 4
    n_rows = 4 if fast else 1
    row_refs, msg_refs, refs = refs[:n_rows], refs[n_rows : n_rows + n_msg], refs[n_rows + n_msg :]
    (taps_ref, bias_ref, step_bias_ref, step_bias_col_ref, log_ref, log_col_ref, skip_ref) = refs[:7]
    (
        normed_ref,
        turned_ref,
        weight_ref,
        state_weight_ref,
        step_weight_ref,
        small_ref,
        raw_ref,
        state_raw_ref,
        step_col_ref,
        step_row_ref,
        act_ref,
        state_ref,
        mixed_ref,
    ) = refs[7:20]
    mask_ref, state_taps_ref, state_bias_ref = refs[20:]
    total, channels = act_ref.shape
    ends = ends_of(lengths_ref)

    if fast:
        depth_part = 128
        small = jnp.zeros(small_ref.shape, f32)
        share = state_weight_ref.shape[0] // 32
        for slot in range(8):
            msg = msg_refs[slot]
            index = place_ref[slot]
            at = pl.multiple_of(index * depth_part, depth_part)
            weight_ref[pl.ds(at, depth_part), :] = msg[:depth_part, :]
            for member in range(4):
                inner = pl.multiple_of(at + place_ref[8 + member] * share, share)
                high, low = depth_part + share * (member // 2), 256 * (member % 2)
                state_weight_ref[pl.ds(inner, share), :] = msg[
                    high : high + share, low : low + 256
                ]
            tail = depth_part + 2 * share
            small = small + msg[tail : tail + 16, :256].astype(f32)
            step_weight_ref[:, pl.ds(at, depth_part)] = msg[tail : tail + 16, 256:384]
        small_ref[...] = small
    else:
        weight_ref[...] = msg_refs[0][...]
        state_weight_ref[...] = msg_refs[1][...]
        step_weight_ref[...] = msg_refs[2][...]
        small_ref[...] = msg_refs[3][...].astype(f32)
    gain = jnp.concatenate([small_ref[i : i + 1, :] for i in range(4)], axis=1)
    taps = taps_ref.shape[0]
    state_taps_ref[...] = small_ref[4 : 4 + taps, :]
    state_bias_ref[...] = small_ref[4 + taps : 5 + taps, :]

    tall = total // n_rows
    for member in range(n_rows):
        at = pl.multiple_of(place_ref[8 + member] * tall, tall) if fast else 0
        value = row_refs[member][:tall, :].astype(f32)
        scale = lax.rsqrt(jnp.mean(value * value, axis=1, keepdims=True) + epsilon)
        normed = (value * scale * gain).astype(bf16)
        normed_ref[pl.ds(at, tall), :] = normed
        turned_ref[:, pl.ds(at, tall)] = normed.astype(f32).T.astype(bf16)

    raw_ref[:pad, :] = jnp.zeros((pad, channels), f32)
    state_raw_ref[:pad, :] = jnp.zeros((pad, state_raw_ref.shape[1]), f32)

    def project(at):
        part = normed_ref[pl.ds(at, 128), :]
        raw_ref[pl.ds(at + pad, 128), :] = mm(part, weight_ref[...])
        state_raw_ref[pl.ds(at + pad, 128), :] = mm(part, state_weight_ref[...])
        step_col_ref[pl.ds(at, 128), :] = mm(part, step_weight_ref[...], (1, 1))

    row_loop(total, 128, project)
    step_row_ref[...] = mm(step_weight_ref[...], normed_ref[...], (1, 1))

    write_masks(mask_ref, ends)

    def activate(x_ref, out_ref, own_taps, own_bias):
        def column(cols):
            for at in range(0, total, 128):
                pre, _ = conv_pre(x_ref, mask_ref, own_taps, own_bias, at, cols, 128)
                out_ref[at : at + 128, cols] = pre * sigmoid(pre)

        column_loop(out_ref.shape[1], column)

    activate(raw_ref, act_ref, taps_ref, bias_ref)
    activate(state_raw_ref, state_ref, state_taps_ref, state_bias_ref)

    steps = step_sizes(
        step_col_ref[...],
        step_row_ref[...],
        step_bias_ref,
        step_bias_col_ref,
        log_ref,
        log_col_ref,
    )
    low_half = iota((span, 128), 1) < head_width
    held = []
    for b in range(total // span):
        block = Block(b, ends, *steps, state_ref)
        for i in range(channels // 128):
            cols = slice(128 * i, 128 * (i + 1))
            pair = (2 * i, 2 * i + 1)
            x = act_ref[block.rows, cols]
            step_wide = wide(low_half, *(block.step[:, h : h + 1] for h in pair))
            x_step = (x * step_wide).astype(bf16)
            y = [mm((block.decay(h) * block.contact).astype(bf16), x_step) for h in pair]
            y = wide(low_half, *y) + skip_ref[:, cols] * x
            if b == 0:
                reach = wide(low_half, *(block.to_edge(h) for h in pair))
                weighted = (x * step_wide * reach).astype(bf16)
                held.append(mm(block.inputs, weighted, (0, 0)).astype(bf16))
            else:
                reach = wide(low_half, *(block.from_edge(h) for h in pair))
                y = y + reach * mm(block.outputs, held[i])
            mixed_ref[block.rows, cols] = y


def grad_in_kernel(fast, place_ref, lengths_ref, *refs):
    n_rows = 4 if fast else 1
    n_msg = 8 if fast else 2
    row_refs, msg_refs, refs = refs[:n_rows], refs[n_rows : n_rows + n_msg], refs[n_rows + n_msg :]
    normed_ref, mixed_ref, norm_ref = refs[:3]
    rows_ref, gate_weight_ref, out_weight_ref, gate_ref, grad_ref, sums_ref, wide_ref = refs[3:]
    total = rows_ref.shape[0]
    ends = ends_of(lengths_ref)
    tall = total // n_rows
    for member in range(n_rows):
        at = pl.multiple_of(place_ref[8 + member] * tall, tall) if fast else 0
        rows_ref[pl.ds(at, tall), :] = row_refs[member][-tall:, :]
    if fast:
        for slot in range(8):
            at = pl.multiple_of(place_ref[slot] * 128, 128)
            gate_weight_ref[pl.ds(at, 128), :] = msg_refs[slot][:128, :]
            out_weight_ref[pl.ds(at, 128), :] = msg_refs[slot][128:, :]
    else:
        gate_weight_ref[...] = msg_refs[0][...]
        out_weight_ref[...] = msg_refs[1][...]

    def part(at):
        rows = pl.ds(at, 128)
        valid = jnp.where(iota((128, 1), 0) + at < ends[-1], 1.0, 0.0)
        grad = mm(rows_ref[rows, :], out_weight_ref[...]) * valid
        grad_ref[rows, :] = grad
        gate = mm(normed_ref[rows, :], gate_weight_ref[...])
        gate_ref[rows, :] = gate
        gated = mixed_ref[rows, :] * (gate * sigmoid(gate))
        square = jnp.sum(gated * gated, axis=1, keepdims=True)
        cross = jnp.sum(grad * norm_ref[...] * gated, axis=1, keepdims=True)
        lane = iota((128, 128), 1)
        wide_ref[rows, :] = jnp.where(lane == 0, square, jnp.where(lane == 1, cross, 0.0))

    row_loop(total, 128, part)
    for at in range(0, total, 128):
        sums_ref[:, at : at + 128] = wide_ref[at : at + 128, :].T[:8, :]


def norm_kernel(inner_total, place_ref, lengths_ref, *refs):
    n_sums = len(refs) - 21
    sums_refs, refs = refs[:n_sums], refs[n_sums:]
    gate_ref, mixed_ref, grad_ref, norm_ref, weight_ref, rows_ref, turned_ref = refs[:7]
    chunk_refs = refs[7:15]
    partial_ref, grad_gate_ref, grad_mixed_ref, norm_grad_ref = refs[15:19]
    wide_ref, out_rows_ref = refs[19:]
    total, channels = gate_ref.shape
    ends = ends_of(lengths_ref)
    for at in range(0, total, 128):
        tile = sum(ref[:, at : at + 128] for ref in sums_refs)
        tile = jnp.concatenate([tile] * 16, axis=0)
        wide_ref[at : at + 128, :] = tile.T
    norm_grad_ref[...] = jnp.zeros(norm_grad_ref.shape, f32)

    def part(at):
        rows = pl.ds(at, 128)
        valid = jnp.where(iota((128, 1), 0) + at < ends[-1], 1.0, 0.0)
        scale = lax.rsqrt(wide_ref[rows, 0:1] / inner_total + epsilon)
        cross = wide_ref[rows, 1:2]
        gate = gate_ref[rows, :]
        mixed = mixed_ref[rows, :]
        sig = sigmoid(gate)
        gate_act = gate * sig
        gated = mixed * gate_act
        grad = grad_ref[rows, :]
        norm = norm_ref[...]
        hat = gated * scale
        out_rows_ref[rows, :] = (hat * norm * valid).astype(bf16)
        norm_grad_ref[...] += jnp.sum(grad * hat, axis=0, keepdims=True)
        grad_gated = scale * (grad * norm) - gated * (scale * scale * scale * cross / inner_total)
        grad_mixed_ref[rows, :] = grad_gated * gate_act
        grad_gate = grad_gated * mixed * sig * (1.0 + gate * (1.0 - sig))
        grad_gate_ref[rows, :] = grad_gate.astype(bf16)

    row_loop(total, 128, part)

    def back(at):
        cols = pl.ds(at, 256)
        partial_ref[:, cols] = mm(out_rows_ref[...], weight_ref[cols, :], (1, 1)).astype(bf16)

    row_loop(weight_ref.shape[0], 256, back)
    tall = chunk_refs[0].shape[0] // 2
    for slot, chunk_ref in enumerate(chunk_refs):
        cols = pl.ds(pl.multiple_of(place_ref[slot] * tall, tall), tall)
        chunk_ref[:tall, :] = mm(turned_ref[cols, :], grad_gate_ref[...]).astype(bf16)
        chunk_ref[tall:, :] = mm(rows_ref[:, cols], out_rows_ref[...], (0, 0)).astype(bf16)


def scan_back_kernel(first_pair, lengths_ref, *refs):
    grad_mixed_ref, act_ref, state_ref, step_col_ref, step_row_ref = refs[:5]
    step_bias_ref, step_bias_col_ref, log_ref, log_col_ref, skip_ref = refs[5:10]
    grad_act_ref, grad_state_ref, step_grad_ref, sums_ref, acc_ref = refs[10:]
    total, own_width = grad_act_ref.shape
    states = state_ref.shape[1] // 2
    ends = ends_of(lengths_ref)
    sums_ref[...] = jnp.zeros(sums_ref.shape, f32)
    raw_row = step_row_ref[...]
    steps = step_sizes(
        step_col_ref[...], raw_row, step_bias_ref, step_bias_col_ref, log_ref, log_col_ref
    )
    rate_row = steps[3]
    low_half = iota((span, 128), 1) < head_width
    lower = jnp.where(iota((span, span), 0) >= iota((span, span), 1), 1.0, 0.0)
    blocks = [Block(b, ends, *steps, state_ref) for b in range(total // span)]
    first, second = blocks
    row_sums, step_rows, out_sums, in_sums = [], [], None, None
    grad_out = jnp.zeros((span, states), f32)
    grad_in = jnp.zeros((span, states), f32)
    head_of = iota((head_rows, 128), 0)
    lane_head = iota((head_rows, 128), 1) // head_width

    for b, block in enumerate(blocks):
        acc_ref[...] = jnp.zeros((span, span), f32)
        row_sum = jnp.zeros((span, 128), f32)
        step_grad = jnp.zeros((head_rows, span), f32)
        lane = iota((span, 128), 1)
        head_row = iota((head_rows, span), 0)
        for i in range(first_pair, first_pair + own_width // 128):
            cols = slice(128 * i, 128 * (i + 1))
            own_cols = slice(128 * (i - first_pair), 128 * (i - first_pair + 1))
            pair = (2 * i, 2 * i + 1)
            x = act_ref[block.rows, cols]
            x_low = x.astype(bf16)
            grad = grad_mixed_ref[block.rows, cols]
            grad_low = grad.astype(bf16)
            halves = (
                jnp.where(low_half, grad, 0.0).astype(bf16),
                jnp.where(low_half, 0.0, grad).astype(bf16),
            )
            step_wide = wide(low_half, *(block.step[:, h : h + 1] for h in pair))
            grads = []
            for h, half in zip(pair, halves):
                decay = block.decay(h)
                spread = mm(half, x_low, (1, 1)) * decay
                stepped = spread * block.step_row[h : h + 1, :]
                acc_ref[...] += stepped
                row_here = jnp.sum(stepped * block.contact, axis=1, keepdims=True)
                row_sum = jnp.where(lane == h, row_here, row_sum)
                step_here = jnp.sum(spread * block.contact, axis=0, keepdims=True)
                step_grad = jnp.where(head_row == h, step_here, step_grad)
                grads.append(mm((decay * block.contact).astype(bf16), grad_low, (0, 0)))
            grad_act = wide(low_half, *grads) * step_wide + skip_ref[:, cols] * grad
            sums_ref[2:3, own_cols] += jnp.sum(grad * x, axis=0, keepdims=True)
            picks = jnp.where(lane_head + 2 * i == head_of, 1.0, 0.0)
            if b == 0:
                reach = wide(low_half, *(second.from_edge(h) for h in pair))
                lead = (grad_mixed_ref[second.rows, cols] * reach).astype(bf16)
                edge = wide(low_half, *(block.to_edge(h) for h in pair))
                weighted = (x * step_wide * edge).astype(bf16)
                held = mm(block.inputs, weighted, (0, 0)).astype(bf16)
                held_grad = mm(second.outputs, lead, (0, 0)).astype(bf16)
                grad_out = grad_out + mm(lead, held, (1, 1))
                grad_in = grad_in + mm(weighted, held_grad, (1, 1))
                back = mm(block.inputs, held_grad) * edge
                grad_act = grad_act + back * step_wide
                ahead = mm(second.outputs, held)
                out_here = mm_exact(picks, lead.astype(f32) * ahead, (1, 1))
                in_here = mm_exact(picks, x * back, (1, 1))
                out_sums = out_here if out_sums is None else out_sums + out_here
                in_sums = in_here if in_sums is None else in_sums + in_here
            grad_act_ref[block.rows, own_cols] = grad_act
        table = (acc_ref[...] * block.mask).astype(bf16)
        grad_c = mm(table, block.inputs)
        grad_b = mm(table, block.outputs, (0, 0))
        if b == 0:
            grad_b = grad_b + grad_in
        else:
            grad_c = grad_c + grad_out
        grad_state_ref[block.rows, :states] = grad_b
        grad_state_ref[block.rows, states:] = grad_c
        row_sums.append(row_sum)
        step_rows.append(step_grad)

    rate_grads = []
    for b, block in enumerate(blocks):
        column = step_rows[b] * block.step_row
        crossing = mm_exact(row_sums[b], lower, (0, 0))[:head_rows] - mm_exact(column, lower)
        if b == 0:
            crossing = crossing + mm_exact(in_sums * block.step_row, 1.0 - lower)
        else:
            crossing = crossing + mm_exact(out_sums, lower)
        rate_grads.append(crossing)
    step_rows[0] = step_rows[0] + in_sums
    rate_grad = jnp.concatenate(rate_grads, axis=1)
    step_grad = jnp.concatenate(step_rows, axis=1) - rate_grad * jnp.exp(log_col_ref[...])
    step_grad = step_grad * sigmoid(raw_row + step_bias_col_ref[...])
    decay_sum = jnp.sum(rate_grad * rate_row, axis=1, keepdims=True)
    bias_sum = jnp.sum(step_grad, axis=1, keepdims=True)
    lane = iota((head_rows, 128), 1)
    head_sums = jnp.where(lane == 0, bias_sum, jnp.where(lane == 1, decay_sum, 0.0))
    head_sums = jnp.concatenate([head_sums] * (128 // head_rows), axis=0).T
    sums_ref[0:2, :128] = head_sums[:2, :]
    step_grad_ref[...] = step_grad


def conv_back(x_ref, mask_ref, grad_ref, held_ref, out_ref, sums_ref, own_taps, own_bias):
    total, taps = out_ref.shape[0], own_taps.shape[0]
    held_ref[total:, :] = jnp.zeros((pad, held_ref.shape[1]), f32)

    def column(cols):
        sums = [jnp.zeros((1, 128), f32) for _ in range(taps + 1)]
        for at in range(0, total, 128):
            pre, shifted = conv_pre(x_ref, mask_ref, own_taps, own_bias, at, cols, 128)
            sig = sigmoid(pre)
            grad = grad_ref[at : at + 128, cols] * sig * (1.0 + pre * (1.0 - sig))
            held_ref[at : at + 128, cols] = grad
            for s in range(taps):
                sums[taps - 1 - s] += jnp.sum(grad * shifted[s], axis=0, keepdims=True)
            sums[taps] += jnp.sum(grad, axis=0, keepdims=True)
        for t, value in enumerate(sums):
            sums_ref[t : t + 1, cols] = value
        for at in range(0, total, 128):
            back = own_taps[taps - 1 : taps, cols] * held_ref[at : at + 128, cols]
            for s in range(1, taps):
                part = held_ref[at + s : at + s + 128, cols]
                part = part * mask_ref[s - 1, at + s : at + s + 128, :]
                back = back + own_taps[taps - 1 - s : taps - s, cols] * part
            out_ref[at : at + 128, cols] = back.astype(bf16)

    column_loop(out_ref.shape[1], column)


def state_back_kernel(fast, place_ref, lengths_ref, *refs):
    state_refs, step_refs, refs = refs[0:2], refs[2:4], refs[4:]
    state_raw_ref, turned_ref, small_ref, grad_state_low_ref, step_low_ref = refs[:5]
    n_out = 4 if fast else 2
    out_refs, refs = refs[5 : 5 + n_out], refs[5 + n_out :]
    mask_ref, taps_ref, bias_ref, grad_state_ref, pre_ref, part_ref, sums_ref = refs
    taps = taps_ref.shape[0]
    taps_ref[...] = small_ref[4 : 4 + taps, :]
    bias_ref[...] = small_ref[4 + taps : 5 + taps, :]
    write_masks(mask_ref, ends_of(lengths_ref))
    grad_state_ref[...] = state_refs[0][...] + state_refs[1][...]
    step_low_ref[...] = (step_refs[0][...] + step_refs[1][...]).astype(bf16)
    sums_ref[...] = jnp.zeros(sums_ref.shape, f32)
    conv_back(
        state_raw_ref,
        mask_ref,
        grad_state_ref,
        pre_ref,
        grad_state_low_ref,
        sums_ref,
        taps_ref,
        bias_ref,
    )

    def chunk(at):
        part = turned_ref[pl.ds(at, 256), :]
        part_ref[pl.ds(at, 256), :] = mm(part, grad_state_low_ref[...]).astype(bf16)

    depth = turned_ref.shape[0]
    row_loop(depth, 256, chunk)
    if fast:
        share = depth // 32
        for member, out_ref in enumerate(out_refs):
            for c in range(8):
                at = pl.multiple_of((4 * c + place_ref[8 + member]) * share, share)
                out_ref[share * c : share * (c + 1), :] = part_ref[pl.ds(at, share), :]
            out_ref[8 * share :, :] = sums_ref[...].astype(bf16)
    else:
        out_refs[0][...] = part_ref[...]
        out_refs[1][...] = sums_ref[...]


def inner_back_kernel(lengths_ref, *refs):
    act_refs, head_refs, refs = refs[0:2], refs[2:4], refs[4:]
    raw_ref, norm_grad_ref, taps_ref, bias_ref, grad_inner_ref, sums_ref = refs[:6]
    mask_ref, grad_act_ref, pre_ref = refs[6:]
    half = grad_inner_ref.shape[1] // 2
    write_masks(mask_ref, ends_of(lengths_ref))
    grad_act_ref[:, :half] = act_refs[0][...]
    grad_act_ref[:, half:] = act_refs[1][...]
    sums_ref[...] = jnp.zeros(sums_ref.shape, f32)
    heads = head_refs[0][:2, :128] + head_refs[1][:2, :128]
    sums_ref[5:6, :] = norm_grad_ref[...]
    sums_ref[6:7, :half] = head_refs[0][2:3, :]
    sums_ref[6:7, half:] = head_refs[1][2:3, :]
    sums_ref[9:10, half : half + 128] = heads[0:1, :]
    sums_ref[9:10, half + 128 :] = heads[1:2, :]
    conv_back(
        raw_ref,
        mask_ref,
        grad_act_ref,
        pre_ref,
        grad_inner_ref,
        sums_ref,
        taps_ref,
        bias_ref,
    )


def message_kernel(grad_inner_ref, step_low_ref, turned_ref, msg_ref):
    chunks = msg_ref.shape[0]
    tall = turned_ref.shape[0] // chunks
    step_low = step_low_ref[...]

    def chunk(c, carry):
        part = turned_ref[pl.ds(pl.multiple_of(c * tall, tall), tall), :]
        msg_ref[c, :tall, :] = mm(part, grad_inner_ref[...]).astype(bf16)
        msg_ref[c, tall:, :tall] = mm(step_low, part, (1, 1)).astype(bf16)
        msg_ref[c, tall:, tall:] = jnp.zeros((head_rows, msg_ref.shape[2] - tall), bf16)
        return carry

    lax.fori_loop(0, chunks, chunk, 0)


def chunk_kernel(slots, n_got, place_ref, *refs):
    grad_inner_ref, step_low_ref, sums_ref = refs[:3]
    state_refs, turned_refs, got_refs = refs[3:7], refs[7:9], refs[9 : 9 + n_got]
    out_refs = refs[9 + n_got :]
    states = state_refs[0].shape[1]
    share = (state_refs[0].shape[0] - 16) // 8

    def state_rows(low, tall):
        return sum(ref[pl.ds(low, tall), :].astype(f32) for ref in state_refs)

    shared = state_rows(8 * share, 16)
    sums = [
        sums_ref[:7, :],
        jnp.concatenate([shared[0:1, :], shared[1:2, :]], axis=1),
        jnp.concatenate([shared[2:3, :], shared[3:4, :]], axis=1),
        jnp.concatenate([shared[4:5, :], sums_ref[9:10, states:]], axis=1),
    ]
    for n, (slot, out_ref) in enumerate(zip(slots, out_refs)):
        index = place_ref[slot]
        part = turned_refs[n][...]
        step = mm(step_low_ref[...], part, (1, 1))
        step = [
            jnp.concatenate([step[4 * k + i : 4 * k + i + 1, :] for i in range(4)], axis=1)
            for k in range(2)
        ]
        state = state_rows(pl.multiple_of(index * share, share), share)
        value = jnp.concatenate(
            [
                mm(part, grad_inner_ref[...]),
                jnp.concatenate([state[:16, :], state[16:, :]], axis=1),
                *sums,
                *step,
                jnp.zeros((4, 2 * states), f32),
            ],
            axis=0,
        )
        tail = value.shape[0] - 16
        main, sums_here = value[:tail, :], value[tail:, :]
        if n < n_got:
            got = got_refs[n]
            main = main + got[:tail, :].astype(f32)
            sums_here = sums_here + got[tail : tail + 16, :].astype(f32)
            sums_here = sums_here + got[tail + 16 :, :].astype(f32)
        out_ref[:tail, :] = main.astype(out_ref.dtype)
        high = sums_here.astype(bf16)
        out_ref[tail : tail + 16, :] = high.astype(out_ref.dtype)
        out_ref[tail + 16 :, :] = (sums_here - high.astype(f32)).astype(out_ref.dtype)


def project_back_kernel(fast, place_ref, *refs):
    grad_refs, step_low_ref, weight_refs, step_weight_ref = refs[:3], refs[3], refs[4:7], refs[7]
    out_refs, held_refs, step_ref = refs[8:10], refs[10:13], refs[13]
    for n, member in enumerate((0, 2, 1, 3)):
        at = pl.multiple_of(place_ref[8 + member] * 128, 128) if fast else 128 * member
        for held_ref, grad_ref in zip(held_refs, grad_refs):
            held_ref[128 * n : 128 * (n + 1), :] = grad_ref[pl.ds(at, 128), :]
        step_ref[:, 128 * n : 128 * (n + 1)] = step_low_ref[:, pl.ds(at, 128)]

    def back(at):
        cols = pl.ds(at, 256)
        grad = mm(step_ref[...], step_weight_ref[:, cols], (0, 0))
        for held_ref, weight_ref in zip(held_refs, weight_refs):
            grad = grad + mm(held_ref[...], weight_ref[cols, :], (1, 1))
        grad = grad.astype(bf16)
        for n in range(4):
            out_refs[n // 2][n % 2, :, cols] = grad[128 * n : 128 * (n + 1), :]

    row_loop(step_weight_ref.shape[1], 256, back)


def prepare_kernel(place_ref, gain_ref, taps_ref, bias_ref, state_ref, shared_ref):
    owner = place_ref[0]
    share, states = state_ref.shape
    shared_ref[:share, :] = state_ref[...]

    def placed(value, at):
        width = value.shape[1]
        pick = iota((width, states), 1) - at == iota((width, states), 0)
        return mm(value, jnp.where(pick, 1.0, 0.0).astype(bf16))

    start = owner * gain_ref.shape[1]
    small = jnp.concatenate(
        [placed(gain_ref[...], start - states * i) for i in range(4)]
        + [placed(taps_ref[...], owner * taps_ref.shape[1])]
        + [placed(bias_ref[...], owner * bias_ref.shape[1])]
        + [jnp.zeros((7, states), f32)],
        axis=0,
    )
    shared_ref[share:, :] = small.astype(bf16)


def prepare_late_kernel(input_ref, out_ref, late_ref):
    depth_part = input_ref.shape[0]
    late_ref[:depth_part, :] = input_ref[:, 0, :]
    late_ref[depth_part:, :] = out_ref[...].astype(f32).T.astype(bf16)


def params_kernel(*refs):
    taps_ref, bias_ref, step_bias_ref, log_ref, skip_ref, norm_ref = refs[:6]
    outs = refs[6:]
    heads = step_bias_ref.shape[1]
    pick = jnp.where(iota((heads, head_rows), 0) == iota((heads, head_rows), 1), 1.0, 0.0)
    square = iota((head_rows, head_rows), 0) == iota((head_rows, head_rows), 1)

    def both(value_ref, row_ref, col_ref):
        row = mm_exact(value_ref[...].astype(f32), pick)
        row_ref[...] = row
        col_ref[...] = jnp.sum(jnp.where(square, row, 0.0), axis=1, keepdims=True)

    outs[0][...] = taps_ref[...].astype(f32)
    outs[1][...] = bias_ref[...].astype(f32)
    both(step_bias_ref, outs[2], outs[3])
    both(log_ref, outs[4], outs[5])
    channels = norm_ref.shape[1]
    own = iota((heads, channels), 1) // (channels // heads) == iota((heads, channels), 0)
    outs[6][...] = mm_exact(skip_ref[...].astype(f32), jnp.where(own, 1.0, 0.0))
    outs[7][...] = norm_ref[...].astype(f32)


def assemble_kernel(input_ref, step_ref, *refs):
    shared_refs, msg_ref = refs[:4], refs[4]
    depth_part, _, channels = input_ref.shape
    share = shared_refs[0].shape[0] - 16
    tail = depth_part + 2 * share
    msg_ref[:depth_part, :] = input_ref[:, 1, :]
    for member, ref in enumerate(shared_refs):
        high, low = depth_part + share * (member // 2), 256 * (member % 2)
        msg_ref[high : high + share, low : low + 256] = ref[:share, :]
    small = sum(ref[share:, :].astype(f32) for ref in shared_refs)
    msg_ref[tail:, :256] = small.astype(bf16)
    msg_ref[tail:, 256:384] = step_ref[...]
    msg_ref[tail:, 384:] = jnp.zeros((16, channels - 384), bf16)


def call(kernel, micros, scalars, arrays, outs, scratch):
    smem = pl.BlockSpec(memory_space=pltpu.SMEM)
    vmem = pl.BlockSpec(memory_space=pltpu.VMEM)
    return pl.pallas_call(
        kernel,
        out_shape=[jax.ShapeDtypeStruct(shape, kind) for shape, kind in outs],
        in_specs=[smem] * len(scalars) + [vmem] * len(arrays),
        out_specs=[vmem] * len(outs),
        scratch_shapes=[pltpu.VMEM(shape, kind) for shape, kind in scratch],
        compiler_params=pltpu.CompilerParams(vmem_limit_bytes=vmem_bytes),
        cost_estimate=pl.CostEstimate(
            flops=int(micros * 1.1e9), bytes_accessed=1 << 20, transcendentals=0
        ),
    )(*scalars, *arrays)


def ring_ok(n_dp, n_tensor):
    return n_dp == 8 and n_tensor == 4


ring_order = (0, 2, 4, 6, 7, 5, 3, 1)


def ring_place(index):
    high, low = index // 2, index % 2
    return jnp.where(low == 0, high, 7 - high)


def ring_index(place):
    place = lax.rem(place + 16, 8)
    return jnp.where(place < 4, 2 * place, 2 * (7 - place) + 1)


def ring_send(value, forward):
    pairs = []
    for place in range(8):
        other = (place + (1 if forward else 7)) % 8
        pairs.append((ring_order[place], ring_order[other]))
    return lax.ppermute(value, "dp", pairs)


def ring_gather(value):
    me = ring_place(lax.axis_index("dp"))
    pieces = [(value, ring_index(me))]
    ahead, back = value, value
    for step in range(1, 5):
        ahead = ring_send(ahead, True)
        pieces.append((ahead, ring_index(me - step)))
        if step < 4:
            back = ring_send(back, False)
            pieces.append((back, ring_index(me + step)))
    return pieces


def dp_swap(value, bit):
    return lax.ppermute(value, "dp", [(i, i ^ bit) for i in range(8)])


def ring_step(held):
    return ring_send(held[0], True), ring_send(held[1], False)


def add_low(got, own):
    return (got.astype(f32) + own.astype(f32)).astype(bf16)


def ordered(first, then):
    return lax.optimization_barrier((first, then))


def tensor_gather(value):
    near = tensor_swap(value, 1)
    far = tensor_swap(value, 2)
    return [value, near, far, tensor_swap(far, 1)]


def tensor_direct(value):
    return [value] + [tensor_swap(value, bit) for bit in range(1, 4)]


def tensor_sum(value, depth):
    parts = value.reshape(4, -1, depth)
    parts = lax.all_to_all(parts, "tensor", 0, 0, tiled=True)
    return jnp.sum(parts.astype(f32), axis=0)


def tensor_swap(value, bit):
    return lax.ppermute(value, "tensor", [(i, i ^ bit) for i in range(4)])


def body(
    tokens,
    lengths,
    cotangent,
    pre_gain,
    input_weight,
    step_weight,
    state_weight,
    conv_inner,
    conv_inner_bias,
    conv_state,
    conv_state_bias,
    step_bias,
    decay_log,
    skip_gain,
    norm_gain,
    output_weight,
):
    n_dp, n_tensor = lax.axis_size("dp"), lax.axis_size("tensor")
    fast = ring_ok(n_dp, n_tensor)
    owners = n_dp * n_tensor
    me = lax.axis_index("tensor")
    owner = lax.axis_index("dp") * n_tensor + me
    own_rows, depth = tokens.shape
    total = own_rows * n_tensor
    states = state_weight.shape[1]
    heads = step_weight.shape[1]
    share = state_weight.shape[0]
    taps = conv_state.shape[0]
    channels = input_weight.shape[2]
    inner_total = channels * n_tensor

    owner_place = jnp.stack([owner, owners]).astype(jnp.int32)
    (shared,) = call(
        prepare_kernel,
        1,
        [owner_place],
        [pre_gain[None, :], conv_state, conv_state_bias[None, :], state_weight],
        [((share + 16, states), bf16)],
        [],
    )
    step_rows = jnp.pad(step_weight.T, ((0, head_rows - heads), (0, 0)))
    shared, out_shard = ordered(shared, output_weight)
    (late,) = call(
        prepare_late_kernel,
        2,
        [],
        [input_weight, out_shard],
        [((input_weight.shape[0] + output_weight.shape[1], channels), bf16)],
        [],
    )
    params = call(
        params_kernel,
        1,
        [],
        [
            conv_inner,
            conv_inner_bias[None, :],
            step_bias[None, :],
            decay_log[None, :],
            skip_gain[None, :],
            norm_gain[None, :],
        ],
        [
            ((taps, channels), f32),
            ((1, channels), f32),
            ((1, head_rows), f32),
            ((head_rows, 1), f32),
            ((1, head_rows), f32),
            ((head_rows, 1), f32),
            ((1, channels), f32),
            ((1, channels), f32),
        ],
        [],
    )
    params = list(params)
    conv_params, head_params, norm_row = params[:2], params[2:7], params[7]
    if fast:
        shared = tensor_direct(shared)
        late_one = ring_step((late, late))
        (msg,) = call(
            assemble_kernel,
            1,
            [],
            [input_weight, step_rows, *shared],
            [((input_weight.shape[0] + 2 * share + 16, channels), bf16)],
            [],
        )
        late_one, msg = ordered(late_one, msg)
        msg = ring_gather(msg)
        weight_pieces = [piece for piece, _ in msg]
        late_two = ring_step(late_one)
        late_three = ring_step(late_two)
        late_pieces = [late, *late_one, *late_two, *late_three, ring_send(late_three[0], True)]
        own_rows_both = jnp.concatenate([tokens, cotangent], axis=0)
        row_pieces = tensor_gather(ordered(shared, own_rows_both)[1])
        grad_pieces = row_pieces
        place = jnp.stack([index for _, index in msg] + [me, me ^ 1, me ^ 2, me ^ 3])
    else:
        row_pieces = [lax.all_gather(tokens, "tensor", axis=0, tiled=True)]
        grad_pieces = [lax.all_gather(cotangent, "tensor", axis=0, tiled=True)]
        gate_weight, inner_weight = late[: input_weight.shape[0]], input_weight[:, 1]
        weight_pieces = [
            lax.all_gather(inner_weight, "dp", axis=0, tiled=True),
            lax.all_gather(state_weight, ("dp", "tensor"), axis=0, tiled=True),
            lax.all_gather(step_rows, "dp", axis=1, tiled=True),
            lax.psum(shared[share:], ("dp", "tensor")),
        ]
        late_pieces = [
            lax.all_gather(gate_weight, "dp", axis=0, tiled=True),
            lax.all_gather(late[input_weight.shape[0] :], "dp", axis=0, tiled=True),
        ]
        place = jnp.concatenate([jnp.arange(8), jnp.arange(4)])
    place = place.astype(jnp.int32)

    masks = ((taps - 1, total + pad, 128), f32)
    state_taps = [((taps, states), f32), ((1, states), f32)]
    (
        normed,
        turned,
        inner_full,
        state_full,
        step_full,
        small_full,
        raw,
        state_raw,
        step_col,
        step_row,
        act,
        state_act,
        mixed,
    ) = call(
        functools.partial(forward_kernel, fast),
        11,
        [place, lengths],
        row_pieces + weight_pieces + conv_params + head_params,
        [
            ((total, depth), bf16),
            ((depth, total), bf16),
            ((depth, channels), bf16),
            ((depth, states), bf16),
            ((head_rows, depth), bf16),
            ((16, states), f32),
            ((total + pad, channels), f32),
            ((total + pad, states), f32),
            ((total, head_rows), f32),
            ((head_rows, total), f32),
            ((total, channels), f32),
            ((total, states), f32),
            ((total, channels), f32),
        ],
        [masks] + state_taps,
    )
    grad_rows, gate_full, output_full, gate, grad_normalized, sums = call(
        functools.partial(grad_in_kernel, fast),
        5,
        [place, lengths],
        grad_pieces + late_pieces + [normed, mixed, norm_row],
        [
            ((total, depth), bf16),
            ((depth, channels), bf16),
            ((depth, channels), bf16),
            ((total, channels), f32),
            ((total, channels), f32),
            ((8, total), f32),
        ],
        [((total, 128), f32)],
    )
    if fast:
        sums = tensor_direct(sums)
    else:
        sums = [lax.psum(sums, "tensor")]
    chunks = 8
    tall = depth // chunks
    norm_outs = call(
        functools.partial(norm_kernel, inner_total),
        9,
        [place, lengths],
        [*sums, gate, mixed, grad_normalized, norm_row, output_full, grad_rows, turned],
        [((2 * tall, channels), bf16)] * chunks
        + [
            ((total, depth), bf16),
            ((total, channels), bf16),
            ((total, channels), f32),
            ((1, channels), f32),
        ],
        [((total, 128), f32), ((total, channels), bf16)],
    )
    gate_chunks = norm_outs[:chunks]
    partial_out, grad_gate, grad_mixed, norm_grad = norm_outs[chunks:]

    def scan_back(first_pair, grad):
        return call(
            functools.partial(scan_back_kernel, first_pair),
            6,
            [lengths],
            [grad, act, state_act, step_col, step_row] + head_params,
            [
                ((total, channels // 2), f32),
                ((total, states), f32),
                ((head_rows, total), f32),
                ((8, channels // 2), f32),
            ],
            [((span, span), f32)],
        )

    if fast:
        got = ring_step((gate_chunks[7], gate_chunks[5]))
        held = add_low(got[0], gate_chunks[6]), add_low(got[1], gate_chunks[3])
    first = scan_back(0, grad_mixed)
    if fast:
        held, grad_mixed = ordered(held, grad_mixed)
        got = ring_step(held)
        held = add_low(got[0], gate_chunks[4]), add_low(got[1], gate_chunks[1])
    second = scan_back(channels // 256, grad_mixed)
    if fast:
        held, state_raw = ordered(held, state_raw)
        got = ring_step(held)
        held, last = add_low(got[0], gate_chunks[2]), got[1]
    share_rows = depth // 4 + 16
    state_outs = call(
        functools.partial(state_back_kernel, fast),
        4,
        [place, lengths],
        [first[1], second[1], first[2], second[2], state_raw, turned, small_full],
        [((total, states), bf16), ((head_rows, total), bf16)]
        + (
            [((share_rows, states), bf16)] * 4
            if fast
            else [((depth, states), bf16), ((16, states), f32)]
        ),
        [
            masks,
            *state_taps,
            ((total, states), f32),
            ((total + pad, states), f32),
            ((depth, states), bf16),
            ((16, states), f32),
        ],
    )
    grad_state_low, step_low = state_outs[:2]
    state_parts = state_outs[2:]
    if fast:
        state_parts = [state_parts[0]] + [tensor_swap(state_parts[i], i) for i in range(1, 4)]
    if fast:
        (held, last), raw = ordered((held, last), raw)
        gate_out = gate_chunks[0].astype(f32) + last.astype(f32)
        gate_out = gate_out + ring_send(held, True).astype(f32)
    grad_inner, sums = call(
        inner_back_kernel,
        6,
        [lengths],
        [first[0], second[0], first[3], second[3], raw, norm_grad] + conv_params,
        [((total, channels), bf16), ((16, channels), f32)],
        [masks, ((total, channels), f32), ((total + pad, channels), f32)],
    )

    def project_back():
        return call(
            functools.partial(project_back_kernel, fast),
            6,
            [place],
            [
                grad_gate,
                grad_inner,
                grad_state_low,
                step_low,
                gate_full,
                inner_full,
                state_full,
                step_full,
            ],
            [((2, 128, depth), bf16)] * 2,
            [
                ((total, channels), bf16),
                ((total, channels), bf16),
                ((total, states), bf16),
                ((head_rows, total), bf16),
            ],
        )

    def chunk_pair(slots, got, after=None, last=bf16):
        grad = grad_inner if after is None else ordered(after, grad_inner)[1]
        arrays = [grad, step_low, sums, *state_parts, turned, turned, *got]

        def whole(array):
            return pl.BlockSpec(array.shape, lambda i, place: (0, 0))

        def block(slot):
            return pl.BlockSpec((tall, total), lambda i, place: (place[slot], 0))

        specs = [whole(array) for array in arrays]
        specs[7:9] = [block(slot) for slot in slots]
        out = pl.BlockSpec((tall + 48, channels), lambda i, place: (0, 0))
        return pl.pallas_call(
            functools.partial(chunk_kernel, slots, len(got)),
            grid_spec=pltpu.PrefetchScalarGridSpec(
                num_scalar_prefetch=1, grid=(1,), in_specs=specs, out_specs=[out, out]
            ),
            out_shape=[
                jax.ShapeDtypeStruct((tall + 48, channels), kind) for kind in (bf16, last)
            ],
            compiler_params=pltpu.CompilerParams(vmem_limit_bytes=vmem_bytes),
            cost_estimate=pl.CostEstimate(
                flops=2_000_000_000, bytes_accessed=1 << 20, transcendentals=0
            ),
        )(place, *arrays)

    if fast:
        held = chunk_pair((7, 5), ())
        got = ring_step(held)
        keep_rows, give_rows = project_back()
        held = chunk_pair((6, 3), got, give_rows)
        partial_out = ordered(held, partial_out)[1]
        got = ring_step(held)
        mixed_rows = tensor_sum(partial_out, depth)
        near = tensor_swap(give_rows, 1)
        far_half = add_low(keep_rows[1], near[1])
        got = ring_step(chunk_pair((4, 1), got))
        held, inner_own = chunk_pair((2, 0), got, (mixed_rows, far_half), last=f32)
        inner_out = inner_own + ring_send(held, True).astype(f32)
    else:
        (inner_msg,) = call(
            message_kernel,
            5,
            [],
            [grad_inner, step_low, turned],
            [((chunks, tall + head_rows, channels), bf16)],
            [],
        )
        keep_rows, give_rows = project_back()

    token_float = tokens.astype(f32)
    gain_full = small_full[: depth // states].reshape(1, depth)

    if fast:
        far = tensor_swap(far_half, 2)
        grad_local = keep_rows[0].astype(f32) + near[0].astype(f32) + far.astype(f32)
        gate_grad, output_grad = gate_out[:tall], gate_out[tall:].T
        inner_grad = inner_out[:tall]
        state_grad = inner_out[tall : tall + 16]
        state_grad = jnp.concatenate([state_grad[:, :states], state_grad[:, states:]], axis=0)
        sums = inner_out[tall + 16 : tall + 32] + inner_out[tall + 32 :]
        step_grad = sums[10:12].reshape(heads, tall).T
        width = states // owners
        conv_state_sum = lax.dynamic_slice(
            sums[7:10].reshape(6, states), (0, owner * width), (taps + 1, width)
        )
        conv_state_grad, conv_state_bias_grad = conv_state_sum[:taps], conv_state_sum[taps]
    else:
        state_part, state_sums = state_parts
        state_grad = lax.psum_scatter(
            state_part.astype(f32), ("dp", "tensor"), scatter_dimension=0, tiled=True
        )
        conv_state_sum = lax.psum_scatter(
            state_sums[: taps + 1], ("dp", "tensor"), scatter_dimension=1, tiled=True
        )
        conv_state_grad, conv_state_bias_grad = conv_state_sum[:taps], conv_state_sum[taps]
        grad_normed = jnp.stack([keep_rows, give_rows], axis=1).reshape(total, depth)
        mixed_rows, grad_local = (
            lax.psum_scatter(part, "tensor", scatter_dimension=0, tiled=True).astype(f32)
            for part in (partial_out, grad_normed)
        )
        both, inner_float = jnp.stack(gate_chunks).astype(f32), inner_msg.astype(f32)
        gate_grad, output_grad, inner_grad = (
            lax.psum_scatter(part.reshape(depth, channels), "dp", scatter_dimension=0, tiled=True)
            for part in (both[:, :tall], both[:, tall:], inner_float[:, :tall])
        )
        output_grad = output_grad.T
        step_part = inner_float[:, tall : tall + heads, :tall].transpose(0, 2, 1)
        step_part = step_part.reshape(depth, heads)
        step_grad = lax.psum_scatter(step_part, "dp", scatter_dimension=0, tiled=True)
        sums = lax.psum(sums, "dp")
    input_grad = jnp.stack([gate_grad, inner_grad], axis=1)
    own_gain = jnp.sum(input_weight.astype(f32) * input_grad, axis=(1, 2))
    own_gain = own_gain + jnp.sum(step_weight.astype(f32) * step_grad, axis=1)
    state_gain = jnp.sum(state_weight.astype(f32) * state_grad, axis=1)
    if fast:
        own_gain = sum(tensor_direct(own_gain))
        own_gain = lax.dynamic_slice(own_gain, (me * share,), (share,))
    else:
        own_gain = lax.psum_scatter(own_gain, "tensor", scatter_dimension=0, tiled=True)
    pre_gain_grad = (own_gain + state_gain) / pre_gain.astype(f32)
    block_out = (token_float + mixed_rows).astype(bf16)
    scale = lax.rsqrt(jnp.mean(token_float * token_float, axis=1, keepdims=True) + epsilon)
    grad_scaled = grad_local * gain_full
    along = jnp.sum(grad_scaled * token_float, axis=1, keepdims=True) / depth
    tokens_grad = (
        scale * grad_scaled
        - token_float * (scale * scale * scale * along)
        + cotangent.astype(f32)
    )
    skip_grad = sums[6].reshape(heads, -1).sum(axis=1)
    return (
        block_out,
        tokens_grad,
        pre_gain_grad,
        input_grad,
        step_grad,
        state_grad,
        sums[:taps],
        sums[taps],
        conv_state_grad,
        conv_state_bias_grad,
        sums[9, states : states + heads],
        sums[9, states + 128 : states + 128 + heads],
        skip_grad,
        sums[5],
        output_grad,
    )


def solution(mesh):
    in_specs = (
        P(("dp", "tensor"), None),
        P("dp", None),
        P(("dp", "tensor"), None),
        P(("dp", "tensor")),
        P("dp", None, "tensor"),
        P("dp", "tensor"),
        P(("dp", "tensor"), None),
        P(None, "tensor"),
        P("tensor"),
        P(None, ("dp", "tensor")),
        P(("dp", "tensor")),
        P("tensor"),
        P("tensor"),
        P("tensor"),
        P("tensor"),
        P("tensor", "dp"),
    )
    out_specs = (
        P(("dp", "tensor"), None),
        P(("dp", "tensor"), None),
        P(("dp", "tensor")),
        P("dp", None, "tensor"),
        P("dp", "tensor"),
        P(("dp", "tensor"), None),
        P(None, "tensor"),
        P("tensor"),
        P(None, ("dp", "tensor")),
        P(("dp", "tensor")),
        P("tensor"),
        P("tensor"),
        P("tensor"),
        P("tensor"),
        P("tensor", "dp"),
    )
    return jax.shard_map(body, mesh=mesh, in_specs=in_specs, out_specs=out_specs, check_vma=False)
```

```python
import functools

import jax
import jax.numpy as jnp
from jax import lax
from jax.experimental import pallas as pl
from jax.experimental.pallas import tpu as pltpu
from jax.sharding import PartitionSpec as P

epsilon = 1e-05
highest = lax.Precision.HIGHEST
f32 = jnp.float32
bf16 = jnp.bfloat16
span = 256
pad = 8
head_rows = 16
head_width = 64
vmem_bytes = 61 * 1024 * 1024


def mm(a, b, over=(1, 0)):
    dims = (((over[0],), (over[1],)), ((), ()))
    return lax.dot_general(a, b, dims, preferred_element_type=f32)


def mm_exact(a, b, over=(1, 0)):
    dims = (((over[0],), (over[1],)), ((), ()))
    return lax.dot_general(a, b, dims, preferred_element_type=f32, precision=highest)


def sigmoid(v):
    return 1.0 / (1.0 + jnp.exp(-v))


def ends_of(lengths_ref):
    ends, total = [], None
    for slot in range(lengths_ref.shape[1]):
        here = lengths_ref[0, slot]
        total = here if total is None else total + here
        ends.append(total)
    return ends


def segment_of(places, ends):
    segment = jnp.zeros(places.shape, jnp.int32)
    for end in ends:
        segment = segment + jnp.where(places >= end, 1, 0)
    return segment


def iota(shape, dim):
    return lax.broadcasted_iota(jnp.int32, shape, dim)


def write_masks(mask_ref, ends):
    rows = mask_ref.shape[1] - pad
    places = iota((rows, 128), 0)
    segment = segment_of(places, ends)
    for shift in range(1, mask_ref.shape[0] + 1):
        same = (segment_of(places - shift, ends) == segment) & (places >= shift)
        mask_ref[shift - 1, :rows, :] = jnp.where(same, 1.0, 0.0)
        mask_ref[shift - 1, rows:, :] = jnp.zeros((pad, 128), f32)


def shifted_rows(x_ref, mask_ref, at, cols, shift, tall):
    part = x_ref[pad + at - shift : pad + at - shift + tall, cols]
    if shift == 0:
        return part
    return part * mask_ref[shift - 1, at : at + tall, :]


def conv_pre(x_ref, mask_ref, taps_ref, bias_ref, at, cols, tall):
    taps = taps_ref.shape[0]
    shifted = [shifted_rows(x_ref, mask_ref, at, cols, s, tall) for s in range(taps)]
    total = bias_ref[:, cols]
    for s in range(taps):
        total = total + taps_ref[taps - 1 - s : taps - s, cols] * shifted[s]
    return total, shifted


def column_loop(width, step):
    def one(c, carry):
        step(pl.ds(pl.multiple_of(c * 128, 128), 128))
        return carry

    lax.fori_loop(0, width // 128, one, 0)


def row_loop(rows, tall, step):
    def one(r, carry):
        step(pl.multiple_of(r * tall, tall))
        return carry

    lax.fori_loop(0, rows // tall, one, 0)


class Block:
    def __init__(self, b, ends, step_col, step_row, rate_col, rate_row, state_ref):
        low, top = b * span, (b + 1) * span
        states = state_ref.shape[1] // 2
        lower = jnp.where(iota((span, span), 0) >= iota((span, span), 1), 1.0, 0.0)
        self.rows = slice(low, top)
        self.step = step_col[low:top]
        self.step_row = step_row[:, low:top]
        self.cum = mm_exact(lower, rate_col[low:top])
        self.cum_row = mm_exact(rate_row[:, low:top], lower, (1, 1))
        self.inputs = state_ref[low:top, :states].astype(bf16)
        self.outputs = state_ref[low:top, states:].astype(bf16)
        segment = segment_of(iota((span, 1), 0) + low, ends)
        segment_row = segment_of(iota((1, span), 1) + low, ends)
        edge = sum(jnp.where(span - 1 >= end, 1, 0) for end in ends)
        self.near_edge = jnp.where(segment == edge, 1.0, 0.0)
        self.mask = jnp.where(segment == segment_row, lower, 0.0)
        self.contact = mm(self.outputs, self.inputs, (1, 1)) * self.mask

    def decay(self, h):
        gap = self.cum[:, h : h + 1] - self.cum_row[h : h + 1, :]
        return jnp.exp(jnp.minimum(gap, 0.0))

    def from_edge(self, h):
        return jnp.exp(self.cum[:, h : h + 1]) * self.near_edge

    def to_edge(self, h):
        last = self.cum[span - 1 : span, h : h + 1]
        return jnp.exp(last - self.cum[:, h : h + 1]) * self.near_edge


def wide(low_half, left, right):
    return jnp.where(low_half, left, right)


def step_sizes(raw_col, raw_row, bias_ref, bias_col_ref, log_ref, log_col_ref):
    def soft(v):
        return jnp.maximum(v, 0.0) + jnp.log1p(jnp.exp(-jnp.abs(v)))

    step_col = soft(raw_col + bias_ref[...])
    step_row = soft(raw_row + bias_col_ref[...])
    rate_col = -step_col * jnp.exp(log_ref[...])
    rate_row = -step_row * jnp.exp(log_col_ref[...])
    return step_col, step_row, rate_col, rate_row


def forward_kernel(fast, place_ref, lengths_ref, *refs):
    n_msg = 8 if fast else 4
    n_rows = 4 if fast else 1
    row_refs, msg_refs, refs = refs[:n_rows], refs[n_rows : n_rows + n_msg], refs[n_rows + n_msg :]
    (taps_ref, bias_ref, step_bias_ref, step_bias_col_ref, log_ref, log_col_ref, skip_ref) = refs[:7]
    (
        normed_ref,
        turned_ref,
        weight_ref,
        state_weight_ref,
        step_weight_ref,
        small_ref,
        raw_ref,
        state_raw_ref,
        step_col_ref,
        step_row_ref,
        act_ref,
        state_ref,
        mixed_ref,
    ) = refs[7:20]
    mask_ref, state_taps_ref, state_bias_ref = refs[20:]
    total, channels = act_ref.shape
    ends = ends_of(lengths_ref)

    if fast:
        depth_part = 128
        small = jnp.zeros(small_ref.shape, f32)
        share = state_weight_ref.shape[0] // 32
        for slot in range(8):
            msg = msg_refs[slot]
            index = place_ref[slot]
            at = pl.multiple_of(index * depth_part, depth_part)
            weight_ref[pl.ds(at, depth_part), :] = msg[:depth_part, :]
            for member in range(4):
                inner = pl.multiple_of(at + place_ref[8 + member] * share, share)
                high, low = depth_part + share * (member // 2), 256 * (member % 2)
                state_weight_ref[pl.ds(inner, share), :] = msg[
                    high : high + share, low : low + 256
                ]
            tail = depth_part + 2 * share
            small = small + msg[tail : tail + 16, :256].astype(f32)
            step_weight_ref[:, pl.ds(at, depth_part)] = msg[tail : tail + 16, 256:384]
        small_ref[...] = small
    else:
        weight_ref[...] = msg_refs[0][...]
        state_weight_ref[...] = msg_refs[1][...]
        step_weight_ref[...] = msg_refs[2][...]
        small_ref[...] = msg_refs[3][...].astype(f32)
    gain = jnp.concatenate([small_ref[i : i + 1, :] for i in range(4)], axis=1)
    taps = taps_ref.shape[0]
    state_taps_ref[...] = small_ref[4 : 4 + taps, :]
    state_bias_ref[...] = small_ref[4 + taps : 5 + taps, :]

    tall = total // n_rows
    for member in range(n_rows):
        at = pl.multiple_of(place_ref[8 + member] * tall, tall) if fast else 0
        value = row_refs[member][:tall, :].astype(f32)
        scale = lax.rsqrt(jnp.mean(value * value, axis=1, keepdims=True) + epsilon)
        normed = (value * scale * gain).astype(bf16)
        normed_ref[pl.ds(at, tall), :] = normed
        turned_ref[:, pl.ds(at, tall)] = normed.astype(f32).T.astype(bf16)

    raw_ref[:pad, :] = jnp.zeros((pad, channels), f32)
    state_raw_ref[:pad, :] = jnp.zeros((pad, state_raw_ref.shape[1]), f32)

    def project(at):
        part = normed_ref[pl.ds(at, 128), :]
        raw_ref[pl.ds(at + pad, 128), :] = mm(part, weight_ref[...])
        state_raw_ref[pl.ds(at + pad, 128), :] = mm(part, state_weight_ref[...])
        step_col_ref[pl.ds(at, 128), :] = mm(part, step_weight_ref[...], (1, 1))

    row_loop(total, 128, project)
    step_row_ref[...] = mm(step_weight_ref[...], normed_ref[...], (1, 1))

    write_masks(mask_ref, ends)

    def activate(x_ref, out_ref, own_taps, own_bias):
        def column(cols):
            for at in range(0, total, 128):
                pre, _ = conv_pre(x_ref, mask_ref, own_taps, own_bias, at, cols, 128)
                out_ref[at : at + 128, cols] = pre * sigmoid(pre)

        column_loop(out_ref.shape[1], column)

    activate(raw_ref, act_ref, taps_ref, bias_ref)
    activate(state_raw_ref, state_ref, state_taps_ref, state_bias_ref)

    steps = step_sizes(
        step_col_ref[...],
        step_row_ref[...],
        step_bias_ref,
        step_bias_col_ref,
        log_ref,
        log_col_ref,
    )
    low_half = iota((span, 128), 1) < head_width
    held = []
    for b in range(total // span):
        block = Block(b, ends, *steps, state_ref)
        for i in range(channels // 128):
            cols = slice(128 * i, 128 * (i + 1))
            pair = (2 * i, 2 * i + 1)
            x = act_ref[block.rows, cols]
            step_wide = wide(low_half, *(block.step[:, h : h + 1] for h in pair))
            x_step = (x * step_wide).astype(bf16)
            y = [mm((block.decay(h) * block.contact).astype(bf16), x_step) for h in pair]
            y = wide(low_half, *y) + skip_ref[:, cols] * x
            if b == 0:
                reach = wide(low_half, *(block.to_edge(h) for h in pair))
                weighted = (x * step_wide * reach).astype(bf16)
                held.append(mm(block.inputs, weighted, (0, 0)).astype(bf16))
            else:
                reach = wide(low_half, *(block.from_edge(h) for h in pair))
                y = y + reach * mm(block.outputs, held[i])
            mixed_ref[block.rows, cols] = y


def grad_in_kernel(fast, place_ref, lengths_ref, *refs):
    n_rows = 4 if fast else 1
    n_msg = 8 if fast else 2
    row_refs, msg_refs, refs = refs[:n_rows], refs[n_rows : n_rows + n_msg], refs[n_rows + n_msg :]
    normed_ref, mixed_ref, norm_ref = refs[:3]
    rows_ref, gate_weight_ref, out_weight_ref, gate_ref, grad_ref, sums_ref, wide_ref = refs[3:]
    total = rows_ref.shape[0]
    ends = ends_of(lengths_ref)
    tall = total // n_rows
    for member in range(n_rows):
        at = pl.multiple_of(place_ref[8 + member] * tall, tall) if fast else 0
        rows_ref[pl.ds(at, tall), :] = row_refs[member][-tall:, :]
    if fast:
        for slot in range(8):
            at = pl.multiple_of(place_ref[slot] * 128, 128)
            gate_weight_ref[pl.ds(at, 128), :] = msg_refs[slot][:128, :]
            out_weight_ref[pl.ds(at, 128), :] = msg_refs[slot][128:, :]
    else:
        gate_weight_ref[...] = msg_refs[0][...]
        out_weight_ref[...] = msg_refs[1][...]

    def part(at):
        rows = pl.ds(at, 128)
        valid = jnp.where(iota((128, 1), 0) + at < ends[-1], 1.0, 0.0)
        grad = mm(rows_ref[rows, :], out_weight_ref[...]) * valid
        grad_ref[rows, :] = grad
        gate = mm(normed_ref[rows, :], gate_weight_ref[...])
        gate_ref[rows, :] = gate
        gated = mixed_ref[rows, :] * (gate * sigmoid(gate))
        square = jnp.sum(gated * gated, axis=1, keepdims=True)
        cross = jnp.sum(grad * norm_ref[...] * gated, axis=1, keepdims=True)
        lane = iota((128, 128), 1)
        wide_ref[rows, :] = jnp.where(lane == 0, square, jnp.where(lane == 1, cross, 0.0))

    row_loop(total, 128, part)
    for at in range(0, total, 128):
        sums_ref[:, at : at + 128] = wide_ref[at : at + 128, :].T[:8, :]


def norm_kernel(inner_total, place_ref, lengths_ref, *refs):
    n_sums = len(refs) - 21
    sums_refs, refs = refs[:n_sums], refs[n_sums:]
    gate_ref, mixed_ref, grad_ref, norm_ref, weight_ref, rows_ref, turned_ref = refs[:7]
    chunk_refs = refs[7:15]
    partial_ref, grad_gate_ref, grad_mixed_ref, norm_grad_ref = refs[15:19]
    wide_ref, out_rows_ref = refs[19:]
    total, channels = gate_ref.shape
    ends = ends_of(lengths_ref)
    for at in range(0, total, 128):
        tile = sum(ref[:, at : at + 128] for ref in sums_refs)
        tile = jnp.concatenate([tile] * 16, axis=0)
        wide_ref[at : at + 128, :] = tile.T
    norm_grad_ref[...] = jnp.zeros(norm_grad_ref.shape, f32)

    def part(at):
        rows = pl.ds(at, 128)
        valid = jnp.where(iota((128, 1), 0) + at < ends[-1], 1.0, 0.0)
        scale = lax.rsqrt(wide_ref[rows, 0:1] / inner_total + epsilon)
        cross = wide_ref[rows, 1:2]
        gate = gate_ref[rows, :]
        mixed = mixed_ref[rows, :]
        sig = sigmoid(gate)
        gate_act = gate * sig
        gated = mixed * gate_act
        grad = grad_ref[rows, :]
        norm = norm_ref[...]
        hat = gated * scale
        out_rows_ref[rows, :] = (hat * norm * valid).astype(bf16)
        norm_grad_ref[...] += jnp.sum(grad * hat, axis=0, keepdims=True)
        grad_gated = scale * (grad * norm) - gated * (scale * scale * scale * cross / inner_total)
        grad_mixed_ref[rows, :] = grad_gated * gate_act
        grad_gate = grad_gated * mixed * sig * (1.0 + gate * (1.0 - sig))
        grad_gate_ref[rows, :] = grad_gate.astype(bf16)

    row_loop(total, 128, part)

    def back(at):
        cols = pl.ds(at, 256)
        partial_ref[:, cols] = mm(out_rows_ref[...], weight_ref[cols, :], (1, 1)).astype(bf16)

    row_loop(weight_ref.shape[0], 256, back)
    tall = chunk_refs[0].shape[0] // 2
    for slot, chunk_ref in enumerate(chunk_refs):
        cols = pl.ds(pl.multiple_of(place_ref[slot] * tall, tall), tall)
        chunk_ref[:tall, :] = mm(turned_ref[cols, :], grad_gate_ref[...]).astype(bf16)
        chunk_ref[tall:, :] = mm(rows_ref[:, cols], out_rows_ref[...], (0, 0)).astype(bf16)


def scan_back_kernel(first_pair, lengths_ref, *refs):
    grad_mixed_ref, act_ref, state_ref, step_col_ref, step_row_ref = refs[:5]
    step_bias_ref, step_bias_col_ref, log_ref, log_col_ref, skip_ref = refs[5:10]
    grad_act_ref, grad_state_ref, step_grad_ref, sums_ref, acc_ref = refs[10:]
    total, own_width = grad_act_ref.shape
    states = state_ref.shape[1] // 2
    ends = ends_of(lengths_ref)
    sums_ref[...] = jnp.zeros(sums_ref.shape, f32)
    raw_row = step_row_ref[...]
    steps = step_sizes(
        step_col_ref[...], raw_row, step_bias_ref, step_bias_col_ref, log_ref, log_col_ref
    )
    rate_row = steps[3]
    low_half = iota((span, 128), 1) < head_width
    lower = jnp.where(iota((span, span), 0) >= iota((span, span), 1), 1.0, 0.0)
    blocks = [Block(b, ends, *steps, state_ref) for b in range(total // span)]
    first, second = blocks
    row_sums, step_rows, out_sums, in_sums = [], [], None, None
    grad_out = jnp.zeros((span, states), f32)
    grad_in = jnp.zeros((span, states), f32)
    head_of = iota((head_rows, 128), 0)
    lane_head = iota((head_rows, 128), 1) // head_width

    for b, block in enumerate(blocks):
        acc_ref[...] = jnp.zeros((span, span), f32)
        row_sum = jnp.zeros((span, 128), f32)
        step_grad = jnp.zeros((head_rows, span), f32)
        lane = iota((span, 128), 1)
        head_row = iota((head_rows, span), 0)
        for i in range(first_pair, first_pair + own_width // 128):
            cols = slice(128 * i, 128 * (i + 1))
            own_cols = slice(128 * (i - first_pair), 128 * (i - first_pair + 1))
            pair = (2 * i, 2 * i + 1)
            x = act_ref[block.rows, cols]
            x_low = x.astype(bf16)
            grad = grad_mixed_ref[block.rows, cols]
            grad_low = grad.astype(bf16)
            halves = (
                jnp.where(low_half, grad, 0.0).astype(bf16),
                jnp.where(low_half, 0.0, grad).astype(bf16),
            )
            step_wide = wide(low_half, *(block.step[:, h : h + 1] for h in pair))
            grads = []
            for h, half in zip(pair, halves):
                decay = block.decay(h)
                spread = mm(half, x_low, (1, 1)) * decay
                stepped = spread * block.step_row[h : h + 1, :]
                acc_ref[...] += stepped
                row_here = jnp.sum(stepped * block.contact, axis=1, keepdims=True)
                row_sum = jnp.where(lane == h, row_here, row_sum)
                step_here = jnp.sum(spread * block.contact, axis=0, keepdims=True)
                step_grad = jnp.where(head_row == h, step_here, step_grad)
                grads.append(mm((decay * block.contact).astype(bf16), grad_low, (0, 0)))
            grad_act = wide(low_half, *grads) * step_wide + skip_ref[:, cols] * grad
            sums_ref[2:3, own_cols] += jnp.sum(grad * x, axis=0, keepdims=True)
            picks = jnp.where(lane_head + 2 * i == head_of, 1.0, 0.0)
            if b == 0:
                reach = wide(low_half, *(second.from_edge(h) for h in pair))
                lead = (grad_mixed_ref[second.rows, cols] * reach).astype(bf16)
                edge = wide(low_half, *(block.to_edge(h) for h in pair))
                weighted = (x * step_wide * edge).astype(bf16)
                held = mm(block.inputs, weighted, (0, 0)).astype(bf16)
                held_grad = mm(second.outputs, lead, (0, 0)).astype(bf16)
                grad_out = grad_out + mm(lead, held, (1, 1))
                grad_in = grad_in + mm(weighted, held_grad, (1, 1))
                back = mm(block.inputs, held_grad) * edge
                grad_act = grad_act + back * step_wide
                ahead = mm(second.outputs, held)
                out_here = mm_exact(picks, lead.astype(f32) * ahead, (1, 1))
                in_here = mm_exact(picks, x * back, (1, 1))
                out_sums = out_here if out_sums is None else out_sums + out_here
                in_sums = in_here if in_sums is None else in_sums + in_here
            grad_act_ref[block.rows, own_cols] = grad_act
        table = (acc_ref[...] * block.mask).astype(bf16)
        grad_c = mm(table, block.inputs)
        grad_b = mm(table, block.outputs, (0, 0))
        if b == 0:
            grad_b = grad_b + grad_in
        else:
            grad_c = grad_c + grad_out
        grad_state_ref[block.rows, :states] = grad_b
        grad_state_ref[block.rows, states:] = grad_c
        row_sums.append(row_sum)
        step_rows.append(step_grad)

    rate_grads = []
    for b, block in enumerate(blocks):
        column = step_rows[b] * block.step_row
        crossing = mm_exact(row_sums[b], lower, (0, 0))[:head_rows] - mm_exact(column, lower)
        if b == 0:
            crossing = crossing + mm_exact(in_sums * block.step_row, 1.0 - lower)
        else:
            crossing = crossing + mm_exact(out_sums, lower)
        rate_grads.append(crossing)
    step_rows[0] = step_rows[0] + in_sums
    rate_grad = jnp.concatenate(rate_grads, axis=1)
    step_grad = jnp.concatenate(step_rows, axis=1) - rate_grad * jnp.exp(log_col_ref[...])
    step_grad = step_grad * sigmoid(raw_row + step_bias_col_ref[...])
    decay_sum = jnp.sum(rate_grad * rate_row, axis=1, keepdims=True)
    bias_sum = jnp.sum(step_grad, axis=1, keepdims=True)
    lane = iota((head_rows, 128), 1)
    head_sums = jnp.where(lane == 0, bias_sum, jnp.where(lane == 1, decay_sum, 0.0))
    head_sums = jnp.concatenate([head_sums] * (128 // head_rows), axis=0).T
    sums_ref[0:2, :128] = head_sums[:2, :]
    step_grad_ref[...] = step_grad


def conv_back(x_ref, mask_ref, grad_ref, held_ref, out_ref, sums_ref, own_taps, own_bias):
    total, taps = out_ref.shape[0], own_taps.shape[0]
    held_ref[total:, :] = jnp.zeros((pad, held_ref.shape[1]), f32)

    def column(cols):
        sums = [jnp.zeros((1, 128), f32) for _ in range(taps + 1)]
        for at in range(0, total, 128):
            pre, shifted = conv_pre(x_ref, mask_ref, own_taps, own_bias, at, cols, 128)
            sig = sigmoid(pre)
            grad = grad_ref[at : at + 128, cols] * sig * (1.0 + pre * (1.0 - sig))
            held_ref[at : at + 128, cols] = grad
            for s in range(taps):
                sums[taps - 1 - s] += jnp.sum(grad * shifted[s], axis=0, keepdims=True)
            sums[taps] += jnp.sum(grad, axis=0, keepdims=True)
        for t, value in enumerate(sums):
            sums_ref[t : t + 1, cols] = value
        for at in range(0, total, 128):
            back = own_taps[taps - 1 : taps, cols] * held_ref[at : at + 128, cols]
            for s in range(1, taps):
                part = held_ref[at + s : at + s + 128, cols]
                part = part * mask_ref[s - 1, at + s : at + s + 128, :]
                back = back + own_taps[taps - 1 - s : taps - s, cols] * part
            out_ref[at : at + 128, cols] = back.astype(bf16)

    column_loop(out_ref.shape[1], column)


def state_back_kernel(fast, place_ref, lengths_ref, *refs):
    state_refs, step_refs, refs = refs[0:2], refs[2:4], refs[4:]
    state_raw_ref, turned_ref, small_ref, grad_state_low_ref, step_low_ref = refs[:5]
    n_out = 4 if fast else 2
    out_refs, refs = refs[5 : 5 + n_out], refs[5 + n_out :]
    mask_ref, taps_ref, bias_ref, grad_state_ref, pre_ref, part_ref, sums_ref = refs
    taps = taps_ref.shape[0]
    taps_ref[...] = small_ref[4 : 4 + taps, :]
    bias_ref[...] = small_ref[4 + taps : 5 + taps, :]
    write_masks(mask_ref, ends_of(lengths_ref))
    grad_state_ref[...] = state_refs[0][...] + state_refs[1][...]
    step_low_ref[...] = (step_refs[0][...] + step_refs[1][...]).astype(bf16)
    sums_ref[...] = jnp.zeros(sums_ref.shape, f32)
    conv_back(
        state_raw_ref,
        mask_ref,
        grad_state_ref,
        pre_ref,
        grad_state_low_ref,
        sums_ref,
        taps_ref,
        bias_ref,
    )

    def chunk(at):
        part = turned_ref[pl.ds(at, 256), :]
        part_ref[pl.ds(at, 256), :] = mm(part, grad_state_low_ref[...]).astype(bf16)

    depth = turned_ref.shape[0]
    row_loop(depth, 256, chunk)
    if fast:
        share = depth // 32
        for member, out_ref in enumerate(out_refs):
            for c in range(8):
                at = pl.multiple_of((4 * c + place_ref[8 + member]) * share, share)
                out_ref[share * c : share * (c + 1), :] = part_ref[pl.ds(at, share), :]
            out_ref[8 * share :, :] = sums_ref[...].astype(bf16)
    else:
        out_refs[0][...] = part_ref[...]
        out_refs[1][...] = sums_ref[...]


def inner_back_kernel(lengths_ref, *refs):
    act_refs, head_refs, refs = refs[0:2], refs[2:4], refs[4:]
    raw_ref, norm_grad_ref, taps_ref, bias_ref, grad_inner_ref, sums_ref = refs[:6]
    mask_ref, grad_act_ref, pre_ref = refs[6:]
    half = grad_inner_ref.shape[1] // 2
    write_masks(mask_ref, ends_of(lengths_ref))
    grad_act_ref[:, :half] = act_refs[0][...]
    grad_act_ref[:, half:] = act_refs[1][...]
    sums_ref[...] = jnp.zeros(sums_ref.shape, f32)
    heads = head_refs[0][:2, :128] + head_refs[1][:2, :128]
    sums_ref[5:6, :] = norm_grad_ref[...]
    sums_ref[6:7, :half] = head_refs[0][2:3, :]
    sums_ref[6:7, half:] = head_refs[1][2:3, :]
    sums_ref[9:10, half : half + 128] = heads[0:1, :]
    sums_ref[9:10, half + 128 :] = heads[1:2, :]
    conv_back(
        raw_ref,
        mask_ref,
        grad_act_ref,
        pre_ref,
        grad_inner_ref,
        sums_ref,
        taps_ref,
        bias_ref,
    )


def message_kernel(grad_inner_ref, step_low_ref, turned_ref, msg_ref):
    chunks = msg_ref.shape[0]
    tall = turned_ref.shape[0] // chunks
    step_low = step_low_ref[...]

    def chunk(c, carry):
        part = turned_ref[pl.ds(pl.multiple_of(c * tall, tall), tall), :]
        msg_ref[c, :tall, :] = mm(part, grad_inner_ref[...]).astype(bf16)
        msg_ref[c, tall:, :tall] = mm(step_low, part, (1, 1)).astype(bf16)
        msg_ref[c, tall:, tall:] = jnp.zeros((head_rows, msg_ref.shape[2] - tall), bf16)
        return carry

    lax.fori_loop(0, chunks, chunk, 0)


def chunk_kernel(slots, n_got, place_ref, *refs):
    grad_inner_ref, step_low_ref, sums_ref = refs[:3]
    state_refs, turned_refs, got_refs = refs[3:7], refs[7:9], refs[9 : 9 + n_got]
    out_refs = refs[9 + n_got :]
    states = state_refs[0].shape[1]
    share = (state_refs[0].shape[0] - 16) // 8

    def state_rows(low, tall):
        return sum(ref[pl.ds(low, tall), :].astype(f32) for ref in state_refs)

    shared = state_rows(8 * share, 16)
    sums = [
        sums_ref[:7, :],
        jnp.concatenate([shared[0:1, :], shared[1:2, :]], axis=1),
        jnp.concatenate([shared[2:3, :], shared[3:4, :]], axis=1),
        jnp.concatenate([shared[4:5, :], sums_ref[9:10, states:]], axis=1),
    ]
    for n, (slot, out_ref) in enumerate(zip(slots, out_refs)):
        index = place_ref[slot]
        part = turned_refs[n][...]
        step = mm(step_low_ref[...], part, (1, 1))
        step = [
            jnp.concatenate([step[4 * k + i : 4 * k + i + 1, :] for i in range(4)], axis=1)
            for k in range(2)
        ]
        state = state_rows(pl.multiple_of(index * share, share), share)
        value = jnp.concatenate(
            [
                mm(part, grad_inner_ref[...]),
                jnp.concatenate([state[:16, :], state[16:, :]], axis=1),
                *sums,
                *step,
                jnp.zeros((4, 2 * states), f32),
            ],
            axis=0,
        )
        tail = value.shape[0] - 16
        main, sums_here = value[:tail, :], value[tail:, :]
        if n < n_got:
            got = got_refs[n]
            main = main + got[:tail, :].astype(f32)
            sums_here = sums_here + got[tail : tail + 16, :].astype(f32)
            sums_here = sums_here + got[tail + 16 :, :].astype(f32)
        out_ref[:tail, :] = main.astype(out_ref.dtype)
        high = sums_here.astype(bf16)
        out_ref[tail : tail + 16, :] = high.astype(out_ref.dtype)
        out_ref[tail + 16 :, :] = (sums_here - high.astype(f32)).astype(out_ref.dtype)


def project_back_kernel(fast, place_ref, *refs):
    grad_refs, step_low_ref, weight_refs, step_weight_ref = refs[:3], refs[3], refs[4:7], refs[7]
    out_refs, held_refs, step_ref = refs[8:10], refs[10:13], refs[13]
    for n, member in enumerate((0, 2, 1, 3)):
        at = pl.multiple_of(place_ref[8 + member] * 128, 128) if fast else 128 * member
        for held_ref, grad_ref in zip(held_refs, grad_refs):
            held_ref[128 * n : 128 * (n + 1), :] = grad_ref[pl.ds(at, 128), :]
        step_ref[:, 128 * n : 128 * (n + 1)] = step_low_ref[:, pl.ds(at, 128)]

    def back(at):
        cols = pl.ds(at, 256)
        grad = mm(step_ref[...], step_weight_ref[:, cols], (0, 0))
        for held_ref, weight_ref in zip(held_refs, weight_refs):
            grad = grad + mm(held_ref[...], weight_ref[cols, :], (1, 1))
        grad = grad.astype(bf16)
        for n in range(4):
            out_refs[n // 2][n % 2, :, cols] = grad[128 * n : 128 * (n + 1), :]

    row_loop(step_weight_ref.shape[1], 256, back)


def prepare_kernel(place_ref, gain_ref, taps_ref, bias_ref, state_ref, shared_ref):
    owner = place_ref[0]
    share, states = state_ref.shape
    shared_ref[:share, :] = state_ref[...]

    def placed(value, at):
        width = value.shape[1]
        pick = iota((width, states), 1) - at == iota((width, states), 0)
        return mm(value, jnp.where(pick, 1.0, 0.0).astype(bf16))

    start = owner * gain_ref.shape[1]
    small = jnp.concatenate(
        [placed(gain_ref[...], start - states * i) for i in range(4)]
        + [placed(taps_ref[...], owner * taps_ref.shape[1])]
        + [placed(bias_ref[...], owner * bias_ref.shape[1])]
        + [jnp.zeros((7, states), f32)],
        axis=0,
    )
    shared_ref[share:, :] = small.astype(bf16)


def prepare_late_kernel(input_ref, out_ref, late_ref):
    depth_part = input_ref.shape[0]
    late_ref[:depth_part, :] = input_ref[:, 0, :]
    late_ref[depth_part:, :] = out_ref[...].astype(f32).T.astype(bf16)


def params_kernel(*refs):
    taps_ref, bias_ref, step_bias_ref, log_ref, skip_ref, norm_ref = refs[:6]
    outs = refs[6:]
    heads = step_bias_ref.shape[1]
    pick = jnp.where(iota((heads, head_rows), 0) == iota((heads, head_rows), 1), 1.0, 0.0)
    square = iota((head_rows, head_rows), 0) == iota((head_rows, head_rows), 1)

    def both(value_ref, row_ref, col_ref):
        row = mm_exact(value_ref[...].astype(f32), pick)
        row_ref[...] = row
        col_ref[...] = jnp.sum(jnp.where(square, row, 0.0), axis=1, keepdims=True)

    outs[0][...] = taps_ref[...].astype(f32)
    outs[1][...] = bias_ref[...].astype(f32)
    both(step_bias_ref, outs[2], outs[3])
    both(log_ref, outs[4], outs[5])
    channels = norm_ref.shape[1]
    own = iota((heads, channels), 1) // (channels // heads) == iota((heads, channels), 0)
    outs[6][...] = mm_exact(skip_ref[...].astype(f32), jnp.where(own, 1.0, 0.0))
    outs[7][...] = norm_ref[...].astype(f32)


def assemble_kernel(input_ref, step_ref, *refs):
    shared_refs, msg_ref = refs[:4], refs[4]
    depth_part, _, channels = input_ref.shape
    share = shared_refs[0].shape[0] - 16
    tail = depth_part + 2 * share
    msg_ref[:depth_part, :] = input_ref[:, 1, :]
    for member, ref in enumerate(shared_refs):
        high, low = depth_part + share * (member // 2), 256 * (member % 2)
        msg_ref[high : high + share, low : low + 256] = ref[:share, :]
    small = sum(ref[share:, :].astype(f32) for ref in shared_refs)
    msg_ref[tail:, :256] = small.astype(bf16)
    msg_ref[tail:, 256:384] = step_ref[...]
    msg_ref[tail:, 384:] = jnp.zeros((16, channels - 384), bf16)


def call(kernel, micros, scalars, arrays, outs, scratch):
    smem = pl.BlockSpec(memory_space=pltpu.SMEM)
    vmem = pl.BlockSpec(memory_space=pltpu.VMEM)
    return pl.pallas_call(
        kernel,
        out_shape=[jax.ShapeDtypeStruct(shape, kind) for shape, kind in outs],
        in_specs=[smem] * len(scalars) + [vmem] * len(arrays),
        out_specs=[vmem] * len(outs),
        scratch_shapes=[pltpu.VMEM(shape, kind) for shape, kind in scratch],
        compiler_params=pltpu.CompilerParams(vmem_limit_bytes=vmem_bytes),
        cost_estimate=pl.CostEstimate(
            flops=int(micros * 1.1e9), bytes_accessed=1 << 20, transcendentals=0
        ),
    )(*scalars, *arrays)


def ring_ok(n_dp, n_tensor):
    return n_dp == 8 and n_tensor == 4


ring_order = (0, 2, 4, 6, 7, 5, 3, 1)


def ring_place(index):
    high, low = index // 2, index % 2
    return jnp.where(low == 0, high, 7 - high)


def ring_index(place):
    place = lax.rem(place + 16, 8)
    return jnp.where(place < 4, 2 * place, 2 * (7 - place) + 1)


def ring_send(value, forward):
    pairs = []
    for place in range(8):
        other = (place + (1 if forward else 7)) % 8
        pairs.append((ring_order[place], ring_order[other]))
    return lax.ppermute(value, "dp", pairs)


def ring_gather(value):
    me = ring_place(lax.axis_index("dp"))
    pieces = [(value, ring_index(me))]
    ahead, back = value, value
    for step in range(1, 5):
        ahead = ring_send(ahead, True)
        pieces.append((ahead, ring_index(me - step)))
        if step < 4:
            back = ring_send(back, False)
            pieces.append((back, ring_index(me + step)))
    return pieces


def dp_swap(value, bit):
    return lax.ppermute(value, "dp", [(i, i ^ bit) for i in range(8)])


def ring_step(held):
    return ring_send(held[0], True), ring_send(held[1], False)


def add_low(got, own):
    return (got.astype(f32) + own.astype(f32)).astype(bf16)


def ordered(first, then):
    return lax.optimization_barrier((first, then))


def tensor_gather(value):
    near = tensor_swap(value, 1)
    far = tensor_swap(value, 2)
    return [value, near, far, tensor_swap(far, 1)]


def tensor_direct(value):
    return [value] + [tensor_swap(value, bit) for bit in range(1, 4)]


def tensor_sum(value, depth):
    parts = value.reshape(4, -1, depth)
    parts = lax.all_to_all(parts, "tensor", 0, 0, tiled=True)
    return jnp.sum(parts.astype(f32), axis=0)


def tensor_swap(value, bit):
    return lax.ppermute(value, "tensor", [(i, i ^ bit) for i in range(4)])


def body(
    tokens,
    lengths,
    cotangent,
    pre_gain,
    input_weight,
    step_weight,
    state_weight,
    conv_inner,
    conv_inner_bias,
    conv_state,
    conv_state_bias,
    step_bias,
    decay_log,
    skip_gain,
    norm_gain,
    output_weight,
):
    n_dp, n_tensor = lax.axis_size("dp"), lax.axis_size("tensor")
    fast = ring_ok(n_dp, n_tensor)
    owners = n_dp * n_tensor
    me = lax.axis_index("tensor")
    owner = lax.axis_index("dp") * n_tensor + me
    own_rows, depth = tokens.shape
    total = own_rows * n_tensor
    states = state_weight.shape[1]
    heads = step_weight.shape[1]
    share = state_weight.shape[0]
    taps = conv_state.shape[0]
    channels = input_weight.shape[2]
    inner_total = channels * n_tensor

    owner_place = jnp.stack([owner, owners]).astype(jnp.int32)
    (shared,) = call(
        prepare_kernel,
        1,
        [owner_place],
        [pre_gain[None, :], conv_state, conv_state_bias[None, :], state_weight],
        [((share + 16, states), bf16)],
        [],
    )
    step_rows = jnp.pad(step_weight.T, ((0, head_rows - heads), (0, 0)))
    shared, out_shard = ordered(shared, output_weight)
    (late,) = call(
        prepare_late_kernel,
        2,
        [],
        [input_weight, out_shard],
        [((input_weight.shape[0] + output_weight.shape[1], channels), bf16)],
        [],
    )
    params = call(
        params_kernel,
        1,
        [],
        [
            conv_inner,
            conv_inner_bias[None, :],
            step_bias[None, :],
            decay_log[None, :],
            skip_gain[None, :],
            norm_gain[None, :],
        ],
        [
            ((taps, channels), f32),
            ((1, channels), f32),
            ((1, head_rows), f32),
            ((head_rows, 1), f32),
            ((1, head_rows), f32),
            ((head_rows, 1), f32),
            ((1, channels), f32),
            ((1, channels), f32),
        ],
        [],
    )
    params = list(params)
    conv_params, head_params, norm_row = params[:2], params[2:7], params[7]
    if fast:
        shared = tensor_direct(shared)
        late_one = ring_step((late, late))
        (msg,) = call(
            assemble_kernel,
            1,
            [],
            [input_weight, step_rows, *shared],
            [((input_weight.shape[0] + 2 * share + 16, channels), bf16)],
            [],
        )
        late_one, msg = ordered(late_one, msg)
        msg = ring_gather(msg)
        weight_pieces = [piece for piece, _ in msg]
        late_two = ring_step(late_one)
        late_three = ring_step(late_two)
        late_pieces = [late, *late_one, *late_two, *late_three, ring_send(late_three[0], True)]
        own_rows_both = jnp.concatenate([tokens, cotangent], axis=0)
        row_pieces = tensor_gather(ordered(shared, own_rows_both)[1])
        grad_pieces = row_pieces
        place = jnp.stack([index for _, index in msg] + [me, me ^ 1, me ^ 2, me ^ 3])
    else:
        row_pieces = [lax.all_gather(tokens, "tensor", axis=0, tiled=True)]
        grad_pieces = [lax.all_gather(cotangent, "tensor", axis=0, tiled=True)]
        gate_weight, inner_weight = late[: input_weight.shape[0]], input_weight[:, 1]
        weight_pieces = [
            lax.all_gather(inner_weight, "dp", axis=0, tiled=True),
            lax.all_gather(state_weight, ("dp", "tensor"), axis=0, tiled=True),
            lax.all_gather(step_rows, "dp", axis=1, tiled=True),
            lax.psum(shared[share:], ("dp", "tensor")),
        ]
        late_pieces = [
            lax.all_gather(gate_weight, "dp", axis=0, tiled=True),
            lax.all_gather(late[input_weight.shape[0] :], "dp", axis=0, tiled=True),
        ]
        place = jnp.concatenate([jnp.arange(8), jnp.arange(4)])
    place = place.astype(jnp.int32)

    masks = ((taps - 1, total + pad, 128), f32)
    state_taps = [((taps, states), f32), ((1, states), f32)]
    (
        normed,
        turned,
        inner_full,
        state_full,
        step_full,
        small_full,
        raw,
        state_raw,
        step_col,
        step_row,
        act,
        state_act,
        mixed,
    ) = call(
        functools.partial(forward_kernel, fast),
        11,
        [place, lengths],
        row_pieces + weight_pieces + conv_params + head_params,
        [
            ((total, depth), bf16),
            ((depth, total), bf16),
            ((depth, channels), bf16),
            ((depth, states), bf16),
            ((head_rows, depth), bf16),
            ((16, states), f32),
            ((total + pad, channels), f32),
            ((total + pad, states), f32),
            ((total, head_rows), f32),
            ((head_rows, total), f32),
            ((total, channels), f32),
            ((total, states), f32),
            ((total, channels), f32),
        ],
        [masks] + state_taps,
    )
    grad_rows, gate_full, output_full, gate, grad_normalized, sums = call(
        functools.partial(grad_in_kernel, fast),
        5,
        [place, lengths],
        grad_pieces + late_pieces + [normed, mixed, norm_row],
        [
            ((total, depth), bf16),
            ((depth, channels), bf16),
            ((depth, channels), bf16),
            ((total, channels), f32),
            ((total, channels), f32),
            ((8, total), f32),
        ],
        [((total, 128), f32)],
    )
    if fast:
        sums = tensor_direct(sums)
    else:
        sums = [lax.psum(sums, "tensor")]
    chunks = 8
    tall = depth // chunks
    norm_outs = call(
        functools.partial(norm_kernel, inner_total),
        9,
        [place, lengths],
        [*sums, gate, mixed, grad_normalized, norm_row, output_full, grad_rows, turned],
        [((2 * tall, channels), bf16)] * chunks
        + [
            ((total, depth), bf16),
            ((total, channels), bf16),
            ((total, channels), f32),
            ((1, channels), f32),
        ],
        [((total, 128), f32), ((total, channels), bf16)],
    )
    gate_chunks = norm_outs[:chunks]
    partial_out, grad_gate, grad_mixed, norm_grad = norm_outs[chunks:]

    def scan_back(first_pair, grad):
        return call(
            functools.partial(scan_back_kernel, first_pair),
            6,
            [lengths],
            [grad, act, state_act, step_col, step_row] + head_params,
            [
                ((total, channels // 2), f32),
                ((total, states), f32),
                ((head_rows, total), f32),
                ((8, channels // 2), f32),
            ],
            [((span, span), f32)],
        )

    if fast:
        got = ring_step((gate_chunks[7], gate_chunks[5]))
        held = add_low(got[0], gate_chunks[6]), add_low(got[1], gate_chunks[3])
    first = scan_back(0, grad_mixed)
    if fast:
        held, grad_mixed = ordered(held, grad_mixed)
        got = ring_step(held)
        held = add_low(got[0], gate_chunks[4]), add_low(got[1], gate_chunks[1])
    second = scan_back(channels // 256, grad_mixed)
    if fast:
        held, state_raw = ordered(held, state_raw)
        got = ring_step(held)
        held, last = add_low(got[0], gate_chunks[2]), got[1]
    share_rows = depth // 4 + 16
    state_outs = call(
        functools.partial(state_back_kernel, fast),
        4,
        [place, lengths],
        [first[1], second[1], first[2], second[2], state_raw, turned, small_full],
        [((total, states), bf16), ((head_rows, total), bf16)]
        + (
            [((share_rows, states), bf16)] * 4
            if fast
            else [((depth, states), bf16), ((16, states), f32)]
        ),
        [
            masks,
            *state_taps,
            ((total, states), f32),
            ((total + pad, states), f32),
            ((depth, states), bf16),
            ((16, states), f32),
        ],
    )
    grad_state_low, step_low = state_outs[:2]
    state_parts = state_outs[2:]
    if fast:
        state_parts = [state_parts[0]] + [tensor_swap(state_parts[i], i) for i in range(1, 4)]
    if fast:
        (held, last), raw = ordered((held, last), raw)
        gate_out = gate_chunks[0].astype(f32) + last.astype(f32)
        gate_out = gate_out + ring_send(held, True).astype(f32)
    grad_inner, sums = call(
        inner_back_kernel,
        6,
        [lengths],
        [first[0], second[0], first[3], second[3], raw, norm_grad] + conv_params,
        [((total, channels), bf16), ((16, channels), f32)],
        [masks, ((total, channels), f32), ((total + pad, channels), f32)],
    )

    def project_back():
        return call(
            functools.partial(project_back_kernel, fast),
            6,
            [place],
            [
                grad_gate,
                grad_inner,
                grad_state_low,
                step_low,
                gate_full,
                inner_full,
                state_full,
                step_full,
            ],
            [((2, 128, depth), bf16)] * 2,
            [
                ((total, channels), bf16),
                ((total, channels), bf16),
                ((total, states), bf16),
                ((head_rows, total), bf16),
            ],
        )

    def chunk_pair(slots, got, after=None, last=bf16):
        grad = grad_inner if after is None else ordered(after, grad_inner)[1]
        arrays = [grad, step_low, sums, *state_parts, turned, turned, *got]

        def whole(array):
            return pl.BlockSpec(array.shape, lambda i, place: (0, 0))

        def block(slot):
            return pl.BlockSpec((tall, total), lambda i, place: (place[slot], 0))

        specs = [whole(array) for array in arrays]
        specs[7:9] = [block(slot) for slot in slots]
        out = pl.BlockSpec((tall + 48, channels), lambda i, place: (0, 0))
        return pl.pallas_call(
            functools.partial(chunk_kernel, slots, len(got)),
            grid_spec=pltpu.PrefetchScalarGridSpec(
                num_scalar_prefetch=1, grid=(1,), in_specs=specs, out_specs=[out, out]
            ),
            out_shape=[
                jax.ShapeDtypeStruct((tall + 48, channels), kind) for kind in (bf16, last)
            ],
            compiler_params=pltpu.CompilerParams(vmem_limit_bytes=vmem_bytes),
            cost_estimate=pl.CostEstimate(
                flops=2_000_000_000, bytes_accessed=1 << 20, transcendentals=0
            ),
        )(place, *arrays)

    if fast:
        held = chunk_pair((7, 5), ())
        got = ring_step(held)
        keep_rows, give_rows = project_back()
        held = chunk_pair((6, 3), got, give_rows)
        partial_out = ordered(held, partial_out)[1]
        got = ring_step(held)
        mixed_rows = tensor_sum(partial_out, depth)
        near = tensor_swap(give_rows, 1)
        far_half = add_low(keep_rows[1], near[1])
        got = ring_step(chunk_pair((4, 1), got))
        held, inner_own = chunk_pair((2, 0), got, (mixed_rows, far_half), last=f32)
        inner_out = inner_own + ring_send(held, True).astype(f32)
    else:
        (inner_msg,) = call(
            message_kernel,
            5,
            [],
            [grad_inner, step_low, turned],
            [((chunks, tall + head_rows, channels), bf16)],
            [],
        )
        keep_rows, give_rows = project_back()

    token_float = tokens.astype(f32)
    gain_full = small_full[: depth // states].reshape(1, depth)

    if fast:
        far = ordered(inner_out, tensor_swap(far_half, 2))[1]
        grad_local = keep_rows[0].astype(f32) + near[0].astype(f32) + far.astype(f32)
        gate_grad, output_grad = gate_out[:tall], gate_out[tall:].T
        inner_grad = inner_out[:tall]
        state_grad = inner_out[tall : tall + 16]
        state_grad = jnp.concatenate([state_grad[:, :states], state_grad[:, states:]], axis=0)
        sums = inner_out[tall + 16 : tall + 32] + inner_out[tall + 32 :]
        step_grad = sums[10:12].reshape(heads, tall).T
        width = states // owners
        conv_state_sum = lax.dynamic_slice(
            sums[7:10].reshape(6, states), (0, owner * width), (taps + 1, width)
        )
        conv_state_grad, conv_state_bias_grad = conv_state_sum[:taps], conv_state_sum[taps]
    else:
        state_part, state_sums = state_parts
        state_grad = lax.psum_scatter(
            state_part.astype(f32), ("dp", "tensor"), scatter_dimension=0, tiled=True
        )
        conv_state_sum = lax.psum_scatter(
            state_sums[: taps + 1], ("dp", "tensor"), scatter_dimension=1, tiled=True
        )
        conv_state_grad, conv_state_bias_grad = conv_state_sum[:taps], conv_state_sum[taps]
        grad_normed = jnp.stack([keep_rows, give_rows], axis=1).reshape(total, depth)
        mixed_rows, grad_local = (
            lax.psum_scatter(part, "tensor", scatter_dimension=0, tiled=True).astype(f32)
            for part in (partial_out, grad_normed)
        )
        both, inner_float = jnp.stack(gate_chunks).astype(f32), inner_msg.astype(f32)
        gate_grad, output_grad, inner_grad = (
            lax.psum_scatter(part.reshape(depth, channels), "dp", scatter_dimension=0, tiled=True)
            for part in (both[:, :tall], both[:, tall:], inner_float[:, :tall])
        )
        output_grad = output_grad.T
        step_part = inner_float[:, tall : tall + heads, :tall].transpose(0, 2, 1)
        step_part = step_part.reshape(depth, heads)
        step_grad = lax.psum_scatter(step_part, "dp", scatter_dimension=0, tiled=True)
        sums = lax.psum(sums, "dp")
    input_grad = jnp.stack([gate_grad, inner_grad], axis=1)
    own_gain = jnp.sum(input_weight.astype(f32) * input_grad, axis=(1, 2))
    own_gain = own_gain + jnp.sum(step_weight.astype(f32) * step_grad, axis=1)
    state_gain = jnp.sum(state_weight.astype(f32) * state_grad, axis=1)
    if fast:
        own_gain = sum(tensor_direct(own_gain))
        own_gain = lax.dynamic_slice(own_gain, (me * share,), (share,))
    else:
        own_gain = lax.psum_scatter(own_gain, "tensor", scatter_dimension=0, tiled=True)
    pre_gain_grad = (own_gain + state_gain) / pre_gain.astype(f32)
    block_out = (token_float + mixed_rows).astype(bf16)
    scale = lax.rsqrt(jnp.mean(token_float * token_float, axis=1, keepdims=True) + epsilon)
    grad_scaled = grad_local * gain_full
    along = jnp.sum(grad_scaled * token_float, axis=1, keepdims=True) / depth
    tokens_grad = (
        scale * grad_scaled
        - token_float * (scale * scale * scale * along)
        + cotangent.astype(f32)
    )
    skip_grad = sums[6].reshape(heads, -1).sum(axis=1)
    return (
        block_out,
        tokens_grad,
        pre_gain_grad,
        input_grad,
        step_grad,
        state_grad,
        sums[:taps],
        sums[taps],
        conv_state_grad,
        conv_state_bias_grad,
        sums[9, states : states + heads],
        sums[9, states + 128 : states + 128 + heads],
        skip_grad,
        sums[5],
        output_grad,
    )


def solution(mesh):
    in_specs = (
        P(("dp", "tensor"), None),
        P("dp", None),
        P(("dp", "tensor"), None),
        P(("dp", "tensor")),
        P("dp", None, "tensor"),
        P("dp", "tensor"),
        P(("dp", "tensor"), None),
        P(None, "tensor"),
        P("tensor"),
        P(None, ("dp", "tensor")),
        P(("dp", "tensor")),
        P("tensor"),
        P("tensor"),
        P("tensor"),
        P("tensor"),
        P("tensor", "dp"),
    )
    out_specs = (
        P(("dp", "tensor"), None),
        P(("dp", "tensor"), None),
        P(("dp", "tensor")),
        P("dp", None, "tensor"),
        P("dp", "tensor"),
        P(("dp", "tensor"), None),
        P(None, "tensor"),
        P("tensor"),
        P(None, ("dp", "tensor")),
        P(("dp", "tensor")),
        P("tensor"),
        P("tensor"),
        P("tensor"),
        P("tensor"),
        P("tensor", "dp"),
    )
    return jax.shard_map(body, mesh=mesh, in_specs=in_specs, out_specs=out_specs, check_vma=False)
```

```python
import functools

import jax
import jax.numpy as jnp
from jax import lax
from jax.experimental import pallas as pl
from jax.experimental.pallas import tpu as pltpu
from jax.sharding import PartitionSpec as P

epsilon = 1e-05
highest = lax.Precision.HIGHEST
f32 = jnp.float32
bf16 = jnp.bfloat16
span = 256
pad = 8
head_rows = 16
head_width = 64
vmem_bytes = 61 * 1024 * 1024


def mm(a, b, over=(1, 0)):
    dims = (((over[0],), (over[1],)), ((), ()))
    return lax.dot_general(a, b, dims, preferred_element_type=f32)


def mm_exact(a, b, over=(1, 0)):
    dims = (((over[0],), (over[1],)), ((), ()))
    return lax.dot_general(a, b, dims, preferred_element_type=f32, precision=highest)


def sigmoid(v):
    return 1.0 / (1.0 + jnp.exp(-v))


def ends_of(lengths_ref):
    ends, total = [], None
    for slot in range(lengths_ref.shape[1]):
        here = lengths_ref[0, slot]
        total = here if total is None else total + here
        ends.append(total)
    return ends


def segment_of(places, ends):
    segment = jnp.zeros(places.shape, jnp.int32)
    for end in ends:
        segment = segment + jnp.where(places >= end, 1, 0)
    return segment


def iota(shape, dim):
    return lax.broadcasted_iota(jnp.int32, shape, dim)


def write_masks(mask_ref, ends):
    rows = mask_ref.shape[1] - pad
    places = iota((rows, 128), 0)
    segment = segment_of(places, ends)
    for shift in range(1, mask_ref.shape[0] + 1):
        same = (segment_of(places - shift, ends) == segment) & (places >= shift)
        mask_ref[shift - 1, :rows, :] = jnp.where(same, 1.0, 0.0)
        mask_ref[shift - 1, rows:, :] = jnp.zeros((pad, 128), f32)


def shifted_rows(x_ref, mask_ref, at, cols, shift, tall):
    part = x_ref[pad + at - shift : pad + at - shift + tall, cols]
    if shift == 0:
        return part
    return part * mask_ref[shift - 1, at : at + tall, :]


def conv_pre(x_ref, mask_ref, taps_ref, bias_ref, at, cols, tall):
    taps = taps_ref.shape[0]
    shifted = [shifted_rows(x_ref, mask_ref, at, cols, s, tall) for s in range(taps)]
    total = bias_ref[:, cols]
    for s in range(taps):
        total = total + taps_ref[taps - 1 - s : taps - s, cols] * shifted[s]
    return total, shifted


def column_loop(width, step):
    def one(c, carry):
        step(pl.ds(pl.multiple_of(c * 128, 128), 128))
        return carry

    lax.fori_loop(0, width // 128, one, 0)


def row_loop(rows, tall, step):
    def one(r, carry):
        step(pl.multiple_of(r * tall, tall))
        return carry

    lax.fori_loop(0, rows // tall, one, 0)


class Block:
    def __init__(self, b, ends, step_col, step_row, rate_col, rate_row, state_ref):
        low, top = b * span, (b + 1) * span
        states = state_ref.shape[1] // 2
        lower = jnp.where(iota((span, span), 0) >= iota((span, span), 1), 1.0, 0.0)
        self.rows = slice(low, top)
        self.step = step_col[low:top]
        self.step_row = step_row[:, low:top]
        self.cum = mm_exact(lower, rate_col[low:top])
        self.cum_row = mm_exact(rate_row[:, low:top], lower, (1, 1))
        self.inputs = state_ref[low:top, :states].astype(bf16)
        self.outputs = state_ref[low:top, states:].astype(bf16)
        segment = segment_of(iota((span, 1), 0) + low, ends)
        segment_row = segment_of(iota((1, span), 1) + low, ends)
        edge = sum(jnp.where(span - 1 >= end, 1, 0) for end in ends)
        self.near_edge = jnp.where(segment == edge, 1.0, 0.0)
        self.mask = jnp.where(segment == segment_row, lower, 0.0)
        self.contact = mm(self.outputs, self.inputs, (1, 1)) * self.mask

    def decay(self, h):
        gap = self.cum[:, h : h + 1] - self.cum_row[h : h + 1, :]
        return jnp.exp(jnp.minimum(gap, 0.0))

    def from_edge(self, h):
        return jnp.exp(self.cum[:, h : h + 1]) * self.near_edge

    def to_edge(self, h):
        last = self.cum[span - 1 : span, h : h + 1]
        return jnp.exp(last - self.cum[:, h : h + 1]) * self.near_edge


def wide(low_half, left, right):
    return jnp.where(low_half, left, right)


def step_sizes(raw_col, raw_row, bias_ref, bias_col_ref, log_ref, log_col_ref):
    def soft(v):
        return jnp.maximum(v, 0.0) + jnp.log1p(jnp.exp(-jnp.abs(v)))

    step_col = soft(raw_col + bias_ref[...])
    step_row = soft(raw_row + bias_col_ref[...])
    rate_col = -step_col * jnp.exp(log_ref[...])
    rate_row = -step_row * jnp.exp(log_col_ref[...])
    return step_col, step_row, rate_col, rate_row


def forward_kernel(fast, place_ref, lengths_ref, *refs):
    n_msg = 8 if fast else 4
    n_rows = 4 if fast else 1
    row_refs, msg_refs, refs = refs[:n_rows], refs[n_rows : n_rows + n_msg], refs[n_rows + n_msg :]
    (taps_ref, bias_ref, step_bias_ref, step_bias_col_ref, log_ref, log_col_ref, skip_ref) = refs[:7]
    (
        normed_ref,
        turned_ref,
        weight_ref,
        state_weight_ref,
        step_weight_ref,
        small_ref,
        raw_ref,
        state_raw_ref,
        step_col_ref,
        step_row_ref,
        act_ref,
        state_ref,
        mixed_ref,
    ) = refs[7:20]
    mask_ref, state_taps_ref, state_bias_ref = refs[20:]
    total, channels = act_ref.shape
    ends = ends_of(lengths_ref)

    if fast:
        depth_part = 128
        small = jnp.zeros(small_ref.shape, f32)
        share = state_weight_ref.shape[0] // 32
        for slot in range(8):
            msg = msg_refs[slot]
            index = place_ref[slot]
            at = pl.multiple_of(index * depth_part, depth_part)
            weight_ref[pl.ds(at, depth_part), :] = msg[:depth_part, :]
            for member in range(4):
                inner = pl.multiple_of(at + place_ref[8 + member] * share, share)
                high, low = depth_part + share * (member // 2), 256 * (member % 2)
                state_weight_ref[pl.ds(inner, share), :] = msg[
                    high : high + share, low : low + 256
                ]
            tail = depth_part + 2 * share
            small = small + msg[tail : tail + 16, :256].astype(f32)
            step_weight_ref[:, pl.ds(at, depth_part)] = msg[tail : tail + 16, 256:384]
        small_ref[...] = small
    else:
        weight_ref[...] = msg_refs[0][...]
        state_weight_ref[...] = msg_refs[1][...]
        step_weight_ref[...] = msg_refs[2][...]
        small_ref[...] = msg_refs[3][...].astype(f32)
    gain = jnp.concatenate([small_ref[i : i + 1, :] for i in range(4)], axis=1)
    taps = taps_ref.shape[0]
    state_taps_ref[...] = small_ref[4 : 4 + taps, :]
    state_bias_ref[...] = small_ref[4 + taps : 5 + taps, :]

    tall = total // n_rows
    for member in range(n_rows):
        at = pl.multiple_of(place_ref[8 + member] * tall, tall) if fast else 0
        value = row_refs[member][:tall, :].astype(f32)
        scale = lax.rsqrt(jnp.mean(value * value, axis=1, keepdims=True) + epsilon)
        normed = (value * scale * gain).astype(bf16)
        normed_ref[pl.ds(at, tall), :] = normed
        turned_ref[:, pl.ds(at, tall)] = normed.astype(f32).T.astype(bf16)

    raw_ref[:pad, :] = jnp.zeros((pad, channels), f32)
    state_raw_ref[:pad, :] = jnp.zeros((pad, state_raw_ref.shape[1]), f32)

    def project(at):
        part = normed_ref[pl.ds(at, 128), :]
        raw_ref[pl.ds(at + pad, 128), :] = mm(part, weight_ref[...])
        state_raw_ref[pl.ds(at + pad, 128), :] = mm(part, state_weight_ref[...])
        step_col_ref[pl.ds(at, 128), :] = mm(part, step_weight_ref[...], (1, 1))

    row_loop(total, 128, project)
    step_row_ref[...] = mm(step_weight_ref[...], normed_ref[...], (1, 1))

    write_masks(mask_ref, ends)

    def activate(x_ref, out_ref, own_taps, own_bias):
        def column(cols):
            for at in range(0, total, 128):
                pre, _ = conv_pre(x_ref, mask_ref, own_taps, own_bias, at, cols, 128)
                out_ref[at : at + 128, cols] = pre * sigmoid(pre)

        column_loop(out_ref.shape[1], column)

    activate(raw_ref, act_ref, taps_ref, bias_ref)
    activate(state_raw_ref, state_ref, state_taps_ref, state_bias_ref)

    steps = step_sizes(
        step_col_ref[...],
        step_row_ref[...],
        step_bias_ref,
        step_bias_col_ref,
        log_ref,
        log_col_ref,
    )
    low_half = iota((span, 128), 1) < head_width
    held = []
    for b in range(total // span):
        block = Block(b, ends, *steps, state_ref)
        for i in range(channels // 128):
            cols = slice(128 * i, 128 * (i + 1))
            pair = (2 * i, 2 * i + 1)
            x = act_ref[block.rows, cols]
            step_wide = wide(low_half, *(block.step[:, h : h + 1] for h in pair))
            x_step = (x * step_wide).astype(bf16)
            y = [mm((block.decay(h) * block.contact).astype(bf16), x_step) for h in pair]
            y = wide(low_half, *y) + skip_ref[:, cols] * x
            if b == 0:
                reach = wide(low_half, *(block.to_edge(h) for h in pair))
                weighted = (x * step_wide * reach).astype(bf16)
                held.append(mm(block.inputs, weighted, (0, 0)).astype(bf16))
            else:
                reach = wide(low_half, *(block.from_edge(h) for h in pair))
                y = y + reach * mm(block.outputs, held[i])
            mixed_ref[block.rows, cols] = y


def grad_in_kernel(fast, place_ref, lengths_ref, *refs):
    n_rows = 4 if fast else 1
    n_msg = 8 if fast else 2
    row_refs, msg_refs, refs = refs[:n_rows], refs[n_rows : n_rows + n_msg], refs[n_rows + n_msg :]
    normed_ref, mixed_ref, norm_ref = refs[:3]
    rows_ref, gate_weight_ref, out_weight_ref, gate_ref, grad_ref, sums_ref, wide_ref = refs[3:]
    total = rows_ref.shape[0]
    ends = ends_of(lengths_ref)
    tall = total // n_rows
    for member in range(n_rows):
        at = pl.multiple_of(place_ref[8 + member] * tall, tall) if fast else 0
        rows_ref[pl.ds(at, tall), :] = row_refs[member][-tall:, :]
    if fast:
        for slot in range(8):
            at = pl.multiple_of(place_ref[slot] * 128, 128)
            gate_weight_ref[pl.ds(at, 128), :] = msg_refs[slot][:128, :]
            out_weight_ref[pl.ds(at, 128), :] = msg_refs[slot][128:, :]
    else:
        gate_weight_ref[...] = msg_refs[0][...]
        out_weight_ref[...] = msg_refs[1][...]

    def part(at):
        rows = pl.ds(at, 128)
        valid = jnp.where(iota((128, 1), 0) + at < ends[-1], 1.0, 0.0)
        grad = mm(rows_ref[rows, :], out_weight_ref[...]) * valid
        grad_ref[rows, :] = grad
        gate = mm(normed_ref[rows, :], gate_weight_ref[...])
        gate_ref[rows, :] = gate
        gated = mixed_ref[rows, :] * (gate * sigmoid(gate))
        square = jnp.sum(gated * gated, axis=1, keepdims=True)
        cross = jnp.sum(grad * norm_ref[...] * gated, axis=1, keepdims=True)
        lane = iota((128, 128), 1)
        wide_ref[rows, :] = jnp.where(lane == 0, square, jnp.where(lane == 1, cross, 0.0))

    row_loop(total, 128, part)
    for at in range(0, total, 128):
        sums_ref[:, at : at + 128] = wide_ref[at : at + 128, :].T[:8, :]


def norm_kernel(inner_total, place_ref, lengths_ref, *refs):
    n_sums = len(refs) - 21
    sums_refs, refs = refs[:n_sums], refs[n_sums:]
    gate_ref, mixed_ref, grad_ref, norm_ref, weight_ref, rows_ref, turned_ref = refs[:7]
    chunk_refs = refs[7:15]
    partial_ref, grad_gate_ref, grad_mixed_ref, norm_grad_ref = refs[15:19]
    wide_ref, out_rows_ref = refs[19:]
    total, channels = gate_ref.shape
    ends = ends_of(lengths_ref)
    for at in range(0, total, 128):
        tile = sum(ref[:, at : at + 128] for ref in sums_refs)
        tile = jnp.concatenate([tile] * 16, axis=0)
        wide_ref[at : at + 128, :] = tile.T
    norm_grad_ref[...] = jnp.zeros(norm_grad_ref.shape, f32)

    def part(at):
        rows = pl.ds(at, 128)
        valid = jnp.where(iota((128, 1), 0) + at < ends[-1], 1.0, 0.0)
        scale = lax.rsqrt(wide_ref[rows, 0:1] / inner_total + epsilon)
        cross = wide_ref[rows, 1:2]
        gate = gate_ref[rows, :]
        mixed = mixed_ref[rows, :]
        sig = sigmoid(gate)
        gate_act = gate * sig
        gated = mixed * gate_act
        grad = grad_ref[rows, :]
        norm = norm_ref[...]
        hat = gated * scale
        out_rows_ref[rows, :] = (hat * norm * valid).astype(bf16)
        norm_grad_ref[...] += jnp.sum(grad * hat, axis=0, keepdims=True)
        grad_gated = scale * (grad * norm) - gated * (scale * scale * scale * cross / inner_total)
        grad_mixed_ref[rows, :] = grad_gated * gate_act
        grad_gate = grad_gated * mixed * sig * (1.0 + gate * (1.0 - sig))
        grad_gate_ref[rows, :] = grad_gate.astype(bf16)

    row_loop(total, 128, part)

    def back(at):
        cols = pl.ds(at, 256)
        partial_ref[:, cols] = mm(out_rows_ref[...], weight_ref[cols, :], (1, 1)).astype(bf16)

    row_loop(weight_ref.shape[0], 256, back)
    tall = chunk_refs[0].shape[0] // 2
    for slot, chunk_ref in enumerate(chunk_refs):
        cols = pl.ds(pl.multiple_of(place_ref[slot] * tall, tall), tall)
        chunk_ref[:tall, :] = mm(turned_ref[cols, :], grad_gate_ref[...]).astype(bf16)
        chunk_ref[tall:, :] = mm(rows_ref[:, cols], out_rows_ref[...], (0, 0)).astype(bf16)


def scan_back_kernel(first_pair, lengths_ref, *refs):
    grad_mixed_ref, act_ref, state_ref, step_col_ref, step_row_ref = refs[:5]
    step_bias_ref, step_bias_col_ref, log_ref, log_col_ref, skip_ref = refs[5:10]
    grad_act_ref, grad_state_ref, step_grad_ref, sums_ref, acc_ref = refs[10:]
    total, own_width = grad_act_ref.shape
    states = state_ref.shape[1] // 2
    ends = ends_of(lengths_ref)
    sums_ref[...] = jnp.zeros(sums_ref.shape, f32)
    raw_row = step_row_ref[...]
    steps = step_sizes(
        step_col_ref[...], raw_row, step_bias_ref, step_bias_col_ref, log_ref, log_col_ref
    )
    rate_row = steps[3]
    low_half = iota((span, 128), 1) < head_width
    lower = jnp.where(iota((span, span), 0) >= iota((span, span), 1), 1.0, 0.0)
    blocks = [Block(b, ends, *steps, state_ref) for b in range(total // span)]
    first, second = blocks
    row_sums, step_rows, out_sums, in_sums = [], [], None, None
    grad_out = jnp.zeros((span, states), f32)
    grad_in = jnp.zeros((span, states), f32)
    head_of = iota((head_rows, 128), 0)
    lane_head = iota((head_rows, 128), 1) // head_width

    for b, block in enumerate(blocks):
        acc_ref[...] = jnp.zeros((span, span), f32)
        row_sum = jnp.zeros((span, 128), f32)
        step_grad = jnp.zeros((head_rows, span), f32)
        lane = iota((span, 128), 1)
        head_row = iota((head_rows, span), 0)
        for i in range(first_pair, first_pair + own_width // 128):
            cols = slice(128 * i, 128 * (i + 1))
            own_cols = slice(128 * (i - first_pair), 128 * (i - first_pair + 1))
            pair = (2 * i, 2 * i + 1)
            x = act_ref[block.rows, cols]
            x_low = x.astype(bf16)
            grad = grad_mixed_ref[block.rows, cols]
            grad_low = grad.astype(bf16)
            halves = (
                jnp.where(low_half, grad, 0.0).astype(bf16),
                jnp.where(low_half, 0.0, grad).astype(bf16),
            )
            step_wide = wide(low_half, *(block.step[:, h : h + 1] for h in pair))
            grads = []
            for h, half in zip(pair, halves):
                decay = block.decay(h)
                spread = mm(half, x_low, (1, 1)) * decay
                stepped = spread * block.step_row[h : h + 1, :]
                acc_ref[...] += stepped
                row_here = jnp.sum(stepped * block.contact, axis=1, keepdims=True)
                row_sum = jnp.where(lane == h, row_here, row_sum)
                step_here = jnp.sum(spread * block.contact, axis=0, keepdims=True)
                step_grad = jnp.where(head_row == h, step_here, step_grad)
                grads.append(mm((decay * block.contact).astype(bf16), grad_low, (0, 0)))
            grad_act = wide(low_half, *grads) * step_wide + skip_ref[:, cols] * grad
            sums_ref[2:3, own_cols] += jnp.sum(grad * x, axis=0, keepdims=True)
            picks = jnp.where(lane_head + 2 * i == head_of, 1.0, 0.0)
            if b == 0:
                reach = wide(low_half, *(second.from_edge(h) for h in pair))
                lead = (grad_mixed_ref[second.rows, cols] * reach).astype(bf16)
                edge = wide(low_half, *(block.to_edge(h) for h in pair))
                weighted = (x * step_wide * edge).astype(bf16)
                held = mm(block.inputs, weighted, (0, 0)).astype(bf16)
                held_grad = mm(second.outputs, lead, (0, 0)).astype(bf16)
                grad_out = grad_out + mm(lead, held, (1, 1))
                grad_in = grad_in + mm(weighted, held_grad, (1, 1))
                back = mm(block.inputs, held_grad) * edge
                grad_act = grad_act + back * step_wide
                ahead = mm(second.outputs, held)
                out_here = mm_exact(picks, lead.astype(f32) * ahead, (1, 1))
                in_here = mm_exact(picks, x * back, (1, 1))
                out_sums = out_here if out_sums is None else out_sums + out_here
                in_sums = in_here if in_sums is None else in_sums + in_here
            grad_act_ref[block.rows, own_cols] = grad_act
        table = (acc_ref[...] * block.mask).astype(bf16)
        grad_c = mm(table, block.inputs)
        grad_b = mm(table, block.outputs, (0, 0))
        if b == 0:
            grad_b = grad_b + grad_in
        else:
            grad_c = grad_c + grad_out
        grad_state_ref[block.rows, :states] = grad_b
        grad_state_ref[block.rows, states:] = grad_c
        row_sums.append(row_sum)
        step_rows.append(step_grad)

    rate_grads = []
    for b, block in enumerate(blocks):
        column = step_rows[b] * block.step_row
        crossing = mm_exact(row_sums[b], lower, (0, 0))[:head_rows] - mm_exact(column, lower)
        if b == 0:
            crossing = crossing + mm_exact(in_sums * block.step_row, 1.0 - lower)
        else:
            crossing = crossing + mm_exact(out_sums, lower)
        rate_grads.append(crossing)
    step_rows[0] = step_rows[0] + in_sums
    rate_grad = jnp.concatenate(rate_grads, axis=1)
    step_grad = jnp.concatenate(step_rows, axis=1) - rate_grad * jnp.exp(log_col_ref[...])
    step_grad = step_grad * sigmoid(raw_row + step_bias_col_ref[...])
    decay_sum = jnp.sum(rate_grad * rate_row, axis=1, keepdims=True)
    bias_sum = jnp.sum(step_grad, axis=1, keepdims=True)
    lane = iota((head_rows, 128), 1)
    head_sums = jnp.where(lane == 0, bias_sum, jnp.where(lane == 1, decay_sum, 0.0))
    head_sums = jnp.concatenate([head_sums] * (128 // head_rows), axis=0).T
    sums_ref[0:2, :128] = head_sums[:2, :]
    step_grad_ref[...] = step_grad


def conv_back(x_ref, mask_ref, grad_ref, held_ref, out_ref, sums_ref, own_taps, own_bias):
    total, taps = out_ref.shape[0], own_taps.shape[0]
    held_ref[total:, :] = jnp.zeros((pad, held_ref.shape[1]), f32)

    def column(cols):
        sums = [jnp.zeros((1, 128), f32) for _ in range(taps + 1)]
        for at in range(0, total, 128):
            pre, shifted = conv_pre(x_ref, mask_ref, own_taps, own_bias, at, cols, 128)
            sig = sigmoid(pre)
            grad = grad_ref[at : at + 128, cols] * sig * (1.0 + pre * (1.0 - sig))
            held_ref[at : at + 128, cols] = grad
            for s in range(taps):
                sums[taps - 1 - s] += jnp.sum(grad * shifted[s], axis=0, keepdims=True)
            sums[taps] += jnp.sum(grad, axis=0, keepdims=True)
        for t, value in enumerate(sums):
            sums_ref[t : t + 1, cols] = value
        for at in range(0, total, 128):
            back = own_taps[taps - 1 : taps, cols] * held_ref[at : at + 128, cols]
            for s in range(1, taps):
                part = held_ref[at + s : at + s + 128, cols]
                part = part * mask_ref[s - 1, at + s : at + s + 128, :]
                back = back + own_taps[taps - 1 - s : taps - s, cols] * part
            out_ref[at : at + 128, cols] = back.astype(bf16)

    column_loop(out_ref.shape[1], column)


def state_back_kernel(fast, place_ref, lengths_ref, *refs):
    state_refs, step_refs, refs = refs[0:2], refs[2:4], refs[4:]
    state_raw_ref, turned_ref, small_ref, grad_state_low_ref, step_low_ref = refs[:5]
    n_out = 4 if fast else 2
    out_refs, refs = refs[5 : 5 + n_out], refs[5 + n_out :]
    mask_ref, taps_ref, bias_ref, grad_state_ref, pre_ref, part_ref, sums_ref = refs
    taps = taps_ref.shape[0]
    taps_ref[...] = small_ref[4 : 4 + taps, :]
    bias_ref[...] = small_ref[4 + taps : 5 + taps, :]
    write_masks(mask_ref, ends_of(lengths_ref))
    grad_state_ref[...] = state_refs[0][...] + state_refs[1][...]
    step_low_ref[...] = (step_refs[0][...] + step_refs[1][...]).astype(bf16)
    sums_ref[...] = jnp.zeros(sums_ref.shape, f32)
    conv_back(
        state_raw_ref,
        mask_ref,
        grad_state_ref,
        pre_ref,
        grad_state_low_ref,
        sums_ref,
        taps_ref,
        bias_ref,
    )

    def chunk(at):
        part = turned_ref[pl.ds(at, 256), :]
        part_ref[pl.ds(at, 256), :] = mm(part, grad_state_low_ref[...]).astype(bf16)

    depth = turned_ref.shape[0]
    row_loop(depth, 256, chunk)
    if fast:
        share = depth // 32
        for member, out_ref in enumerate(out_refs):
            for c in range(8):
                at = pl.multiple_of((4 * c + place_ref[8 + member]) * share, share)
                out_ref[share * c : share * (c + 1), :] = part_ref[pl.ds(at, share), :]
            out_ref[8 * share :, :] = sums_ref[...].astype(bf16)
    else:
        out_refs[0][...] = part_ref[...]
        out_refs[1][...] = sums_ref[...]


def inner_back_kernel(lengths_ref, *refs):
    act_refs, head_refs, refs = refs[0:2], refs[2:4], refs[4:]
    raw_ref, norm_grad_ref, taps_ref, bias_ref, grad_inner_ref, sums_ref = refs[:6]
    mask_ref, grad_act_ref, pre_ref = refs[6:]
    half = grad_inner_ref.shape[1] // 2
    write_masks(mask_ref, ends_of(lengths_ref))
    grad_act_ref[:, :half] = act_refs[0][...]
    grad_act_ref[:, half:] = act_refs[1][...]
    sums_ref[...] = jnp.zeros(sums_ref.shape, f32)
    heads = head_refs[0][:2, :128] + head_refs[1][:2, :128]
    sums_ref[5:6, :] = norm_grad_ref[...]
    sums_ref[6:7, :half] = head_refs[0][2:3, :]
    sums_ref[6:7, half:] = head_refs[1][2:3, :]
    sums_ref[9:10, half : half + 128] = heads[0:1, :]
    sums_ref[9:10, half + 128 :] = heads[1:2, :]
    conv_back(
        raw_ref,
        mask_ref,
        grad_act_ref,
        pre_ref,
        grad_inner_ref,
        sums_ref,
        taps_ref,
        bias_ref,
    )


def message_kernel(grad_inner_ref, step_low_ref, turned_ref, msg_ref):
    chunks = msg_ref.shape[0]
    tall = turned_ref.shape[0] // chunks
    step_low = step_low_ref[...]

    def chunk(c, carry):
        part = turned_ref[pl.ds(pl.multiple_of(c * tall, tall), tall), :]
        msg_ref[c, :tall, :] = mm(part, grad_inner_ref[...]).astype(bf16)
        msg_ref[c, tall:, :tall] = mm(step_low, part, (1, 1)).astype(bf16)
        msg_ref[c, tall:, tall:] = jnp.zeros((head_rows, msg_ref.shape[2] - tall), bf16)
        return carry

    lax.fori_loop(0, chunks, chunk, 0)


def chunk_kernel(slots, n_got, place_ref, *refs):
    grad_inner_ref, step_low_ref, sums_ref = refs[:3]
    state_refs, turned_refs, got_refs = refs[3:7], refs[7:9], refs[9 : 9 + n_got]
    out_refs = refs[9 + n_got :]
    states = state_refs[0].shape[1]
    share = (state_refs[0].shape[0] - 16) // 8

    def state_rows(low, tall):
        return sum(ref[pl.ds(low, tall), :].astype(f32) for ref in state_refs)

    shared = state_rows(8 * share, 16)
    sums = [
        sums_ref[:7, :],
        jnp.concatenate([shared[0:1, :], shared[1:2, :]], axis=1),
        jnp.concatenate([shared[2:3, :], shared[3:4, :]], axis=1),
        jnp.concatenate([shared[4:5, :], sums_ref[9:10, states:]], axis=1),
    ]
    for n, (slot, out_ref) in enumerate(zip(slots, out_refs)):
        index = place_ref[slot]
        part = turned_refs[n][...]
        step = mm(step_low_ref[...], part, (1, 1))
        step = [
            jnp.concatenate([step[4 * k + i : 4 * k + i + 1, :] for i in range(4)], axis=1)
            for k in range(2)
        ]
        state = state_rows(pl.multiple_of(index * share, share), share)
        value = jnp.concatenate(
            [
                mm(part, grad_inner_ref[...]),
                jnp.concatenate([state[:16, :], state[16:, :]], axis=1),
                *sums,
                *step,
                jnp.zeros((4, 2 * states), f32),
            ],
            axis=0,
        )
        tail = value.shape[0] - 16
        main, sums_here = value[:tail, :], value[tail:, :]
        if n < n_got:
            got = got_refs[n]
            main = main + got[:tail, :].astype(f32)
            sums_here = sums_here + got[tail : tail + 16, :].astype(f32)
            sums_here = sums_here + got[tail + 16 :, :].astype(f32)
        out_ref[:tail, :] = main.astype(out_ref.dtype)
        high = sums_here.astype(bf16)
        out_ref[tail : tail + 16, :] = high.astype(out_ref.dtype)
        out_ref[tail + 16 :, :] = (sums_here - high.astype(f32)).astype(out_ref.dtype)


def project_back_kernel(fast, place_ref, *refs):
    grad_refs, step_low_ref, weight_refs, step_weight_ref = refs[:3], refs[3], refs[4:7], refs[7]
    out_refs, held_refs, step_ref = refs[8:10], refs[10:13], refs[13]
    for n, member in enumerate((0, 2, 1, 3)):
        at = pl.multiple_of(place_ref[8 + member] * 128, 128) if fast else 128 * member
        for held_ref, grad_ref in zip(held_refs, grad_refs):
            held_ref[128 * n : 128 * (n + 1), :] = grad_ref[pl.ds(at, 128), :]
        step_ref[:, 128 * n : 128 * (n + 1)] = step_low_ref[:, pl.ds(at, 128)]

    def back(at):
        cols = pl.ds(at, 256)
        grad = mm(step_ref[...], step_weight_ref[:, cols], (0, 0))
        for held_ref, weight_ref in zip(held_refs, weight_refs):
            grad = grad + mm(held_ref[...], weight_ref[cols, :], (1, 1))
        grad = grad.astype(bf16)
        for n in range(4):
            out_refs[n // 2][n % 2, :, cols] = grad[128 * n : 128 * (n + 1), :]

    row_loop(step_weight_ref.shape[1], 256, back)


def prepare_kernel(place_ref, gain_ref, taps_ref, bias_ref, state_ref, shared_ref):
    owner = place_ref[0]
    share, states = state_ref.shape
    shared_ref[:share, :] = state_ref[...]

    def placed(value, at):
        width = value.shape[1]
        pick = iota((width, states), 1) - at == iota((width, states), 0)
        return mm(value, jnp.where(pick, 1.0, 0.0).astype(bf16))

    start = owner * gain_ref.shape[1]
    small = jnp.concatenate(
        [placed(gain_ref[...], start - states * i) for i in range(4)]
        + [placed(taps_ref[...], owner * taps_ref.shape[1])]
        + [placed(bias_ref[...], owner * bias_ref.shape[1])]
        + [jnp.zeros((7, states), f32)],
        axis=0,
    )
    shared_ref[share:, :] = small.astype(bf16)


def prepare_late_kernel(input_ref, out_ref, late_ref):
    depth_part = input_ref.shape[0]
    late_ref[:depth_part, :] = input_ref[:, 0, :]
    late_ref[depth_part:, :] = out_ref[...].astype(f32).T.astype(bf16)


def params_kernel(*refs):
    taps_ref, bias_ref, step_bias_ref, log_ref, skip_ref, norm_ref = refs[:6]
    outs = refs[6:]
    heads = step_bias_ref.shape[1]
    pick = jnp.where(iota((heads, head_rows), 0) == iota((heads, head_rows), 1), 1.0, 0.0)
    square = iota((head_rows, head_rows), 0) == iota((head_rows, head_rows), 1)

    def both(value_ref, row_ref, col_ref):
        row = mm_exact(value_ref[...].astype(f32), pick)
        row_ref[...] = row
        col_ref[...] = jnp.sum(jnp.where(square, row, 0.0), axis=1, keepdims=True)

    outs[0][...] = taps_ref[...].astype(f32)
    outs[1][...] = bias_ref[...].astype(f32)
    both(step_bias_ref, outs[2], outs[3])
    both(log_ref, outs[4], outs[5])
    channels = norm_ref.shape[1]
    own = iota((heads, channels), 1) // (channels // heads) == iota((heads, channels), 0)
    outs[6][...] = mm_exact(skip_ref[...].astype(f32), jnp.where(own, 1.0, 0.0))
    outs[7][...] = norm_ref[...].astype(f32)


def assemble_kernel(input_ref, step_ref, *refs):
    shared_refs, msg_ref = refs[:4], refs[4]
    depth_part, _, channels = input_ref.shape
    share = shared_refs[0].shape[0] - 16
    tail = depth_part + 2 * share
    msg_ref[:depth_part, :] = input_ref[:, 1, :]
    for member, ref in enumerate(shared_refs):
        high, low = depth_part + share * (member // 2), 256 * (member % 2)
        msg_ref[high : high + share, low : low + 256] = ref[:share, :]
    small = sum(ref[share:, :].astype(f32) for ref in shared_refs)
    msg_ref[tail:, :256] = small.astype(bf16)
    msg_ref[tail:, 256:384] = step_ref[...]
    msg_ref[tail:, 384:] = jnp.zeros((16, channels - 384), bf16)


def call(kernel, micros, scalars, arrays, outs, scratch):
    smem = pl.BlockSpec(memory_space=pltpu.SMEM)
    vmem = pl.BlockSpec(memory_space=pltpu.VMEM)
    return pl.pallas_call(
        kernel,
        out_shape=[jax.ShapeDtypeStruct(shape, kind) for shape, kind in outs],
        in_specs=[smem] * len(scalars) + [vmem] * len(arrays),
        out_specs=[vmem] * len(outs),
        scratch_shapes=[pltpu.VMEM(shape, kind) for shape, kind in scratch],
        compiler_params=pltpu.CompilerParams(vmem_limit_bytes=vmem_bytes),
        cost_estimate=pl.CostEstimate(
            flops=int(micros * 1.1e9), bytes_accessed=1 << 20, transcendentals=0
        ),
    )(*scalars, *arrays)


def ring_ok(n_dp, n_tensor):
    return n_dp == 8 and n_tensor == 4


ring_order = (0, 2, 4, 6, 7, 5, 3, 1)


def ring_place(index):
    high, low = index // 2, index % 2
    return jnp.where(low == 0, high, 7 - high)


def ring_index(place):
    place = lax.rem(place + 16, 8)
    return jnp.where(place < 4, 2 * place, 2 * (7 - place) + 1)


def ring_send(value, forward):
    pairs = []
    for place in range(8):
        other = (place + (1 if forward else 7)) % 8
        pairs.append((ring_order[place], ring_order[other]))
    return lax.ppermute(value, "dp", pairs)


def ring_gather(value):
    me = ring_place(lax.axis_index("dp"))
    pieces = [(value, ring_index(me))]
    ahead, back = value, value
    for step in range(1, 5):
        ahead = ring_send(ahead, True)
        pieces.append((ahead, ring_index(me - step)))
        if step < 4:
            back = ring_send(back, False)
            pieces.append((back, ring_index(me + step)))
    return pieces


def dp_swap(value, bit):
    return lax.ppermute(value, "dp", [(i, i ^ bit) for i in range(8)])


def ring_step(held):
    return ring_send(held[0], True), ring_send(held[1], False)


def add_low(got, own):
    return (got.astype(f32) + own.astype(f32)).astype(bf16)


def ordered(first, then):
    return lax.optimization_barrier((first, then))


def tensor_gather(value):
    near = tensor_swap(value, 1)
    far = tensor_swap(value, 2)
    return [value, near, far, tensor_swap(far, 1)]


def tensor_direct(value):
    return [value] + [tensor_swap(value, bit) for bit in range(1, 4)]


def tensor_sum(value, depth):
    parts = value.reshape(4, -1, depth)
    parts = lax.all_to_all(parts, "tensor", 0, 0, tiled=True)
    return jnp.sum(parts.astype(f32), axis=0)


def tensor_swap(value, bit):
    return lax.ppermute(value, "tensor", [(i, i ^ bit) for i in range(4)])


def body(
    tokens,
    lengths,
    cotangent,
    pre_gain,
    input_weight,
    step_weight,
    state_weight,
    conv_inner,
    conv_inner_bias,
    conv_state,
    conv_state_bias,
    step_bias,
    decay_log,
    skip_gain,
    norm_gain,
    output_weight,
):
    n_dp, n_tensor = lax.axis_size("dp"), lax.axis_size("tensor")
    fast = ring_ok(n_dp, n_tensor)
    owners = n_dp * n_tensor
    me = lax.axis_index("tensor")
    owner = lax.axis_index("dp") * n_tensor + me
    own_rows, depth = tokens.shape
    total = own_rows * n_tensor
    states = state_weight.shape[1]
    heads = step_weight.shape[1]
    share = state_weight.shape[0]
    taps = conv_state.shape[0]
    channels = input_weight.shape[2]
    inner_total = channels * n_tensor

    owner_place = jnp.stack([owner, owners]).astype(jnp.int32)
    (shared,) = call(
        prepare_kernel,
        1,
        [owner_place],
        [pre_gain[None, :], conv_state, conv_state_bias[None, :], state_weight],
        [((share + 16, states), bf16)],
        [],
    )
    step_rows = jnp.pad(step_weight.T, ((0, head_rows - heads), (0, 0)))
    shared, out_shard = ordered(shared, output_weight)
    (late,) = call(
        prepare_late_kernel,
        2,
        [],
        [input_weight, out_shard],
        [((input_weight.shape[0] + output_weight.shape[1], channels), bf16)],
        [],
    )
    params = call(
        params_kernel,
        1,
        [],
        [
            conv_inner,
            conv_inner_bias[None, :],
            step_bias[None, :],
            decay_log[None, :],
            skip_gain[None, :],
            norm_gain[None, :],
        ],
        [
            ((taps, channels), f32),
            ((1, channels), f32),
            ((1, head_rows), f32),
            ((head_rows, 1), f32),
            ((1, head_rows), f32),
            ((head_rows, 1), f32),
            ((1, channels), f32),
            ((1, channels), f32),
        ],
        [],
    )
    params = list(params)
    conv_params, head_params, norm_row = params[:2], params[2:7], params[7]
    if fast:
        shared = tensor_direct(shared)
        late_one = ring_step((late, late))
        (msg,) = call(
            assemble_kernel,
            1,
            [],
            [input_weight, step_rows, *shared],
            [((input_weight.shape[0] + 2 * share + 16, channels), bf16)],
            [],
        )
        late_one, msg = ordered(late_one, msg)
        msg = ring_gather(msg)
        weight_pieces = [piece for piece, _ in msg]
        late_two = ring_step(late_one)
        late_three = ring_step(late_two)
        late_pieces = [late, *late_one, *late_two, *late_three, ring_send(late_three[0], True)]
        own_rows_both = jnp.concatenate([tokens, cotangent], axis=0)
        row_pieces = tensor_gather(ordered(shared, own_rows_both)[1])
        grad_pieces = row_pieces
        place = jnp.stack([index for _, index in msg] + [me, me ^ 1, me ^ 2, me ^ 3])
    else:
        row_pieces = [lax.all_gather(tokens, "tensor", axis=0, tiled=True)]
        grad_pieces = [lax.all_gather(cotangent, "tensor", axis=0, tiled=True)]
        gate_weight, inner_weight = late[: input_weight.shape[0]], input_weight[:, 1]
        weight_pieces = [
            lax.all_gather(inner_weight, "dp", axis=0, tiled=True),
            lax.all_gather(state_weight, ("dp", "tensor"), axis=0, tiled=True),
            lax.all_gather(step_rows, "dp", axis=1, tiled=True),
            lax.psum(shared[share:], ("dp", "tensor")),
        ]
        late_pieces = [
            lax.all_gather(gate_weight, "dp", axis=0, tiled=True),
            lax.all_gather(late[input_weight.shape[0] :], "dp", axis=0, tiled=True),
        ]
        place = jnp.concatenate([jnp.arange(8), jnp.arange(4)])
    place = place.astype(jnp.int32)

    masks = ((taps - 1, total + pad, 128), f32)
    state_taps = [((taps, states), f32), ((1, states), f32)]
    (
        normed,
        turned,
        inner_full,
        state_full,
        step_full,
        small_full,
        raw,
        state_raw,
        step_col,
        step_row,
        act,
        state_act,
        mixed,
    ) = call(
        functools.partial(forward_kernel, fast),
        11,
        [place, lengths],
        row_pieces + weight_pieces + conv_params + head_params,
        [
            ((total, depth), bf16),
            ((depth, total), bf16),
            ((depth, channels), bf16),
            ((depth, states), bf16),
            ((head_rows, depth), bf16),
            ((16, states), f32),
            ((total + pad, channels), f32),
            ((total + pad, states), f32),
            ((total, head_rows), f32),
            ((head_rows, total), f32),
            ((total, channels), f32),
            ((total, states), f32),
            ((total, channels), f32),
        ],
        [masks] + state_taps,
    )
    grad_rows, gate_full, output_full, gate, grad_normalized, sums = call(
        functools.partial(grad_in_kernel, fast),
        5,
        [place, lengths],
        grad_pieces + late_pieces + [normed, mixed, norm_row],
        [
            ((total, depth), bf16),
            ((depth, channels), bf16),
            ((depth, channels), bf16),
            ((total, channels), f32),
            ((total, channels), f32),
            ((8, total), f32),
        ],
        [((total, 128), f32)],
    )
    if fast:
        sums = tensor_direct(sums)
    else:
        sums = [lax.psum(sums, "tensor")]
    chunks = 8
    tall = depth // chunks
    norm_outs = call(
        functools.partial(norm_kernel, inner_total),
        9,
        [place, lengths],
        [*sums, gate, mixed, grad_normalized, norm_row, output_full, grad_rows, turned],
        [((2 * tall, channels), bf16)] * chunks
        + [
            ((total, depth), bf16),
            ((total, channels), bf16),
            ((total, channels), f32),
            ((1, channels), f32),
        ],
        [((total, 128), f32), ((total, channels), bf16)],
    )
    gate_chunks = norm_outs[:chunks]
    partial_out, grad_gate, grad_mixed, norm_grad = norm_outs[chunks:]

    def scan_back(first_pair, grad):
        return call(
            functools.partial(scan_back_kernel, first_pair),
            6,
            [lengths],
            [grad, act, state_act, step_col, step_row] + head_params,
            [
                ((total, channels // 2), f32),
                ((total, states), f32),
                ((head_rows, total), f32),
                ((8, channels // 2), f32),
            ],
            [((span, span), f32)],
        )

    if fast:
        got = ring_step((gate_chunks[7], gate_chunks[5]))
        held = add_low(got[0], gate_chunks[6]), add_low(got[1], gate_chunks[3])
    first = scan_back(0, grad_mixed)
    if fast:
        held, grad_mixed = ordered(held, grad_mixed)
        got = ring_step(held)
        held = add_low(got[0], gate_chunks[4]), add_low(got[1], gate_chunks[1])
    second = scan_back(channels // 256, grad_mixed)
    if fast:
        held, state_raw = ordered(held, state_raw)
        got = ring_step(held)
        held, last = add_low(got[0], gate_chunks[2]), got[1]
    share_rows = depth // 4 + 16
    state_outs = call(
        functools.partial(state_back_kernel, fast),
        4,
        [place, lengths],
        [first[1], second[1], first[2], second[2], state_raw, turned, small_full],
        [((total, states), bf16), ((head_rows, total), bf16)]
        + (
            [((share_rows, states), bf16)] * 4
            if fast
            else [((depth, states), bf16), ((16, states), f32)]
        ),
        [
            masks,
            *state_taps,
            ((total, states), f32),
            ((total + pad, states), f32),
            ((depth, states), bf16),
            ((16, states), f32),
        ],
    )
    grad_state_low, step_low = state_outs[:2]
    state_parts = state_outs[2:]
    if fast:
        state_parts = [state_parts[0]] + [tensor_swap(state_parts[i], i) for i in range(1, 4)]
    if fast:
        (held, last), raw = ordered((held, last), raw)
        gate_out = gate_chunks[0].astype(f32) + last.astype(f32)
        gate_out = gate_out + ring_send(held, True).astype(f32)
    grad_inner, sums = call(
        inner_back_kernel,
        6,
        [lengths],
        [first[0], second[0], first[3], second[3], raw, norm_grad] + conv_params,
        [((total, channels), bf16), ((16, channels), f32)],
        [masks, ((total, channels), f32), ((total + pad, channels), f32)],
    )

    def project_back():
        return call(
            functools.partial(project_back_kernel, fast),
            6,
            [place],
            [
                grad_gate,
                grad_inner,
                grad_state_low,
                step_low,
                gate_full,
                inner_full,
                state_full,
                step_full,
            ],
            [((2, 128, depth), bf16)] * 2,
            [
                ((total, channels), bf16),
                ((total, channels), bf16),
                ((total, states), bf16),
                ((head_rows, total), bf16),
            ],
        )

    def chunk_pair(slots, got, after=None, last=bf16):
        grad = grad_inner if after is None else ordered(after, grad_inner)[1]
        arrays = [grad, step_low, sums, *state_parts, turned, turned, *got]

        def whole(array):
            return pl.BlockSpec(array.shape, lambda i, place: (0, 0))

        def block(slot):
            return pl.BlockSpec((tall, total), lambda i, place: (place[slot], 0))

        specs = [whole(array) for array in arrays]
        specs[7:9] = [block(slot) for slot in slots]
        out = pl.BlockSpec((tall + 48, channels), lambda i, place: (0, 0))
        return pl.pallas_call(
            functools.partial(chunk_kernel, slots, len(got)),
            grid_spec=pltpu.PrefetchScalarGridSpec(
                num_scalar_prefetch=1, grid=(1,), in_specs=specs, out_specs=[out, out]
            ),
            out_shape=[
                jax.ShapeDtypeStruct((tall + 48, channels), kind) for kind in (bf16, last)
            ],
            compiler_params=pltpu.CompilerParams(vmem_limit_bytes=vmem_bytes),
            cost_estimate=pl.CostEstimate(
                flops=2_000_000_000, bytes_accessed=1 << 20, transcendentals=0
            ),
        )(place, *arrays)

    if fast:
        held = chunk_pair((7, 5), ())
        got = ring_step(held)
        keep_rows, give_rows = project_back()
        got = ring_step(chunk_pair((6, 3), got, give_rows))
        near = tensor_swap(give_rows, 1)
        far_half = add_low(keep_rows[1], near[1])
        held = chunk_pair((4, 1), got, far_half)
        mixed_rows = tensor_sum(ordered(held, partial_out)[1], depth)
        got = ring_step(held)
        held, inner_own = chunk_pair((2, 0), got, last=f32)
        inner_out = inner_own + ring_send(held, True).astype(f32)
    else:
        (inner_msg,) = call(
            message_kernel,
            5,
            [],
            [grad_inner, step_low, turned],
            [((chunks, tall + head_rows, channels), bf16)],
            [],
        )
        keep_rows, give_rows = project_back()

    token_float = tokens.astype(f32)
    gain_full = small_full[: depth // states].reshape(1, depth)

    if fast:
        far, mixed_rows = ordered(inner_out, (tensor_swap(far_half, 2), mixed_rows))[1]
        grad_local = keep_rows[0].astype(f32) + near[0].astype(f32) + far.astype(f32)
        gate_grad, output_grad = gate_out[:tall], gate_out[tall:].T
        inner_grad = inner_out[:tall]
        state_grad = inner_out[tall : tall + 16]
        state_grad = jnp.concatenate([state_grad[:, :states], state_grad[:, states:]], axis=0)
        sums = inner_out[tall + 16 : tall + 32] + inner_out[tall + 32 :]
        step_grad = sums[10:12].reshape(heads, tall).T
        width = states // owners
        conv_state_sum = lax.dynamic_slice(
            sums[7:10].reshape(6, states), (0, owner * width), (taps + 1, width)
        )
        conv_state_grad, conv_state_bias_grad = conv_state_sum[:taps], conv_state_sum[taps]
    else:
        state_part, state_sums = state_parts
        state_grad = lax.psum_scatter(
            state_part.astype(f32), ("dp", "tensor"), scatter_dimension=0, tiled=True
        )
        conv_state_sum = lax.psum_scatter(
            state_sums[: taps + 1], ("dp", "tensor"), scatter_dimension=1, tiled=True
        )
        conv_state_grad, conv_state_bias_grad = conv_state_sum[:taps], conv_state_sum[taps]
        grad_normed = jnp.stack([keep_rows, give_rows], axis=1).reshape(total, depth)
        mixed_rows, grad_local = (
            lax.psum_scatter(part, "tensor", scatter_dimension=0, tiled=True).astype(f32)
            for part in (partial_out, grad_normed)
        )
        both, inner_float = jnp.stack(gate_chunks).astype(f32), inner_msg.astype(f32)
        gate_grad, output_grad, inner_grad = (
            lax.psum_scatter(part.reshape(depth, channels), "dp", scatter_dimension=0, tiled=True)
            for part in (both[:, :tall], both[:, tall:], inner_float[:, :tall])
        )
        output_grad = output_grad.T
        step_part = inner_float[:, tall : tall + heads, :tall].transpose(0, 2, 1)
        step_part = step_part.reshape(depth, heads)
        step_grad = lax.psum_scatter(step_part, "dp", scatter_dimension=0, tiled=True)
        sums = lax.psum(sums, "dp")
    input_grad = jnp.stack([gate_grad, inner_grad], axis=1)
    own_gain = jnp.sum(input_weight.astype(f32) * input_grad, axis=(1, 2))
    own_gain = own_gain + jnp.sum(step_weight.astype(f32) * step_grad, axis=1)
    state_gain = jnp.sum(state_weight.astype(f32) * state_grad, axis=1)
    if fast:
        own_gain = sum(tensor_direct(own_gain))
        own_gain = lax.dynamic_slice(own_gain, (me * share,), (share,))
    else:
        own_gain = lax.psum_scatter(own_gain, "tensor", scatter_dimension=0, tiled=True)
    pre_gain_grad = (own_gain + state_gain) / pre_gain.astype(f32)
    block_out = (token_float + mixed_rows).astype(bf16)
    scale = lax.rsqrt(jnp.mean(token_float * token_float, axis=1, keepdims=True) + epsilon)
    grad_scaled = grad_local * gain_full
    along = jnp.sum(grad_scaled * token_float, axis=1, keepdims=True) / depth
    tokens_grad = (
        scale * grad_scaled
        - token_float * (scale * scale * scale * along)
        + cotangent.astype(f32)
    )
    skip_grad = sums[6].reshape(heads, -1).sum(axis=1)
    return (
        block_out,
        tokens_grad,
        pre_gain_grad,
        input_grad,
        step_grad,
        state_grad,
        sums[:taps],
        sums[taps],
        conv_state_grad,
        conv_state_bias_grad,
        sums[9, states : states + heads],
        sums[9, states + 128 : states + 128 + heads],
        skip_grad,
        sums[5],
        output_grad,
    )


def solution(mesh):
    in_specs = (
        P(("dp", "tensor"), None),
        P("dp", None),
        P(("dp", "tensor"), None),
        P(("dp", "tensor")),
        P("dp", None, "tensor"),
        P("dp", "tensor"),
        P(("dp", "tensor"), None),
        P(None, "tensor"),
        P("tensor"),
        P(None, ("dp", "tensor")),
        P(("dp", "tensor")),
        P("tensor"),
        P("tensor"),
        P("tensor"),
        P("tensor"),
        P("tensor", "dp"),
    )
    out_specs = (
        P(("dp", "tensor"), None),
        P(("dp", "tensor"), None),
        P(("dp", "tensor")),
        P("dp", None, "tensor"),
        P("dp", "tensor"),
        P(("dp", "tensor"), None),
        P(None, "tensor"),
        P("tensor"),
        P(None, ("dp", "tensor")),
        P(("dp", "tensor")),
        P("tensor"),
        P("tensor"),
        P("tensor"),
        P("tensor"),
        P("tensor", "dp"),
    )
    return jax.shard_map(body, mesh=mesh, in_specs=in_specs, out_specs=out_specs, check_vma=False)
```

```python
import functools

import jax
import jax.numpy as jnp
from jax import lax
from jax.experimental import pallas as pl
from jax.experimental.pallas import tpu as pltpu
from jax.sharding import PartitionSpec as P

epsilon = 1e-05
highest = lax.Precision.HIGHEST
f32 = jnp.float32
bf16 = jnp.bfloat16
span = 256
pad = 8
head_rows = 16
head_width = 64
vmem_bytes = 57 * 1024 * 1024


def mm(a, b, over=(1, 0)):
    dims = (((over[0],), (over[1],)), ((), ()))
    return lax.dot_general(a, b, dims, preferred_element_type=f32)


def mm_exact(a, b, over=(1, 0)):
    dims = (((over[0],), (over[1],)), ((), ()))
    return lax.dot_general(a, b, dims, preferred_element_type=f32, precision=highest)


def sigmoid(v):
    return 1.0 / (1.0 + jnp.exp(-v))


def ends_of(lengths_ref):
    ends, total = [], None
    for slot in range(lengths_ref.shape[1]):
        here = lengths_ref[0, slot]
        total = here if total is None else total + here
        ends.append(total)
    return ends


def segment_of(places, ends):
    segment = jnp.zeros(places.shape, jnp.int32)
    for end in ends:
        segment = segment + jnp.where(places >= end, 1, 0)
    return segment


def iota(shape, dim):
    return lax.broadcasted_iota(jnp.int32, shape, dim)


def write_masks(mask_ref, ends):
    rows = mask_ref.shape[1] - pad
    places = iota((rows, 128), 0)
    segment = segment_of(places, ends)
    for shift in range(1, mask_ref.shape[0] + 1):
        same = (segment_of(places - shift, ends) == segment) & (places >= shift)
        mask_ref[shift - 1, :rows, :] = jnp.where(same, 1.0, 0.0)
        mask_ref[shift - 1, rows:, :] = jnp.zeros((pad, 128), f32)


def shifted_rows(x_ref, mask_ref, at, cols, shift, tall):
    part = x_ref[pad + at - shift : pad + at - shift + tall, cols]
    if shift == 0:
        return part
    return part * mask_ref[shift - 1, at : at + tall, :]


def conv_pre(x_ref, mask_ref, taps_ref, bias_ref, at, cols, tall):
    taps = taps_ref.shape[0]
    shifted = [shifted_rows(x_ref, mask_ref, at, cols, s, tall) for s in range(taps)]
    total = bias_ref[:, cols]
    for s in range(taps):
        total = total + taps_ref[taps - 1 - s : taps - s, cols] * shifted[s]
    return total, shifted


def column_loop(width, step):
    def one(c, carry):
        step(pl.ds(pl.multiple_of(c * 128, 128), 128))
        return carry

    lax.fori_loop(0, width // 128, one, 0)


def row_loop(rows, tall, step):
    def one(r, carry):
        step(pl.multiple_of(r * tall, tall))
        return carry

    lax.fori_loop(0, rows // tall, one, 0)


class Block:
    def __init__(self, b, ends, step_col, step_row, rate_col, rate_row, state_ref):
        low, top = b * span, (b + 1) * span
        states = state_ref.shape[1] // 2
        lower = jnp.where(iota((span, span), 0) >= iota((span, span), 1), 1.0, 0.0)
        self.rows = slice(low, top)
        self.step = step_col[low:top]
        self.step_row = step_row[:, low:top]
        self.cum = mm_exact(lower, rate_col[low:top])
        self.cum_row = mm_exact(rate_row[:, low:top], lower, (1, 1))
        self.inputs = state_ref[low:top, :states].astype(bf16)
        self.outputs = state_ref[low:top, states:].astype(bf16)
        segment = segment_of(iota((span, 1), 0) + low, ends)
        segment_row = segment_of(iota((1, span), 1) + low, ends)
        edge = sum(jnp.where(span - 1 >= end, 1, 0) for end in ends)
        self.near_edge = jnp.where(segment == edge, 1.0, 0.0)
        self.mask = jnp.where(segment == segment_row, lower, 0.0)
        self.contact = mm(self.outputs, self.inputs, (1, 1)) * self.mask

    def decay(self, h):
        gap = self.cum[:, h : h + 1] - self.cum_row[h : h + 1, :]
        return jnp.exp(jnp.minimum(gap, 0.0))

    def from_edge(self, h):
        return jnp.exp(self.cum[:, h : h + 1]) * self.near_edge

    def to_edge(self, h):
        last = self.cum[span - 1 : span, h : h + 1]
        return jnp.exp(last - self.cum[:, h : h + 1]) * self.near_edge


def wide(low_half, left, right):
    return jnp.where(low_half, left, right)


def step_sizes(raw_col, raw_row, bias_ref, bias_col_ref, log_ref, log_col_ref):
    def soft(v):
        return jnp.maximum(v, 0.0) + jnp.log1p(jnp.exp(-jnp.abs(v)))

    step_col = soft(raw_col + bias_ref[...])
    step_row = soft(raw_row + bias_col_ref[...])
    rate_col = -step_col * jnp.exp(log_ref[...])
    rate_row = -step_row * jnp.exp(log_col_ref[...])
    return step_col, step_row, rate_col, rate_row


def forward_kernel(fast, place_ref, lengths_ref, *refs):
    n_msg = 8 if fast else 4
    n_rows = 4 if fast else 1
    row_refs, msg_refs, refs = refs[:n_rows], refs[n_rows : n_rows + n_msg], refs[n_rows + n_msg :]
    (taps_ref, bias_ref, step_bias_ref, step_bias_col_ref, log_ref, log_col_ref, skip_ref) = refs[:7]
    (
        normed_ref,
        turned_ref,
        weight_ref,
        state_weight_ref,
        step_weight_ref,
        small_ref,
        raw_ref,
        state_raw_ref,
        step_col_ref,
        step_row_ref,
        act_ref,
        state_ref,
        mixed_ref,
    ) = refs[7:20]
    mask_ref, state_taps_ref, state_bias_ref = refs[20:]
    total, channels = act_ref.shape
    ends = ends_of(lengths_ref)

    if fast:
        depth_part = 128
        small = jnp.zeros(small_ref.shape, f32)
        share = state_weight_ref.shape[0] // 32
        for slot in range(8):
            msg = msg_refs[slot]
            index = place_ref[slot]
            at = pl.multiple_of(index * depth_part, depth_part)
            weight_ref[pl.ds(at, depth_part), :] = msg[:depth_part, :]
            for member in range(4):
                inner = pl.multiple_of(at + place_ref[8 + member] * share, share)
                high, low = depth_part + share * (member // 2), 256 * (member % 2)
                state_weight_ref[pl.ds(inner, share), :] = msg[
                    high : high + share, low : low + 256
                ]
            tail = depth_part + 2 * share
            small = small + msg[tail : tail + 16, :256].astype(f32)
            step_weight_ref[:, pl.ds(at, depth_part)] = msg[tail : tail + 16, 256:384]
        small_ref[...] = small
    else:
        weight_ref[...] = msg_refs[0][...]
        state_weight_ref[...] = msg_refs[1][...]
        step_weight_ref[...] = msg_refs[2][...]
        small_ref[...] = msg_refs[3][...].astype(f32)
    gain = jnp.concatenate([small_ref[i : i + 1, :] for i in range(4)], axis=1)
    taps = taps_ref.shape[0]
    state_taps_ref[...] = small_ref[4 : 4 + taps, :]
    state_bias_ref[...] = small_ref[4 + taps : 5 + taps, :]

    tall = total // n_rows
    for member in range(n_rows):
        at = pl.multiple_of(place_ref[8 + member] * tall, tall) if fast else 0
        value = row_refs[member][:tall, :].astype(f32)
        scale = lax.rsqrt(jnp.mean(value * value, axis=1, keepdims=True) + epsilon)
        normed = (value * scale * gain).astype(bf16)
        normed_ref[pl.ds(at, tall), :] = normed
        turned_ref[:, pl.ds(at, tall)] = normed.astype(f32).T.astype(bf16)

    raw_ref[:pad, :] = jnp.zeros((pad, channels), f32)
    state_raw_ref[:pad, :] = jnp.zeros((pad, state_raw_ref.shape[1]), f32)

    def project(at):
        part = normed_ref[pl.ds(at, 128), :]
        raw_ref[pl.ds(at + pad, 128), :] = mm(part, weight_ref[...])
        state_raw_ref[pl.ds(at + pad, 128), :] = mm(part, state_weight_ref[...])
        step_col_ref[pl.ds(at, 128), :] = mm(part, step_weight_ref[...], (1, 1))

    row_loop(total, 128, project)
    step_row_ref[...] = mm(step_weight_ref[...], normed_ref[...], (1, 1))

    write_masks(mask_ref, ends)

    def activate(x_ref, out_ref, own_taps, own_bias):
        def column(cols):
            for at in range(0, total, 128):
                pre, _ = conv_pre(x_ref, mask_ref, own_taps, own_bias, at, cols, 128)
                out_ref[at : at + 128, cols] = pre * sigmoid(pre)

        column_loop(out_ref.shape[1], column)

    activate(raw_ref, act_ref, taps_ref, bias_ref)
    activate(state_raw_ref, state_ref, state_taps_ref, state_bias_ref)

    steps = step_sizes(
        step_col_ref[...],
        step_row_ref[...],
        step_bias_ref,
        step_bias_col_ref,
        log_ref,
        log_col_ref,
    )
    low_half = iota((span, 128), 1) < head_width
    held = []
    for b in range(total // span):
        block = Block(b, ends, *steps, state_ref)
        for i in range(channels // 128):
            cols = slice(128 * i, 128 * (i + 1))
            pair = (2 * i, 2 * i + 1)
            x = act_ref[block.rows, cols]
            step_wide = wide(low_half, *(block.step[:, h : h + 1] for h in pair))
            x_step = (x * step_wide).astype(bf16)
            y = [mm((block.decay(h) * block.contact).astype(bf16), x_step) for h in pair]
            y = wide(low_half, *y) + skip_ref[:, cols] * x
            if b == 0:
                reach = wide(low_half, *(block.to_edge(h) for h in pair))
                weighted = (x * step_wide * reach).astype(bf16)
                held.append(mm(block.inputs, weighted, (0, 0)).astype(bf16))
            else:
                reach = wide(low_half, *(block.from_edge(h) for h in pair))
                y = y + reach * mm(block.outputs, held[i])
            mixed_ref[block.rows, cols] = y


def grad_in_kernel(fast, place_ref, lengths_ref, *refs):
    n_rows = 4 if fast else 1
    n_msg = 8 if fast else 2
    row_refs, msg_refs, refs = refs[:n_rows], refs[n_rows : n_rows + n_msg], refs[n_rows + n_msg :]
    normed_ref, mixed_ref, norm_ref = refs[:3]
    rows_ref, gate_weight_ref, out_weight_ref, gate_ref, grad_ref, sums_ref, wide_ref = refs[3:]
    total = rows_ref.shape[0]
    ends = ends_of(lengths_ref)
    tall = total // n_rows
    for member in range(n_rows):
        at = pl.multiple_of(place_ref[8 + member] * tall, tall) if fast else 0
        rows_ref[pl.ds(at, tall), :] = row_refs[member][-tall:, :]
    if fast:
        for slot in range(8):
            at = pl.multiple_of(place_ref[slot] * 128, 128)
            gate_weight_ref[pl.ds(at, 128), :] = msg_refs[slot][:128, :]
            out_weight_ref[pl.ds(at, 128), :] = msg_refs[slot][128:, :]
    else:
        gate_weight_ref[...] = msg_refs[0][...]
        out_weight_ref[...] = msg_refs[1][...]

    def part(at):
        rows = pl.ds(at, 128)
        valid = jnp.where(iota((128, 1), 0) + at < ends[-1], 1.0, 0.0)
        grad = mm(rows_ref[rows, :], out_weight_ref[...]) * valid
        grad_ref[rows, :] = grad
        gate = mm(normed_ref[rows, :], gate_weight_ref[...])
        gate_ref[rows, :] = gate
        gated = mixed_ref[rows, :] * (gate * sigmoid(gate))
        square = jnp.sum(gated * gated, axis=1, keepdims=True)
        cross = jnp.sum(grad * norm_ref[...] * gated, axis=1, keepdims=True)
        lane = iota((128, 128), 1)
        wide_ref[rows, :] = jnp.where(lane == 0, square, jnp.where(lane == 1, cross, 0.0))

    row_loop(total, 128, part)
    for at in range(0, total, 128):
        sums_ref[:, at : at + 128] = wide_ref[at : at + 128, :].T[:8, :]


def norm_kernel(inner_total, place_ref, lengths_ref, *refs):
    n_sums = len(refs) - 21
    sums_refs, refs = refs[:n_sums], refs[n_sums:]
    gate_ref, mixed_ref, grad_ref, norm_ref, weight_ref, rows_ref, turned_ref = refs[:7]
    chunk_refs = refs[7:15]
    partial_ref, grad_gate_ref, grad_mixed_ref, norm_grad_ref = refs[15:19]
    wide_ref, out_rows_ref = refs[19:]
    total, channels = gate_ref.shape
    ends = ends_of(lengths_ref)
    for at in range(0, total, 128):
        tile = sum(ref[:, at : at + 128] for ref in sums_refs)
        tile = jnp.concatenate([tile] * 16, axis=0)
        wide_ref[at : at + 128, :] = tile.T
    norm_grad_ref[...] = jnp.zeros(norm_grad_ref.shape, f32)

    def part(at):
        rows = pl.ds(at, 128)
        valid = jnp.where(iota((128, 1), 0) + at < ends[-1], 1.0, 0.0)
        scale = lax.rsqrt(wide_ref[rows, 0:1] / inner_total + epsilon)
        cross = wide_ref[rows, 1:2]
        gate = gate_ref[rows, :]
        mixed = mixed_ref[rows, :]
        sig = sigmoid(gate)
        gate_act = gate * sig
        gated = mixed * gate_act
        grad = grad_ref[rows, :]
        norm = norm_ref[...]
        hat = gated * scale
        out_rows_ref[rows, :] = (hat * norm * valid).astype(bf16)
        norm_grad_ref[...] += jnp.sum(grad * hat, axis=0, keepdims=True)
        grad_gated = scale * (grad * norm) - gated * (scale * scale * scale * cross / inner_total)
        grad_mixed_ref[rows, :] = grad_gated * gate_act
        grad_gate = grad_gated * mixed * sig * (1.0 + gate * (1.0 - sig))
        grad_gate_ref[rows, :] = grad_gate.astype(bf16)

    row_loop(total, 128, part)

    def back(at):
        cols = pl.ds(at, 256)
        partial_ref[:, cols] = mm(out_rows_ref[...], weight_ref[cols, :], (1, 1)).astype(bf16)

    row_loop(weight_ref.shape[0], 256, back)
    tall = chunk_refs[0].shape[0] // 2
    for slot, chunk_ref in enumerate(chunk_refs):
        cols = pl.ds(pl.multiple_of(place_ref[slot] * tall, tall), tall)
        chunk_ref[:tall, :] = mm(turned_ref[cols, :], grad_gate_ref[...]).astype(bf16)
        chunk_ref[tall:, :] = mm(rows_ref[:, cols], out_rows_ref[...], (0, 0)).astype(bf16)


def scan_back_kernel(first_pair, lengths_ref, *refs):
    grad_mixed_ref, act_ref, state_ref, step_col_ref, step_row_ref = refs[:5]
    step_bias_ref, step_bias_col_ref, log_ref, log_col_ref, skip_ref = refs[5:10]
    grad_act_ref, grad_state_ref, step_grad_ref, sums_ref, acc_ref = refs[10:]
    total, own_width = grad_act_ref.shape
    states = state_ref.shape[1] // 2
    ends = ends_of(lengths_ref)
    sums_ref[...] = jnp.zeros(sums_ref.shape, f32)
    raw_row = step_row_ref[...]
    steps = step_sizes(
        step_col_ref[...], raw_row, step_bias_ref, step_bias_col_ref, log_ref, log_col_ref
    )
    rate_row = steps[3]
    low_half = iota((span, 128), 1) < head_width
    lower = jnp.where(iota((span, span), 0) >= iota((span, span), 1), 1.0, 0.0)
    blocks = [Block(b, ends, *steps, state_ref) for b in range(total // span)]
    first, second = blocks
    row_sums, step_rows, out_sums, in_sums = [], [], None, None
    grad_out = jnp.zeros((span, states), f32)
    grad_in = jnp.zeros((span, states), f32)
    head_of = iota((head_rows, 128), 0)
    lane_head = iota((head_rows, 128), 1) // head_width

    for b, block in enumerate(blocks):
        acc_ref[...] = jnp.zeros((span, span), f32)
        row_sum = jnp.zeros((span, 128), f32)
        step_grad = jnp.zeros((head_rows, span), f32)
        lane = iota((span, 128), 1)
        head_row = iota((head_rows, span), 0)
        for i in range(first_pair, first_pair + own_width // 128):
            cols = slice(128 * i, 128 * (i + 1))
            own_cols = slice(128 * (i - first_pair), 128 * (i - first_pair + 1))
            pair = (2 * i, 2 * i + 1)
            x = act_ref[block.rows, cols]
            x_low = x.astype(bf16)
            grad = grad_mixed_ref[block.rows, cols]
            grad_low = grad.astype(bf16)
            halves = (
                jnp.where(low_half, grad, 0.0).astype(bf16),
                jnp.where(low_half, 0.0, grad).astype(bf16),
            )
            step_wide = wide(low_half, *(block.step[:, h : h + 1] for h in pair))
            grads = []
            for h, half in zip(pair, halves):
                decay = block.decay(h)
                spread = mm(half, x_low, (1, 1)) * decay
                stepped = spread * block.step_row[h : h + 1, :]
                acc_ref[...] += stepped
                row_here = jnp.sum(stepped * block.contact, axis=1, keepdims=True)
                row_sum = jnp.where(lane == h, row_here, row_sum)
                step_here = jnp.sum(spread * block.contact, axis=0, keepdims=True)
                step_grad = jnp.where(head_row == h, step_here, step_grad)
                grads.append(mm((decay * block.contact).astype(bf16), grad_low, (0, 0)))
            grad_act = wide(low_half, *grads) * step_wide + skip_ref[:, cols] * grad
            sums_ref[2:3, own_cols] += jnp.sum(grad * x, axis=0, keepdims=True)
            picks = jnp.where(lane_head + 2 * i == head_of, 1.0, 0.0)
            if b == 0:
                reach = wide(low_half, *(second.from_edge(h) for h in pair))
                lead = (grad_mixed_ref[second.rows, cols] * reach).astype(bf16)
                edge = wide(low_half, *(block.to_edge(h) for h in pair))
                weighted = (x * step_wide * edge).astype(bf16)
                held = mm(block.inputs, weighted, (0, 0)).astype(bf16)
                held_grad = mm(second.outputs, lead, (0, 0)).astype(bf16)
                grad_out = grad_out + mm(lead, held, (1, 1))
                grad_in = grad_in + mm(weighted, held_grad, (1, 1))
                back = mm(block.inputs, held_grad) * edge
                grad_act = grad_act + back * step_wide
                ahead = mm(second.outputs, held)
                out_here = mm_exact(picks, lead.astype(f32) * ahead, (1, 1))
                in_here = mm_exact(picks, x * back, (1, 1))
                out_sums = out_here if out_sums is None else out_sums + out_here
                in_sums = in_here if in_sums is None else in_sums + in_here
            grad_act_ref[block.rows, own_cols] = grad_act
        table = (acc_ref[...] * block.mask).astype(bf16)
        grad_c = mm(table, block.inputs)
        grad_b = mm(table, block.outputs, (0, 0))
        if b == 0:
            grad_b = grad_b + grad_in
        else:
            grad_c = grad_c + grad_out
        grad_state_ref[block.rows, :states] = grad_b
        grad_state_ref[block.rows, states:] = grad_c
        row_sums.append(row_sum)
        step_rows.append(step_grad)

    rate_grads = []
    for b, block in enumerate(blocks):
        column = step_rows[b] * block.step_row
        crossing = mm_exact(row_sums[b], lower, (0, 0))[:head_rows] - mm_exact(column, lower)
        if b == 0:
            crossing = crossing + mm_exact(in_sums * block.step_row, 1.0 - lower)
        else:
            crossing = crossing + mm_exact(out_sums, lower)
        rate_grads.append(crossing)
    step_rows[0] = step_rows[0] + in_sums
    rate_grad = jnp.concatenate(rate_grads, axis=1)
    step_grad = jnp.concatenate(step_rows, axis=1) - rate_grad * jnp.exp(log_col_ref[...])
    step_grad = step_grad * sigmoid(raw_row + step_bias_col_ref[...])
    decay_sum = jnp.sum(rate_grad * rate_row, axis=1, keepdims=True)
    bias_sum = jnp.sum(step_grad, axis=1, keepdims=True)
    lane = iota((head_rows, 128), 1)
    head_sums = jnp.where(lane == 0, bias_sum, jnp.where(lane == 1, decay_sum, 0.0))
    head_sums = jnp.concatenate([head_sums] * (128 // head_rows), axis=0).T
    sums_ref[0:2, :128] = head_sums[:2, :]
    step_grad_ref[...] = step_grad


def conv_back(x_ref, mask_ref, grad_ref, held_ref, out_ref, sums_ref, own_taps, own_bias):
    total, taps = out_ref.shape[0], own_taps.shape[0]
    held_ref[total:, :] = jnp.zeros((pad, held_ref.shape[1]), f32)

    def column(cols):
        sums = [jnp.zeros((1, 128), f32) for _ in range(taps + 1)]
        for at in range(0, total, 128):
            pre, shifted = conv_pre(x_ref, mask_ref, own_taps, own_bias, at, cols, 128)
            sig = sigmoid(pre)
            grad = grad_ref[at : at + 128, cols] * sig * (1.0 + pre * (1.0 - sig))
            held_ref[at : at + 128, cols] = grad
            for s in range(taps):
                sums[taps - 1 - s] += jnp.sum(grad * shifted[s], axis=0, keepdims=True)
            sums[taps] += jnp.sum(grad, axis=0, keepdims=True)
        for t, value in enumerate(sums):
            sums_ref[t : t + 1, cols] = value
        for at in range(0, total, 128):
            back = own_taps[taps - 1 : taps, cols] * held_ref[at : at + 128, cols]
            for s in range(1, taps):
                part = held_ref[at + s : at + s + 128, cols]
                part = part * mask_ref[s - 1, at + s : at + s + 128, :]
                back = back + own_taps[taps - 1 - s : taps - s, cols] * part
            out_ref[at : at + 128, cols] = back.astype(bf16)

    column_loop(out_ref.shape[1], column)


def state_back_kernel(fast, place_ref, lengths_ref, *refs):
    state_refs, step_refs, refs = refs[0:2], refs[2:4], refs[4:]
    state_raw_ref, turned_ref, small_ref, grad_state_low_ref, step_low_ref = refs[:5]
    n_out = 4 if fast else 2
    out_refs, refs = refs[5 : 5 + n_out], refs[5 + n_out :]
    mask_ref, taps_ref, bias_ref, grad_state_ref, pre_ref, part_ref, sums_ref = refs
    taps = taps_ref.shape[0]
    taps_ref[...] = small_ref[4 : 4 + taps, :]
    bias_ref[...] = small_ref[4 + taps : 5 + taps, :]
    write_masks(mask_ref, ends_of(lengths_ref))
    grad_state_ref[...] = state_refs[0][...] + state_refs[1][...]
    step_low_ref[...] = (step_refs[0][...] + step_refs[1][...]).astype(bf16)
    sums_ref[...] = jnp.zeros(sums_ref.shape, f32)
    conv_back(
        state_raw_ref,
        mask_ref,
        grad_state_ref,
        pre_ref,
        grad_state_low_ref,
        sums_ref,
        taps_ref,
        bias_ref,
    )

    def chunk(at):
        part = turned_ref[pl.ds(at, 256), :]
        part_ref[pl.ds(at, 256), :] = mm(part, grad_state_low_ref[...]).astype(bf16)

    depth = turned_ref.shape[0]
    row_loop(depth, 256, chunk)
    if fast:
        share = depth // 32
        for member, out_ref in enumerate(out_refs):
            for c in range(8):
                at = pl.multiple_of((4 * c + place_ref[8 + member]) * share, share)
                out_ref[share * c : share * (c + 1), :] = part_ref[pl.ds(at, share), :]
            out_ref[8 * share :, :] = sums_ref[...].astype(bf16)
    else:
        out_refs[0][...] = part_ref[...]
        out_refs[1][...] = sums_ref[...]


def inner_back_kernel(lengths_ref, *refs):
    act_refs, head_refs, refs = refs[0:2], refs[2:4], refs[4:]
    raw_ref, norm_grad_ref, taps_ref, bias_ref, grad_inner_ref, sums_ref = refs[:6]
    mask_ref, grad_act_ref, pre_ref = refs[6:]
    half = grad_inner_ref.shape[1] // 2
    write_masks(mask_ref, ends_of(lengths_ref))
    grad_act_ref[:, :half] = act_refs[0][...]
    grad_act_ref[:, half:] = act_refs[1][...]
    sums_ref[...] = jnp.zeros(sums_ref.shape, f32)
    heads = head_refs[0][:2, :128] + head_refs[1][:2, :128]
    sums_ref[5:6, :] = norm_grad_ref[...]
    sums_ref[6:7, :half] = head_refs[0][2:3, :]
    sums_ref[6:7, half:] = head_refs[1][2:3, :]
    sums_ref[9:10, half : half + 128] = heads[0:1, :]
    sums_ref[9:10, half + 128 :] = heads[1:2, :]
    conv_back(
        raw_ref,
        mask_ref,
        grad_act_ref,
        pre_ref,
        grad_inner_ref,
        sums_ref,
        taps_ref,
        bias_ref,
    )


def message_kernel(grad_inner_ref, step_low_ref, turned_ref, msg_ref):
    chunks = msg_ref.shape[0]
    tall = turned_ref.shape[0] // chunks
    step_low = step_low_ref[...]

    def chunk(c, carry):
        part = turned_ref[pl.ds(pl.multiple_of(c * tall, tall), tall), :]
        msg_ref[c, :tall, :] = mm(part, grad_inner_ref[...]).astype(bf16)
        msg_ref[c, tall:, :tall] = mm(step_low, part, (1, 1)).astype(bf16)
        msg_ref[c, tall:, tall:] = jnp.zeros((head_rows, msg_ref.shape[2] - tall), bf16)
        return carry

    lax.fori_loop(0, chunks, chunk, 0)


def chunk_kernel(slots, n_got, place_ref, *refs):
    grad_inner_ref, step_low_ref, sums_ref = refs[:3]
    state_refs, turned_refs, got_refs = refs[3:7], refs[7:9], refs[9 : 9 + n_got]
    out_refs = refs[9 + n_got :]
    states = state_refs[0].shape[1]
    share = (state_refs[0].shape[0] - 16) // 8

    def state_rows(low, tall):
        return sum(ref[pl.ds(low, tall), :].astype(f32) for ref in state_refs)

    shared = state_rows(8 * share, 16)
    sums = [
        sums_ref[:7, :],
        jnp.concatenate([shared[0:1, :], shared[1:2, :]], axis=1),
        jnp.concatenate([shared[2:3, :], shared[3:4, :]], axis=1),
        jnp.concatenate([shared[4:5, :], sums_ref[9:10, states:]], axis=1),
    ]
    for n, (slot, out_ref) in enumerate(zip(slots, out_refs)):
        index = place_ref[slot]
        part = turned_refs[n][...]
        step = mm(step_low_ref[...], part, (1, 1))
        step = [
            jnp.concatenate([step[4 * k + i : 4 * k + i + 1, :] for i in range(4)], axis=1)
            for k in range(2)
        ]
        state = state_rows(pl.multiple_of(index * share, share), share)
        value = jnp.concatenate(
            [
                mm(part, grad_inner_ref[...]),
                jnp.concatenate([state[:16, :], state[16:, :]], axis=1),
                *sums,
                *step,
                jnp.zeros((4, 2 * states), f32),
            ],
            axis=0,
        )
        tail = value.shape[0] - 16
        main, sums_here = value[:tail, :], value[tail:, :]
        if n < n_got:
            got = got_refs[n]
            main = main + got[:tail, :].astype(f32)
            sums_here = sums_here + got[tail : tail + 16, :].astype(f32)
            sums_here = sums_here + got[tail + 16 :, :].astype(f32)
        out_ref[:tail, :] = main.astype(out_ref.dtype)
        high = sums_here.astype(bf16)
        out_ref[tail : tail + 16, :] = high.astype(out_ref.dtype)
        out_ref[tail + 16 :, :] = (sums_here - high.astype(f32)).astype(out_ref.dtype)


def project_back_kernel(fast, place_ref, *refs):
    grad_refs, step_low_ref, weight_refs, step_weight_ref = refs[:3], refs[3], refs[4:7], refs[7]
    out_refs, held_refs, step_ref = refs[8:10], refs[10:13], refs[13]
    for n, member in enumerate((0, 2, 1, 3)):
        at = pl.multiple_of(place_ref[8 + member] * 128, 128) if fast else 128 * member
        for held_ref, grad_ref in zip(held_refs, grad_refs):
            held_ref[128 * n : 128 * (n + 1), :] = grad_ref[pl.ds(at, 128), :]
        step_ref[:, 128 * n : 128 * (n + 1)] = step_low_ref[:, pl.ds(at, 128)]

    def back(at):
        cols = pl.ds(at, 256)
        grad = mm(step_ref[...], step_weight_ref[:, cols], (0, 0))
        for held_ref, weight_ref in zip(held_refs, weight_refs):
            grad = grad + mm(held_ref[...], weight_ref[cols, :], (1, 1))
        grad = grad.astype(bf16)
        for n in range(4):
            out_refs[n // 2][n % 2, :, cols] = grad[128 * n : 128 * (n + 1), :]

    row_loop(step_weight_ref.shape[1], 256, back)


def prepare_kernel(place_ref, gain_ref, taps_ref, bias_ref, state_ref, shared_ref):
    owner = place_ref[0]
    share, states = state_ref.shape
    shared_ref[:share, :] = state_ref[...]

    def placed(value, at):
        width = value.shape[1]
        pick = iota((width, states), 1) - at == iota((width, states), 0)
        return mm(value, jnp.where(pick, 1.0, 0.0).astype(bf16))

    start = owner * gain_ref.shape[1]
    small = jnp.concatenate(
        [placed(gain_ref[...], start - states * i) for i in range(4)]
        + [placed(taps_ref[...], owner * taps_ref.shape[1])]
        + [placed(bias_ref[...], owner * bias_ref.shape[1])]
        + [jnp.zeros((7, states), f32)],
        axis=0,
    )
    shared_ref[share:, :] = small.astype(bf16)


def prepare_late_kernel(input_ref, out_ref, late_ref):
    depth_part = input_ref.shape[0]
    late_ref[:depth_part, :] = input_ref[:, 0, :]
    late_ref[depth_part:, :] = out_ref[...].astype(f32).T.astype(bf16)


def params_kernel(*refs):
    taps_ref, bias_ref, step_bias_ref, log_ref, skip_ref, norm_ref = refs[:6]
    outs = refs[6:]
    heads = step_bias_ref.shape[1]
    pick = jnp.where(iota((heads, head_rows), 0) == iota((heads, head_rows), 1), 1.0, 0.0)
    square = iota((head_rows, head_rows), 0) == iota((head_rows, head_rows), 1)

    def both(value_ref, row_ref, col_ref):
        row = mm_exact(value_ref[...].astype(f32), pick)
        row_ref[...] = row
        col_ref[...] = jnp.sum(jnp.where(square, row, 0.0), axis=1, keepdims=True)

    outs[0][...] = taps_ref[...].astype(f32)
    outs[1][...] = bias_ref[...].astype(f32)
    both(step_bias_ref, outs[2], outs[3])
    both(log_ref, outs[4], outs[5])
    channels = norm_ref.shape[1]
    own = iota((heads, channels), 1) // (channels // heads) == iota((heads, channels), 0)
    outs[6][...] = mm_exact(skip_ref[...].astype(f32), jnp.where(own, 1.0, 0.0))
    outs[7][...] = norm_ref[...].astype(f32)


def assemble_kernel(input_ref, step_ref, *refs):
    shared_refs, msg_ref = refs[:4], refs[4]
    depth_part, _, channels = input_ref.shape
    share = shared_refs[0].shape[0] - 16
    tail = depth_part + 2 * share
    msg_ref[:depth_part, :] = input_ref[:, 1, :]
    for member, ref in enumerate(shared_refs):
        high, low = depth_part + share * (member // 2), 256 * (member % 2)
        msg_ref[high : high + share, low : low + 256] = ref[:share, :]
    small = sum(ref[share:, :].astype(f32) for ref in shared_refs)
    msg_ref[tail:, :256] = small.astype(bf16)
    msg_ref[tail:, 256:384] = step_ref[...]
    msg_ref[tail:, 384:] = jnp.zeros((16, channels - 384), bf16)


def call(kernel, micros, scalars, arrays, outs, scratch):
    smem = pl.BlockSpec(memory_space=pltpu.SMEM)
    vmem = pl.BlockSpec(memory_space=pltpu.VMEM)
    return pl.pallas_call(
        kernel,
        out_shape=[jax.ShapeDtypeStruct(shape, kind) for shape, kind in outs],
        in_specs=[smem] * len(scalars) + [vmem] * len(arrays),
        out_specs=[vmem] * len(outs),
        scratch_shapes=[pltpu.VMEM(shape, kind) for shape, kind in scratch],
        compiler_params=pltpu.CompilerParams(vmem_limit_bytes=vmem_bytes),
        cost_estimate=pl.CostEstimate(
            flops=int(micros * 1.1e9), bytes_accessed=1 << 20, transcendentals=0
        ),
    )(*scalars, *arrays)


def ring_ok(n_dp, n_tensor):
    return n_dp == 8 and n_tensor == 4


ring_order = (0, 2, 4, 6, 7, 5, 3, 1)


def ring_place(index):
    high, low = index // 2, index % 2
    return jnp.where(low == 0, high, 7 - high)


def ring_index(place):
    place = lax.rem(place + 16, 8)
    return jnp.where(place < 4, 2 * place, 2 * (7 - place) + 1)


def ring_send(value, forward):
    pairs = []
    for place in range(8):
        other = (place + (1 if forward else 7)) % 8
        pairs.append((ring_order[place], ring_order[other]))
    return lax.ppermute(value, "dp", pairs)


def ring_gather(value):
    me = ring_place(lax.axis_index("dp"))
    pieces = [(value, ring_index(me))]
    ahead, back = value, value
    for step in range(1, 5):
        ahead = ring_send(ahead, True)
        pieces.append((ahead, ring_index(me - step)))
        if step < 4:
            back = ring_send(back, False)
            pieces.append((back, ring_index(me + step)))
    return pieces


def dp_swap(value, bit):
    return lax.ppermute(value, "dp", [(i, i ^ bit) for i in range(8)])


def ring_step(held):
    return ring_send(held[0], True), ring_send(held[1], False)


def add_low(got, own):
    return (got.astype(f32) + own.astype(f32)).astype(bf16)


def ordered(first, then):
    return lax.optimization_barrier((first, then))


def tensor_gather(value):
    near = tensor_swap(value, 1)
    far = tensor_swap(value, 2)
    return [value, near, far, tensor_swap(far, 1)]


def tensor_direct(value):
    return [value] + [tensor_swap(value, bit) for bit in range(1, 4)]


def tensor_sum(value, depth):
    parts = value.reshape(4, -1, depth)
    parts = lax.all_to_all(parts, "tensor", 0, 0, tiled=True)
    return jnp.sum(parts.astype(f32), axis=0)


def tensor_swap(value, bit):
    return lax.ppermute(value, "tensor", [(i, i ^ bit) for i in range(4)])


def body(
    tokens,
    lengths,
    cotangent,
    pre_gain,
    input_weight,
    step_weight,
    state_weight,
    conv_inner,
    conv_inner_bias,
    conv_state,
    conv_state_bias,
    step_bias,
    decay_log,
    skip_gain,
    norm_gain,
    output_weight,
):
    n_dp, n_tensor = lax.axis_size("dp"), lax.axis_size("tensor")
    fast = ring_ok(n_dp, n_tensor)
    owners = n_dp * n_tensor
    me = lax.axis_index("tensor")
    owner = lax.axis_index("dp") * n_tensor + me
    own_rows, depth = tokens.shape
    total = own_rows * n_tensor
    states = state_weight.shape[1]
    heads = step_weight.shape[1]
    share = state_weight.shape[0]
    taps = conv_state.shape[0]
    channels = input_weight.shape[2]
    inner_total = channels * n_tensor

    owner_place = jnp.stack([owner, owners]).astype(jnp.int32)
    (shared,) = call(
        prepare_kernel,
        1,
        [owner_place],
        [pre_gain[None, :], conv_state, conv_state_bias[None, :], state_weight],
        [((share + 16, states), bf16)],
        [],
    )
    step_rows = jnp.pad(step_weight.T, ((0, head_rows - heads), (0, 0)))
    shared, out_shard = ordered(shared, output_weight)
    (late,) = call(
        prepare_late_kernel,
        2,
        [],
        [input_weight, out_shard],
        [((input_weight.shape[0] + output_weight.shape[1], channels), bf16)],
        [],
    )
    params = call(
        params_kernel,
        1,
        [],
        [
            conv_inner,
            conv_inner_bias[None, :],
            step_bias[None, :],
            decay_log[None, :],
            skip_gain[None, :],
            norm_gain[None, :],
        ],
        [
            ((taps, channels), f32),
            ((1, channels), f32),
            ((1, head_rows), f32),
            ((head_rows, 1), f32),
            ((1, head_rows), f32),
            ((head_rows, 1), f32),
            ((1, channels), f32),
            ((1, channels), f32),
        ],
        [],
    )
    params = list(params)
    conv_params, head_params, norm_row = params[:2], params[2:7], params[7]
    if fast:
        shared = tensor_direct(shared)
        late_one = ring_step((late, late))
        (msg,) = call(
            assemble_kernel,
            1,
            [],
            [input_weight, step_rows, *shared],
            [((input_weight.shape[0] + 2 * share + 16, channels), bf16)],
            [],
        )
        late_one, msg = ordered(late_one, msg)
        msg = ring_gather(msg)
        weight_pieces = [piece for piece, _ in msg]
        late_two = ring_step(late_one)
        late_three = ring_step(late_two)
        late_pieces = [late, *late_one, *late_two, *late_three, ring_send(late_three[0], True)]
        own_rows_both = jnp.concatenate([tokens, cotangent], axis=0)
        row_pieces = tensor_gather(ordered(shared, own_rows_both)[1])
        grad_pieces = row_pieces
        place = jnp.stack([index for _, index in msg] + [me, me ^ 1, me ^ 2, me ^ 3])
    else:
        row_pieces = [lax.all_gather(tokens, "tensor", axis=0, tiled=True)]
        grad_pieces = [lax.all_gather(cotangent, "tensor", axis=0, tiled=True)]
        gate_weight, inner_weight = late[: input_weight.shape[0]], input_weight[:, 1]
        weight_pieces = [
            lax.all_gather(inner_weight, "dp", axis=0, tiled=True),
            lax.all_gather(state_weight, ("dp", "tensor"), axis=0, tiled=True),
            lax.all_gather(step_rows, "dp", axis=1, tiled=True),
            lax.psum(shared[share:], ("dp", "tensor")),
        ]
        late_pieces = [
            lax.all_gather(gate_weight, "dp", axis=0, tiled=True),
            lax.all_gather(late[input_weight.shape[0] :], "dp", axis=0, tiled=True),
        ]
        place = jnp.concatenate([jnp.arange(8), jnp.arange(4)])
    place = place.astype(jnp.int32)

    masks = ((taps - 1, total + pad, 128), f32)
    state_taps = [((taps, states), f32), ((1, states), f32)]
    (
        normed,
        turned,
        inner_full,
        state_full,
        step_full,
        small_full,
        raw,
        state_raw,
        step_col,
        step_row,
        act,
        state_act,
        mixed,
    ) = call(
        functools.partial(forward_kernel, fast),
        11,
        [place, lengths],
        row_pieces + weight_pieces + conv_params + head_params,
        [
            ((total, depth), bf16),
            ((depth, total), bf16),
            ((depth, channels), bf16),
            ((depth, states), bf16),
            ((head_rows, depth), bf16),
            ((16, states), f32),
            ((total + pad, channels), f32),
            ((total + pad, states), f32),
            ((total, head_rows), f32),
            ((head_rows, total), f32),
            ((total, channels), f32),
            ((total, states), f32),
            ((total, channels), f32),
        ],
        [masks] + state_taps,
    )
    grad_rows, gate_full, output_full, gate, grad_normalized, sums = call(
        functools.partial(grad_in_kernel, fast),
        5,
        [place, lengths],
        grad_pieces + late_pieces + [normed, mixed, norm_row],
        [
            ((total, depth), bf16),
            ((depth, channels), bf16),
            ((depth, channels), bf16),
            ((total, channels), f32),
            ((total, channels), f32),
            ((8, total), f32),
        ],
        [((total, 128), f32)],
    )
    if fast:
        sums = tensor_direct(sums)
    else:
        sums = [lax.psum(sums, "tensor")]
    chunks = 8
    tall = depth // chunks
    norm_outs = call(
        functools.partial(norm_kernel, inner_total),
        9,
        [place, lengths],
        [*sums, gate, mixed, grad_normalized, norm_row, output_full, grad_rows, turned],
        [((2 * tall, channels), bf16)] * chunks
        + [
            ((total, depth), bf16),
            ((total, channels), bf16),
            ((total, channels), f32),
            ((1, channels), f32),
        ],
        [((total, 128), f32), ((total, channels), bf16)],
    )
    gate_chunks = norm_outs[:chunks]
    partial_out, grad_gate, grad_mixed, norm_grad = norm_outs[chunks:]

    def scan_back(first_pair, grad):
        return call(
            functools.partial(scan_back_kernel, first_pair),
            6,
            [lengths],
            [grad, act, state_act, step_col, step_row] + head_params,
            [
                ((total, channels // 2), f32),
                ((total, states), f32),
                ((head_rows, total), f32),
                ((8, channels // 2), f32),
            ],
            [((span, span), f32)],
        )

    if fast:
        got = ring_step((gate_chunks[7], gate_chunks[5]))
        held = add_low(got[0], gate_chunks[6]), add_low(got[1], gate_chunks[3])
    first = scan_back(0, grad_mixed)
    if fast:
        held, grad_mixed = ordered(held, grad_mixed)
        got = ring_step(held)
        held = add_low(got[0], gate_chunks[4]), add_low(got[1], gate_chunks[1])
    second = scan_back(channels // 256, grad_mixed)
    if fast:
        held, state_raw = ordered(held, state_raw)
        got = ring_step(held)
        held, last = add_low(got[0], gate_chunks[2]), got[1]
    share_rows = depth // 4 + 16
    state_outs = call(
        functools.partial(state_back_kernel, fast),
        4,
        [place, lengths],
        [first[1], second[1], first[2], second[2], state_raw, turned, small_full],
        [((total, states), bf16), ((head_rows, total), bf16)]
        + (
            [((share_rows, states), bf16)] * 4
            if fast
            else [((depth, states), bf16), ((16, states), f32)]
        ),
        [
            masks,
            *state_taps,
            ((total, states), f32),
            ((total + pad, states), f32),
            ((depth, states), bf16),
            ((16, states), f32),
        ],
    )
    grad_state_low, step_low = state_outs[:2]
    state_parts = state_outs[2:]
    if fast:
        state_parts = [state_parts[0]] + [tensor_swap(state_parts[i], i) for i in range(1, 4)]
    if fast:
        (held, last), raw = ordered((held, last), raw)
        gate_out = gate_chunks[0].astype(f32) + last.astype(f32)
        gate_out = gate_out + ring_send(held, True).astype(f32)
    grad_inner, sums = call(
        inner_back_kernel,
        6,
        [lengths],
        [first[0], second[0], first[3], second[3], raw, norm_grad] + conv_params,
        [((total, channels), bf16), ((16, channels), f32)],
        [masks, ((total, channels), f32), ((total + pad, channels), f32)],
    )

    def project_back():
        return call(
            functools.partial(project_back_kernel, fast),
            6,
            [place],
            [
                grad_gate,
                grad_inner,
                grad_state_low,
                step_low,
                gate_full,
                inner_full,
                state_full,
                step_full,
            ],
            [((2, 128, depth), bf16)] * 2,
            [
                ((total, channels), bf16),
                ((total, channels), bf16),
                ((total, states), bf16),
                ((head_rows, total), bf16),
            ],
        )

    def chunk_pair(slots, got, after=None, last=bf16):
        grad = grad_inner if after is None else ordered(after, grad_inner)[1]
        arrays = [grad, step_low, sums, *state_parts, turned, turned, *got]

        def whole(array):
            return pl.BlockSpec(array.shape, lambda i, place: (0, 0))

        def block(slot):
            return pl.BlockSpec((tall, total), lambda i, place: (place[slot], 0))

        specs = [whole(array) for array in arrays]
        specs[7:9] = [block(slot) for slot in slots]
        out = pl.BlockSpec((tall + 48, channels), lambda i, place: (0, 0))
        return pl.pallas_call(
            functools.partial(chunk_kernel, slots, len(got)),
            grid_spec=pltpu.PrefetchScalarGridSpec(
                num_scalar_prefetch=1, grid=(1,), in_specs=specs, out_specs=[out, out]
            ),
            out_shape=[
                jax.ShapeDtypeStruct((tall + 48, channels), kind) for kind in (bf16, last)
            ],
            compiler_params=pltpu.CompilerParams(vmem_limit_bytes=vmem_bytes),
            cost_estimate=pl.CostEstimate(
                flops=2_000_000_000, bytes_accessed=1 << 20, transcendentals=0
            ),
        )(place, *arrays)

    if fast:
        held = chunk_pair((7, 5), ())
        got = ring_step(held)
        keep_rows, give_rows = project_back()
        held = chunk_pair((6, 3), got, give_rows)
        partial_out = ordered(held, partial_out)[1]
        got = ring_step(held)
        mixed_rows = tensor_sum(partial_out, depth)
        near = tensor_swap(give_rows, 1)
        far_half = add_low(keep_rows[1], near[1])
        got = ring_step(chunk_pair((4, 1), got))
        held, inner_own = chunk_pair((2, 0), got, (mixed_rows, far_half), last=f32)
        inner_out = inner_own + ring_send(held, True).astype(f32)
    else:
        (inner_msg,) = call(
            message_kernel,
            5,
            [],
            [grad_inner, step_low, turned],
            [((chunks, tall + head_rows, channels), bf16)],
            [],
        )
        keep_rows, give_rows = project_back()

    token_float = tokens.astype(f32)
    gain_full = small_full[: depth // states].reshape(1, depth)

    if fast:
        far = ordered(inner_out, tensor_swap(far_half, 2))[1]
        grad_local = keep_rows[0].astype(f32) + near[0].astype(f32) + far.astype(f32)
        gate_grad, output_grad = gate_out[:tall], gate_out[tall:].T
        inner_grad = inner_out[:tall]
        state_grad = inner_out[tall : tall + 16]
        state_grad = jnp.concatenate([state_grad[:, :states], state_grad[:, states:]], axis=0)
        sums = inner_out[tall + 16 : tall + 32] + inner_out[tall + 32 :]
        step_grad = sums[10:12].reshape(heads, tall).T
        width = states // owners
        conv_state_sum = lax.dynamic_slice(
            sums[7:10].reshape(6, states), (0, owner * width), (taps + 1, width)
        )
        conv_state_grad, conv_state_bias_grad = conv_state_sum[:taps], conv_state_sum[taps]
    else:
        state_part, state_sums = state_parts
        state_grad = lax.psum_scatter(
            state_part.astype(f32), ("dp", "tensor"), scatter_dimension=0, tiled=True
        )
        conv_state_sum = lax.psum_scatter(
            state_sums[: taps + 1], ("dp", "tensor"), scatter_dimension=1, tiled=True
        )
        conv_state_grad, conv_state_bias_grad = conv_state_sum[:taps], conv_state_sum[taps]
        grad_normed = jnp.stack([keep_rows, give_rows], axis=1).reshape(total, depth)
        mixed_rows, grad_local = (
            lax.psum_scatter(part, "tensor", scatter_dimension=0, tiled=True).astype(f32)
            for part in (partial_out, grad_normed)
        )
        both, inner_float = jnp.stack(gate_chunks).astype(f32), inner_msg.astype(f32)
        gate_grad, output_grad, inner_grad = (
            lax.psum_scatter(part.reshape(depth, channels), "dp", scatter_dimension=0, tiled=True)
            for part in (both[:, :tall], both[:, tall:], inner_float[:, :tall])
        )
        output_grad = output_grad.T
        step_part = inner_float[:, tall : tall + heads, :tall].transpose(0, 2, 1)
        step_part = step_part.reshape(depth, heads)
        step_grad = lax.psum_scatter(step_part, "dp", scatter_dimension=0, tiled=True)
        sums = lax.psum(sums, "dp")
    input_grad = jnp.stack([gate_grad, inner_grad], axis=1)
    own_gain = jnp.sum(input_weight.astype(f32) * input_grad, axis=(1, 2))
    own_gain = own_gain + jnp.sum(step_weight.astype(f32) * step_grad, axis=1)
    state_gain = jnp.sum(state_weight.astype(f32) * state_grad, axis=1)
    if fast:
        own_gain = sum(tensor_direct(own_gain))
        own_gain = lax.dynamic_slice(own_gain, (me * share,), (share,))
    else:
        own_gain = lax.psum_scatter(own_gain, "tensor", scatter_dimension=0, tiled=True)
    pre_gain_grad = (own_gain + state_gain) / pre_gain.astype(f32)
    block_out = (token_float + mixed_rows).astype(bf16)
    scale = lax.rsqrt(jnp.mean(token_float * token_float, axis=1, keepdims=True) + epsilon)
    grad_scaled = grad_local * gain_full
    along = jnp.sum(grad_scaled * token_float, axis=1, keepdims=True) / depth
    tokens_grad = (
        scale * grad_scaled
        - token_float * (scale * scale * scale * along)
        + cotangent.astype(f32)
    )
    skip_grad = sums[6].reshape(heads, -1).sum(axis=1)
    return (
        block_out,
        tokens_grad,
        pre_gain_grad,
        input_grad,
        step_grad,
        state_grad,
        sums[:taps],
        sums[taps],
        conv_state_grad,
        conv_state_bias_grad,
        sums[9, states : states + heads],
        sums[9, states + 128 : states + 128 + heads],
        skip_grad,
        sums[5],
        output_grad,
    )


def solution(mesh):
    in_specs = (
        P(("dp", "tensor"), None),
        P("dp", None),
        P(("dp", "tensor"), None),
        P(("dp", "tensor")),
        P("dp", None, "tensor"),
        P("dp", "tensor"),
        P(("dp", "tensor"), None),
        P(None, "tensor"),
        P("tensor"),
        P(None, ("dp", "tensor")),
        P(("dp", "tensor")),
        P("tensor"),
        P("tensor"),
        P("tensor"),
        P("tensor"),
        P("tensor", "dp"),
    )
    out_specs = (
        P(("dp", "tensor"), None),
        P(("dp", "tensor"), None),
        P(("dp", "tensor")),
        P("dp", None, "tensor"),
        P("dp", "tensor"),
        P(("dp", "tensor"), None),
        P(None, "tensor"),
        P("tensor"),
        P(None, ("dp", "tensor")),
        P(("dp", "tensor")),
        P("tensor"),
        P("tensor"),
        P("tensor"),
        P("tensor"),
        P("tensor", "dp"),
    )
    return jax.shard_map(body, mesh=mesh, in_specs=in_specs, out_specs=out_specs, check_vma=False)
```
